32 devices in a mesh: seq: 8 (over z, core), chan: 4 (over y, x).
Axes of the slice: x: 2, y: 2, z: 4, core: 2. Of those that a mesh axis runs over, the one named last changes fastest.
Arguments:
- hyena_in: bfloat16 [2048, 3, 4096], P('seq', None, 'chan'), may hold values from -6 to 6
- prior_kv: bfloat16 [127, 4096], P(None, 'chan'), may hold values from -6 to 6
- filters: float32 [256, 128], P('chan'), may hold values from -0.5 to 0.5
- gain: float32 [4096], replicated, may hold values from 0.5 to 1.5
- w_qkv: bfloat16 [4096, 3, 4096], P('seq', None, 'chan'), may hold values from -0.09375 to 0.09375
- cache_k: bfloat16 [1216, 4096], P('seq', 'chan'), may hold values from -110 to 110
- cache_v: bfloat16 [1216, 4096], P('seq', 'chan'), may hold values from -6 to 6
Outputs:
- attn_out: bfloat16 [2048, 4096], P('seq', 'chan')
The draws below stay inside these ranges and needn't reach their ends.
All inputs are finite; a program needn't handle non-finite values.
Results may differ from the reference program's by a relative error of at most 0.019.
The reference program's roundings to bfloat16 on the way (of `kv_prod`, `hyena_out`, `normed`, `qkv` and `probs`) count: a program that leaves them out, or rounds other values in their place, can miss the bound.
Values may be sent and summed in bfloat16 or wider, within the bound.
No kernel may reach another device: no remote copies, remote signals or barrier semaphores. Data moves between devices by JAX's collectives and lax.ppermute only.
A program may use at most 128 MiB of HBM per device.

```python
import jax
import jax.numpy as jnp
from jax import lax

D = 4096
HEADS = 32
HEAD_DIM = 128
GROUP = 16
TAPS = 128
TOKENS = 2048
CACHE = 1216
FILTERS = 256
HIST = 127


def draw_cache_k(key, part):
    first_key = jax.random.fold_in(key, 0)
    values = jnp.clip(jax.random.normal(first_key, (CACHE, D), jnp.float32), -6.0, 6.0)
    return values.astype(jnp.bfloat16)


def level_of(own_key, extent, cuts, smallest, top_value):
    def one(dim, shards_of):
        steps = jax.random.uniform(jax.random.fold_in(jax.random.fold_in(own_key, 6), dim), (shards_of,), jnp.float32, smallest / len(cuts), top_value / len(cuts))
        return jnp.repeat(jnp.exp(steps), extent[dim] // shards_of).reshape((-1,) + (1,) * (len(extent) - dim - 1))

    factor_of = one(*cuts[0])
    for cut in cuts[1:]:
        factor_of = factor_of * one(*cut)
    return factor_of


def noise(rng, dims, scale, most, shards=(), kind=jnp.bfloat16):
    level = level_of(rng, dims, shards, -0.22, 0.18) if shards else 1.0
    array = jax.random.normal(rng, dims, jnp.float32) * scale * level
    return jnp.minimum(jnp.maximum(array, -most), most).astype(kind)


def setup_inputs(seed: int = 0) -> dict:
    seeds = jax.random.split(jax.random.key(seed), 8)
    return {
        "hyena_in": noise(seeds[0], (TOKENS, 3, D), 1.0, 6.0, ((0, 8), (2, 4))),
        "prior_kv": noise(seeds[1], (HIST, D), 1.0, 6.0, ((1, 4),)),
        "filters": noise(seeds[2], (FILTERS, TAPS), TAPS ** -0.5, 0.5, ((0, 4),), jnp.float32),
        "gain": jnp.clip(1.0 + 0.1 * jax.random.normal(seeds[3], (D,), jnp.float32), 0.5, 1.5),
        "w_qkv": noise(seeds[4], (D, 3, D), D ** -0.5, 0.09375, ((0, 8), (2, 4))),
        "cache_k": draw_cache_k(jax.random.fold_in(seeds[7], 71), 0),
        "cache_v": noise(seeds[6], (CACHE, D), 1.0, 6.0, ((0, 8), (1, 4))),
    }


def reference(hyena_in, prior_kv, filters, gain, w_qkv, cache_k, cache_v):
    stream_q = hyena_in[:, 0].astype(jnp.float32)
    kv_prod = (hyena_in[:, 1].astype(jnp.float32) * hyena_in[:, 2].astype(jnp.float32)).astype(jnp.bfloat16)
    extended = jnp.concatenate([prior_kv, kv_prod], axis=0).astype(jnp.float32)
    tap_table = jnp.repeat(filters, GROUP, axis=0).T

    def add_tap(tap_index, total):
        offset = (TAPS - 1 - tap_index).astype(jnp.int32)
        window = lax.dynamic_slice_in_dim(extended, offset, TOKENS, 0)
        coeff = lax.dynamic_index_in_dim(tap_table, tap_index.astype(jnp.int32), 0, keepdims=True)
        return total + coeff * window
    conv = lax.fori_loop(0, TAPS, add_tap, jnp.zeros((TOKENS, D), jnp.float32))
    hyena_out = (stream_q * conv).astype(jnp.bfloat16)
    as_float = hyena_out.astype(jnp.float32)
    mean_sq = lax.optimization_barrier(jnp.mean(as_float * as_float, axis=-1, keepdims=True))
    normed = (as_float * lax.rsqrt(mean_sq + 1e-06) * gain[None, :]).astype(jnp.bfloat16)
    qkv = jnp.dot(normed, w_qkv.reshape(D, 3 * D), preferred_element_type=jnp.float32).astype(jnp.bfloat16)
    qkv = qkv.reshape(TOKENS, 3, D)
    queries = jnp.moveaxis(qkv[:, 0].reshape(TOKENS, HEADS, HEAD_DIM), 1, 0)
    keys_all = jnp.concatenate([cache_k, qkv[:, 1]], axis=0).reshape(CACHE + TOKENS, HEADS, HEAD_DIM)
    vals_all = jnp.concatenate([cache_v, qkv[:, 2]], axis=0).reshape(CACHE + TOKENS, HEADS, HEAD_DIM)
    keys_all = jnp.moveaxis(keys_all, 1, 0)
    vals_all = jnp.moveaxis(vals_all, 1, 0)
    query_pos = jnp.arange(TOKENS, dtype=jnp.int32)
    key_pos = jnp.concatenate([jnp.full((CACHE,), -1, jnp.int32), jnp.arange(TOKENS, dtype=jnp.int32)])
    visible = key_pos[None, :] <= query_pos[:, None]
    scale = 1.0 / HEAD_DIM ** 0.5

    def one_head(operands):
        head_q, head_k, head_v = operands
        scores = jnp.dot(head_q, head_k.T, preferred_element_type=jnp.float32) * scale
        scores = jnp.where(visible, scores, jnp.float32(-1e+30))
        top = lax.optimization_barrier(jnp.max(scores, axis=-1, keepdims=True))
        weights = jnp.where(visible, jnp.exp(scores - top), jnp.float32(0.0))
        probs = weights.astype(jnp.bfloat16)
        summed = jnp.dot(probs, head_v, preferred_element_type=jnp.float32)
        return summed / lax.optimization_barrier(jnp.sum(weights, axis=-1, keepdims=True))
    result = lax.map(one_head, (queries, keys_all, vals_all))
    return jnp.moveaxis(result, 0, 1).reshape(TOKENS, D).astype(jnp.bfloat16)
```

```python
import functools

import jax
import jax.numpy as jnp
from jax import lax
from jax.experimental import pallas as pl
from jax.experimental.pallas import tpu as pltpu
from jax.sharding import PartitionSpec as P

D = 4096
HEADS = 32
HEAD = D // HEADS
LANES = 128
BF16 = jnp.bfloat16
F32 = jnp.float32
VMEM_LIMIT = 56 * 1024 * 1024


def whole(shape):
    return pl.BlockSpec(shape, lambda *_: (0,) * len(shape))


def conv_kernel(group, hin_ref, halo_ref, taps_ref, out_ref):
    taps = taps_ref[...]
    count = taps.shape[0]
    width = taps.shape[1]
    kv = (hin_ref[1].astype(F32) * hin_ref[2].astype(F32)).astype(BF16)
    ext = jnp.concatenate([halo_ref[...], kv], axis=0)
    rows = kv.shape[0]
    blocks = rows // width
    windows = jnp.concatenate(
        [ext[b * width : (b + 2) * width] for b in range(blocks)], axis=1
    )
    high = taps.astype(BF16)
    low = (taps - high.astype(F32)).astype(BF16)
    source = lax.broadcasted_iota(jnp.int32, (width, 2 * width), 0)
    column = lax.broadcasted_iota(jnp.int32, (width, 2 * width), 1)
    flip = jnp.where(source + column == width, 1.0, 0.0).astype(BF16)
    total = None
    for part in (high, low):
        first = jnp.dot(part, flip, preferred_element_type=F32)
        toeplitz = jnp.concatenate(
            [
                pltpu.roll(
                    jnp.broadcast_to(first[g : g + 1], (width, 2 * width)),
                    0,
                    1,
                    stride=1,
                    stride_axis=0,
                ).astype(BF16)
                for g in range(count)
            ],
            axis=0,
        )
        product = jnp.dot(toeplitz, windows, preferred_element_type=F32)
        total = product if total is None else total + product
    owner = lax.broadcasted_iota(jnp.int32, (width, blocks * LANES), 1) % LANES // group
    conv = total[:width]
    for g in range(1, count):
        conv = jnp.where(owner == g, total[g * width : (g + 1) * width], conv)
    query = hin_ref[0].astype(F32)
    for b in range(blocks):
        piece = query[b * width : (b + 1) * width] * conv[:, b * LANES : (b + 1) * LANES]
        out_ref[b * width : (b + 1) * width, :] = piece.astype(BF16)


def hyena(hin, halo, filters):
    _, rows, width = hin.shape
    taps = filters.shape[1]
    group = width // filters.shape[0]
    per_tile = LANES // group
    return pl.pallas_call(
        functools.partial(conv_kernel, group),
        grid=(width // LANES,),
        in_specs=[
            pl.BlockSpec((3, rows, LANES), lambda i: (0, 0, i)),
            pl.BlockSpec((taps, LANES), lambda i: (0, i)),
            pl.BlockSpec((per_tile, taps), lambda i: (i, 0)),
        ],
        out_specs=pl.BlockSpec((rows, LANES), lambda i: (0, i)),
        out_shape=jax.ShapeDtypeStruct((rows, width), BF16),
        compiler_params=pltpu.CompilerParams(vmem_limit_bytes=VMEM_LIMIT),
        name="hyena_filters",
    )(hin, halo, filters)


def norm_kernel(place_ref, own_ref, x_ref, y_ref, d0_ref, d1_ref, gain_ref, out_ref):
    chan = place_ref[0]
    half = d0_ref.shape[0]
    rows = own_ref.shape[0]
    for part in range(rows // half):
        band = pl.ds(part * half, half)
        diag_ref = (d0_ref, d1_ref)[part]
        parts = [
            own_ref[band, :].astype(F32),
            x_ref[band, :].astype(F32),
            y_ref[band, :].astype(F32),
            diag_ref[...].astype(F32),
        ]
        total = sum(jnp.sum(p * p, axis=-1, keepdims=True) for p in parts)
        factor = lax.rsqrt(total / D + 1e-6)
        for m, p in enumerate(parts):
            where = chan ^ m
            out_ref[where, band, :] = (p * factor * gain_ref[where]).astype(BF16)


def norm(place, own, from_x, from_y, diag0, diag1, gain):
    rows, width = own.shape
    half = diag0.shape[0]
    return pl.pallas_call(
        norm_kernel,
        in_specs=[pl.BlockSpec(memory_space=pltpu.SMEM)]
        + [whole((rows, width))] * 3
        + [whole((half, width))] * 2
        + [whole((4, 1, width))],
        out_specs=whole((4, rows, width)),
        out_shape=jax.ShapeDtypeStruct((4, rows, width), BF16),
        compiler_params=pltpu.CompilerParams(vmem_limit_bytes=VMEM_LIMIT),
        name="norm",
    )(place, own, from_x, from_y, diag0, diag1, gain)


def project_kernel(shift, last, zs, place_ref, *refs):
    normed, (own_ref, sib_ref), rest = refs[:zs], refs[zs : zs + 2], refs[zs + 2 :]
    before_ref = rest[0] if len(rest) == 2 else None
    out_ref = rest[-1]
    core = place_ref[2]
    block = lax.rem(place_ref[1] + zs - shift, zs)
    rows = normed[0].shape[1]
    depth = normed[0].shape[2] // 2
    cols = own_ref.shape[1]
    for j in range(zs):
        for p in range(3):
            total = None
            for k, w_ref in enumerate((own_ref, sib_ref)):
                at = pl.multiple_of((core ^ k) * depth, depth)
                left = normed[j][block, :, pl.ds(at, depth)]
                right = w_ref[p * depth : (p + 1) * depth, :]
                term = jnp.dot(left, right, preferred_element_type=F32)
                total = term if total is None else total + term
            if before_ref is not None:
                total = total + before_ref[j, :, p * cols : (p + 1) * cols]
            out_ref[j, :, p * cols : (p + 1) * cols] = total.astype(out_ref.dtype)


def project(shift, last, place, normed, own, sib, before):
    zs = len(normed)
    rows = normed[0].shape[1]
    cols = own.shape[1]
    out = (zs, rows, 3 * cols)
    args = [place, *normed, own, sib] + ([] if before is None else [before])
    return pl.pallas_call(
        functools.partial(project_kernel, shift, last, zs),
        in_specs=[pl.BlockSpec(memory_space=pltpu.SMEM)] + [whole(a.shape) for a in args[1:]],
        out_specs=whole(out),
        out_shape=jax.ShapeDtypeStruct(out, BF16 if last else F32),
        compiler_params=pltpu.CompilerParams(vmem_limit_bytes=VMEM_LIMIT),
        name="project",
    )(*args)


NT = (((1,), (1,)), ((), ()))


def attend_kernel(place_ref, mine_ref, sib_ref, ck_ref, cv_ref, out_ref):
    z, core = place_ref[1], place_ref[2]
    zs, rows, _ = mine_ref.shape
    cols = ck_ref.shape[1]
    heads = cols // HEAD
    factor = 1.4426950408889634 / HEAD**0.5
    low = -1e30
    row = lax.broadcasted_iota(jnp.int32, (rows, rows), 0)
    col = lax.broadcasted_iota(jnp.int32, (rows, rows), 1)
    causal = col <= row
    for zq in range(zs):
        at = [lax.rem(z + zs - b, zs) for b in range(zq + 1)]
        for h in range(heads):
            q = mine_ref[at[zq], :, h * HEAD : (h + 1) * HEAD]
            kcol = slice(cols + h * HEAD, cols + (h + 1) * HEAD)
            vcol = slice(2 * cols + h * HEAD, 2 * cols + (h + 1) * HEAD)
            kcol_sib = slice(h * HEAD, (h + 1) * HEAD)
            vcol_sib = slice(cols + h * HEAD, cols + (h + 1) * HEAD)
            hcol = slice(h * HEAD, (h + 1) * HEAD)
            scores = [lax.dot_general(q, ck_ref[:, hcol], NT, preferred_element_type=F32)]
            values = [lambda: cv_ref[:, hcol]]
            for b in range(zq + 1):
                s = lax.dot_general(q, mine_ref[at[b], :, kcol], NT, preferred_element_type=F32)
                if b == zq:
                    s = jnp.where(causal, s, low)
                scores.append(s)
                values.append(lambda b=b: mine_ref[at[b], :, vcol])
                s = lax.dot_general(q, sib_ref[at[b], :, kcol_sib], NT, preferred_element_type=F32)
                if b == zq:
                    s = jnp.where(core == 1, s, low)
                scores.append(s)
                values.append(lambda b=b: sib_ref[at[b], :, vcol_sib])
            top = functools.reduce(
                jnp.maximum, [jnp.max(s, axis=-1, keepdims=True) for s in scores]
            )
            top = top * factor
            total, summed = None, None
            for s, value in zip(scores, values):
                weights = jnp.exp2(s * factor - top)
                part = jnp.sum(weights, axis=-1, keepdims=True)
                added = jnp.dot(weights.astype(BF16), value(), preferred_element_type=F32)
                total = part if total is None else total + part
                summed = added if summed is None else summed + added
            out_ref[zq, :, hcol] = (summed / total).astype(BF16)


def attend(place, mine, sib, cache_k, cache_v):
    zs, rows, _ = mine.shape
    out = (zs, rows, cache_k.shape[1])
    args = (mine, sib, cache_k, cache_v)
    return pl.pallas_call(
        attend_kernel,
        in_specs=[pl.BlockSpec(memory_space=pltpu.SMEM)] + [whole(a.shape) for a in args],
        out_specs=whole(out),
        out_shape=jax.ShapeDtypeStruct(out, BF16),
        compiler_params=pltpu.CompilerParams(vmem_limit_bytes=VMEM_LIMIT),
        name="attend",
    )(place, *args)


def join_kernel(place_ref, *refs):
    pieces, out_ref = refs[:-1], refs[-1]
    zs = len(pieces)
    cols = pieces[0].shape[1]
    for r, piece in enumerate(pieces):
        at = lax.rem(place_ref[1] + zs - r, zs) * cols
        out_ref[:, pl.ds(pl.multiple_of(at, cols), cols)] = piece[...]


def join(place, pieces):
    rows, cols = pieces[0].shape
    out = (rows, cols * len(pieces))
    return pl.pallas_call(
        join_kernel,
        in_specs=[pl.BlockSpec(memory_space=pltpu.SMEM)] + [whole(p.shape) for p in pieces],
        out_specs=whole(out),
        out_shape=jax.ShapeDtypeStruct(out, BF16),
        name="join",
    )(place, *pieces)


def shift_z(value, steps, zs):
    pairs = [(2 * a + k, 2 * ((a + steps) % zs) + k) for a in range(zs) for k in range(2)]
    return lax.ppermute(value, "seq", pairs)


def swap_core(value, zs):
    return lax.ppermute(value, "seq", [(2 * a + k, 2 * a + 1 - k) for a in range(zs) for k in range(2)])


def swap_chan(value, bit):
    return lax.ppermute(value, "chan", [(c, c ^ bit) for c in range(4)])


def fast_body(hyena_in, prior_kv, filters, gain, w_qkv, cache_k, cache_v):
    rows, _, width = hyena_in.shape
    seqs = lax.axis_size("seq")
    zs = seqs // 2
    taps = filters.shape[1]
    cols = width // zs
    my_seq = lax.axis_index("seq")
    z, core = my_seq // 2, my_seq % 2
    chan = lax.axis_index("chan")
    place = jnp.stack([chan, z, core]).astype(jnp.int32)

    hin = jnp.transpose(hyena_in, (1, 0, 2))
    tail = (hin[1, rows - taps :].astype(F32) * hin[2, rows - taps :].astype(F32)).astype(BF16)
    halo = lax.ppermute(tail, "seq", [(s, s + 1) for s in range(seqs - 1)])
    halo = jnp.where(my_seq == 0, jnp.pad(prior_kv, ((taps - prior_kv.shape[0], 0), (0, 0))), halo)

    depth = w_qkv.shape[0]
    w_t = jnp.transpose(w_qkv, (1, 0, 2)).reshape(3 * depth, width)
    weights, caches = [], []
    for r in range(zs):
        at = (z + r) % zs * cols
        parcel = jnp.concatenate(
            [lax.dynamic_slice_in_dim(a, at, cols, 1) for a in (w_t, cache_k, cache_v)], axis=0
        )
        if r:
            parcel = shift_z(parcel, r, zs)
        both = (parcel, swap_core(parcel, zs))
        weights.append(both)
        caches += [p[3 * depth :] for p in both]
    crow = cache_k.shape[0]
    ck = jnp.concatenate([c[:crow] for c in caches], axis=0)
    cv = jnp.concatenate([c[crow:] for c in caches], axis=0)

    own = hyena(hin, halo, filters)
    gain4 = gain.reshape(4, 1, width)
    normed = []
    half = rows // 2
    for j in range(zs):
        from_x, from_y = swap_chan(own, 1), swap_chan(own, 2)
        diag0 = swap_chan(from_x[:half], 2)
        diag1 = swap_chan(from_y[half:], 1)
        normed.append(norm(place, own, from_x, from_y, diag0, diag1, gain4))
        if j + 1 < zs:
            own = shift_z(own, 1, zs)

    total = None
    for r in range(zs):
        total = project(r, r == zs - 1, place, normed, *weights[r], total)
    sib = swap_core(total[:, :, cols:], zs)
    out = attend(place, total, sib, ck, cv)
    pieces = []
    for r in range(zs):
        piece = lax.dynamic_index_in_dim(out, (z + r) % zs, 0, keepdims=False)
        pieces.append(shift_z(piece, r, zs) if r else piece)
    return join(place, pieces)


def shifted(value, axis, steps):
    count = lax.axis_size(axis)
    leading, last = (max(0, -steps), min(count, count - steps))
    return lax.ppermute(value, axis, [(source, source + steps) for source in range(leading, last)])


def body(hyena_in, prior_kv, filters, gain, w_qkv, cache_k, cache_v):
    rows_dev = hyena_in.shape[0]
    width = hyena_in.shape[2]
    history = prior_kv.shape[0]
    tap_count = filters.shape[1]
    head_size = D // HEADS
    heads_dev = width // head_size
    cache_rows = cache_k.shape[0]
    stride = cache_rows + rows_dev
    my_index = lax.axis_index("seq")
    stream_q = hyena_in[:, 0].astype(jnp.float32)
    kv_prod = (hyena_in[:, 1].astype(jnp.float32) * hyena_in[:, 2].astype(jnp.float32)).astype(
        jnp.bfloat16
    )
    before = shifted(kv_prod[rows_dev - history :], "seq", 1)
    before = jnp.where(my_index == 0, prior_kv, before)
    extended = jnp.concatenate([before, kv_prod], axis=0).astype(jnp.float32)
    tap_table = jnp.repeat(filters, width // filters.shape[0], axis=0).T

    def add_tap(tap_index, total):
        offset = (tap_count - 1 - tap_index).astype(jnp.int32)
        window = lax.dynamic_slice_in_dim(extended, offset, rows_dev, 0)
        coeff = lax.dynamic_index_in_dim(tap_table, tap_index.astype(jnp.int32), 0, keepdims=True)
        return total + coeff * window

    conv = lax.fori_loop(0, tap_count, add_tap, jnp.zeros((rows_dev, width), jnp.float32))
    hyena_out = (stream_q * conv).astype(jnp.bfloat16)
    whole = lax.all_gather(hyena_out, "chan", axis=1, tiled=True)
    as_float = whole.astype(jnp.float32)
    mean_sq = jnp.mean(as_float * as_float, axis=-1, keepdims=True)
    normed = (as_float * lax.rsqrt(mean_sq + 1e-06) * gain[None, :]).astype(jnp.bfloat16)
    piece = lax.all_gather(w_qkv, "seq", axis=0, tiled=True)
    flat_piece = piece.reshape(piece.shape[0], 3 * width)
    projected = jnp.dot(normed, flat_piece, preferred_element_type=jnp.float32)
    qkv = projected.astype(jnp.bfloat16).reshape(rows_dev, 3, width)
    scale = 1.0 / head_size**0.5
    keys_local = jnp.concatenate([cache_k, qkv[:, 1]], axis=0)
    vals_local = jnp.concatenate([cache_v, qkv[:, 2]], axis=0)
    head_q = qkv[:, 0].reshape(rows_dev, heads_dev, head_size)
    query_pos = my_index * rows_dev + jnp.arange(rows_dev, dtype=jnp.int32)
    run_max = jnp.full((heads_dev, rows_dev), -1e30, jnp.float32)
    key_piece = lax.all_gather(keys_local, "seq", axis=0, tiled=True)
    val_piece = lax.all_gather(vals_local, "seq", axis=0, tiled=True)
    count = key_piece.shape[0]
    row_ids = jnp.arange(count, dtype=jnp.int32)
    source = row_ids // stride
    within = row_ids % stride
    key_pos = jnp.where(within < cache_rows, -1, source * rows_dev + within - cache_rows)
    visible = (key_pos[None, :] <= query_pos[:, None])[None]
    scores = (
        jnp.einsum(
            "qhd,khd->hqk",
            head_q,
            key_piece.reshape(count, heads_dev, head_size),
            preferred_element_type=jnp.float32,
        )
        * scale
    )
    scores = jnp.where(visible, scores, jnp.float32(-1e30))
    new_max = jnp.maximum(run_max, jnp.max(scores, axis=-1))
    weights = jnp.where(visible, jnp.exp(scores - new_max[..., None]), jnp.float32(0.0))
    new_sum = jnp.sum(weights, axis=-1)
    probs = weights.astype(jnp.bfloat16)
    added = jnp.einsum(
        "hqk,khd->hqd",
        probs,
        val_piece.reshape(count, heads_dev, head_size),
        preferred_element_type=jnp.float32,
    )
    result = jnp.transpose(added / new_sum[..., None], (1, 0, 2))
    return result.reshape(rows_dev, width).astype(jnp.bfloat16)


def solution(mesh):
    sizes = mesh.shape
    paired = sizes["chan"] == 4 and HEADS // sizes["chan"] == sizes["seq"]
    return jax.shard_map(
        fast_body if paired else body,
        mesh=mesh,
        in_specs=(
            P("seq", None, "chan"),
            P(None, "chan"),
            P("chan", None),
            P(),
            P("seq", None, "chan"),
            P("seq", "chan"),
            P("seq", "chan"),
        ),
        out_specs=P("seq", "chan"),
        check_vma=False,
    )
```

```python
import functools

import jax
import jax.numpy as jnp
from jax import lax
from jax.experimental import pallas as pl
from jax.experimental.pallas import tpu as pltpu
from jax.sharding import PartitionSpec as P

D = 4096
HEADS = 32
HEAD = D // HEADS
LANES = 128
BF16 = jnp.bfloat16
F32 = jnp.float32
VMEM_LIMIT = 56 * 1024 * 1024


def whole(shape):
    return pl.BlockSpec(shape, lambda *_: (0,) * len(shape))


def conv_kernel(group, hin_ref, halo_ref, taps_ref, out_ref):
    taps = taps_ref[...]
    count = taps.shape[0]
    width = taps.shape[1]
    kv = (hin_ref[1].astype(F32) * hin_ref[2].astype(F32)).astype(BF16)
    ext = jnp.concatenate([halo_ref[...], kv], axis=0)
    rows = kv.shape[0]
    blocks = rows // width
    windows = jnp.concatenate(
        [ext[b * width : (b + 2) * width] for b in range(blocks)], axis=1
    )
    high = taps.astype(BF16)
    low = (taps - high.astype(F32)).astype(BF16)
    source = lax.broadcasted_iota(jnp.int32, (width, 2 * width), 0)
    column = lax.broadcasted_iota(jnp.int32, (width, 2 * width), 1)
    flip = jnp.where(source + column == width, 1.0, 0.0).astype(BF16)
    total = None
    for part in (high, low):
        first = jnp.dot(part, flip, preferred_element_type=F32)
        toeplitz = jnp.concatenate(
            [
                pltpu.roll(
                    jnp.broadcast_to(first[g : g + 1], (width, 2 * width)),
                    0,
                    1,
                    stride=1,
                    stride_axis=0,
                ).astype(BF16)
                for g in range(count)
            ],
            axis=0,
        )
        product = jnp.dot(toeplitz, windows, preferred_element_type=F32)
        total = product if total is None else total + product
    owner = lax.broadcasted_iota(jnp.int32, (width, blocks * LANES), 1) % LANES // group
    conv = total[:width]
    for g in range(1, count):
        conv = jnp.where(owner == g, total[g * width : (g + 1) * width], conv)
    query = hin_ref[0].astype(F32)
    for b in range(blocks):
        piece = query[b * width : (b + 1) * width] * conv[:, b * LANES : (b + 1) * LANES]
        out_ref[b * width : (b + 1) * width, :] = piece.astype(BF16)


def hyena(hin, halo, filters):
    _, rows, width = hin.shape
    taps = filters.shape[1]
    group = width // filters.shape[0]
    per_tile = LANES // group
    return pl.pallas_call(
        functools.partial(conv_kernel, group),
        grid=(width // LANES,),
        in_specs=[
            pl.BlockSpec((3, rows, LANES), lambda i: (0, 0, i)),
            pl.BlockSpec((taps, LANES), lambda i: (0, i)),
            pl.BlockSpec((per_tile, taps), lambda i: (i, 0)),
        ],
        out_specs=pl.BlockSpec((rows, LANES), lambda i: (0, i)),
        out_shape=jax.ShapeDtypeStruct((rows, width), BF16),
        compiler_params=pltpu.CompilerParams(vmem_limit_bytes=VMEM_LIMIT),
        name="hyena_filters",
    )(hin, halo, filters)


def norm_kernel(half, place_ref, own_ref, x_ref, y_ref, d0_ref, d1_ref, gain_ref, *rest):
    out_ref = rest[-1]
    chan = place_ref[0]
    step = pl.program_id(0)
    diag = jnp.where(step < half, d0_ref[...], d1_ref[...])
    parts = [r.astype(F32) for r in (own_ref[...], x_ref[...], y_ref[...], diag)]
    total = sum(jnp.sum(p * p, axis=-1, keepdims=True) for p in parts)
    factor = lax.rsqrt(total / D + 1e-6)
    for m, p in enumerate(parts):
        where = chan ^ m
        out_ref[0, where] = (p * factor * gain_ref[where]).astype(BF16)


def norm(place, j, zs, own, from_x, from_y, diag0, diag1, gain, buffer):
    rows, width = own.shape
    step = min(64, rows // 2)
    half = rows // 2 // step
    band = pl.BlockSpec((step, width), lambda i: (i, 0))
    args = [place, own, from_x, from_y, diag0, diag1, gain]
    specs = [
        pl.BlockSpec(memory_space=pltpu.SMEM),
        band,
        band,
        band,
        pl.BlockSpec((step, width), lambda i: (jnp.minimum(i, half - 1), 0)),
        pl.BlockSpec((step, width), lambda i: (jnp.maximum(i - half, 0), 0)),
        whole((4, 1, width)),
    ]
    aliases = {}
    if buffer is not None:
        aliases = {len(args): 0}
        args.append(buffer)
        specs.append(pl.BlockSpec(memory_space=pl.ANY))
    return pl.pallas_call(
        functools.partial(norm_kernel, half),
        grid=(2 * half,),
        in_specs=specs,
        out_specs=pl.BlockSpec((1, 4, step, width), lambda i: (j, 0, i, 0)),
        out_shape=jax.ShapeDtypeStruct((zs, 4, rows, width), BF16),
        input_output_aliases=aliases,
        compiler_params=pltpu.CompilerParams(vmem_limit_bytes=VMEM_LIMIT),
        name="norm",
    )(*args)


def project_kernel(zs, place_ref, normed_ref, *refs):
    own, sib, out_ref = refs[:zs], refs[zs : 2 * zs], refs[-1]
    z, core = place_ref[1], place_ref[2]
    depth, cols = own[0].shape
    total = None
    for shift in range(zs):
        block = lax.rem(z + zs - shift, zs)
        for k, w_ref in enumerate((own[shift], sib[shift])):
            at = pl.multiple_of((core ^ k) * depth, depth)
            left = normed_ref[0, block, :, pl.ds(at, depth)]
            term = jnp.dot(left, w_ref[...], preferred_element_type=F32)
            total = term if total is None else total + term
    out_ref[0] = total.astype(BF16)


def project(place, normed, own, sib):
    zs, parts, rows, width = normed.shape
    cols = own[0].shape[1]
    return pl.pallas_call(
        functools.partial(project_kernel, zs),
        grid=(zs,),
        in_specs=[
            pl.BlockSpec(memory_space=pltpu.SMEM),
            pl.BlockSpec((1, parts, rows, width), lambda j: (j, 0, 0, 0)),
        ]
        + [whole(w.shape) for w in (*own, *sib)],
        out_specs=pl.BlockSpec((1, rows, cols), lambda j: (j, 0, 0)),
        out_shape=jax.ShapeDtypeStruct((zs, rows, cols), BF16),
        compiler_params=pltpu.CompilerParams(vmem_limit_bytes=VMEM_LIMIT),
        name="project",
    )(place, normed, *own, *sib)


NT = (((1,), (1,)), ((), ()))


def attend_kernel(shifts, place_ref, q_ref, k_ref, v_ref, ks_ref, vs_ref, c_ref, cs_ref, out_ref):
    z, core = place_ref[1], place_ref[2]
    zs, rows, cols = k_ref.shape
    heads = cols // HEAD
    factor = 1.4426950408889634 / HEAD**0.5
    low = -1e30
    row = lax.broadcasted_iota(jnp.int32, (rows, rows), 0)
    col = lax.broadcasted_iota(jnp.int32, (rows, rows), 1)
    causal = col <= row
    step = pl.program_id(0)
    shift = jnp.int32(shifts[0])
    for i, s in enumerate(shifts):
        shift = jnp.where(step == i, s, shift)
    block = lax.rem(z + shift, zs)

    def one(zq):
        at = [lax.rem(z + zs - b, zs) for b in range(zq + 1)]
        for h in range(heads):
            hcol = slice(h * HEAD, (h + 1) * HEAD)
            vcol = slice(cols + h * HEAD, cols + (h + 1) * HEAD)
            q = q_ref[0, :, hcol]
            keys = [(c_ref[:, hcol], c_ref[:, vcol], None), (cs_ref[:, hcol], cs_ref[:, vcol], None)]
            for b in range(zq + 1):
                keys.append((k_ref[at[b], :, hcol], v_ref[at[b], :, hcol], causal if b == zq else None))
                keys.append((ks_ref[at[b], :, hcol], vs_ref[at[b], :, hcol], core == 1 if b == zq else None))
            scores = []
            for key, _, mask in keys:
                s = lax.dot_general(q, key, NT, preferred_element_type=F32)
                scores.append(s if mask is None else jnp.where(mask, s, low))
            top = functools.reduce(jnp.maximum, [jnp.max(s, axis=-1, keepdims=True) for s in scores])
            top = top * factor
            total, summed = None, None
            for s, (_, value, _) in zip(scores, keys):
                weights = jnp.exp2(s * factor - top)
                part = jnp.sum(weights, axis=-1, keepdims=True)
                added = jnp.dot(weights.astype(BF16), value, preferred_element_type=F32)
                total = part if total is None else total + part
                summed = added if summed is None else summed + added
            out_ref[0, :, hcol] = (summed / total).astype(BF16)

    for zq in range(zs):
        pl.when(block == zq)(functools.partial(one, zq))


def attend(shifts, place, q, k, v, k_sib, v_sib, cache, cache_sib):
    zs, rows, cols = k.shape

    def slab(i, place_ref):
        shift = jnp.int32(shifts[0])
        for n, s in enumerate(shifts):
            shift = jnp.where(i == n, s, shift)
        return lax.rem(zs - shift, zs), 0, 0

    args = (k, v, k_sib, v_sib, cache, cache_sib)
    return pl.pallas_call(
        functools.partial(attend_kernel, shifts),
        grid_spec=pltpu.PrefetchScalarGridSpec(
            num_scalar_prefetch=1,
            grid=(len(shifts),),
            in_specs=[pl.BlockSpec((1, rows, cols), slab)] + [whole(a.shape) for a in args],
            out_specs=pl.BlockSpec((1, rows, cols), lambda i, place_ref: (i, 0, 0)),
        ),
        out_shape=jax.ShapeDtypeStruct((len(shifts), rows, cols), BF16),
        compiler_params=pltpu.CompilerParams(vmem_limit_bytes=VMEM_LIMIT),
        name="attend",
    )(place, q, *args)


def join_kernel(place_ref, *refs):
    pieces, out_ref = refs[:-1], refs[-1]
    zs = len(pieces)
    cols = pieces[0].shape[1]
    for r, piece in enumerate(pieces):
        at = lax.rem(place_ref[1] + zs - r, zs) * cols
        out_ref[:, pl.ds(pl.multiple_of(at, cols), cols)] = piece[...]


def join(place, pieces):
    rows, cols = pieces[0].shape
    out = (rows, cols * len(pieces))
    return pl.pallas_call(
        join_kernel,
        in_specs=[pl.BlockSpec(memory_space=pltpu.SMEM)] + [whole(p.shape) for p in pieces],
        out_specs=whole(out),
        out_shape=jax.ShapeDtypeStruct(out, BF16),
        name="join",
    )(place, *pieces)


def shift_z(value, steps, zs):
    pairs = [(2 * a + k, 2 * ((a + steps) % zs) + k) for a in range(zs) for k in range(2)]
    return lax.ppermute(value, "seq", pairs)


def swap_core(value, zs):
    return lax.ppermute(value, "seq", [(2 * a + k, 2 * a + 1 - k) for a in range(zs) for k in range(2)])


def swap_chan(value, bit):
    return lax.ppermute(value, "chan", [(c, c ^ bit) for c in range(4)])


def after(value, *others):
    return lax.optimization_barrier((value, *others))[0]


def fast_body(hyena_in, prior_kv, filters, gain, w_qkv, cache_k, cache_v):
    rows, _, width = hyena_in.shape
    seqs = lax.axis_size("seq")
    zs = seqs // 2
    taps = filters.shape[1]
    cols = width // zs
    my_seq = lax.axis_index("seq")
    z, core = my_seq // 2, my_seq % 2
    chan = lax.axis_index("chan")
    place = jnp.stack([chan, z, core]).astype(jnp.int32)

    hin = jnp.transpose(hyena_in, (1, 0, 2))
    tail = (hin[1, rows - taps :].astype(F32) * hin[2, rows - taps :].astype(F32)).astype(BF16)
    halo = lax.ppermute(tail, "seq", [(s, s + 1) for s in range(seqs - 1)])
    halo = jnp.where(my_seq == 0, jnp.pad(prior_kv, ((taps - prior_kv.shape[0], 0), (0, 0))), halo)

    w_t = jnp.transpose(w_qkv, (1, 0, 2))

    def parcel(p, r):
        at = (z + r) % zs * cols
        if p == 3:
            return jnp.concatenate(
                [lax.dynamic_slice_in_dim(a, at, cols, 1) for a in (cache_k, cache_v)], axis=1
            )
        return lax.dynamic_slice_in_dim(w_t[p], at, cols, 1)

    order = [(p, r) for p in (1, 0, 3, 2) for r in (2, 1, 3)]
    here = {(p, 0): parcel(p, 0) for p in range(4)}
    sent = []
    for n, (p, r) in enumerate(order):
        value = parcel(p, r)
        if n >= 2:
            value = after(value, sent[n - 2])
        sent.append(shift_z(value, r, zs))
        here[p, r] = sent[-1]
    cache = jnp.concatenate([here[3, r] for r in range(zs)], axis=0)
    cache_sib = swap_core(cache, zs)
    there = {(p, r): swap_core(here[p, r], zs) for p in range(3) for r in range(zs)}

    own = hyena(hin, halo, filters)
    gain4 = gain.reshape(4, 1, width)
    half = rows // 2
    normed = None
    for j in range(zs):
        from_x, from_y = swap_chan(own, 1), swap_chan(own, 2)
        diag0 = swap_chan(from_x[:half], 2)
        diag1 = swap_chan(from_y[half:], 1)
        normed = norm(place, j, zs, own, from_x, from_y, diag0, diag1, gain4, normed)
        if j + 1 < zs:
            own = shift_z(own, 1, zs)

    q, k, v = [
        project(place, normed, [here[p, r] for r in range(zs)], [there[p, r] for r in range(zs)])
        for p in range(3)
    ]
    k_sib, v_sib = swap_core(k, zs), swap_core(v, zs)
    pieces = {}
    for shifts in ((2,), (1, 3), (0,)):
        out = attend(shifts, place, q, k, v, k_sib, v_sib, cache, cache_sib)
        for i, r in enumerate(shifts):
            pieces[r] = shift_z(out[i], r, zs) if r else out[i]
    return join(place, [pieces[r] for r in range(zs)])


def shifted(value, axis, steps):
    count = lax.axis_size(axis)
    leading, last = (max(0, -steps), min(count, count - steps))
    return lax.ppermute(value, axis, [(source, source + steps) for source in range(leading, last)])


def body(hyena_in, prior_kv, filters, gain, w_qkv, cache_k, cache_v):
    rows_dev = hyena_in.shape[0]
    width = hyena_in.shape[2]
    history = prior_kv.shape[0]
    tap_count = filters.shape[1]
    head_size = D // HEADS
    heads_dev = width // head_size
    cache_rows = cache_k.shape[0]
    stride = cache_rows + rows_dev
    my_index = lax.axis_index("seq")
    stream_q = hyena_in[:, 0].astype(jnp.float32)
    kv_prod = (hyena_in[:, 1].astype(jnp.float32) * hyena_in[:, 2].astype(jnp.float32)).astype(
        jnp.bfloat16
    )
    before = shifted(kv_prod[rows_dev - history :], "seq", 1)
    before = jnp.where(my_index == 0, prior_kv, before)
    extended = jnp.concatenate([before, kv_prod], axis=0).astype(jnp.float32)
    tap_table = jnp.repeat(filters, width // filters.shape[0], axis=0).T

    def add_tap(tap_index, total):
        offset = (tap_count - 1 - tap_index).astype(jnp.int32)
        window = lax.dynamic_slice_in_dim(extended, offset, rows_dev, 0)
        coeff = lax.dynamic_index_in_dim(tap_table, tap_index.astype(jnp.int32), 0, keepdims=True)
        return total + coeff * window

    conv = lax.fori_loop(0, tap_count, add_tap, jnp.zeros((rows_dev, width), jnp.float32))
    hyena_out = (stream_q * conv).astype(jnp.bfloat16)
    whole = lax.all_gather(hyena_out, "chan", axis=1, tiled=True)
    as_float = whole.astype(jnp.float32)
    mean_sq = jnp.mean(as_float * as_float, axis=-1, keepdims=True)
    normed = (as_float * lax.rsqrt(mean_sq + 1e-06) * gain[None, :]).astype(jnp.bfloat16)
    piece = lax.all_gather(w_qkv, "seq", axis=0, tiled=True)
    flat_piece = piece.reshape(piece.shape[0], 3 * width)
    projected = jnp.dot(normed, flat_piece, preferred_element_type=jnp.float32)
    qkv = projected.astype(jnp.bfloat16).reshape(rows_dev, 3, width)
    scale = 1.0 / head_size**0.5
    keys_local = jnp.concatenate([cache_k, qkv[:, 1]], axis=0)
    vals_local = jnp.concatenate([cache_v, qkv[:, 2]], axis=0)
    head_q = qkv[:, 0].reshape(rows_dev, heads_dev, head_size)
    query_pos = my_index * rows_dev + jnp.arange(rows_dev, dtype=jnp.int32)
    run_max = jnp.full((heads_dev, rows_dev), -1e30, jnp.float32)
    key_piece = lax.all_gather(keys_local, "seq", axis=0, tiled=True)
    val_piece = lax.all_gather(vals_local, "seq", axis=0, tiled=True)
    count = key_piece.shape[0]
    row_ids = jnp.arange(count, dtype=jnp.int32)
    source = row_ids // stride
    within = row_ids % stride
    key_pos = jnp.where(within < cache_rows, -1, source * rows_dev + within - cache_rows)
    visible = (key_pos[None, :] <= query_pos[:, None])[None]
    scores = (
        jnp.einsum(
            "qhd,khd->hqk",
            head_q,
            key_piece.reshape(count, heads_dev, head_size),
            preferred_element_type=jnp.float32,
        )
        * scale
    )
    scores = jnp.where(visible, scores, jnp.float32(-1e30))
    new_max = jnp.maximum(run_max, jnp.max(scores, axis=-1))
    weights = jnp.where(visible, jnp.exp(scores - new_max[..., None]), jnp.float32(0.0))
    new_sum = jnp.sum(weights, axis=-1)
    probs = weights.astype(jnp.bfloat16)
    added = jnp.einsum(
        "hqk,khd->hqd",
        probs,
        val_piece.reshape(count, heads_dev, head_size),
        preferred_element_type=jnp.float32,
    )
    result = jnp.transpose(added / new_sum[..., None], (1, 0, 2))
    return result.reshape(rows_dev, width).astype(jnp.bfloat16)


def solution(mesh):
    sizes = mesh.shape
    paired = sizes["chan"] == 4 and HEADS // sizes["chan"] == sizes["seq"]
    return jax.shard_map(
        fast_body if paired else body,
        mesh=mesh,
        in_specs=(
            P("seq", None, "chan"),
            P(None, "chan"),
            P("chan", None),
            P(),
            P("seq", None, "chan"),
            P("seq", "chan"),
            P("seq", "chan"),
        ),
        out_specs=P("seq", "chan"),
        check_vma=False,
    )
```

```python
import functools

import jax
import jax.numpy as jnp
from jax import lax
from jax.experimental import pallas as pl
from jax.experimental.pallas import tpu as pltpu
from jax.sharding import PartitionSpec as P

D = 4096
HEADS = 32
HEAD = D // HEADS
LANES = 128
PAD = 8
BF16 = jnp.bfloat16
F32 = jnp.float32
MIB = 1024 * 1024


def whole(shape):
    return pl.BlockSpec(shape, lambda *_: (0,) * len(shape))


def conv_kernel(group, hin_ref, halo_ref, taps_ref, out_ref):
    taps = taps_ref[...]
    count = taps.shape[0]
    width = taps.shape[1]
    kv = (hin_ref[1].astype(F32) * hin_ref[2].astype(F32)).astype(BF16)
    ext = jnp.concatenate([halo_ref[...], kv], axis=0)
    rows = kv.shape[0]
    blocks = rows // width
    windows = jnp.concatenate(
        [ext[b * width : (b + 2) * width] for b in range(blocks)], axis=1
    )
    high = taps.astype(BF16)
    low = (taps - high.astype(F32)).astype(BF16)
    source = lax.broadcasted_iota(jnp.int32, (width, 2 * width), 0)
    column = lax.broadcasted_iota(jnp.int32, (width, 2 * width), 1)
    flip = jnp.where(source + column == width, 1.0, 0.0).astype(BF16)
    total = None
    for part in (high, low):
        first = jnp.dot(part, flip, preferred_element_type=F32)
        toeplitz = jnp.concatenate(
            [
                pltpu.roll(
                    jnp.broadcast_to(first[g : g + 1], (width, 2 * width)),
                    0,
                    1,
                    stride=1,
                    stride_axis=0,
                ).astype(BF16)
                for g in range(count)
            ],
            axis=0,
        )
        product = jnp.dot(toeplitz, windows, preferred_element_type=F32)
        total = product if total is None else total + product
    owner = lax.broadcasted_iota(jnp.int32, (width, blocks * LANES), 1) % LANES // group
    conv = total[:width]
    for g in range(1, count):
        conv = jnp.where(owner == g, total[g * width : (g + 1) * width], conv)
    query = hin_ref[0].astype(F32)
    for b in range(blocks):
        piece = query[b * width : (b + 1) * width] * conv[:, b * LANES : (b + 1) * LANES]
        out_ref[b * width : (b + 1) * width, :] = piece.astype(BF16)


def hyena(hin, halo, filters):
    _, rows, width = hin.shape
    taps = filters.shape[1]
    group = width // filters.shape[0]
    per_tile = LANES // group
    return pl.pallas_call(
        functools.partial(conv_kernel, group),
        grid=(width // LANES,),
        in_specs=[
            pl.BlockSpec((3, rows, LANES), lambda i: (0, 0, i)),
            pl.BlockSpec((taps, LANES), lambda i: (0, i)),
            pl.BlockSpec((per_tile, taps), lambda i: (i, 0)),
        ],
        out_specs=pl.BlockSpec((rows, LANES), lambda i: (0, i)),
        out_shape=jax.ShapeDtypeStruct((rows, width), BF16),
        compiler_params=pltpu.CompilerParams(vmem_limit_bytes=12 * MIB),
        name="hyena_filters",
    )(hin, halo, filters)


def norm_kernel(half, place_ref, own_ref, x_ref, y_ref, d0_ref, d1_ref, gain_ref, *rest):
    out_ref = rest[-1]
    chan = place_ref[0]
    step = pl.program_id(0)
    diag = jnp.where(step < half, d0_ref[...], d1_ref[...])
    parts = [r.astype(F32) for r in (own_ref[...], x_ref[...], y_ref[...], diag)]
    total = sum(jnp.sum(p * p, axis=-1, keepdims=True) for p in parts)
    factor = lax.rsqrt(total / D + 1e-6)
    for m, p in enumerate(parts):
        where = chan ^ m
        out_ref[0, where] = (p * factor * gain_ref[where]).astype(BF16)


def norm(place, j, zs, own, from_x, from_y, diag0, diag1, gain, buffer):
    rows, width = own.shape
    step = min(64, rows // 2)
    half = rows // 2 // step
    band = pl.BlockSpec((step, width), lambda i: (i, 0))
    args = [place, own, from_x, from_y, diag0, diag1, gain]
    specs = [
        pl.BlockSpec(memory_space=pltpu.SMEM),
        band,
        band,
        band,
        pl.BlockSpec((step, width), lambda i: (jnp.minimum(i, half - 1), 0)),
        pl.BlockSpec((step, width), lambda i: (jnp.maximum(i - half, 0), 0)),
        whole((4, 1, width)),
    ]
    aliases = {}
    if buffer is not None:
        aliases = {len(args): 0}
        args.append(buffer)
        specs.append(pl.BlockSpec(memory_space=pl.ANY))
    return pl.pallas_call(
        functools.partial(norm_kernel, half),
        grid=(2 * half,),
        in_specs=specs,
        out_specs=pl.BlockSpec((1, 4, step, width), lambda i: (j, 0, i, 0)),
        out_shape=jax.ShapeDtypeStruct((zs, 4, rows, width), BF16),
        input_output_aliases=aliases,
        compiler_params=pltpu.CompilerParams(vmem_limit_bytes=16 * MIB),
        name="norm",
    )(*args)


def project_kernel(zs, place_ref, normed_ref, *refs):
    own, sib, out_ref = refs[:zs], refs[zs : 2 * zs], refs[-1]
    z, core = place_ref[1], place_ref[2]
    depth, cols = own[0].shape
    total = None
    for shift in range(zs):
        block = lax.rem(z + zs - shift, zs)
        for k, w_ref in enumerate((own[shift], sib[shift])):
            at = pl.multiple_of((core ^ k) * depth, depth)
            left = normed_ref[0, block, :, pl.ds(at, depth)]
            term = jnp.dot(left, w_ref[...], preferred_element_type=F32)
            total = term if total is None else total + term
    out_ref[0] = total.astype(BF16)


def project(place, normed, own, sib, part, depth):
    zs, parts, rows, width = normed.shape
    cols = own[0].shape[1]
    weights = pl.BlockSpec((depth, cols), lambda j: (part, 0))
    return pl.pallas_call(
        functools.partial(project_kernel, zs),
        grid=(zs,),
        in_specs=[
            pl.BlockSpec(memory_space=pltpu.SMEM),
            pl.BlockSpec((1, parts, rows, width), lambda j: (j, 0, 0, 0)),
        ]
        + [weights] * (2 * zs),
        out_specs=pl.BlockSpec((1, rows, cols), lambda j: (j, 0, 0)),
        out_shape=jax.ShapeDtypeStruct((zs, rows, cols), BF16),
        compiler_params=pltpu.CompilerParams(vmem_limit_bytes=24 * MIB),
        name="project",
    )(place, normed, *own, *sib)


NT = (((1,), (1,)), ((), ()))


def attend_kernel(shifts, place_ref, q_ref, k_ref, v_ref, ks_ref, vs_ref, ck_ref, cv_ref, out_ref):
    z, core = place_ref[1], place_ref[2]
    zs, rows, cols = k_ref.shape
    heads = cols // HEAD
    factor = 1.4426950408889634 / HEAD**0.5
    low = -1e30
    row = lax.broadcasted_iota(jnp.int32, (rows, rows), 0)
    col = lax.broadcasted_iota(jnp.int32, (rows, rows), 1)
    causal = col <= row
    step = pl.program_id(0)
    shift = jnp.int32(shifts[0])
    for i, s in enumerate(shifts):
        shift = jnp.where(step == i, s, shift)
    block = lax.rem(z + shift, zs)

    def one(zq):
        at = [lax.rem(z + zs - b, zs) for b in range(zq + 1)]
        for h in range(heads):
            hcol = slice(h * HEAD, (h + 1) * HEAD)
            q = q_ref[0, :, hcol]
            keys = [(ck_ref[:, hcol], cv_ref[:, hcol], None)]
            for b in range(zq + 1):
                keys.append((k_ref[at[b], :, hcol], v_ref[at[b], :, hcol], causal if b == zq else None))
                keys.append((ks_ref[at[b], :, hcol], vs_ref[at[b], :, hcol], core == 1 if b == zq else None))
            scores = []
            for key, _, mask in keys:
                s = lax.dot_general(q, key, NT, preferred_element_type=F32)
                scores.append(s if mask is None else jnp.where(mask, s, low))
            top = functools.reduce(jnp.maximum, [jnp.max(s, axis=-1, keepdims=True) for s in scores])
            top = top * factor
            total, summed = None, None
            for s, (_, value, _) in zip(scores, keys):
                weights = jnp.exp2(s * factor - top)
                part = jnp.sum(weights, axis=-1, keepdims=True)
                added = jnp.dot(weights.astype(BF16), value, preferred_element_type=F32)
                total = part if total is None else total + part
                summed = added if summed is None else summed + added
            out_ref[0, :, hcol] = (summed / total).astype(BF16)

    for zq in range(zs):
        pl.when(block == zq)(functools.partial(one, zq))


def attend(shifts, place, q, k, v, k_sib, v_sib, ck, cv):
    zs, rows, cols = k.shape

    def slab(i, place_ref):
        shift = jnp.int32(shifts[0])
        for n, s in enumerate(shifts):
            shift = jnp.where(i == n, s, shift)
        return lax.rem(zs - shift, zs), 0, 0

    args = (k, v, k_sib, v_sib, ck, cv)
    return pl.pallas_call(
        functools.partial(attend_kernel, shifts),
        grid_spec=pltpu.PrefetchScalarGridSpec(
            num_scalar_prefetch=1,
            grid=(len(shifts),),
            in_specs=[pl.BlockSpec((1, rows, cols), slab)] + [whole(a.shape) for a in args],
            out_specs=pl.BlockSpec((1, rows, cols), lambda i, place_ref: (i, 0, 0)),
        ),
        out_shape=jax.ShapeDtypeStruct((len(shifts), rows, cols), BF16),
        compiler_params=pltpu.CompilerParams(vmem_limit_bytes=32 * MIB),
        name="attend",
    )(place, q, *args)


def pack_kernel(at, crow, *refs):
    parcels, (out_ref, scratch) = refs[:-2], refs[-2:]
    for i, piece in enumerate(parcels):
        band = piece[at : at + crow + PAD].astype(F32)
        scratch[i * crow : (i + 1) * crow, :] = band[:crow]
    out_ref[...] = scratch[...].astype(BF16)


def pack(parcels, at, crow):
    cols = parcels[0].shape[1]
    out = (len(parcels) * crow, cols)
    return pl.pallas_call(
        functools.partial(pack_kernel, at, crow),
        in_specs=[whole(p.shape) for p in parcels],
        out_specs=whole(out),
        out_shape=jax.ShapeDtypeStruct(out, BF16),
        scratch_shapes=[pltpu.VMEM(out, F32)],
        compiler_params=pltpu.CompilerParams(vmem_limit_bytes=24 * MIB),
        name="pack",
    )(*parcels)


def join_kernel(place_ref, *refs):
    pieces, out_ref = refs[:-1], refs[-1]
    zs = len(pieces)
    cols = pieces[0].shape[1]
    for r, piece in enumerate(pieces):
        at = lax.rem(place_ref[1] + zs - r, zs) * cols
        out_ref[:, pl.ds(pl.multiple_of(at, cols), cols)] = piece[...]


def join(place, pieces):
    rows, cols = pieces[0].shape
    out = (rows, cols * len(pieces))
    return pl.pallas_call(
        join_kernel,
        in_specs=[pl.BlockSpec(memory_space=pltpu.SMEM)] + [whole(p.shape) for p in pieces],
        out_specs=whole(out),
        out_shape=jax.ShapeDtypeStruct(out, BF16),
        name="join",
    )(place, *pieces)


def shift_z(value, steps, zs):
    pairs = [(2 * a + k, 2 * ((a + steps) % zs) + k) for a in range(zs) for k in range(2)]
    return lax.ppermute(value, "seq", pairs)


def swap_core(value, zs):
    return lax.ppermute(value, "seq", [(2 * a + k, 2 * a + 1 - k) for a in range(zs) for k in range(2)])


def swap_chan(value, bit):
    return lax.ppermute(value, "chan", [(c, c ^ bit) for c in range(4)])


def after(value, *others):
    return lax.optimization_barrier((value, *others))[0]


def fast_body(hyena_in, prior_kv, filters, gain, w_qkv, cache_k, cache_v):
    rows, _, width = hyena_in.shape
    seqs = lax.axis_size("seq")
    zs = seqs // 2
    taps = filters.shape[1]
    depth, crow = w_qkv.shape[0], cache_k.shape[0]
    cols = width // zs
    my_seq = lax.axis_index("seq")
    z, core = my_seq // 2, my_seq % 2
    chan = lax.axis_index("chan")
    place = jnp.stack([chan, z, core]).astype(jnp.int32)

    w_t = jnp.transpose(w_qkv, (1, 0, 2))

    caches = [jnp.pad(c, ((0, PAD), (0, 0))) for c in (cache_k, cache_v)]

    def parcel(kind, r):
        at = (z + r) % zs * cols
        parts = (w_t[1], w_t[0], caches[0], caches[1]) if kind == "kq" else (w_t[2],)
        return jnp.concatenate([lax.dynamic_slice_in_dim(a, at, cols, 1) for a in parts], axis=0)

    hin = jnp.transpose(hyena_in, (1, 0, 2))
    tail = (hin[1, rows - taps :].astype(F32) * hin[2, rows - taps :].astype(F32)).astype(BF16)
    halo = lax.ppermute(tail, "seq", [(s, s + 1) for s in range(seqs - 1)])
    halo = jnp.where(my_seq == 0, jnp.pad(prior_kv, ((taps - prior_kv.shape[0], 0), (0, 0))), halo)

    order = [("kq", 1), "acts", ("v", 1), "acts", ("v", 3), "acts", ("kq", 3), ("kq", 2), ("v", 2)]
    here = {(kind, 0): parcel(kind, 0) for kind in ("kq", "v")}
    acts = [hyena(hin, halo, filters)]
    sent = []
    for n, item in enumerate(order):
        value, steps = (acts[-1], 1) if item == "acts" else (parcel(*item), item[1])
        if n >= 2:
            value = after(value, sent[n - 2])
        sent.append(shift_z(value, steps, zs))
        if item == "acts":
            acts.append(sent[-1])
        else:
            here[item] = sent[-1]
    there = {("kq", r): swap_core(here["kq", r], zs) for r in range(zs)}

    pace = [("kq", 1), ("v", 1), ("v", 3), ("kq", 3)]
    gain4 = gain.reshape(4, 1, width)
    half = rows // 2
    normed, diag0, diag1 = None, None, None
    for j, own in enumerate(acts):
        own = after(own, here[pace[j]], *([diag0, diag1] if j else []))
        from_x, from_y = swap_chan(own, 1), swap_chan(own, 2)
        if j:
            from_x, from_y = after(from_x, normed), after(from_y, normed)
        diag0 = swap_chan(from_x[:half], 2)
        diag1 = swap_chan(from_y[half:], 1)
        normed = norm(place, j, zs, own, from_x, from_y, diag0, diag1, gain4, normed)

    mine = [here["kq", r] for r in range(zs)]
    theirs = [there["kq", r] for r in range(zs)]
    k = project(place, normed, mine, theirs, 0, depth)
    q = project(place, normed, mine, theirs, 1, depth)
    k_sib = swap_core(k, zs)
    ck, cv = [pack(mine + theirs, 2 * depth + i * (crow + PAD), crow) for i in range(2)]
    for r in range(zs):
        there["v", r] = swap_core(here["v", r] if r != 2 else after(here["v", r], k, q, ck, cv), zs)
    v = project(place, normed, [here["v", r] for r in range(zs)], [there["v", r] for r in range(zs)], 0, depth)
    v_sib = swap_core(v, zs)

    pieces, out = {}, None
    for shifts in ((2,), (1, 3), (0,)):
        out = attend(shifts, place, q if out is None else after(q, out), k, v, k_sib, v_sib, ck, cv)
        for i, r in enumerate(shifts):
            pieces[r] = shift_z(out[i], r, zs) if r else out[i]
    return join(place, [pieces[r] for r in range(zs)])


def shifted(value, axis, steps):
    count = lax.axis_size(axis)
    leading, last = (max(0, -steps), min(count, count - steps))
    return lax.ppermute(value, axis, [(source, source + steps) for source in range(leading, last)])


def body(hyena_in, prior_kv, filters, gain, w_qkv, cache_k, cache_v):
    rows_dev = hyena_in.shape[0]
    width = hyena_in.shape[2]
    history = prior_kv.shape[0]
    tap_count = filters.shape[1]
    head_size = D // HEADS
    heads_dev = width // head_size
    cache_rows = cache_k.shape[0]
    stride = cache_rows + rows_dev
    my_index = lax.axis_index("seq")
    stream_q = hyena_in[:, 0].astype(jnp.float32)
    kv_prod = (hyena_in[:, 1].astype(jnp.float32) * hyena_in[:, 2].astype(jnp.float32)).astype(
        jnp.bfloat16
    )
    before = shifted(kv_prod[rows_dev - history :], "seq", 1)
    before = jnp.where(my_index == 0, prior_kv, before)
    extended = jnp.concatenate([before, kv_prod], axis=0).astype(jnp.float32)
    tap_table = jnp.repeat(filters, width // filters.shape[0], axis=0).T

    def add_tap(tap_index, total):
        offset = (tap_count - 1 - tap_index).astype(jnp.int32)
        window = lax.dynamic_slice_in_dim(extended, offset, rows_dev, 0)
        coeff = lax.dynamic_index_in_dim(tap_table, tap_index.astype(jnp.int32), 0, keepdims=True)
        return total + coeff * window

    conv = lax.fori_loop(0, tap_count, add_tap, jnp.zeros((rows_dev, width), jnp.float32))
    hyena_out = (stream_q * conv).astype(jnp.bfloat16)
    whole = lax.all_gather(hyena_out, "chan", axis=1, tiled=True)
    as_float = whole.astype(jnp.float32)
    mean_sq = jnp.mean(as_float * as_float, axis=-1, keepdims=True)
    normed = (as_float * lax.rsqrt(mean_sq + 1e-06) * gain[None, :]).astype(jnp.bfloat16)
    piece = lax.all_gather(w_qkv, "seq", axis=0, tiled=True)
    flat_piece = piece.reshape(piece.shape[0], 3 * width)
    projected = jnp.dot(normed, flat_piece, preferred_element_type=jnp.float32)
    qkv = projected.astype(jnp.bfloat16).reshape(rows_dev, 3, width)
    scale = 1.0 / head_size**0.5
    keys_local = jnp.concatenate([cache_k, qkv[:, 1]], axis=0)
    vals_local = jnp.concatenate([cache_v, qkv[:, 2]], axis=0)
    head_q = qkv[:, 0].reshape(rows_dev, heads_dev, head_size)
    query_pos = my_index * rows_dev + jnp.arange(rows_dev, dtype=jnp.int32)
    run_max = jnp.full((heads_dev, rows_dev), -1e30, jnp.float32)
    key_piece = lax.all_gather(keys_local, "seq", axis=0, tiled=True)
    val_piece = lax.all_gather(vals_local, "seq", axis=0, tiled=True)
    count = key_piece.shape[0]
    row_ids = jnp.arange(count, dtype=jnp.int32)
    source = row_ids // stride
    within = row_ids % stride
    key_pos = jnp.where(within < cache_rows, -1, source * rows_dev + within - cache_rows)
    visible = (key_pos[None, :] <= query_pos[:, None])[None]
    scores = (
        jnp.einsum(
            "qhd,khd->hqk",
            head_q,
            key_piece.reshape(count, heads_dev, head_size),
            preferred_element_type=jnp.float32,
        )
        * scale
    )
    scores = jnp.where(visible, scores, jnp.float32(-1e30))
    new_max = jnp.maximum(run_max, jnp.max(scores, axis=-1))
    weights = jnp.where(visible, jnp.exp(scores - new_max[..., None]), jnp.float32(0.0))
    new_sum = jnp.sum(weights, axis=-1)
    probs = weights.astype(jnp.bfloat16)
    added = jnp.einsum(
        "hqk,khd->hqd",
        probs,
        val_piece.reshape(count, heads_dev, head_size),
        preferred_element_type=jnp.float32,
    )
    result = jnp.transpose(added / new_sum[..., None], (1, 0, 2))
    return result.reshape(rows_dev, width).astype(jnp.bfloat16)


def solution(mesh):
    sizes = mesh.shape
    paired = sizes["chan"] == 4 and HEADS // sizes["chan"] == sizes["seq"]
    return jax.shard_map(
        fast_body if paired else body,
        mesh=mesh,
        in_specs=(
            P("seq", None, "chan"),
            P(None, "chan"),
            P("chan", None),
            P(),
            P("seq", None, "chan"),
            P("seq", "chan"),
            P("seq", "chan"),
        ),
        out_specs=P("seq", "chan"),
        check_vma=False,
    )
```

```python
import functools

import jax
import jax.numpy as jnp
from jax import lax
from jax.experimental import pallas as pl
from jax.experimental.pallas import tpu as pltpu
from jax.sharding import PartitionSpec as P

D = 4096
HEADS = 32
HEAD = D // HEADS
LANES = 128
PAD = 8
BF16 = jnp.bfloat16
F32 = jnp.float32
MIB = 1024 * 1024


BRIEF = pl.CostEstimate(flops=1, transcendentals=0, bytes_accessed=1)


def whole(shape):
    return pl.BlockSpec(shape, lambda *_: (0,) * len(shape))


def conv_kernel(group, hin_ref, halo_ref, taps_ref, out_ref):
    taps = taps_ref[...]
    count = taps.shape[0]
    width = taps.shape[1]
    kv = (hin_ref[1].astype(F32) * hin_ref[2].astype(F32)).astype(BF16)
    ext = jnp.concatenate([halo_ref[...], kv], axis=0)
    rows = kv.shape[0]
    blocks = rows // width
    windows = jnp.concatenate(
        [ext[b * width : (b + 2) * width] for b in range(blocks)], axis=1
    )
    high = taps.astype(BF16)
    low = (taps - high.astype(F32)).astype(BF16)
    source = lax.broadcasted_iota(jnp.int32, (width, 2 * width), 0)
    column = lax.broadcasted_iota(jnp.int32, (width, 2 * width), 1)
    flip = jnp.where(source + column == width, 1.0, 0.0).astype(BF16)
    total = None
    for part in (high, low):
        first = jnp.dot(part, flip, preferred_element_type=F32)
        toeplitz = jnp.concatenate(
            [
                pltpu.roll(
                    jnp.broadcast_to(first[g : g + 1], (width, 2 * width)),
                    0,
                    1,
                    stride=1,
                    stride_axis=0,
                ).astype(BF16)
                for g in range(count)
            ],
            axis=0,
        )
        product = jnp.dot(toeplitz, windows, preferred_element_type=F32)
        total = product if total is None else total + product
    owner = lax.broadcasted_iota(jnp.int32, (width, blocks * LANES), 1) % LANES // group
    conv = total[:width]
    for g in range(1, count):
        conv = jnp.where(owner == g, total[g * width : (g + 1) * width], conv)
    query = hin_ref[0].astype(F32)
    for b in range(blocks):
        piece = query[b * width : (b + 1) * width] * conv[:, b * LANES : (b + 1) * LANES]
        out_ref[b * width : (b + 1) * width, :] = piece.astype(BF16)


def hyena(hin, halo, filters):
    _, rows, width = hin.shape
    taps = filters.shape[1]
    group = width // filters.shape[0]
    per_tile = LANES // group
    return pl.pallas_call(
        functools.partial(conv_kernel, group),
        grid=(width // LANES,),
        in_specs=[
            pl.BlockSpec((3, rows, LANES), lambda i: (0, 0, i)),
            pl.BlockSpec((taps, LANES), lambda i: (0, i)),
            pl.BlockSpec((per_tile, taps), lambda i: (i, 0)),
        ],
        out_specs=pl.BlockSpec((rows, LANES), lambda i: (0, i)),
        out_shape=jax.ShapeDtypeStruct((rows, width), BF16),
        compiler_params=pltpu.CompilerParams(vmem_limit_bytes=12 * MIB),
        cost_estimate=BRIEF,
        name="hyena_filters",
    )(hin, halo, filters)


def norm_kernel(half, place_ref, own_ref, x_ref, y_ref, d0_ref, d1_ref, gain_ref, *rest):
    out_ref = rest[-1]
    chan = place_ref[0]
    step = pl.program_id(0)
    diag = jnp.where(step < half, d0_ref[...], d1_ref[...])
    parts = [r.astype(F32) for r in (own_ref[...], x_ref[...], y_ref[...], diag)]
    total = sum(jnp.sum(p * p, axis=-1, keepdims=True) for p in parts)
    factor = lax.rsqrt(total / D + 1e-6)
    for m, p in enumerate(parts):
        where = chan ^ m
        out_ref[0, where] = (p * factor * gain_ref[where]).astype(BF16)


def norm(place, j, zs, own, from_x, from_y, diag0, diag1, gain, buffer):
    rows, width = own.shape
    step = min(64, rows // 2)
    half = rows // 2 // step
    band = pl.BlockSpec((step, width), lambda i: (i, 0))
    args = [place, own, from_x, from_y, diag0, diag1, gain]
    specs = [
        pl.BlockSpec(memory_space=pltpu.SMEM),
        band,
        band,
        band,
        pl.BlockSpec((step, width), lambda i: (jnp.minimum(i, half - 1), 0)),
        pl.BlockSpec((step, width), lambda i: (jnp.maximum(i - half, 0), 0)),
        whole((4, 1, width)),
    ]
    aliases = {}
    if buffer is not None:
        aliases = {len(args): 0}
        args.append(buffer)
        specs.append(pl.BlockSpec(memory_space=pl.ANY))
    return pl.pallas_call(
        functools.partial(norm_kernel, half),
        grid=(2 * half,),
        in_specs=specs,
        out_specs=pl.BlockSpec((1, 4, step, width), lambda i: (j, 0, i, 0)),
        out_shape=jax.ShapeDtypeStruct((zs, 4, rows, width), BF16),
        input_output_aliases=aliases,
        compiler_params=pltpu.CompilerParams(vmem_limit_bytes=16 * MIB),
        cost_estimate=BRIEF,
        name="norm",
    )(*args)


def project_kernel(zs, depth, place_ref, normed_ref, *refs):
    own, sib, outs = refs[:zs], refs[zs : 2 * zs], refs[2 * zs :]
    z, core = place_ref[1], place_ref[2]
    for part, out_ref in enumerate(outs):
        total = None
        for shift in range(zs):
            block = lax.rem(z + zs - shift, zs)
            for k, w_ref in enumerate((own[shift], sib[shift])):
                at = pl.multiple_of((core ^ k) * depth, depth)
                left = normed_ref[0, block, :, pl.ds(at, depth)]
                right = w_ref[part * depth : (part + 1) * depth, :]
                term = jnp.dot(left, right, preferred_element_type=F32)
                total = term if total is None else total + term
        out_ref[0] = total.astype(BF16)


def project(place, normed, own, sib, count, depth):
    zs, parts, rows, width = normed.shape
    cols = own[0].shape[1]
    weights = pl.BlockSpec((count * depth, cols), lambda j: (0, 0))
    return pl.pallas_call(
        functools.partial(project_kernel, zs, depth),
        grid=(zs,),
        in_specs=[
            pl.BlockSpec(memory_space=pltpu.SMEM),
            pl.BlockSpec((1, parts, rows, width), lambda j: (j, 0, 0, 0)),
        ]
        + [weights] * (2 * zs),
        out_specs=[pl.BlockSpec((1, rows, cols), lambda j: (j, 0, 0))] * count,
        out_shape=[jax.ShapeDtypeStruct((zs, rows, cols), BF16)] * count,
        compiler_params=pltpu.CompilerParams(vmem_limit_bytes=24 * MIB),
        cost_estimate=BRIEF,
        name="project",
    )(place, normed, *own, *sib)


NT = (((1,), (1,)), ((), ()))


def attend_kernel(shifts, place_ref, q_ref, k_ref, v_ref, ks_ref, vs_ref, ck_ref, cv_ref, out_ref):
    z, core = place_ref[1], place_ref[2]
    zs, rows, cols = k_ref.shape
    heads = range(cols // HEAD)
    factor = 1.4426950408889634 / HEAD**0.5
    shift = jnp.int32(shifts[0])
    for i, s in enumerate(shifts):
        shift = jnp.where(pl.program_id(0) == i, s, shift)
    block = lax.rem(z + shift, zs)
    hcols = [slice(h * HEAD, (h + 1) * HEAD) for h in heads]
    queries = [q_ref[0, :, hcol] for hcol in hcols]

    def fold(state, h, key, value, mask):
        s = lax.dot_general(queries[h], key, NT, preferred_element_type=F32)
        if mask is not None:
            s = jnp.where(mask, s, -1e30)
        top = jnp.max(s, axis=-1, keepdims=True) * factor
        if state is not None:
            top = jnp.maximum(top, state[0])
        weights = jnp.exp2(s * factor - top)
        total = jnp.sum(weights, axis=-1, keepdims=True)
        summed = jnp.dot(weights.astype(BF16), value, preferred_element_type=F32)
        if state is not None:
            scale = jnp.exp2(state[0] - top)
            total, summed = total + state[1] * scale, summed + state[2] * scale
        return top, total, summed

    def both(b, h):
        at = lax.rem(z + zs - b, zs)
        key = jnp.concatenate([k_ref[at, :, hcols[h]], ks_ref[at, :, hcols[h]]], axis=0)
        value = jnp.concatenate([v_ref[at, :, hcols[h]], vs_ref[at, :, hcols[h]]], axis=0)
        return key, value

    def earlier(b, states):
        return tuple(fold(states[h], h, *both(b, h), None) for h in heads)

    states = tuple(fold(None, h, ck_ref[:, hcols[h]], cv_ref[:, hcols[h]], None) for h in heads)
    states = lax.fori_loop(0, block, earlier, states)
    row = lax.broadcasted_iota(jnp.int32, (rows, 2 * rows), 0)
    col = lax.broadcasted_iota(jnp.int32, (rows, 2 * rows), 1)
    visible = jnp.where(col < rows, col, jnp.where(core == 1, 0, rows)) <= row
    for h in heads:
        _, total, summed = fold(states[h], h, *both(block, h), visible)
        out_ref[0, :, hcols[h]] = (summed / total).astype(BF16)


def attend(shifts, place, q, k, v, k_sib, v_sib, ck, cv):
    zs, rows, cols = q.shape

    def slab(i, place_ref):
        shift = jnp.int32(shifts[0])
        for n, s in enumerate(shifts):
            shift = jnp.where(i == n, s, shift)
        return lax.rem(zs - shift, zs), 0, 0

    args = (k, v, k_sib, v_sib, ck, cv)
    return pl.pallas_call(
        functools.partial(attend_kernel, shifts),
        grid_spec=pltpu.PrefetchScalarGridSpec(
            num_scalar_prefetch=1,
            grid=(len(shifts),),
            in_specs=[pl.BlockSpec((1, rows, cols), slab)] + [whole(a.shape) for a in args],
            out_specs=pl.BlockSpec((1, rows, cols), lambda i, place_ref: (i, 0, 0)),
        ),
        out_shape=jax.ShapeDtypeStruct((len(shifts), rows, cols), BF16),
        compiler_params=pltpu.CompilerParams(vmem_limit_bytes=32 * MIB),
        cost_estimate=BRIEF,
        name="attend",
    )(place, q, *args)


def pack_kernel(at, crow, *refs):
    parcels, (out_ref, scratch) = refs[:-2], refs[-2:]
    for i, piece in enumerate(parcels):
        band = piece[at : at + crow + PAD].astype(F32)
        scratch[i * crow : (i + 1) * crow, :] = band[:crow]
    out_ref[...] = scratch[...].astype(BF16)


def pack(parcels, at, crow):
    cols = parcels[0].shape[1]
    out = (len(parcels) * crow, cols)
    return pl.pallas_call(
        functools.partial(pack_kernel, at, crow),
        in_specs=[whole(p.shape) for p in parcels],
        out_specs=whole(out),
        out_shape=jax.ShapeDtypeStruct(out, BF16),
        scratch_shapes=[pltpu.VMEM(out, F32)],
        compiler_params=pltpu.CompilerParams(vmem_limit_bytes=24 * MIB),
        cost_estimate=BRIEF,
        name="pack",
    )(*parcels)


def join_kernel(place_ref, *refs):
    pieces, out_ref = refs[:-1], refs[-1]
    zs = len(pieces)
    cols = pieces[0].shape[1]
    for r, piece in enumerate(pieces):
        at = lax.rem(place_ref[1] + zs - r, zs) * cols
        out_ref[:, pl.ds(pl.multiple_of(at, cols), cols)] = piece[...]


def join(place, pieces):
    rows, cols = pieces[0].shape
    out = (rows, cols * len(pieces))
    return pl.pallas_call(
        join_kernel,
        in_specs=[pl.BlockSpec(memory_space=pltpu.SMEM)] + [whole(p.shape) for p in pieces],
        out_specs=whole(out),
        out_shape=jax.ShapeDtypeStruct(out, BF16),
        name="join",
    )(place, *pieces)


def shift_z(value, steps, zs):
    pairs = [(2 * a + k, 2 * ((a + steps) % zs) + k) for a in range(zs) for k in range(2)]
    return lax.ppermute(value, "seq", pairs)


def swap_core(value, zs):
    return lax.ppermute(value, "seq", [(2 * a + k, 2 * a + 1 - k) for a in range(zs) for k in range(2)])


def swap_chan(value, bit):
    return lax.ppermute(value, "chan", [(c, c ^ bit) for c in range(4)])


def after(value, *others):
    return lax.optimization_barrier((value, *others))[0]


def fast_body(hyena_in, prior_kv, filters, gain, w_qkv, cache_k, cache_v):
    rows, _, width = hyena_in.shape
    seqs = lax.axis_size("seq")
    zs = seqs // 2
    taps = filters.shape[1]
    depth, crow = w_qkv.shape[0], cache_k.shape[0]
    cols = width // zs
    my_seq = lax.axis_index("seq")
    z, core = my_seq // 2, my_seq % 2
    chan = lax.axis_index("chan")
    place = jnp.stack([chan, z, core]).astype(jnp.int32)

    w_t = jnp.transpose(w_qkv, (1, 0, 2))
    caches = [jnp.pad(c, ((0, PAD), (0, 0))) for c in (cache_k, cache_v)]

    def parcel(kind, r):
        at = (z + r) % zs * cols
        parts = [
            lax.dynamic_slice(w_t, (p, 0, at), (1, depth, cols))[0]
            for p in ((1, 2) if kind == "kv" else (0,))
        ]
        if kind == "kv":
            parts += [lax.dynamic_slice_in_dim(c, at, cols, 1) for c in caches]
        return jnp.concatenate(parts, axis=0)

    hin = jnp.transpose(hyena_in, (1, 0, 2))
    tail = (hin[1, rows - taps :].astype(F32) * hin[2, rows - taps :].astype(F32)).astype(BF16)
    halo = lax.ppermute(tail, "seq", [(s, s + 1) for s in range(seqs - 1)])
    halo = jnp.where(my_seq == 0, jnp.pad(prior_kv, ((taps - prior_kv.shape[0], 0), (0, 0))), halo)

    order = [("kv", 1), "acts", ("q", 1), "acts", ("q", 3), "acts", ("kv", 3), ("kv", 2), ("q", 2)]
    here = {(kind, 0): parcel(kind, 0) for kind in ("kv", "q")}
    acts = [hyena(hin, halo, filters)]
    sent = []
    for n, item in enumerate(order):
        value, steps = (acts[-1], 1) if item == "acts" else (parcel(*item), item[1])
        if n == 0:
            value = after(value, halo)
        if n >= 2:
            value = after(value, sent[n - 1] if item == ("kv", 3) else sent[n - 2])
        sent.append(shift_z(value, steps, zs))
        if item == "acts":
            acts.append(sent[-1])
        else:
            here[item] = sent[-1]
    there = {item: swap_core(here[item], zs) for item in here if item != ("q", 2)}

    pace = [("kv", 1), ("q", 1), ("q", 3), None]
    swapped = [[], [("kv", 0), ("q", 0)], [("kv", 1), ("q", 1)], [("q", 3)]]
    gain4 = gain.reshape(4, 1, width)
    half = rows // 2
    normed, diag0, diag1 = None, None, None
    for j, own in enumerate(acts):
        own = after(own, *([here[pace[j]]] if pace[j] else []), *([diag0, diag1] if j else []))
        from_x, from_y = swap_chan(own, 1), swap_chan(own, 2)
        if j:
            settled = [normed] + [there[item] for item in swapped[j]]
            from_x, from_y = after(from_x, *settled), after(from_y, *settled)
        diag0 = swap_chan(from_x[:half], 2)
        diag1 = swap_chan(from_y[half:], 1)
        normed = norm(place, j, zs, own, from_x, from_y, diag0, diag1, gain4, normed)

    mine = [here["kv", r] for r in range(zs)]
    theirs = [there["kv", r] for r in range(zs)]
    ck, cv = [pack(mine + theirs, 2 * depth + i * (crow + PAD), crow) for i in range(2)]
    k, v = project(place, after(normed, ck, cv), mine, theirs, 2, depth)
    k_sib, v_sib = swap_core(k, zs), swap_core(v, zs)
    there["q", 2] = swap_core(after(here["q", 2], k), zs)
    queries = [[side["q", r] for r in range(zs)] for side in (here, there)]
    (q,) = project(place, normed, *queries, 1, depth)
    pieces, out = {}, None
    for shifts, wait in (((2,), ()), ((1, 3), ()), ((0,), (2,))):
        ready = q if out is None else after(q, out, *[pieces[r] for r in wait])
        out = attend(shifts, place, ready, k, v, k_sib, v_sib, ck, cv)
        for i, r in enumerate(shifts):
            pieces[r] = shift_z(out[i], r, zs) if r else out[i]
    return join(place, [pieces[r] for r in range(zs)])


def shifted(value, axis, steps):
    count = lax.axis_size(axis)
    leading, last = (max(0, -steps), min(count, count - steps))
    return lax.ppermute(value, axis, [(source, source + steps) for source in range(leading, last)])


def body(hyena_in, prior_kv, filters, gain, w_qkv, cache_k, cache_v):
    rows_dev = hyena_in.shape[0]
    width = hyena_in.shape[2]
    history = prior_kv.shape[0]
    tap_count = filters.shape[1]
    head_size = D // HEADS
    heads_dev = width // head_size
    cache_rows = cache_k.shape[0]
    stride = cache_rows + rows_dev
    my_index = lax.axis_index("seq")
    stream_q = hyena_in[:, 0].astype(jnp.float32)
    kv_prod = (hyena_in[:, 1].astype(jnp.float32) * hyena_in[:, 2].astype(jnp.float32)).astype(
        jnp.bfloat16
    )
    before = shifted(kv_prod[rows_dev - history :], "seq", 1)
    before = jnp.where(my_index == 0, prior_kv, before)
    extended = jnp.concatenate([before, kv_prod], axis=0).astype(jnp.float32)
    tap_table = jnp.repeat(filters, width // filters.shape[0], axis=0).T

    def add_tap(tap_index, total):
        offset = (tap_count - 1 - tap_index).astype(jnp.int32)
        window = lax.dynamic_slice_in_dim(extended, offset, rows_dev, 0)
        coeff = lax.dynamic_index_in_dim(tap_table, tap_index.astype(jnp.int32), 0, keepdims=True)
        return total + coeff * window

    conv = lax.fori_loop(0, tap_count, add_tap, jnp.zeros((rows_dev, width), jnp.float32))
    hyena_out = (stream_q * conv).astype(jnp.bfloat16)
    whole = lax.all_gather(hyena_out, "chan", axis=1, tiled=True)
    as_float = whole.astype(jnp.float32)
    mean_sq = jnp.mean(as_float * as_float, axis=-1, keepdims=True)
    normed = (as_float * lax.rsqrt(mean_sq + 1e-06) * gain[None, :]).astype(jnp.bfloat16)
    piece = lax.all_gather(w_qkv, "seq", axis=0, tiled=True)
    flat_piece = piece.reshape(piece.shape[0], 3 * width)
    projected = jnp.dot(normed, flat_piece, preferred_element_type=jnp.float32)
    qkv = projected.astype(jnp.bfloat16).reshape(rows_dev, 3, width)
    scale = 1.0 / head_size**0.5
    keys_local = jnp.concatenate([cache_k, qkv[:, 1]], axis=0)
    vals_local = jnp.concatenate([cache_v, qkv[:, 2]], axis=0)
    head_q = qkv[:, 0].reshape(rows_dev, heads_dev, head_size)
    query_pos = my_index * rows_dev + jnp.arange(rows_dev, dtype=jnp.int32)
    run_max = jnp.full((heads_dev, rows_dev), -1e30, jnp.float32)
    key_piece = lax.all_gather(keys_local, "seq", axis=0, tiled=True)
    val_piece = lax.all_gather(vals_local, "seq", axis=0, tiled=True)
    count = key_piece.shape[0]
    row_ids = jnp.arange(count, dtype=jnp.int32)
    source = row_ids // stride
    within = row_ids % stride
    key_pos = jnp.where(within < cache_rows, -1, source * rows_dev + within - cache_rows)
    visible = (key_pos[None, :] <= query_pos[:, None])[None]
    scores = (
        jnp.einsum(
            "qhd,khd->hqk",
            head_q,
            key_piece.reshape(count, heads_dev, head_size),
            preferred_element_type=jnp.float32,
        )
        * scale
    )
    scores = jnp.where(visible, scores, jnp.float32(-1e30))
    new_max = jnp.maximum(run_max, jnp.max(scores, axis=-1))
    weights = jnp.where(visible, jnp.exp(scores - new_max[..., None]), jnp.float32(0.0))
    new_sum = jnp.sum(weights, axis=-1)
    probs = weights.astype(jnp.bfloat16)
    added = jnp.einsum(
        "hqk,khd->hqd",
        probs,
        val_piece.reshape(count, heads_dev, head_size),
        preferred_element_type=jnp.float32,
    )
    result = jnp.transpose(added / new_sum[..., None], (1, 0, 2))
    return result.reshape(rows_dev, width).astype(jnp.bfloat16)


def solution(mesh):
    sizes = mesh.shape
    paired = sizes["chan"] == 4 and HEADS // sizes["chan"] == sizes["seq"]
    return jax.shard_map(
        fast_body if paired else body,
        mesh=mesh,
        in_specs=(
            P("seq", None, "chan"),
            P(None, "chan"),
            P("chan", None),
            P(),
            P("seq", None, "chan"),
            P("seq", "chan"),
            P("seq", "chan"),
        ),
        out_specs=P("seq", "chan"),
        check_vma=False,
    )
```

```python
import functools

import jax
import jax.numpy as jnp
from jax import lax
from jax.experimental import pallas as pl
from jax.experimental.pallas import tpu as pltpu
from jax.sharding import PartitionSpec as P

D = 4096
HEADS = 32
HEAD = D // HEADS
LANES = 128
PAD = 8
BF16 = jnp.bfloat16
F32 = jnp.float32
MIB = 1024 * 1024


BRIEF = pl.CostEstimate(flops=1, transcendentals=0, bytes_accessed=1)


VMEM = pl.BlockSpec(memory_space=pltpu.VMEM)
SMEM = pl.BlockSpec(memory_space=pltpu.SMEM)


def whole(shape):
    return pl.BlockSpec(shape, lambda *_: (0,) * len(shape))


def conv_kernel(group, hin_ref, halo_ref, taps_ref, out_ref):
    taps = taps_ref[...]
    count = taps.shape[0]
    width = taps.shape[1]
    kv = (hin_ref[1].astype(F32) * hin_ref[2].astype(F32)).astype(BF16)
    ext = jnp.concatenate([halo_ref[...], kv], axis=0)
    rows = kv.shape[0]
    blocks = rows // width
    windows = jnp.concatenate(
        [ext[b * width : (b + 2) * width] for b in range(blocks)], axis=1
    )
    high = taps.astype(BF16)
    low = (taps - high.astype(F32)).astype(BF16)
    source = lax.broadcasted_iota(jnp.int32, (width, 2 * width), 0)
    column = lax.broadcasted_iota(jnp.int32, (width, 2 * width), 1)
    flip = jnp.where(source + column == width, 1.0, 0.0).astype(BF16)
    total = None
    for part in (high, low):
        first = jnp.dot(part, flip, preferred_element_type=F32)
        toeplitz = jnp.concatenate(
            [
                pltpu.roll(
                    jnp.broadcast_to(first[g : g + 1], (width, 2 * width)),
                    0,
                    1,
                    stride=1,
                    stride_axis=0,
                ).astype(BF16)
                for g in range(count)
            ],
            axis=0,
        )
        product = jnp.dot(toeplitz, windows, preferred_element_type=F32)
        total = product if total is None else total + product
    owner = lax.broadcasted_iota(jnp.int32, (width, blocks * LANES), 1) % LANES // group
    conv = total[:width]
    for g in range(1, count):
        conv = jnp.where(owner == g, total[g * width : (g + 1) * width], conv)
    query = hin_ref[0].astype(F32)
    for b in range(blocks):
        piece = query[b * width : (b + 1) * width] * conv[:, b * LANES : (b + 1) * LANES]
        out_ref[b * width : (b + 1) * width, :] = piece.astype(BF16)


def hyena(hin, halo, filters):
    _, rows, width = hin.shape
    taps = filters.shape[1]
    group = width // filters.shape[0]
    per_tile = LANES // group
    return pl.pallas_call(
        functools.partial(conv_kernel, group),
        grid=(width // LANES,),
        in_specs=[
            pl.BlockSpec((3, rows, LANES), lambda i: (0, 0, i)),
            pl.BlockSpec((taps, LANES), lambda i: (0, i)),
            pl.BlockSpec((per_tile, taps), lambda i: (i, 0)),
        ],
        out_specs=pl.BlockSpec((rows, LANES), lambda i: (0, i)),
        out_shape=jax.ShapeDtypeStruct((rows, width), BF16),
        compiler_params=pltpu.CompilerParams(vmem_limit_bytes=12 * MIB),
        cost_estimate=BRIEF,
        name="hyena_filters",
    )(hin, halo, filters)


def norm_kernel(j, place_ref, own_ref, x_ref, y_ref, d0_ref, d1_ref, gain_ref, *rest):
    out_ref = rest[-1]
    chan = place_ref[0]
    half = d0_ref.shape[0]
    step = 16

    def band(i, diag_ref, start):
        at = pl.ds(pl.multiple_of(start + i * step, step), step)
        refs = (own_ref.at[at], x_ref.at[at], y_ref.at[at], diag_ref.at[pl.ds(pl.multiple_of(i * step, step), step)])
        parts = [r[...].astype(F32) for r in refs]
        total = sum(jnp.sum(p * p, axis=-1, keepdims=True) for p in parts)
        factor = lax.rsqrt(total / D + 1e-6)
        for m, p in enumerate(parts):
            where = chan ^ m
            out_ref[j, where, at, :] = (p * factor * gain_ref[where]).astype(BF16)

    for diag_ref, start in ((d0_ref, 0), (d1_ref, half)):
        pl.loop(0, half // step, unroll=2)(functools.partial(band, diag_ref=diag_ref, start=start))


def norm(place, j, zs, own, from_x, from_y, diag0, diag1, gain, buffer):
    rows, width = own.shape
    args = [place, own, from_x, from_y, diag0, diag1, gain] + ([] if buffer is None else [buffer])
    return pl.pallas_call(
        functools.partial(norm_kernel, j),
        in_specs=[SMEM] + [VMEM] * (len(args) - 1),
        out_specs=VMEM,
        out_shape=jax.ShapeDtypeStruct((zs, 4, rows, width), BF16),
        input_output_aliases={} if buffer is None else {7: 0},
        compiler_params=pltpu.CompilerParams(vmem_limit_bytes=16 * MIB),
        cost_estimate=BRIEF,
        name="norm",
    )(*args)


def project_kernel(shifts, zs, count, place_ref, normed_ref, *refs):
    n = len(shifts)
    own, sib, rest = refs[:n], refs[n : 2 * n], refs[2 * n :]
    before, outs = rest[:-count], rest[-count:]
    z, core = place_ref[1], place_ref[2]
    depth = normed_ref.shape[3] // 2
    for part, out_ref in enumerate(outs):
        for j in range(zs):
            total = before[part][j] if before else None
            for i, shift in enumerate(shifts):
                block = lax.rem(z + zs - shift, zs)
                for k, w_ref in enumerate((own[i], sib[i])):
                    at = pl.multiple_of((core ^ k) * depth, depth)
                    left = normed_ref[j, block, :, pl.ds(at, depth)]
                    right = w_ref[part * depth : (part + 1) * depth, :]
                    term = jnp.dot(left, right, preferred_element_type=F32)
                    total = term if total is None else total + term
            out_ref[j] = total.astype(out_ref.dtype)


def project(place, normed, own, sib, shifts, count, rounded, before=()):
    zs, _, rows, _ = normed.shape
    cols = own[0].shape[1]
    args = [place, normed, *own, *sib, *before]
    return pl.pallas_call(
        functools.partial(project_kernel, shifts, zs, count),
        in_specs=[SMEM] + [VMEM] * (len(args) - 1),
        out_specs=[VMEM] * count,
        out_shape=[jax.ShapeDtypeStruct((zs, rows, cols), BF16 if rounded else F32)] * count,
        compiler_params=pltpu.CompilerParams(vmem_limit_bytes=16 * MIB),
        cost_estimate=BRIEF,
        name="project",
    )(*args)


NT = (((1,), (1,)), ((), ()))


def attend_kernel(shifts, place_ref, q_ref, k_ref, v_ref, ks_ref, vs_ref, ck_ref, cv_ref, *outs):
    z, core = place_ref[1], place_ref[2]
    zs, rows, cols = k_ref.shape
    heads = range(cols // HEAD)
    factor = 1.4426950408889634 / HEAD**0.5
    hcols = [slice(h * HEAD, (h + 1) * HEAD) for h in heads]
    row = lax.broadcasted_iota(jnp.int32, (rows, 2 * rows), 0)
    col = lax.broadcasted_iota(jnp.int32, (rows, 2 * rows), 1)
    visible = jnp.where(col < rows, col, jnp.where(core == 1, 0, rows)) <= row

    def fold(state, query, key, value, mask):
        s = lax.dot_general(query, key, NT, preferred_element_type=F32)
        if mask is not None:
            s = jnp.where(mask, s, -1e30)
        top = jnp.max(s, axis=-1, keepdims=True) * factor
        if state is not None:
            top = jnp.maximum(top, state[0])
        weights = jnp.exp2(s * factor - top)
        total = jnp.sum(weights, axis=-1, keepdims=True)
        summed = jnp.dot(weights.astype(BF16), value, preferred_element_type=F32)
        if state is not None:
            scale = jnp.exp2(state[0] - top)
            total, summed = total + state[1] * scale, summed + state[2] * scale
        return top, total, summed

    def both(b, h):
        at = lax.rem(z + zs - b, zs)
        key = jnp.concatenate([k_ref[at, :, hcols[h]], ks_ref[at, :, hcols[h]]], axis=0)
        value = jnp.concatenate([v_ref[at, :, hcols[h]], vs_ref[at, :, hcols[h]]], axis=0)
        return key, value

    for shift, out_ref in zip(shifts, outs):
        block = lax.rem(z + shift, zs)
        mine = lax.rem(zs - shift, zs)
        queries = [q_ref[mine, :, hcol] for hcol in hcols]

        def earlier(b, states):
            return tuple(fold(states[h], queries[h], *both(b, h), None) for h in heads)

        states = tuple(fold(None, queries[h], ck_ref[:, hcols[h]], cv_ref[:, hcols[h]], None) for h in heads)
        states = lax.fori_loop(0, block, earlier, states)
        for h in heads:
            _, total, summed = fold(states[h], queries[h], *both(block, h), visible)
            out_ref[:, hcols[h]] = (summed / total).astype(BF16)


def attend(shifts, place, q, k, v, k_sib, v_sib, ck, cv):
    _, rows, cols = q.shape
    return pl.pallas_call(
        functools.partial(attend_kernel, shifts),
        in_specs=[SMEM] + [VMEM] * 7,
        out_specs=[VMEM] * len(shifts),
        out_shape=[jax.ShapeDtypeStruct((rows, cols), BF16)] * len(shifts),
        compiler_params=pltpu.CompilerParams(vmem_limit_bytes=20 * MIB),
        cost_estimate=BRIEF,
        name="attend",
    )(place, q, k, v, k_sib, v_sib, ck, cv)


def pack_kernel(at, crow, *refs):
    parcels, (out_ref, scratch) = refs[:-2], refs[-2:]
    for i, piece in enumerate(parcels):
        band = piece[at : at + crow + PAD].astype(F32)
        scratch[i * crow : (i + 1) * crow, :] = band[:crow]
    out_ref[...] = scratch[...].astype(BF16)


def pack(parcels, at, crow):
    cols = parcels[0].shape[1]
    out = (len(parcels) * crow, cols)
    return pl.pallas_call(
        functools.partial(pack_kernel, at, crow),
        in_specs=[VMEM] * len(parcels),
        out_specs=VMEM,
        out_shape=jax.ShapeDtypeStruct(out, BF16),
        scratch_shapes=[pltpu.VMEM(out, F32)],
        compiler_params=pltpu.CompilerParams(vmem_limit_bytes=24 * MIB),
        cost_estimate=BRIEF,
        name="pack",
    )(*parcels)


def join_kernel(place_ref, *refs):
    pieces, out_ref = refs[:-1], refs[-1]
    zs = len(pieces)
    cols = pieces[0].shape[1]
    for r, piece in enumerate(pieces):
        at = lax.rem(place_ref[1] + zs - r, zs) * cols
        out_ref[:, pl.ds(pl.multiple_of(at, cols), cols)] = piece[...]


def join(place, pieces):
    rows, cols = pieces[0].shape
    out = (rows, cols * len(pieces))
    return pl.pallas_call(
        join_kernel,
        in_specs=[SMEM] + [VMEM] * len(pieces),
        out_specs=whole(out),
        out_shape=jax.ShapeDtypeStruct(out, BF16),
        name="join",
    )(place, *pieces)


def shift_z(value, steps, zs):
    pairs = [(2 * a + k, 2 * ((a + steps) % zs) + k) for a in range(zs) for k in range(2)]
    return lax.ppermute(value, "seq", pairs)


def swap_core(value, zs):
    return lax.ppermute(value, "seq", [(2 * a + k, 2 * a + 1 - k) for a in range(zs) for k in range(2)])


def swap_chan(value, bit):
    return lax.ppermute(value, "chan", [(c, c ^ bit) for c in range(4)])


def after(value, *others):
    return lax.optimization_barrier((value, *others))[0]


def fast_body(hyena_in, prior_kv, filters, gain, w_qkv, cache_k, cache_v):
    rows, _, width = hyena_in.shape
    seqs = lax.axis_size("seq")
    zs = seqs // 2
    taps = filters.shape[1]
    depth, crow = w_qkv.shape[0], cache_k.shape[0]
    cols = width // zs
    my_seq = lax.axis_index("seq")
    z, core = my_seq // 2, my_seq % 2
    chan = lax.axis_index("chan")
    place = jnp.stack([chan, z, core]).astype(jnp.int32)

    w_t = jnp.transpose(w_qkv, (1, 0, 2))
    caches = [jnp.pad(c, ((0, PAD), (0, 0))) for c in (cache_k, cache_v)]

    def parcel(kind, r):
        at = (z + r) % zs * cols
        parts = [
            lax.dynamic_slice(w_t, (p, 0, at), (1, depth, cols))[0]
            for p in ((1, 2) if kind == "kv" else (0,))
        ]
        if kind == "kv":
            parts += [lax.dynamic_slice_in_dim(c, at, cols, 1) for c in caches]
        return jnp.concatenate(parts, axis=0)

    hin = jnp.transpose(hyena_in, (1, 0, 2))
    tail = (hin[1, rows - taps :].astype(F32) * hin[2, rows - taps :].astype(F32)).astype(BF16)
    halo = lax.ppermute(tail, "seq", [(s, s + 1) for s in range(seqs - 1)])
    halo = jnp.where(my_seq == 0, jnp.pad(prior_kv, ((taps - prior_kv.shape[0], 0), (0, 0))), halo)

    order = [("q", 1), ("q", 3), "acts", ("kv", 1), "acts", ("kv", 3), "acts", ("kv", 2), ("q", 2)]
    here = {(kind, 0): parcel(kind, 0) for kind in ("kv", "q")}
    acts = [hyena(hin, halo, filters)]
    sent = []
    for n, item in enumerate(order):
        value, steps = (acts[-1], 1) if item == "acts" else (parcel(*item), item[1])
        if n >= 2:
            value = after(value, sent[n - 2])
        sent.append(shift_z(value, steps, zs))
        if item == "acts":
            acts.append(sent[-1])
        else:
            here[item] = sent[-1]
    late = [("kv", 2), ("q", 2)]
    there = {item: swap_core(here[item], zs) for item in here if item not in late}

    pace = [[("q", 1), ("q", 3)], [], [("kv", 1)], []]
    swapped = [[], [("kv", 0), ("q", 0)], [("q", 1), ("q", 3)], [("kv", 1)]]
    gain4 = gain.reshape(4, 1, width)
    half = rows // 2
    normed, diag0, diag1 = None, None, None
    for j, own in enumerate(acts):
        own = after(own, *[here[item] for item in pace[j]], *([diag0, diag1] if j else []))
        from_x, from_y = swap_chan(own, 1), swap_chan(own, 2)
        if j:
            settled = [normed] + [there[item] for item in swapped[j]]
            from_x, from_y = after(from_x, *settled), after(from_y, *settled)
        diag0 = swap_chan(from_x[:half], 2)
        diag1 = swap_chan(from_y[half:], 1)
        normed = norm(place, j, zs, own, from_x, from_y, diag0, diag1, gain4, normed)

    def sides(kind, shifts):
        return [[side[kind, r] for r in shifts] for side in (here, there)]

    every = tuple(range(zs))
    early = tuple(r for r in every if r != 2)
    (q_early,) = project(place, normed, *sides("q", early), early, 1, False)
    there["kv", 2] = swap_core(after(here["kv", 2], diag0, diag1), zs)
    mine, theirs = sides("kv", every)
    ck, cv = [pack(mine + theirs, 2 * depth + i * (crow + PAD), crow) for i in range(2)]
    k, v = project(place, after(normed, ck, cv, q_early), mine, theirs, every, 2, True)
    k_sib, v_sib = swap_core(k, zs), swap_core(v, zs)
    there["q", 2] = swap_core(after(here["q", 2], k), zs)
    (q,) = project(place, normed, *sides("q", (2,)), (2,), 1, True, (q_early,))
    pieces, out = {}, None
    for shifts, wait in (((2,), ()), ((1, 3), ()), ((0,), (2,))):
        ready = q if out is None else after(q, out[0], *[pieces[r] for r in wait])
        out = attend(shifts, place, ready, k, v, k_sib, v_sib, ck, cv)
        for r, piece in zip(shifts, out):
            pieces[r] = shift_z(piece, r, zs) if r else piece
    return join(place, [pieces[r] for r in range(zs)])


def shifted(value, axis, steps):
    count = lax.axis_size(axis)
    leading, last = (max(0, -steps), min(count, count - steps))
    return lax.ppermute(value, axis, [(source, source + steps) for source in range(leading, last)])


def body(hyena_in, prior_kv, filters, gain, w_qkv, cache_k, cache_v):
    rows_dev = hyena_in.shape[0]
    width = hyena_in.shape[2]
    history = prior_kv.shape[0]
    tap_count = filters.shape[1]
    head_size = D // HEADS
    heads_dev = width // head_size
    cache_rows = cache_k.shape[0]
    stride = cache_rows + rows_dev
    my_index = lax.axis_index("seq")
    stream_q = hyena_in[:, 0].astype(jnp.float32)
    kv_prod = (hyena_in[:, 1].astype(jnp.float32) * hyena_in[:, 2].astype(jnp.float32)).astype(
        jnp.bfloat16
    )
    before = shifted(kv_prod[rows_dev - history :], "seq", 1)
    before = jnp.where(my_index == 0, prior_kv, before)
    extended = jnp.concatenate([before, kv_prod], axis=0).astype(jnp.float32)
    tap_table = jnp.repeat(filters, width // filters.shape[0], axis=0).T

    def add_tap(tap_index, total):
        offset = (tap_count - 1 - tap_index).astype(jnp.int32)
        window = lax.dynamic_slice_in_dim(extended, offset, rows_dev, 0)
        coeff = lax.dynamic_index_in_dim(tap_table, tap_index.astype(jnp.int32), 0, keepdims=True)
        return total + coeff * window

    conv = lax.fori_loop(0, tap_count, add_tap, jnp.zeros((rows_dev, width), jnp.float32))
    hyena_out = (stream_q * conv).astype(jnp.bfloat16)
    whole = lax.all_gather(hyena_out, "chan", axis=1, tiled=True)
    as_float = whole.astype(jnp.float32)
    mean_sq = jnp.mean(as_float * as_float, axis=-1, keepdims=True)
    normed = (as_float * lax.rsqrt(mean_sq + 1e-06) * gain[None, :]).astype(jnp.bfloat16)
    piece = lax.all_gather(w_qkv, "seq", axis=0, tiled=True)
    flat_piece = piece.reshape(piece.shape[0], 3 * width)
    projected = jnp.dot(normed, flat_piece, preferred_element_type=jnp.float32)
    qkv = projected.astype(jnp.bfloat16).reshape(rows_dev, 3, width)
    scale = 1.0 / head_size**0.5
    keys_local = jnp.concatenate([cache_k, qkv[:, 1]], axis=0)
    vals_local = jnp.concatenate([cache_v, qkv[:, 2]], axis=0)
    head_q = qkv[:, 0].reshape(rows_dev, heads_dev, head_size)
    query_pos = my_index * rows_dev + jnp.arange(rows_dev, dtype=jnp.int32)
    run_max = jnp.full((heads_dev, rows_dev), -1e30, jnp.float32)
    key_piece = lax.all_gather(keys_local, "seq", axis=0, tiled=True)
    val_piece = lax.all_gather(vals_local, "seq", axis=0, tiled=True)
    count = key_piece.shape[0]
    row_ids = jnp.arange(count, dtype=jnp.int32)
    source = row_ids // stride
    within = row_ids % stride
    key_pos = jnp.where(within < cache_rows, -1, source * rows_dev + within - cache_rows)
    visible = (key_pos[None, :] <= query_pos[:, None])[None]
    scores = (
        jnp.einsum(
            "qhd,khd->hqk",
            head_q,
            key_piece.reshape(count, heads_dev, head_size),
            preferred_element_type=jnp.float32,
        )
        * scale
    )
    scores = jnp.where(visible, scores, jnp.float32(-1e30))
    new_max = jnp.maximum(run_max, jnp.max(scores, axis=-1))
    weights = jnp.where(visible, jnp.exp(scores - new_max[..., None]), jnp.float32(0.0))
    new_sum = jnp.sum(weights, axis=-1)
    probs = weights.astype(jnp.bfloat16)
    added = jnp.einsum(
        "hqk,khd->hqd",
        probs,
        val_piece.reshape(count, heads_dev, head_size),
        preferred_element_type=jnp.float32,
    )
    result = jnp.transpose(added / new_sum[..., None], (1, 0, 2))
    return result.reshape(rows_dev, width).astype(jnp.bfloat16)


def solution(mesh):
    sizes = mesh.shape
    paired = sizes["chan"] == 4 and HEADS // sizes["chan"] == sizes["seq"]
    return jax.shard_map(
        fast_body if paired else body,
        mesh=mesh,
        in_specs=(
            P("seq", None, "chan"),
            P(None, "chan"),
            P("chan", None),
            P(),
            P("seq", None, "chan"),
            P("seq", "chan"),
            P("seq", "chan"),
        ),
        out_specs=P("seq", "chan"),
        check_vma=False,
    )
```

```python
import functools

import jax
import jax.numpy as jnp
from jax import lax
from jax.experimental import pallas as pl
from jax.experimental.pallas import tpu as pltpu
from jax.sharding import PartitionSpec as P

D = 4096
HEADS = 32
HEAD = D // HEADS
LANES = 128
PAD = 8
BF16 = jnp.bfloat16
F32 = jnp.float32
MIB = 1024 * 1024


BRIEF = pl.CostEstimate(flops=1, transcendentals=0, bytes_accessed=1)


VMEM = pl.BlockSpec(memory_space=pltpu.VMEM)
SMEM = pl.BlockSpec(memory_space=pltpu.SMEM)


def whole(shape):
    return pl.BlockSpec(shape, lambda *_: (0,) * len(shape))


def conv_kernel(group, hin_ref, halo_ref, taps_ref, out_ref):
    taps = taps_ref[...]
    count = taps.shape[0]
    width = taps.shape[1]
    kv = (hin_ref[1].astype(F32) * hin_ref[2].astype(F32)).astype(BF16)
    ext = jnp.concatenate([halo_ref[...], kv], axis=0)
    rows = kv.shape[0]
    blocks = rows // width
    windows = jnp.concatenate(
        [ext[b * width : (b + 2) * width] for b in range(blocks)], axis=1
    )
    high = taps.astype(BF16)
    low = (taps - high.astype(F32)).astype(BF16)
    source = lax.broadcasted_iota(jnp.int32, (width, 2 * width), 0)
    column = lax.broadcasted_iota(jnp.int32, (width, 2 * width), 1)
    flip = jnp.where(source + column == width, 1.0, 0.0).astype(BF16)
    total = None
    for part in (high, low):
        first = jnp.dot(part, flip, preferred_element_type=F32)
        toeplitz = jnp.concatenate(
            [
                pltpu.roll(
                    jnp.broadcast_to(first[g : g + 1], (width, 2 * width)),
                    0,
                    1,
                    stride=1,
                    stride_axis=0,
                ).astype(BF16)
                for g in range(count)
            ],
            axis=0,
        )
        product = jnp.dot(toeplitz, windows, preferred_element_type=F32)
        total = product if total is None else total + product
    owner = lax.broadcasted_iota(jnp.int32, (width, blocks * LANES), 1) % LANES // group
    conv = total[:width]
    for g in range(1, count):
        conv = jnp.where(owner == g, total[g * width : (g + 1) * width], conv)
    query = hin_ref[0].astype(F32)
    for b in range(blocks):
        piece = query[b * width : (b + 1) * width] * conv[:, b * LANES : (b + 1) * LANES]
        out_ref[b * width : (b + 1) * width, :] = piece.astype(BF16)


def hyena(hin, halo, filters):
    _, rows, width = hin.shape
    taps = filters.shape[1]
    group = width // filters.shape[0]
    per_tile = LANES // group
    return pl.pallas_call(
        functools.partial(conv_kernel, group),
        grid=(width // LANES,),
        in_specs=[
            pl.BlockSpec((3, rows, LANES), lambda i: (0, 0, i)),
            pl.BlockSpec((taps, LANES), lambda i: (0, i)),
            pl.BlockSpec((per_tile, taps), lambda i: (i, 0)),
        ],
        out_specs=pl.BlockSpec((rows, LANES), lambda i: (0, i)),
        out_shape=jax.ShapeDtypeStruct((rows, width), BF16),
        compiler_params=pltpu.CompilerParams(vmem_limit_bytes=12 * MIB),
        cost_estimate=BRIEF,
        name="hyena_filters",
    )(hin, halo, filters)


def norm_kernel(j, place_ref, own_ref, x_ref, y_ref, d0_ref, d1_ref, gain_ref, *rest):
    out_ref = rest[-1]
    chan = place_ref[0]
    half = d0_ref.shape[0]
    step = 16

    def band(i, diag_ref, start):
        at = pl.ds(pl.multiple_of(start + i * step, step), step)
        refs = (own_ref.at[at], x_ref.at[at], y_ref.at[at], diag_ref.at[pl.ds(pl.multiple_of(i * step, step), step)])
        parts = [r[...].astype(F32) for r in refs]
        total = sum(jnp.sum(p * p, axis=-1, keepdims=True) for p in parts)
        factor = lax.rsqrt(total / D + 1e-6)
        for m, p in enumerate(parts):
            where = chan ^ m
            out_ref[j, where, at, :] = (p * factor * gain_ref[where]).astype(BF16)

    for diag_ref, start in ((d0_ref, 0), (d1_ref, half)):
        pl.loop(0, half // step, unroll=2)(functools.partial(band, diag_ref=diag_ref, start=start))


def norm(place, j, zs, own, from_x, from_y, diag0, diag1, gain, buffer):
    rows, width = own.shape
    args = [place, own, from_x, from_y, diag0, diag1, gain] + ([] if buffer is None else [buffer])
    return pl.pallas_call(
        functools.partial(norm_kernel, j),
        in_specs=[SMEM] + [VMEM] * (len(args) - 1),
        out_specs=VMEM,
        out_shape=jax.ShapeDtypeStruct((zs, 4, rows, width), BF16),
        input_output_aliases={} if buffer is None else {7: 0},
        compiler_params=pltpu.CompilerParams(vmem_limit_bytes=16 * MIB),
        cost_estimate=BRIEF,
        name="norm",
    )(*args)


def project_kernel(shifts, zs, count, place_ref, normed_ref, *refs):
    n = len(shifts)
    own, sib, rest = refs[:n], refs[n : 2 * n], refs[2 * n :]
    before, outs = rest[:-count], rest[-count:]
    z, core = place_ref[1], place_ref[2]
    depth = normed_ref.shape[3] // 2
    for part, out_ref in enumerate(outs):
        for j in range(zs):
            total = before[part][j] if before else None
            for i, shift in enumerate(shifts):
                block = lax.rem(z + zs - shift, zs)
                for k, w_ref in enumerate((own[i], sib[i])):
                    at = pl.multiple_of((core ^ k) * depth, depth)
                    left = normed_ref[j, block, :, pl.ds(at, depth)]
                    right = w_ref[part * depth : (part + 1) * depth, :]
                    term = jnp.dot(left, right, preferred_element_type=F32)
                    total = term if total is None else total + term
            out_ref[j] = total.astype(out_ref.dtype)


def project(place, normed, own, sib, shifts, count, rounded, before=()):
    zs, _, rows, _ = normed.shape
    cols = own[0].shape[1]
    args = [place, normed, *own, *sib, *before]
    return pl.pallas_call(
        functools.partial(project_kernel, shifts, zs, count),
        in_specs=[SMEM] + [VMEM] * (len(args) - 1),
        out_specs=[VMEM] * count,
        out_shape=[jax.ShapeDtypeStruct((zs, rows, cols), BF16 if rounded else F32)] * count,
        compiler_params=pltpu.CompilerParams(vmem_limit_bytes=16 * MIB),
        cost_estimate=BRIEF,
        name="project",
    )(*args)


NT = (((1,), (1,)), ((), ()))


def lanes(op, s):
    full = s.shape[1] - s.shape[1] % LANES
    rest = s[:, full:] if full < s.shape[1] else None
    return functools.reduce(op, [s[:, i : i + LANES] for i in range(0, full, LANES)]), rest


def attend_kernel(shifts, place_ref, q_ref, k_ref, v_ref, ks_ref, vs_ref, ck_ref, cv_ref, *refs):
    outs, (old, new) = refs[: len(shifts)], refs[len(shifts) :]
    z, core = place_ref[1], place_ref[2]
    zs, rows, cols = k_ref.shape
    heads = range(cols // HEAD)
    factor = 1.4426950408889634 / HEAD**0.5
    low = -1e30
    hcols = [slice(h * HEAD, (h + 1) * HEAD) for h in heads]
    row = lax.broadcasted_iota(jnp.int32, (rows, rows), 0)
    col = lax.broadcasted_iota(jnp.int32, (rows, rows), 1)
    causal = col <= row

    for shift, out_ref in zip(shifts, outs):
        block = lax.rem(z + shift, zs)
        mine = lax.rem(zs - shift, zs)
        queries = [q_ref[mine, :, hcol] for hcol in hcols]

        def score(b, tops, diagonal):
            at = lax.rem(z + zs - b, zs)
            result = []
            for h, top in zip(heads, tops):
                s = lax.dot_general(queries[h], k_ref[at, :, hcols[h]], NT, preferred_element_type=F32)
                t = lax.dot_general(queries[h], ks_ref[at, :, hcols[h]], NT, preferred_element_type=F32)
                if diagonal:
                    s, t = jnp.where(causal, s, low), jnp.where(core == 1, t, low)
                new[h, b, :, :rows] = s
                new[h, b, :, rows:] = t
                folded = jnp.maximum(lanes(jnp.maximum, s)[0], lanes(jnp.maximum, t)[0])
                result.append(jnp.maximum(top, folded))
            return tuple(result)

        tops, ends = [], []
        for h in heads:
            s = lax.dot_general(queries[h], ck_ref[:, hcols[h]], NT, preferred_element_type=F32)
            old[h] = s
            folded, rest = lanes(jnp.maximum, s)
            tops.append(folded)
            ends.append(low if rest is None else jnp.max(rest, axis=-1, keepdims=True))
        tops = lax.fori_loop(0, block, functools.partial(score, diagonal=False), tuple(tops))
        tops = score(block, tops, True)
        tops = [
            jnp.maximum(jnp.max(top, axis=-1, keepdims=True), end) * factor
            for top, end in zip(tops, ends)
        ]

        def weigh(b, state):
            at = lax.rem(z + zs - b, zs)
            result = []
            for h, (total, summed) in zip(heads, state):
                weights = jnp.exp2(new[h, b] * factor - tops[h])
                probs = weights.astype(BF16)
                summed += jnp.dot(probs[:, :rows], v_ref[at, :, hcols[h]], preferred_element_type=F32)
                summed += jnp.dot(probs[:, rows:], vs_ref[at, :, hcols[h]], preferred_element_type=F32)
                result.append((total + lanes(jnp.add, weights)[0], summed))
            return tuple(result)

        state, ends = [], []
        for h in heads:
            weights = jnp.exp2(old[h] * factor - tops[h])
            folded, rest = lanes(jnp.add, weights)
            ends.append(0.0 if rest is None else jnp.sum(rest, axis=-1, keepdims=True))
            state.append(
                (folded, jnp.dot(weights.astype(BF16), cv_ref[:, hcols[h]], preferred_element_type=F32))
            )
        state = lax.fori_loop(0, block + 1, weigh, tuple(state))
        for h, (total, summed), end in zip(heads, state, ends):
            total = jnp.sum(total, axis=-1, keepdims=True) + end
            out_ref[:, hcols[h]] = (summed / total).astype(BF16)


def attend(shifts, place, q, k, v, k_sib, v_sib, ck, cv):
    zs, rows, cols = q.shape
    heads = cols // HEAD
    return pl.pallas_call(
        functools.partial(attend_kernel, shifts),
        in_specs=[SMEM] + [VMEM] * 7,
        out_specs=[VMEM] * len(shifts),
        out_shape=[jax.ShapeDtypeStruct((rows, cols), BF16)] * len(shifts),
        scratch_shapes=[
            pltpu.VMEM((heads, rows, ck.shape[0]), F32),
            pltpu.VMEM((heads, zs, rows, 2 * rows), F32),
        ],
        compiler_params=pltpu.CompilerParams(vmem_limit_bytes=20 * MIB),
        cost_estimate=BRIEF,
        name="attend",
    )(place, q, k, v, k_sib, v_sib, ck, cv)


def pack_kernel(at, crow, *refs):
    parcels, (out_ref, scratch) = refs[:-2], refs[-2:]
    for i, piece in enumerate(parcels):
        band = piece[at : at + crow + PAD].astype(F32)
        scratch[i * crow : (i + 1) * crow, :] = band[:crow]
    out_ref[...] = scratch[...].astype(BF16)


def pack(parcels, at, crow):
    cols = parcels[0].shape[1]
    out = (len(parcels) * crow, cols)
    return pl.pallas_call(
        functools.partial(pack_kernel, at, crow),
        in_specs=[VMEM] * len(parcels),
        out_specs=VMEM,
        out_shape=jax.ShapeDtypeStruct(out, BF16),
        scratch_shapes=[pltpu.VMEM(out, F32)],
        compiler_params=pltpu.CompilerParams(vmem_limit_bytes=24 * MIB),
        cost_estimate=BRIEF,
        name="pack",
    )(*parcels)


def join_kernel(place_ref, *refs):
    pieces, out_ref = refs[:-1], refs[-1]
    zs = len(pieces)
    cols = pieces[0].shape[1]
    for r, piece in enumerate(pieces):
        at = lax.rem(place_ref[1] + zs - r, zs) * cols
        out_ref[:, pl.ds(pl.multiple_of(at, cols), cols)] = piece[...]


def join(place, pieces):
    rows, cols = pieces[0].shape
    out = (rows, cols * len(pieces))
    return pl.pallas_call(
        join_kernel,
        in_specs=[SMEM] + [VMEM] * len(pieces),
        out_specs=whole(out),
        out_shape=jax.ShapeDtypeStruct(out, BF16),
        name="join",
    )(place, *pieces)


def shift_z(value, steps, zs):
    pairs = [(2 * a + k, 2 * ((a + steps) % zs) + k) for a in range(zs) for k in range(2)]
    return lax.ppermute(value, "seq", pairs)


def swap_core(value, zs):
    return lax.ppermute(value, "seq", [(2 * a + k, 2 * a + 1 - k) for a in range(zs) for k in range(2)])


def swap_chan(value, bit):
    return lax.ppermute(value, "chan", [(c, c ^ bit) for c in range(4)])


def after(value, *others):
    return lax.optimization_barrier((value, *others))[0]


def fast_body(hyena_in, prior_kv, filters, gain, w_qkv, cache_k, cache_v):
    rows, _, width = hyena_in.shape
    seqs = lax.axis_size("seq")
    zs = seqs // 2
    taps = filters.shape[1]
    depth, crow = w_qkv.shape[0], cache_k.shape[0]
    cols = width // zs
    my_seq = lax.axis_index("seq")
    z, core = my_seq // 2, my_seq % 2
    chan = lax.axis_index("chan")
    place = jnp.stack([chan, z, core]).astype(jnp.int32)

    w_t = jnp.transpose(w_qkv, (1, 0, 2))
    caches = [jnp.pad(c, ((0, PAD), (0, 0))) for c in (cache_k, cache_v)]

    def parcel(kind, r):
        at = (z + r) % zs * cols
        parts = [
            lax.dynamic_slice(w_t, (p, 0, at), (1, depth, cols))[0]
            for p in ((1, 2) if kind == "kv" else (0,))
        ]
        if kind == "kv":
            parts += [lax.dynamic_slice_in_dim(c, at, cols, 1) for c in caches]
        return jnp.concatenate(parts, axis=0)

    hin = jnp.transpose(hyena_in, (1, 0, 2))
    tail = (hin[1, rows - taps :].astype(F32) * hin[2, rows - taps :].astype(F32)).astype(BF16)
    halo = lax.ppermute(tail, "seq", [(s, s + 1) for s in range(seqs - 1)])
    halo = jnp.where(my_seq == 0, jnp.pad(prior_kv, ((taps - prior_kv.shape[0], 0), (0, 0))), halo)

    order = [("q", 1), ("q", 3), "acts", ("kv", 1), "acts", ("kv", 3), "acts", ("kv", 2), ("q", 2)]
    here = {(kind, 0): parcel(kind, 0) for kind in ("kv", "q")}
    acts = [hyena(hin, halo, filters)]
    sent = []
    for n, item in enumerate(order):
        value, steps = (acts[-1], 1) if item == "acts" else (parcel(*item), item[1])
        if n >= 2:
            value = after(value, sent[n - 2])
        sent.append(shift_z(value, steps, zs))
        if item == "acts":
            acts.append(sent[-1])
        else:
            here[item] = sent[-1]
    late = [("kv", 2), ("q", 2)]
    there = {item: swap_core(here[item], zs) for item in here if item not in late}

    pace = [[("q", 1), ("q", 3)], [("kv", 1)], [("kv", 3)], []]
    swapped = [[], [("kv", 0), ("q", 0)], [("q", 1), ("q", 3)], [("kv", 1)]]
    gain4 = gain.reshape(4, 1, width)
    half = rows // 2
    normed, diag0, diag1 = None, None, None
    for j, own in enumerate(acts):
        own = after(own, *[here[item] for item in pace[j]], *([diag0, diag1] if j else []))
        from_x, from_y = swap_chan(own, 1), swap_chan(own, 2)
        if j:
            settled = [normed] + [there[item] for item in swapped[j]]
            from_x, from_y = after(from_x, *settled), after(from_y, *settled)
        diag0 = swap_chan(from_x[:half], 2)
        diag1 = swap_chan(from_y[half:], 1)
        normed = norm(place, j, zs, own, from_x, from_y, diag0, diag1, gain4, normed)

    def sides(kind, shifts):
        return [[side[kind, r] for r in shifts] for side in (here, there)]

    every = tuple(range(zs))
    early = tuple(r for r in every if r != 2)
    (q_early,) = project(place, normed, *sides("q", early), early, 1, False)
    there["kv", 2] = swap_core(after(here["kv", 2], diag0, diag1), zs)
    mine, theirs = sides("kv", every)
    ck, cv = [pack(mine + theirs, 2 * depth + i * (crow + PAD), crow) for i in range(2)]
    k, v = project(place, after(normed, ck, cv, q_early), mine, theirs, every, 2, True)
    k_sib, v_sib = swap_core(k, zs), swap_core(v, zs)
    there["q", 2] = swap_core(after(here["q", 2], k), zs)
    (q,) = project(place, normed, *sides("q", (2,)), (2,), 1, True, (q_early,))
    pieces, out = {}, None
    for shifts, wait in (((2,), ()), ((1, 3), ()), ((0,), (2,))):
        ready = q if out is None else after(q, out[0], *[pieces[r] for r in wait])
        out = attend(shifts, place, ready, k, v, k_sib, v_sib, ck, cv)
        for r, piece in zip(shifts, out):
            pieces[r] = shift_z(piece, r, zs) if r else piece
    return join(place, [pieces[r] for r in range(zs)])


def shifted(value, axis, steps):
    count = lax.axis_size(axis)
    leading, last = (max(0, -steps), min(count, count - steps))
    return lax.ppermute(value, axis, [(source, source + steps) for source in range(leading, last)])


def body(hyena_in, prior_kv, filters, gain, w_qkv, cache_k, cache_v):
    rows_dev = hyena_in.shape[0]
    width = hyena_in.shape[2]
    history = prior_kv.shape[0]
    tap_count = filters.shape[1]
    head_size = D // HEADS
    heads_dev = width // head_size
    cache_rows = cache_k.shape[0]
    stride = cache_rows + rows_dev
    my_index = lax.axis_index("seq")
    stream_q = hyena_in[:, 0].astype(jnp.float32)
    kv_prod = (hyena_in[:, 1].astype(jnp.float32) * hyena_in[:, 2].astype(jnp.float32)).astype(
        jnp.bfloat16
    )
    before = shifted(kv_prod[rows_dev - history :], "seq", 1)
    before = jnp.where(my_index == 0, prior_kv, before)
    extended = jnp.concatenate([before, kv_prod], axis=0).astype(jnp.float32)
    tap_table = jnp.repeat(filters, width // filters.shape[0], axis=0).T

    def add_tap(tap_index, total):
        offset = (tap_count - 1 - tap_index).astype(jnp.int32)
        window = lax.dynamic_slice_in_dim(extended, offset, rows_dev, 0)
        coeff = lax.dynamic_index_in_dim(tap_table, tap_index.astype(jnp.int32), 0, keepdims=True)
        return total + coeff * window

    conv = lax.fori_loop(0, tap_count, add_tap, jnp.zeros((rows_dev, width), jnp.float32))
    hyena_out = (stream_q * conv).astype(jnp.bfloat16)
    whole = lax.all_gather(hyena_out, "chan", axis=1, tiled=True)
    as_float = whole.astype(jnp.float32)
    mean_sq = jnp.mean(as_float * as_float, axis=-1, keepdims=True)
    normed = (as_float * lax.rsqrt(mean_sq + 1e-06) * gain[None, :]).astype(jnp.bfloat16)
    piece = lax.all_gather(w_qkv, "seq", axis=0, tiled=True)
    flat_piece = piece.reshape(piece.shape[0], 3 * width)
    projected = jnp.dot(normed, flat_piece, preferred_element_type=jnp.float32)
    qkv = projected.astype(jnp.bfloat16).reshape(rows_dev, 3, width)
    scale = 1.0 / head_size**0.5
    keys_local = jnp.concatenate([cache_k, qkv[:, 1]], axis=0)
    vals_local = jnp.concatenate([cache_v, qkv[:, 2]], axis=0)
    head_q = qkv[:, 0].reshape(rows_dev, heads_dev, head_size)
    query_pos = my_index * rows_dev + jnp.arange(rows_dev, dtype=jnp.int32)
    run_max = jnp.full((heads_dev, rows_dev), -1e30, jnp.float32)
    key_piece = lax.all_gather(keys_local, "seq", axis=0, tiled=True)
    val_piece = lax.all_gather(vals_local, "seq", axis=0, tiled=True)
    count = key_piece.shape[0]
    row_ids = jnp.arange(count, dtype=jnp.int32)
    source = row_ids // stride
    within = row_ids % stride
    key_pos = jnp.where(within < cache_rows, -1, source * rows_dev + within - cache_rows)
    visible = (key_pos[None, :] <= query_pos[:, None])[None]
    scores = (
        jnp.einsum(
            "qhd,khd->hqk",
            head_q,
            key_piece.reshape(count, heads_dev, head_size),
            preferred_element_type=jnp.float32,
        )
        * scale
    )
    scores = jnp.where(visible, scores, jnp.float32(-1e30))
    new_max = jnp.maximum(run_max, jnp.max(scores, axis=-1))
    weights = jnp.where(visible, jnp.exp(scores - new_max[..., None]), jnp.float32(0.0))
    new_sum = jnp.sum(weights, axis=-1)
    probs = weights.astype(jnp.bfloat16)
    added = jnp.einsum(
        "hqk,khd->hqd",
        probs,
        val_piece.reshape(count, heads_dev, head_size),
        preferred_element_type=jnp.float32,
    )
    result = jnp.transpose(added / new_sum[..., None], (1, 0, 2))
    return result.reshape(rows_dev, width).astype(jnp.bfloat16)


def solution(mesh):
    sizes = mesh.shape
    paired = sizes["chan"] == 4 and HEADS // sizes["chan"] == sizes["seq"]
    return jax.shard_map(
        fast_body if paired else body,
        mesh=mesh,
        in_specs=(
            P("seq", None, "chan"),
            P(None, "chan"),
            P("chan", None),
            P(),
            P("seq", None, "chan"),
            P("seq", "chan"),
            P("seq", "chan"),
        ),
        out_specs=P("seq", "chan"),
        check_vma=False,
    )
```

```python
import functools

import jax
import jax.numpy as jnp
from jax import lax
from jax.experimental import pallas as pl
from jax.experimental.pallas import tpu as pltpu
from jax.sharding import PartitionSpec as P

D = 4096
HEADS = 32
HEAD = D // HEADS
LANES = 128
PAD = 8
BF16 = jnp.bfloat16
F32 = jnp.float32
MIB = 1024 * 1024


BRIEF = pl.CostEstimate(flops=1, transcendentals=0, bytes_accessed=1)


VMEM = pl.BlockSpec(memory_space=pltpu.VMEM)
SMEM = pl.BlockSpec(memory_space=pltpu.SMEM)


def whole(shape):
    return pl.BlockSpec(shape, lambda *_: (0,) * len(shape))


def conv_kernel(group, hin_ref, halo_ref, taps_ref, out_ref):
    taps = taps_ref[...]
    count = taps.shape[0]
    width = taps.shape[1]
    kv = (hin_ref[1].astype(F32) * hin_ref[2].astype(F32)).astype(BF16)
    ext = jnp.concatenate([halo_ref[...], kv], axis=0)
    rows = kv.shape[0]
    blocks = rows // width
    windows = jnp.concatenate(
        [ext[b * width : (b + 2) * width] for b in range(blocks)], axis=1
    )
    high = taps.astype(BF16)
    low = (taps - high.astype(F32)).astype(BF16)
    source = lax.broadcasted_iota(jnp.int32, (width, 2 * width), 0)
    column = lax.broadcasted_iota(jnp.int32, (width, 2 * width), 1)
    flip = jnp.where(source + column == width, 1.0, 0.0).astype(BF16)
    total = None
    for part in (high, low):
        first = jnp.dot(part, flip, preferred_element_type=F32)
        toeplitz = jnp.concatenate(
            [
                pltpu.roll(
                    jnp.broadcast_to(first[g : g + 1], (width, 2 * width)),
                    0,
                    1,
                    stride=1,
                    stride_axis=0,
                ).astype(BF16)
                for g in range(count)
            ],
            axis=0,
        )
        product = jnp.dot(toeplitz, windows, preferred_element_type=F32)
        total = product if total is None else total + product
    owner = lax.broadcasted_iota(jnp.int32, (width, blocks * LANES), 1) % LANES // group
    conv = total[:width]
    for g in range(1, count):
        conv = jnp.where(owner == g, total[g * width : (g + 1) * width], conv)
    query = hin_ref[0].astype(F32)
    for b in range(blocks):
        piece = query[b * width : (b + 1) * width] * conv[:, b * LANES : (b + 1) * LANES]
        out_ref[b * width : (b + 1) * width, :] = piece.astype(BF16)


def hyena(hin, halo, filters):
    _, rows, width = hin.shape
    taps = filters.shape[1]
    group = width // filters.shape[0]
    per_tile = LANES // group
    return pl.pallas_call(
        functools.partial(conv_kernel, group),
        grid=(width // LANES,),
        in_specs=[
            pl.BlockSpec((3, rows, LANES), lambda i: (0, 0, i)),
            pl.BlockSpec((taps, LANES), lambda i: (0, i)),
            pl.BlockSpec((per_tile, taps), lambda i: (i, 0)),
        ],
        out_specs=pl.BlockSpec((rows, LANES), lambda i: (0, i)),
        out_shape=jax.ShapeDtypeStruct((rows, width), BF16),
        compiler_params=pltpu.CompilerParams(vmem_limit_bytes=12 * MIB),
        cost_estimate=BRIEF,
        name="hyena_filters",
    )(hin, halo, filters)


def norm_kernel(j, place_ref, own_ref, x_ref, y_ref, d0_ref, d1_ref, gain_ref, *rest):
    out_ref = rest[-1]
    chan = place_ref[0]
    half = d0_ref.shape[0]
    step = 16

    def band(i, diag_ref, start):
        at = pl.ds(pl.multiple_of(start + i * step, step), step)
        refs = (own_ref.at[at], x_ref.at[at], y_ref.at[at], diag_ref.at[pl.ds(pl.multiple_of(i * step, step), step)])
        parts = [r[...].astype(F32) for r in refs]
        total = sum(jnp.sum(p * p, axis=-1, keepdims=True) for p in parts)
        factor = lax.rsqrt(total / D + 1e-6)
        for m, p in enumerate(parts):
            where = chan ^ m
            out_ref[j, where, at, :] = (p * factor * gain_ref[where]).astype(BF16)

    for diag_ref, start in ((d0_ref, 0), (d1_ref, half)):
        pl.loop(0, half // step, unroll=2)(functools.partial(band, diag_ref=diag_ref, start=start))


def norm(place, j, zs, own, from_x, from_y, diag0, diag1, gain, buffer):
    rows, width = own.shape
    args = [place, own, from_x, from_y, diag0, diag1, gain] + ([] if buffer is None else [buffer])
    return pl.pallas_call(
        functools.partial(norm_kernel, j),
        in_specs=[SMEM] + [VMEM] * (len(args) - 1),
        out_specs=VMEM,
        out_shape=jax.ShapeDtypeStruct((zs, 4, rows, width), BF16),
        input_output_aliases={} if buffer is None else {7: 0},
        compiler_params=pltpu.CompilerParams(vmem_limit_bytes=16 * MIB),
        cost_estimate=BRIEF,
        name="norm",
    )(*args)


def project_kernel(shifts, zs, count, place_ref, normed_ref, *refs):
    n = len(shifts)
    own, sib, rest = refs[:n], refs[n : 2 * n], refs[2 * n :]
    before, outs = rest[:-count], rest[-count:]
    z, core = place_ref[1], place_ref[2]
    depth = normed_ref.shape[3] // 2
    for part, out_ref in enumerate(outs):
        for j in range(zs):
            total = before[part][j] if before else None
            for i, shift in enumerate(shifts):
                block = lax.rem(z + zs - shift, zs)
                for k, w_ref in enumerate((own[i], sib[i])):
                    at = pl.multiple_of((core ^ k) * depth, depth)
                    left = normed_ref[j, block, :, pl.ds(at, depth)]
                    right = w_ref[part * depth : (part + 1) * depth, :]
                    term = jnp.dot(left, right, preferred_element_type=F32)
                    total = term if total is None else total + term
            out_ref[j] = total.astype(out_ref.dtype)


def project(place, normed, own, sib, shifts, count, rounded, before=()):
    zs, _, rows, _ = normed.shape
    cols = own[0].shape[1]
    args = [place, normed, *own, *sib, *before]
    return pl.pallas_call(
        functools.partial(project_kernel, shifts, zs, count),
        in_specs=[SMEM] + [VMEM] * (len(args) - 1),
        out_specs=[VMEM] * count,
        out_shape=[jax.ShapeDtypeStruct((zs, rows, cols), BF16 if rounded else F32)] * count,
        compiler_params=pltpu.CompilerParams(vmem_limit_bytes=16 * MIB),
        cost_estimate=BRIEF,
        name="project",
    )(*args)


NT = (((1,), (1,)), ((), ()))


def lanes(op, s):
    full = s.shape[1] - s.shape[1] % LANES
    rest = s[:, full:] if full < s.shape[1] else None
    return functools.reduce(op, [s[:, i : i + LANES] for i in range(0, full, LANES)]), rest


def attend_kernel(shifts, place_ref, q_ref, k_ref, v_ref, ks_ref, vs_ref, ck_ref, cv_ref, *refs):
    outs, (old, new) = refs[: len(shifts)], refs[len(shifts) :]
    z, core = place_ref[1], place_ref[2]
    zs, rows, cols = k_ref.shape
    heads = range(cols // HEAD)
    factor = 1.4426950408889634 / HEAD**0.5
    low = -1e30
    hcols = [slice(h * HEAD, (h + 1) * HEAD) for h in heads]
    row = lax.broadcasted_iota(jnp.int32, (rows, rows), 0)
    col = lax.broadcasted_iota(jnp.int32, (rows, rows), 1)
    causal = col <= row

    for shift, out_ref in zip(shifts, outs):
        block = lax.rem(z + shift, zs)
        mine = lax.rem(zs - shift, zs)
        queries = [q_ref[mine, :, hcol] for hcol in hcols]

        def score(b, tops, diagonal):
            at = lax.rem(z + zs - b, zs)
            result = []
            for h, top in zip(heads, tops):
                s = lax.dot_general(queries[h], k_ref[at, :, hcols[h]], NT, preferred_element_type=F32)
                t = lax.dot_general(queries[h], ks_ref[at, :, hcols[h]], NT, preferred_element_type=F32)
                if diagonal:
                    s, t = jnp.where(causal, s, low), jnp.where(core == 1, t, low)
                new[h, b, :, :rows] = s
                new[h, b, :, rows:] = t
                folded = jnp.maximum(lanes(jnp.maximum, s)[0], lanes(jnp.maximum, t)[0])
                result.append(jnp.maximum(top, folded))
            return tuple(result)

        tops, ends = [], []
        for h in heads:
            s = lax.dot_general(queries[h], ck_ref[:, hcols[h]], NT, preferred_element_type=F32)
            old[h] = s
            folded, rest = lanes(jnp.maximum, s)
            tops.append(folded)
            ends.append(low if rest is None else jnp.max(rest, axis=-1, keepdims=True))
        tops = lax.fori_loop(0, block, functools.partial(score, diagonal=False), tuple(tops))
        tops = score(block, tops, True)
        tops = [
            jnp.maximum(jnp.max(top, axis=-1, keepdims=True), end) * factor
            for top, end in zip(tops, ends)
        ]

        def weigh(b, state):
            at = lax.rem(z + zs - b, zs)
            result = []
            for h, (total, summed) in zip(heads, state):
                weights = jnp.exp2(new[h, b] * factor - tops[h])
                probs = weights.astype(BF16)
                summed += jnp.dot(probs[:, :rows], v_ref[at, :, hcols[h]], preferred_element_type=F32)
                summed += jnp.dot(probs[:, rows:], vs_ref[at, :, hcols[h]], preferred_element_type=F32)
                result.append((total + lanes(jnp.add, weights)[0], summed))
            return tuple(result)

        state, ends = [], []
        for h in heads:
            weights = jnp.exp2(old[h] * factor - tops[h])
            folded, rest = lanes(jnp.add, weights)
            ends.append(0.0 if rest is None else jnp.sum(rest, axis=-1, keepdims=True))
            state.append(
                (folded, jnp.dot(weights.astype(BF16), cv_ref[:, hcols[h]], preferred_element_type=F32))
            )
        state = lax.fori_loop(0, block + 1, weigh, tuple(state))
        for h, (total, summed), end in zip(heads, state, ends):
            total = jnp.sum(total, axis=-1, keepdims=True) + end
            out_ref[:, hcols[h]] = (summed / total).astype(BF16)


def attend(shifts, place, q, k, v, k_sib, v_sib, ck, cv):
    zs, rows, cols = q.shape
    heads = cols // HEAD
    return pl.pallas_call(
        functools.partial(attend_kernel, shifts),
        in_specs=[SMEM] + [VMEM] * 7,
        out_specs=[VMEM] * len(shifts),
        out_shape=[jax.ShapeDtypeStruct((rows, cols), BF16)] * len(shifts),
        scratch_shapes=[
            pltpu.VMEM((heads, rows, ck.shape[0]), F32),
            pltpu.VMEM((heads, zs, rows, 2 * rows), F32),
        ],
        compiler_params=pltpu.CompilerParams(vmem_limit_bytes=20 * MIB),
        cost_estimate=BRIEF,
        name="attend",
    )(place, q, k, v, k_sib, v_sib, ck, cv)


def pack_kernel(places, crow, *refs):
    parcels, outs, scratch = refs[: len(places)], refs[len(places) : -1], refs[-1]
    for n, out_ref in enumerate(outs):
        for i, (piece, at) in enumerate(zip(parcels, places)):
            at += n * (crow + PAD)
            scratch[i * crow : (i + 1) * crow, :] = piece[at : at + crow + PAD].astype(F32)[:crow]
        out_ref[...] = scratch[...].astype(BF16)


def pack(parcels, places, crow):
    out = (len(parcels) * crow, parcels[0].shape[1])
    return pl.pallas_call(
        functools.partial(pack_kernel, places, crow),
        in_specs=[VMEM] * len(parcels),
        out_specs=[VMEM] * 2,
        out_shape=[jax.ShapeDtypeStruct(out, BF16)] * 2,
        scratch_shapes=[pltpu.VMEM(out, F32)],
        compiler_params=pltpu.CompilerParams(vmem_limit_bytes=12 * MIB),
        cost_estimate=BRIEF,
        name="pack",
    )(*parcels)


def join_kernel(place_ref, *refs):
    pieces, out_ref = refs[:-1], refs[-1]
    zs = len(pieces)
    cols = pieces[0].shape[1]
    for r, piece in enumerate(pieces):
        at = lax.rem(place_ref[1] + zs - r, zs) * cols
        out_ref[:, pl.ds(pl.multiple_of(at, cols), cols)] = piece[...]


def join(place, pieces):
    rows, cols = pieces[0].shape
    out = (rows, cols * len(pieces))
    return pl.pallas_call(
        join_kernel,
        in_specs=[SMEM] + [VMEM] * len(pieces),
        out_specs=whole(out),
        out_shape=jax.ShapeDtypeStruct(out, BF16),
        name="join",
    )(place, *pieces)


def shift_z(value, steps, zs):
    pairs = [(2 * a + k, 2 * ((a + steps) % zs) + k) for a in range(zs) for k in range(2)]
    return lax.ppermute(value, "seq", pairs)


def swap_core(value, zs):
    return lax.ppermute(value, "seq", [(2 * a + k, 2 * a + 1 - k) for a in range(zs) for k in range(2)])


def swap_chan(value, bit):
    return lax.ppermute(value, "chan", [(c, c ^ bit) for c in range(4)])


def after(value, *others):
    return lax.optimization_barrier((value, *others))[0]


def fast_body(hyena_in, prior_kv, filters, gain, w_qkv, cache_k, cache_v):
    rows, _, width = hyena_in.shape
    seqs = lax.axis_size("seq")
    zs = seqs // 2
    taps = filters.shape[1]
    depth, crow = w_qkv.shape[0], cache_k.shape[0]
    cols = width // zs
    my_seq = lax.axis_index("seq")
    z, core = my_seq // 2, my_seq % 2
    chan = lax.axis_index("chan")
    place = jnp.stack([chan, z, core]).astype(jnp.int32)

    w_t = jnp.transpose(w_qkv, (1, 0, 2))
    caches = [jnp.pad(c, ((0, PAD), (0, 0))) for c in (cache_k, cache_v)]

    def parcel(kind, r, *others):
        at = (z + r) % zs * cols
        source = after(w_t, *others) if others else w_t
        parts = [
            lax.dynamic_slice(source, ("qkv".index(p), 0, at), (1, depth, cols))[0]
            for p in kind
            if p != "c"
        ]
        if "c" in kind:
            parts += [lax.dynamic_slice_in_dim(c, at, cols, 1) for c in caches]
        return jnp.concatenate(parts, axis=0)

    hin = jnp.transpose(hyena_in, (1, 0, 2))
    tail = (hin[1, rows - taps :].astype(F32) * hin[2, rows - taps :].astype(F32)).astype(BF16)
    halo = lax.ppermute(tail, "seq", [(s, s + 1) for s in range(seqs - 1)])
    halo = jnp.where(my_seq == 0, jnp.pad(prior_kv, ((taps - prior_kv.shape[0], 0), (0, 0))), halo)

    order = ["q1", "q3", "acts", "kvc1", "acts", "kvc3", "acts", "q2", "kc2", "v2"]
    acts = [hyena(hin, halo, filters)]
    here = {kind + "0": parcel(kind, 0, acts[0]) for kind in ("kvc", "q")}
    sent = []
    for n, item in enumerate(order):
        if item == "acts":
            value, steps = acts[-1], 1
        else:
            kind, steps = item[:-1], int(item[-1])
            value = parcel(kind, steps, *acts[: int(n >= 2)])
        if n >= 2:
            value = after(value, sent[n - 2])
        sent.append(shift_z(value, steps, zs))
        if item == "acts":
            acts.append(sent[-1])
        else:
            here[item] = sent[-1]
    late = ["q2", "kc2", "v2"]
    there = {item: swap_core(here[item], zs) for item in here if item not in late}

    pace = [[], ["kvc1"], ["kvc3"], ["q2"]]
    swapped = [[], ["kvc0", "q0"], ["q1", "q3"], ["kvc1"]]
    gain4 = gain.reshape(4, 1, width)
    half = rows // 2
    normed, diag0, diag1 = None, None, None
    for j, own in enumerate(acts):
        own = after(own, *([diag0, diag1] if j else [here["q1"], here["q3"]]))
        from_x, from_y = swap_chan(own, 1), swap_chan(own, 2)
        if j:
            settled = [normed] + [there[item] for item in swapped[j]] + [here[item] for item in pace[j]]
            from_x, from_y = after(from_x, *settled), after(from_y, *settled)
        diag0 = swap_chan(from_x[:half], 2)
        diag1 = swap_chan(from_y[half:], 1)
        normed = norm(place, j, zs, own, from_x, from_y, diag0, diag1, gain4, normed)

    def sides(*items):
        return [[side[item] for item in items] for side in (here, there)]

    early = (0, 1, 3)
    there["q2"] = swap_core(after(here["q2"], diag0, diag1), zs)
    there["kc2"] = swap_core(after(here["kc2"], diag0, diag1), zs)
    (q,) = project(place, normed, *sides("q0", "q1", "q3", "q2"), early + (2,), 1, True)
    k_early, v_early = project(place, normed, *sides("kvc0", "kvc1", "kvc3"), early, 2, False)
    kept = sum(sides("kvc0", "kvc1", "kc2", "kvc3"), [])
    ck, cv = pack(kept, [depth if i % zs == 2 else 2 * depth for i in range(2 * zs)], crow)
    (k,) = project(place, after(normed, q, ck), *sides("kc2"), (2,), 1, True, (k_early,))
    k_sib = swap_core(k, zs)
    there["v2"] = swap_core(after(here["v2"], k), zs)
    (v,) = project(place, normed, *sides("v2"), (2,), 1, True, (v_early,))
    v_sib = swap_core(v, zs)
    pieces, out = {}, None
    for shifts, wait in (((2,), ()), ((1, 3), ()), ((0,), (2,))):
        ready = q if out is None else after(q, out[0], *[pieces[r] for r in wait])
        out = attend(shifts, place, ready, k, v, k_sib, v_sib, ck, cv)
        for r, piece in zip(shifts, out):
            pieces[r] = shift_z(piece, r, zs) if r else piece
    return join(place, [pieces[r] for r in range(zs)])


def shifted(value, axis, steps):
    count = lax.axis_size(axis)
    leading, last = (max(0, -steps), min(count, count - steps))
    return lax.ppermute(value, axis, [(source, source + steps) for source in range(leading, last)])


def body(hyena_in, prior_kv, filters, gain, w_qkv, cache_k, cache_v):
    rows_dev = hyena_in.shape[0]
    width = hyena_in.shape[2]
    history = prior_kv.shape[0]
    tap_count = filters.shape[1]
    head_size = D // HEADS
    heads_dev = width // head_size
    cache_rows = cache_k.shape[0]
    stride = cache_rows + rows_dev
    my_index = lax.axis_index("seq")
    stream_q = hyena_in[:, 0].astype(jnp.float32)
    kv_prod = (hyena_in[:, 1].astype(jnp.float32) * hyena_in[:, 2].astype(jnp.float32)).astype(
        jnp.bfloat16
    )
    before = shifted(kv_prod[rows_dev - history :], "seq", 1)
    before = jnp.where(my_index == 0, prior_kv, before)
    extended = jnp.concatenate([before, kv_prod], axis=0).astype(jnp.float32)
    tap_table = jnp.repeat(filters, width // filters.shape[0], axis=0).T

    def add_tap(tap_index, total):
        offset = (tap_count - 1 - tap_index).astype(jnp.int32)
        window = lax.dynamic_slice_in_dim(extended, offset, rows_dev, 0)
        coeff = lax.dynamic_index_in_dim(tap_table, tap_index.astype(jnp.int32), 0, keepdims=True)
        return total + coeff * window

    conv = lax.fori_loop(0, tap_count, add_tap, jnp.zeros((rows_dev, width), jnp.float32))
    hyena_out = (stream_q * conv).astype(jnp.bfloat16)
    whole = lax.all_gather(hyena_out, "chan", axis=1, tiled=True)
    as_float = whole.astype(jnp.float32)
    mean_sq = jnp.mean(as_float * as_float, axis=-1, keepdims=True)
    normed = (as_float * lax.rsqrt(mean_sq + 1e-06) * gain[None, :]).astype(jnp.bfloat16)
    piece = lax.all_gather(w_qkv, "seq", axis=0, tiled=True)
    flat_piece = piece.reshape(piece.shape[0], 3 * width)
    projected = jnp.dot(normed, flat_piece, preferred_element_type=jnp.float32)
    qkv = projected.astype(jnp.bfloat16).reshape(rows_dev, 3, width)
    scale = 1.0 / head_size**0.5
    keys_local = jnp.concatenate([cache_k, qkv[:, 1]], axis=0)
    vals_local = jnp.concatenate([cache_v, qkv[:, 2]], axis=0)
    head_q = qkv[:, 0].reshape(rows_dev, heads_dev, head_size)
    query_pos = my_index * rows_dev + jnp.arange(rows_dev, dtype=jnp.int32)
    run_max = jnp.full((heads_dev, rows_dev), -1e30, jnp.float32)
    key_piece = lax.all_gather(keys_local, "seq", axis=0, tiled=True)
    val_piece = lax.all_gather(vals_local, "seq", axis=0, tiled=True)
    count = key_piece.shape[0]
    row_ids = jnp.arange(count, dtype=jnp.int32)
    source = row_ids // stride
    within = row_ids % stride
    key_pos = jnp.where(within < cache_rows, -1, source * rows_dev + within - cache_rows)
    visible = (key_pos[None, :] <= query_pos[:, None])[None]
    scores = (
        jnp.einsum(
            "qhd,khd->hqk",
            head_q,
            key_piece.reshape(count, heads_dev, head_size),
            preferred_element_type=jnp.float32,
        )
        * scale
    )
    scores = jnp.where(visible, scores, jnp.float32(-1e30))
    new_max = jnp.maximum(run_max, jnp.max(scores, axis=-1))
    weights = jnp.where(visible, jnp.exp(scores - new_max[..., None]), jnp.float32(0.0))
    new_sum = jnp.sum(weights, axis=-1)
    probs = weights.astype(jnp.bfloat16)
    added = jnp.einsum(
        "hqk,khd->hqd",
        probs,
        val_piece.reshape(count, heads_dev, head_size),
        preferred_element_type=jnp.float32,
    )
    result = jnp.transpose(added / new_sum[..., None], (1, 0, 2))
    return result.reshape(rows_dev, width).astype(jnp.bfloat16)


def solution(mesh):
    sizes = mesh.shape
    paired = sizes["chan"] == 4 and HEADS // sizes["chan"] == sizes["seq"]
    return jax.shard_map(
        fast_body if paired else body,
        mesh=mesh,
        in_specs=(
            P("seq", None, "chan"),
            P(None, "chan"),
            P("chan", None),
            P(),
            P("seq", None, "chan"),
            P("seq", "chan"),
            P("seq", "chan"),
        ),
        out_specs=P("seq", "chan"),
        check_vma=False,
    )
```

```python
import functools

import jax
import jax.numpy as jnp
from jax import lax
from jax.experimental import pallas as pl
from jax.experimental.pallas import tpu as pltpu
from jax.sharding import PartitionSpec as P

D = 4096
HEADS = 32
HEAD = D // HEADS
LANES = 128
PAD = 8
BF16 = jnp.bfloat16
F32 = jnp.float32
MIB = 1024 * 1024


BRIEF = pl.CostEstimate(flops=1, transcendentals=0, bytes_accessed=1)


VMEM = pl.BlockSpec(memory_space=pltpu.VMEM)
SMEM = pl.BlockSpec(memory_space=pltpu.SMEM)


def whole(shape):
    return pl.BlockSpec(shape, lambda *_: (0,) * len(shape))


def conv_kernel(group, hin_ref, halo_ref, taps_ref, out_ref):
    taps = taps_ref[...]
    count = taps.shape[0]
    width = taps.shape[1]
    kv = (hin_ref[1].astype(F32) * hin_ref[2].astype(F32)).astype(BF16)
    ext = jnp.concatenate([halo_ref[...], kv], axis=0)
    rows = kv.shape[0]
    blocks = rows // width
    windows = jnp.concatenate(
        [ext[b * width : (b + 2) * width] for b in range(blocks)], axis=1
    )
    high = taps.astype(BF16)
    low = (taps - high.astype(F32)).astype(BF16)
    source = lax.broadcasted_iota(jnp.int32, (width, 2 * width), 0)
    column = lax.broadcasted_iota(jnp.int32, (width, 2 * width), 1)
    flip = jnp.where(source + column == width, 1.0, 0.0).astype(BF16)
    total = None
    for part in (high, low):
        first = jnp.dot(part, flip, preferred_element_type=F32)
        toeplitz = jnp.concatenate(
            [
                pltpu.roll(
                    jnp.broadcast_to(first[g : g + 1], (width, 2 * width)),
                    0,
                    1,
                    stride=1,
                    stride_axis=0,
                ).astype(BF16)
                for g in range(count)
            ],
            axis=0,
        )
        product = jnp.dot(toeplitz, windows, preferred_element_type=F32)
        total = product if total is None else total + product
    owner = lax.broadcasted_iota(jnp.int32, (width, blocks * LANES), 1) % LANES // group
    conv = total[:width]
    for g in range(1, count):
        conv = jnp.where(owner == g, total[g * width : (g + 1) * width], conv)
    query = hin_ref[0].astype(F32)
    for b in range(blocks):
        piece = query[b * width : (b + 1) * width] * conv[:, b * LANES : (b + 1) * LANES]
        out_ref[b * width : (b + 1) * width, :] = piece.astype(BF16)


def hyena(hin, halo, filters):
    _, rows, width = hin.shape
    taps = filters.shape[1]
    group = width // filters.shape[0]
    per_tile = LANES // group
    return pl.pallas_call(
        functools.partial(conv_kernel, group),
        grid=(width // LANES,),
        in_specs=[
            pl.BlockSpec((3, rows, LANES), lambda i: (0, 0, i)),
            pl.BlockSpec((taps, LANES), lambda i: (0, i)),
            pl.BlockSpec((per_tile, taps), lambda i: (i, 0)),
        ],
        out_specs=pl.BlockSpec((rows, LANES), lambda i: (0, i)),
        out_shape=jax.ShapeDtypeStruct((rows, width), BF16),
        compiler_params=pltpu.CompilerParams(vmem_limit_bytes=12 * MIB),
        cost_estimate=BRIEF,
        name="hyena_filters",
    )(hin, halo, filters)


def norm_kernel(j, place_ref, own_ref, x_ref, y_ref, d0_ref, d1_ref, gain_ref, *rest):
    out_ref = rest[-1]
    chan = place_ref[0]
    half = d0_ref.shape[0]
    step = 16

    def band(i, diag_ref, start):
        at = pl.ds(pl.multiple_of(start + i * step, step), step)
        refs = (own_ref.at[at], x_ref.at[at], y_ref.at[at], diag_ref.at[pl.ds(pl.multiple_of(i * step, step), step)])
        parts = [r[...].astype(F32) for r in refs]
        total = sum(jnp.sum(p * p, axis=-1, keepdims=True) for p in parts)
        factor = lax.rsqrt(total / D + 1e-6)
        for m, p in enumerate(parts):
            where = chan ^ m
            out_ref[j, where, at, :] = (p * factor * gain_ref[where]).astype(BF16)

    for diag_ref, start in ((d0_ref, 0), (d1_ref, half)):
        pl.loop(0, half // step, unroll=2)(functools.partial(band, diag_ref=diag_ref, start=start))


def norm(place, j, zs, own, from_x, from_y, diag0, diag1, gain, buffer):
    rows, width = own.shape
    args = [place, own, from_x, from_y, diag0, diag1, gain] + ([] if buffer is None else [buffer])
    return pl.pallas_call(
        functools.partial(norm_kernel, j),
        in_specs=[SMEM] + [VMEM] * (len(args) - 1),
        out_specs=VMEM,
        out_shape=jax.ShapeDtypeStruct((zs, 4, rows, width), BF16),
        input_output_aliases={} if buffer is None else {7: 0},
        compiler_params=pltpu.CompilerParams(vmem_limit_bytes=16 * MIB),
        cost_estimate=BRIEF,
        name="norm",
    )(*args)


def project_kernel(shifts, zs, count, place_ref, normed_ref, *refs):
    n = len(shifts)
    own, sib, rest = refs[:n], refs[n : 2 * n], refs[2 * n :]
    before, outs = rest[:-count], rest[-count:]
    z, core = place_ref[1], place_ref[2]
    depth = normed_ref.shape[3] // 2
    for part, out_ref in enumerate(outs):
        for j in range(zs):
            total = before[part][j] if before else None
            for i, shift in enumerate(shifts):
                block = lax.rem(z + zs - shift, zs)
                for k, w_ref in enumerate((own[i], sib[i])):
                    at = pl.multiple_of((core ^ k) * depth, depth)
                    left = normed_ref[j, block, :, pl.ds(at, depth)]
                    right = w_ref[part * depth : (part + 1) * depth, :]
                    term = jnp.dot(left, right, preferred_element_type=F32)
                    total = term if total is None else total + term
            out_ref[j] = total.astype(out_ref.dtype)


def project(place, normed, own, sib, shifts, count, rounded, before=()):
    zs, _, rows, _ = normed.shape
    cols = own[0].shape[1]
    args = [place, normed, *own, *sib, *before]
    return pl.pallas_call(
        functools.partial(project_kernel, shifts, zs, count),
        in_specs=[SMEM] + [VMEM] * (len(args) - 1),
        out_specs=[VMEM] * count,
        out_shape=[jax.ShapeDtypeStruct((zs, rows, cols), BF16 if rounded else F32)] * count,
        compiler_params=pltpu.CompilerParams(vmem_limit_bytes=16 * MIB),
        cost_estimate=BRIEF,
        name="project",
    )(*args)


NT = (((1,), (1,)), ((), ()))


def lanes(op, s):
    full = s.shape[1] - s.shape[1] % LANES
    rest = s[:, full:] if full < s.shape[1] else None
    return functools.reduce(op, [s[:, i : i + LANES] for i in range(0, full, LANES)]), rest


def attend_kernel(shifts, place_ref, q_ref, k_ref, v_ref, ks_ref, vs_ref, ck_ref, cv_ref, *refs):
    outs, (old, new) = refs[: len(shifts)], refs[len(shifts) :]
    z, core = place_ref[1], place_ref[2]
    zs, rows, cols = k_ref.shape
    heads = range(cols // HEAD)
    factor = 1.4426950408889634 / HEAD**0.5
    low = -1e30
    hcols = [slice(h * HEAD, (h + 1) * HEAD) for h in heads]
    row = lax.broadcasted_iota(jnp.int32, (rows, rows), 0)
    col = lax.broadcasted_iota(jnp.int32, (rows, rows), 1)
    causal = col <= row

    for shift, out_ref in zip(shifts, outs):
        block = lax.rem(z + shift, zs)
        queries = [q_ref[place_ref[3 + block], :, hcol] for hcol in hcols]

        def score(b, tops, diagonal):
            at = place_ref[3 + b]
            result = []
            for h, top in zip(heads, tops):
                s = lax.dot_general(queries[h], k_ref[at, :, hcols[h]], NT, preferred_element_type=F32)
                t = lax.dot_general(queries[h], ks_ref[at, :, hcols[h]], NT, preferred_element_type=F32)
                if diagonal:
                    s, t = jnp.where(causal, s, low), jnp.where(core == 1, t, low)
                new[h, b, :, :rows] = s
                new[h, b, :, rows:] = t
                folded = jnp.maximum(lanes(jnp.maximum, s)[0], lanes(jnp.maximum, t)[0])
                result.append(jnp.maximum(top, folded))
            return tuple(result)

        tops, ends = [], []
        for h in heads:
            s = lax.dot_general(queries[h], ck_ref[:, hcols[h]], NT, preferred_element_type=F32)
            old[h] = s
            folded, rest = lanes(jnp.maximum, s)
            tops.append(folded)
            ends.append(low if rest is None else jnp.max(rest, axis=-1, keepdims=True))
        tops = lax.fori_loop(0, block, functools.partial(score, diagonal=False), tuple(tops))
        tops = score(block, tops, True)
        tops = [
            jnp.maximum(jnp.max(top, axis=-1, keepdims=True), end) * factor
            for top, end in zip(tops, ends)
        ]

        def weigh(b, state):
            at = place_ref[3 + b]
            result = []
            for h, (total, summed) in zip(heads, state):
                weights = jnp.exp2(new[h, b] * factor - tops[h])
                probs = weights.astype(BF16)
                summed += jnp.dot(probs[:, :rows], v_ref[at, :, hcols[h]], preferred_element_type=F32)
                summed += jnp.dot(probs[:, rows:], vs_ref[at, :, hcols[h]], preferred_element_type=F32)
                result.append((total + lanes(jnp.add, weights)[0], summed))
            return tuple(result)

        state, ends = [], []
        for h in heads:
            weights = jnp.exp2(old[h] * factor - tops[h])
            folded, rest = lanes(jnp.add, weights)
            ends.append(0.0 if rest is None else jnp.sum(rest, axis=-1, keepdims=True))
            state.append(
                (folded, jnp.dot(weights.astype(BF16), cv_ref[:, hcols[h]], preferred_element_type=F32))
            )
        state = lax.fori_loop(0, block + 1, weigh, tuple(state))
        for h, (total, summed), end in zip(heads, state, ends):
            total = jnp.sum(total, axis=-1, keepdims=True) + end
            out_ref[:, hcols[h]] = (summed / total).astype(BF16)


def attend(shifts, place, q, k, v, k_sib, v_sib, ck, cv):
    zs, rows, cols = q.shape
    heads = cols // HEAD
    return pl.pallas_call(
        functools.partial(attend_kernel, shifts),
        in_specs=[SMEM] + [VMEM] * 7,
        out_specs=[VMEM] * len(shifts),
        out_shape=[jax.ShapeDtypeStruct((rows, cols), BF16)] * len(shifts),
        scratch_shapes=[
            pltpu.VMEM((heads, rows, ck.shape[0]), F32),
            pltpu.VMEM((heads, zs, rows, 2 * rows), F32),
        ],
        compiler_params=pltpu.CompilerParams(vmem_limit_bytes=20 * MIB),
        cost_estimate=BRIEF,
        name="attend",
    )(place, q, k, v, k_sib, v_sib, ck, cv)


def pack_kernel(places, crow, *refs):
    parcels, outs, scratch = refs[: len(places)], refs[len(places) : -1], refs[-1]
    for n, out_ref in enumerate(outs):
        for i, (piece, at) in enumerate(zip(parcels, places)):
            at += n * (crow + PAD)
            scratch[i * crow : (i + 1) * crow, :] = piece[at : at + crow + PAD].astype(F32)[:crow]
        out_ref[...] = scratch[...].astype(BF16)


def pack(parcels, places, crow):
    out = (len(parcels) * crow, parcels[0].shape[1])
    return pl.pallas_call(
        functools.partial(pack_kernel, places, crow),
        in_specs=[VMEM] * len(parcels),
        out_specs=[VMEM] * 2,
        out_shape=[jax.ShapeDtypeStruct(out, BF16)] * 2,
        scratch_shapes=[pltpu.VMEM(out, F32)],
        compiler_params=pltpu.CompilerParams(vmem_limit_bytes=12 * MIB),
        cost_estimate=BRIEF,
        name="pack",
    )(*parcels)


def join_kernel(place_ref, *refs):
    pieces, out_ref = refs[:-1], refs[-1]
    zs = len(pieces)
    cols = pieces[0].shape[1]
    for r, piece in enumerate(pieces):
        at = lax.rem(place_ref[1] + zs - r, zs) * cols
        out_ref[:, pl.ds(pl.multiple_of(at, cols), cols)] = piece[...]


def join(place, pieces):
    rows, cols = pieces[0].shape
    out = (rows, cols * len(pieces))
    return pl.pallas_call(
        join_kernel,
        in_specs=[SMEM] + [VMEM] * len(pieces),
        out_specs=whole(out),
        out_shape=jax.ShapeDtypeStruct(out, BF16),
        name="join",
    )(place, *pieces)


def shift_z(value, steps, zs):
    pairs = [(2 * a + k, 2 * ((a + steps) % zs) + k) for a in range(zs) for k in range(2)]
    return lax.ppermute(value, "seq", pairs)


def step_z(value, steps, sources):
    return lax.ppermute(value, "seq", [(2 * a + k, 2 * (a + steps) + k) for a in sources for k in range(2)])


def swap_core(value, zs):
    return lax.ppermute(value, "seq", [(2 * a + k, 2 * a + 1 - k) for a in range(zs) for k in range(2)])


def swap_chan(value, bit):
    return lax.ppermute(value, "chan", [(c, c ^ bit) for c in range(4)])


def after(value, *others):
    return lax.optimization_barrier((value, *others))[0]


def fast_body(hyena_in, prior_kv, filters, gain, w_qkv, cache_k, cache_v):
    rows, _, width = hyena_in.shape
    seqs = lax.axis_size("seq")
    zs = seqs // 2
    taps = filters.shape[1]
    depth, crow = w_qkv.shape[0], cache_k.shape[0]
    cols = width // zs
    my_seq = lax.axis_index("seq")
    z, core = my_seq // 2, my_seq % 2
    chan = lax.axis_index("chan")
    slabs = jnp.array([[0, 1, 2, 3], [3, 0, 1, 2], [2, 1, 0, 3], [3, 2, 1, 0]], jnp.int32)
    place = jnp.concatenate([jnp.stack([chan, z, core]).astype(jnp.int32), slabs[z]])

    w_t = jnp.transpose(w_qkv, (1, 0, 2))
    caches = [jnp.pad(c, ((0, PAD), (0, 0))) for c in (cache_k, cache_v)]

    def parcel(kind, r, *others):
        at = (z + r) % zs * cols
        source = after(w_t, *others) if others else w_t
        parts = [
            lax.dynamic_slice(source, ("qkv".index(p), 0, at), (1, depth, cols))[0]
            for p in kind
            if p != "c"
        ]
        if "c" in kind:
            parts += [lax.dynamic_slice_in_dim(c, at, cols, 1) for c in caches]
        return jnp.concatenate(parts, axis=0)

    hin = jnp.transpose(hyena_in, (1, 0, 2))
    tail = (hin[1, rows - taps :].astype(F32) * hin[2, rows - taps :].astype(F32)).astype(BF16)
    halo = lax.ppermute(tail, "seq", [(s, s + 1) for s in range(seqs - 1)])
    halo = jnp.where(my_seq == 0, jnp.pad(prior_kv, ((taps - prior_kv.shape[0], 0), (0, 0))), halo)

    here, there = {}, {}

    def send(item, *others):
        kind, shift = item[:-1], int(item[-1])
        value = parcel(kind, shift, *others)
        here[item] = shift_z(after(value, *others), shift, zs) if shift else value

    def swap(item, *others):
        there[item] = swap_core(after(here[item], *others) if others else here[item], zs)

    send("q1")
    own = after(hyena(hin, halo, filters), here["q1"])
    gain4 = gain.reshape(4, 1, width)
    half = rows // 2

    def near(slab, *others):
        slab = after(slab, *others) if others else slab
        return slab, swap_chan(slab, 1), swap_chan(slab, 2)

    def far(slab, from_x, from_y, *others):
        from_x, from_y = after(from_x, *others), after(from_y, *others)
        return slab, from_x, from_y, swap_chan(from_x[:half], 2), swap_chan(from_y[half:], 1)

    slab0 = near(own)
    up, down = step_z(own, 1, (0, 1, 2)), step_z(own, -1, (1, 2, 3))
    send("kvc1", own)
    send("kvc0", own)
    send("q0", own)
    slab = jnp.where(z < 2, down, up)
    rest = jnp.where(z == 1, up, down)
    up, down = after(up, *slab0), after(down, *slab0)
    up, down = step_z(up, 1, (1, 2)), step_z(down, -1, (1, 2))
    send("kvc3", here["kvc1"])
    swap("kvc0")
    swap("q0")
    slab0 = far(*slab0, here["q0"])
    slab1 = near(slab, *slab0[3:])
    normed = norm(place, 0, zs, *slab0, gain4, None)
    slab = jnp.where(z < 2, down, up)
    ends = [(2 * a + k, 2 * b + k) for a, b in ((1, 0), (2, 3)) for k in range(2)]
    end = lax.ppermute(after(slab, *slab1), "seq", ends)
    send("q3", here["kvc3"])
    slab1 = far(*slab1, normed, here["kvc1"], there["kvc0"], there["q0"])
    slab2 = near(slab, *slab1[3:])
    normed = norm(place, 1, zs, *slab1, gain4, normed)
    slab = jnp.where(z % 3 == 0, end, rest)
    send("q2", end)
    swap("q1")
    swap("kvc1")
    slab2 = far(*slab2, normed, here["kvc3"], there["q1"], there["kvc1"])
    slab3 = near(slab, *slab2[3:])
    normed = norm(place, 2, zs, *slab2, gain4, normed)
    send("kc2", here["q3"])
    send("v2", here["q2"])
    swap("q3")
    swap("kvc3")
    slab3 = far(*slab3, normed, here["q2"], there["q3"])
    normed = norm(place, 3, zs, *slab3, gain4, normed)

    def sides(*items):
        return [[side[item] for item in items] for side in (here, there)]

    early = (0, 1, 3)
    swap("q2", *slab3[3:])
    swap("kc2", *slab3[3:])
    (q,) = project(place, normed, *sides("q0", "q1", "q3", "q2"), early + (2,), 1, True)
    k_early, v_early = project(place, normed, *sides("kvc0", "kvc1", "kvc3"), early, 2, False)
    kept = sum(sides("kvc0", "kvc1", "kc2", "kvc3"), [])
    ck, cv = pack(kept, [depth if i % zs == 2 else 2 * depth for i in range(2 * zs)], crow)
    (k,) = project(place, after(normed, q, ck), *sides("kc2"), (2,), 1, True, (k_early,))
    k_sib = swap_core(k, zs)
    swap("v2", k)
    (v,) = project(place, normed, *sides("v2"), (2,), 1, True, (v_early,))
    v_sib = swap_core(v, zs)
    pieces, out = {}, None
    for shifts, wait in (((2,), ()), ((1, 3), ()), ((0,), (2,))):
        ready = q if out is None else after(q, out[0], *[pieces[r] for r in wait])
        out = attend(shifts, place, ready, k, v, k_sib, v_sib, ck, cv)
        for r, piece in zip(shifts, out):
            pieces[r] = shift_z(piece, r, zs) if r else piece
    return join(place, [pieces[r] for r in range(zs)])


def shifted(value, axis, steps):
    count = lax.axis_size(axis)
    leading, last = (max(0, -steps), min(count, count - steps))
    return lax.ppermute(value, axis, [(source, source + steps) for source in range(leading, last)])


def body(hyena_in, prior_kv, filters, gain, w_qkv, cache_k, cache_v):
    rows_dev = hyena_in.shape[0]
    width = hyena_in.shape[2]
    history = prior_kv.shape[0]
    tap_count = filters.shape[1]
    head_size = D // HEADS
    heads_dev = width // head_size
    cache_rows = cache_k.shape[0]
    stride = cache_rows + rows_dev
    my_index = lax.axis_index("seq")
    stream_q = hyena_in[:, 0].astype(jnp.float32)
    kv_prod = (hyena_in[:, 1].astype(jnp.float32) * hyena_in[:, 2].astype(jnp.float32)).astype(
        jnp.bfloat16
    )
    before = shifted(kv_prod[rows_dev - history :], "seq", 1)
    before = jnp.where(my_index == 0, prior_kv, before)
    extended = jnp.concatenate([before, kv_prod], axis=0).astype(jnp.float32)
    tap_table = jnp.repeat(filters, width // filters.shape[0], axis=0).T

    def add_tap(tap_index, total):
        offset = (tap_count - 1 - tap_index).astype(jnp.int32)
        window = lax.dynamic_slice_in_dim(extended, offset, rows_dev, 0)
        coeff = lax.dynamic_index_in_dim(tap_table, tap_index.astype(jnp.int32), 0, keepdims=True)
        return total + coeff * window

    conv = lax.fori_loop(0, tap_count, add_tap, jnp.zeros((rows_dev, width), jnp.float32))
    hyena_out = (stream_q * conv).astype(jnp.bfloat16)
    whole = lax.all_gather(hyena_out, "chan", axis=1, tiled=True)
    as_float = whole.astype(jnp.float32)
    mean_sq = jnp.mean(as_float * as_float, axis=-1, keepdims=True)
    normed = (as_float * lax.rsqrt(mean_sq + 1e-06) * gain[None, :]).astype(jnp.bfloat16)
    piece = lax.all_gather(w_qkv, "seq", axis=0, tiled=True)
    flat_piece = piece.reshape(piece.shape[0], 3 * width)
    projected = jnp.dot(normed, flat_piece, preferred_element_type=jnp.float32)
    qkv = projected.astype(jnp.bfloat16).reshape(rows_dev, 3, width)
    scale = 1.0 / head_size**0.5
    keys_local = jnp.concatenate([cache_k, qkv[:, 1]], axis=0)
    vals_local = jnp.concatenate([cache_v, qkv[:, 2]], axis=0)
    head_q = qkv[:, 0].reshape(rows_dev, heads_dev, head_size)
    query_pos = my_index * rows_dev + jnp.arange(rows_dev, dtype=jnp.int32)
    run_max = jnp.full((heads_dev, rows_dev), -1e30, jnp.float32)
    key_piece = lax.all_gather(keys_local, "seq", axis=0, tiled=True)
    val_piece = lax.all_gather(vals_local, "seq", axis=0, tiled=True)
    count = key_piece.shape[0]
    row_ids = jnp.arange(count, dtype=jnp.int32)
    source = row_ids // stride
    within = row_ids % stride
    key_pos = jnp.where(within < cache_rows, -1, source * rows_dev + within - cache_rows)
    visible = (key_pos[None, :] <= query_pos[:, None])[None]
    scores = (
        jnp.einsum(
            "qhd,khd->hqk",
            head_q,
            key_piece.reshape(count, heads_dev, head_size),
            preferred_element_type=jnp.float32,
        )
        * scale
    )
    scores = jnp.where(visible, scores, jnp.float32(-1e30))
    new_max = jnp.maximum(run_max, jnp.max(scores, axis=-1))
    weights = jnp.where(visible, jnp.exp(scores - new_max[..., None]), jnp.float32(0.0))
    new_sum = jnp.sum(weights, axis=-1)
    probs = weights.astype(jnp.bfloat16)
    added = jnp.einsum(
        "hqk,khd->hqd",
        probs,
        val_piece.reshape(count, heads_dev, head_size),
        preferred_element_type=jnp.float32,
    )
    result = jnp.transpose(added / new_sum[..., None], (1, 0, 2))
    return result.reshape(rows_dev, width).astype(jnp.bfloat16)


def solution(mesh):
    sizes = mesh.shape
    paired = sizes["chan"] == 4 and sizes["seq"] == 8
    return jax.shard_map(
        fast_body if paired else body,
        mesh=mesh,
        in_specs=(
            P("seq", None, "chan"),
            P(None, "chan"),
            P("chan", None),
            P(),
            P("seq", None, "chan"),
            P("seq", "chan"),
            P("seq", "chan"),
        ),
        out_specs=P("seq", "chan"),
        check_vma=False,
    )
```

```python
import functools

import jax
import jax.numpy as jnp
from jax import lax
from jax.experimental import pallas as pl
from jax.experimental.pallas import tpu as pltpu
from jax.sharding import PartitionSpec as P

D = 4096
HEADS = 32
HEAD = D // HEADS
LANES = 128
PAD = 8
BF16 = jnp.bfloat16
F32 = jnp.float32
MIB = 1024 * 1024


BRIEF = pl.CostEstimate(flops=1, transcendentals=0, bytes_accessed=1)


VMEM = pl.BlockSpec(memory_space=pltpu.VMEM)
SMEM = pl.BlockSpec(memory_space=pltpu.SMEM)


def whole(shape):
    return pl.BlockSpec(shape, lambda *_: (0,) * len(shape))


def conv_kernel(group, hin_ref, halo_ref, taps_ref, out_ref):
    taps = taps_ref[...]
    count = taps.shape[0]
    width = taps.shape[1]
    kv = (hin_ref[1].astype(F32) * hin_ref[2].astype(F32)).astype(BF16)
    ext = jnp.concatenate([halo_ref[...], kv], axis=0)
    rows = kv.shape[0]
    blocks = rows // width
    windows = jnp.concatenate(
        [ext[b * width : (b + 2) * width] for b in range(blocks)], axis=1
    )
    high = taps.astype(BF16)
    low = (taps - high.astype(F32)).astype(BF16)
    source = lax.broadcasted_iota(jnp.int32, (width, 2 * width), 0)
    column = lax.broadcasted_iota(jnp.int32, (width, 2 * width), 1)
    flip = jnp.where(source + column == width, 1.0, 0.0).astype(BF16)
    total = None
    for part in (high, low):
        first = jnp.dot(part, flip, preferred_element_type=F32)
        toeplitz = jnp.concatenate(
            [
                pltpu.roll(
                    jnp.broadcast_to(first[g : g + 1], (width, 2 * width)),
                    0,
                    1,
                    stride=1,
                    stride_axis=0,
                ).astype(BF16)
                for g in range(count)
            ],
            axis=0,
        )
        product = jnp.dot(toeplitz, windows, preferred_element_type=F32)
        total = product if total is None else total + product
    owner = lax.broadcasted_iota(jnp.int32, (width, blocks * LANES), 1) % LANES // group
    conv = total[:width]
    for g in range(1, count):
        conv = jnp.where(owner == g, total[g * width : (g + 1) * width], conv)
    query = hin_ref[0].astype(F32)
    for b in range(blocks):
        piece = query[b * width : (b + 1) * width] * conv[:, b * LANES : (b + 1) * LANES]
        out_ref[b * width : (b + 1) * width, :] = piece.astype(BF16)


def hyena(hin, halo, filters):
    _, rows, width = hin.shape
    taps = filters.shape[1]
    group = width // filters.shape[0]
    per_tile = LANES // group
    return pl.pallas_call(
        functools.partial(conv_kernel, group),
        grid=(width // LANES,),
        in_specs=[
            pl.BlockSpec((3, rows, LANES), lambda i: (0, 0, i)),
            pl.BlockSpec((taps, LANES), lambda i: (0, i)),
            pl.BlockSpec((per_tile, taps), lambda i: (i, 0)),
        ],
        out_specs=pl.BlockSpec((rows, LANES), lambda i: (0, i)),
        out_shape=jax.ShapeDtypeStruct((rows, width), BF16),
        compiler_params=pltpu.CompilerParams(vmem_limit_bytes=8 * MIB),
        cost_estimate=BRIEF,
        name="hyena_filters",
    )(hin, halo, filters)


def norm_kernel(j, place_ref, own_ref, x_ref, y_ref, d0_ref, d1_ref, gain_ref, *rest):
    out_ref = rest[-1]
    chan = place_ref[0]
    half = d0_ref.shape[0]
    step = 16

    def band(i, diag_ref, start):
        at = pl.ds(pl.multiple_of(start + i * step, step), step)
        refs = (own_ref.at[at], x_ref.at[at], y_ref.at[at], diag_ref.at[pl.ds(pl.multiple_of(i * step, step), step)])
        parts = [r[...].astype(F32) for r in refs]
        total = sum(jnp.sum(p * p, axis=-1, keepdims=True) for p in parts)
        factor = lax.rsqrt(total / D + 1e-6)
        for m, p in enumerate(parts):
            where = chan ^ m
            out_ref[j, where, at, :] = (p * factor * gain_ref[where]).astype(BF16)

    for diag_ref, start in ((d0_ref, 0), (d1_ref, half)):
        pl.loop(0, half // step, unroll=2)(functools.partial(band, diag_ref=diag_ref, start=start))


def norm(place, j, zs, own, from_x, from_y, diag0, diag1, gain, buffer):
    rows, width = own.shape
    args = [place, own, from_x, from_y, diag0, diag1, gain] + ([] if buffer is None else [buffer])
    return pl.pallas_call(
        functools.partial(norm_kernel, j),
        in_specs=[SMEM] + [VMEM] * (len(args) - 1),
        out_specs=VMEM,
        out_shape=jax.ShapeDtypeStruct((zs, 4, rows, width), BF16),
        input_output_aliases={} if buffer is None else {7: 0},
        compiler_params=pltpu.CompilerParams(vmem_limit_bytes=4 * MIB),
        cost_estimate=BRIEF,
        name="norm",
    )(*args)


def project_kernel(shifts, slabs, parts, zs, extra, apart, place_ref, normed_ref, *refs):
    groups = 1 + max(group for group, _ in parts)
    n = len(shifts)
    weights, rest = refs[: 2 * n * groups], refs[2 * n * groups :]
    before, outs = rest[:extra], rest[-len(parts) * (zs if apart else 1) :]
    z, core = place_ref[1], place_ref[2]
    depth = normed_ref.shape[3] // 2
    for part, (group, row) in enumerate(parts):
        for j in slabs:
            total = before[part][j] if before else None
            for i, shift in enumerate(shifts):
                block = lax.rem(z + zs - shift, zs)
                for k in range(2):
                    at = pl.multiple_of((core ^ k) * depth, depth)
                    left = normed_ref[j, block, :, pl.ds(at, depth)]
                    right = weights[(2 * group + k) * n + i][row : row + depth, :]
                    term = jnp.dot(left, right, preferred_element_type=F32)
                    total = term if total is None else total + term
            if apart:
                outs[part * zs + j][...] = total.astype(outs[0].dtype)
            else:
                outs[part][j] = total.astype(outs[0].dtype)


def project(place, normed, groups, parts, shifts, slabs, rounded, before=(), into=(), apart=False):
    zs, _, rows, _ = normed.shape
    weights = [w for own, sib in groups for w in (*own, *sib)]
    args = [place, normed, *weights, *before, *into]
    shape = (rows, weights[0].shape[1]) if apart else (zs, rows, weights[0].shape[1])
    out = [jax.ShapeDtypeStruct(shape, BF16 if rounded else F32)] * (len(parts) * (zs if apart else 1))
    return pl.pallas_call(
        functools.partial(project_kernel, shifts, slabs, parts, zs, len(before), apart),
        in_specs=[SMEM] + [VMEM] * (len(args) - 1),
        out_specs=[VMEM] * len(out),
        out_shape=out,
        input_output_aliases={len(args) - len(into) + i: i for i in range(len(into))},
        compiler_params=pltpu.CompilerParams(vmem_limit_bytes=8 * MIB),
        cost_estimate=BRIEF,
        name="project",
    )(*args)


NT = (((1,), (1,)), ((), ()))


def lanes(op, s):
    full = s.shape[1] - s.shape[1] % LANES
    rest = s[:, full:] if full < s.shape[1] else None
    return functools.reduce(op, [s[:, i : i + LANES] for i in range(0, full, LANES)]), rest


def weigh_kernel(place_ref, q_ref, ck_ref, *refs):
    z, core = place_ref[1], place_ref[2]
    zs, rows, cols = q_ref.shape
    k_refs, ks_refs, (old_ref, new_ref, sum_ref, k_ref, ks_ref, scratch) = refs[:zs], refs[zs : 2 * zs], refs[2 * zs :]
    for j in range(zs):
        k_ref[j], ks_ref[j] = k_refs[j][...], ks_refs[j][...]
    crow = ck_ref.shape[0]
    factor = 1.4426950408889634 / HEAD**0.5
    row = lax.broadcasted_iota(jnp.int32, (rows, rows), 0)
    col = lax.broadcasted_iota(jnp.int32, (rows, rows), 1)
    causal = col <= row
    slab = [lax.rem(z + zs - b, zs) for b in range(zs)]

    for block in range(zs):
        for h in range(cols // HEAD):
            hcol = slice(h * HEAD, (h + 1) * HEAD)
            query = q_ref[slab[block], :, hcol]

            def score(key):
                return lax.dot_general(query, key, NT, preferred_element_type=F32)

            s = score(ck_ref[:, hcol])
            scratch[h, :, :crow] = s
            top, end = lanes(jnp.maximum, s)
            for b in range(block + 1):
                s, t = score(k_ref[slab[b], :, hcol]), score(ks_ref[slab[b], :, hcol])
                if b == block:
                    s, t = jnp.where(causal, s, -1e30), jnp.where(core == 1, t, -1e30)
                at = crow + 2 * rows * b
                scratch[h, :, at : at + rows] = s
                scratch[h, :, at + rows : at + 2 * rows] = t
                top = jnp.maximum(top, jnp.maximum(lanes(jnp.maximum, s)[0], lanes(jnp.maximum, t)[0]))
            top = jnp.max(top, axis=-1, keepdims=True)
            if end is not None:
                top = jnp.maximum(top, jnp.max(end, axis=-1, keepdims=True))
            top = top * factor

            weights = jnp.exp2(scratch[h, :, :crow] * factor - top)
            old_ref[block, h] = weights.astype(BF16)
            total, end = lanes(jnp.add, weights)
            for b in range(block + 1):
                at = crow + 2 * rows * b
                weights = jnp.exp2(scratch[h, :, at : at + 2 * rows] * factor - top)
                new_ref[block, h, b] = weights.astype(BF16)
                total = total + lanes(jnp.add, weights)[0]
            total = jnp.sum(total, axis=-1, keepdims=True)
            if end is not None:
                total = total + jnp.sum(end, axis=-1, keepdims=True)
            sum_ref[block, h] = jnp.broadcast_to(total, (rows, HEAD))


def weigh(place, q, k, k_sib, ck):
    zs, rows, cols = q.shape
    heads, crow = cols // HEAD, ck.shape[0]
    return pl.pallas_call(
        weigh_kernel,
        in_specs=[SMEM] + [VMEM] * (2 + 2 * zs),
        out_specs=[VMEM] * 3,
        out_shape=[
            jax.ShapeDtypeStruct((zs, heads, rows, crow), BF16),
            jax.ShapeDtypeStruct((zs, heads, zs, rows, 2 * rows), BF16),
            jax.ShapeDtypeStruct((zs, heads, rows, HEAD), F32),
        ],
        scratch_shapes=[pltpu.VMEM((zs, rows, cols), BF16)] * 2
        + [pltpu.VMEM((heads, rows, -(-(crow + 2 * rows * zs) // LANES) * LANES), F32)],
        compiler_params=pltpu.CompilerParams(vmem_limit_bytes=14 * MIB),
        cost_estimate=BRIEF,
        name="weigh",
    )(place, q, ck, *k, *k_sib)


def mix_kernel(shifts, place_ref, old_ref, new_ref, sum_ref, v_ref, vs_ref, cv_ref, *outs):
    z = place_ref[1]
    zs, rows, cols = v_ref.shape
    heads = range(cols // HEAD)
    hcols = [slice(h * HEAD, (h + 1) * HEAD) for h in heads]
    for shift, out_ref in zip(shifts, outs):
        block = lax.rem(z + shift, zs)

        def add(b, state):
            at = lax.rem(z + zs - b, zs)
            result = []
            for h, summed in zip(heads, state):
                probs = new_ref[block, h, b]
                value = jnp.concatenate([v_ref[at, :, hcols[h]], vs_ref[at, :, hcols[h]]], axis=0)
                result.append(summed + jnp.dot(probs, value, preferred_element_type=F32))
            return tuple(result)

        state = tuple(
            jnp.dot(old_ref[block, h], cv_ref[:, hcols[h]], preferred_element_type=F32) for h in heads
        )
        state = lax.fori_loop(0, block + 1, add, state)
        for h, summed in zip(heads, state):
            out_ref[:, hcols[h]] = (summed / sum_ref[block, h]).astype(BF16)


def mix(shifts, place, old, new, sums, v, v_sib, cv):
    _, rows, cols = v.shape
    return pl.pallas_call(
        functools.partial(mix_kernel, shifts),
        in_specs=[SMEM] + [VMEM] * 6,
        out_specs=[VMEM] * len(shifts),
        out_shape=[jax.ShapeDtypeStruct((rows, cols), BF16)] * len(shifts),
        compiler_params=pltpu.CompilerParams(vmem_limit_bytes=8 * MIB),
        cost_estimate=BRIEF,
        name="mix",
    )(place, old, new, sums, v, v_sib, cv)


def pack_kernel(places, crow, *refs):
    parcels, outs, scratch = refs[: len(places)], refs[len(places) : -1], refs[-1]
    for n, out_ref in enumerate(outs):
        for i, (piece, at) in enumerate(zip(parcels, places)):
            at += n * (crow + PAD)
            scratch[i * crow : (i + 1) * crow, :] = piece[at : at + crow + PAD].astype(F32)[:crow]
        out_ref[...] = scratch[...].astype(BF16)


def pack(parcels, places, crow):
    out = (len(parcels) * crow, parcels[0].shape[1])
    return pl.pallas_call(
        functools.partial(pack_kernel, places, crow),
        in_specs=[VMEM] * len(parcels),
        out_specs=[VMEM] * 2,
        out_shape=[jax.ShapeDtypeStruct(out, BF16)] * 2,
        scratch_shapes=[pltpu.VMEM(out, F32)],
        compiler_params=pltpu.CompilerParams(vmem_limit_bytes=8 * MIB),
        cost_estimate=BRIEF,
        name="pack",
    )(*parcels)


def join_kernel(place_ref, *refs):
    pieces, out_ref = refs[:-1], refs[-1]
    zs = len(pieces)
    cols = pieces[0].shape[1]
    for r, piece in enumerate(pieces):
        at = lax.rem(place_ref[1] + zs - r, zs) * cols
        out_ref[:, pl.ds(pl.multiple_of(at, cols), cols)] = piece[...]


def join(place, pieces):
    rows, cols = pieces[0].shape
    out = (rows, cols * len(pieces))
    return pl.pallas_call(
        join_kernel,
        in_specs=[SMEM] + [VMEM] * len(pieces),
        out_specs=whole(out),
        out_shape=jax.ShapeDtypeStruct(out, BF16),
        name="join",
    )(place, *pieces)


def shift_z(value, steps, zs):
    pairs = [(2 * a + k, 2 * ((a + steps) % zs) + k) for a in range(zs) for k in range(2)]
    return lax.ppermute(value, "seq", pairs)


def swap_core(value, zs):
    return lax.ppermute(value, "seq", [(2 * a + k, 2 * a + 1 - k) for a in range(zs) for k in range(2)])


def swap_chan(value, bit):
    return lax.ppermute(value, "chan", [(c, c ^ bit) for c in range(4)])


def after(value, *others):
    return lax.optimization_barrier((value, *others))[0]


def fast_body(hyena_in, prior_kv, filters, gain, w_qkv, cache_k, cache_v):
    rows, _, width = hyena_in.shape
    seqs = lax.axis_size("seq")
    zs = seqs // 2
    taps = filters.shape[1]
    depth, crow = w_qkv.shape[0], cache_k.shape[0]
    cols = width // zs
    my_seq = lax.axis_index("seq")
    z, core = my_seq // 2, my_seq % 2
    chan = lax.axis_index("chan")
    place = jnp.stack([chan, z, core]).astype(jnp.int32)

    w_t = jnp.transpose(w_qkv, (1, 0, 2))
    caches = [jnp.pad(c, ((0, PAD), (0, 0))) for c in (cache_k, cache_v)]

    def parcel(kind, r, *others):
        at = (z + r) % zs * cols
        source = after(w_t, *others) if others else w_t
        parts = [
            lax.dynamic_slice(source, ("qkv".index(p), 0, at), (1, depth, cols))[0]
            for p in kind
            if p != "c"
        ]
        if "c" in kind:
            parts += [lax.dynamic_slice_in_dim(c, at, cols, 1) for c in caches]
        return jnp.concatenate(parts, axis=0)

    hin = jnp.transpose(hyena_in, (1, 0, 2))
    tail = (hin[1, rows - taps :].astype(F32) * hin[2, rows - taps :].astype(F32)).astype(BF16)
    halo = lax.ppermute(tail, "seq", [(s, s + 1) for s in range(seqs - 1)])
    halo = jnp.where(my_seq == 0, jnp.pad(prior_kv, ((taps - prior_kv.shape[0], 0), (0, 0))), halo)

    order = ["q1", "q3", "acts", "kvc1", "acts", "kvc3", "acts", "q2", "kc2", "v2"]
    acts = [hyena(hin, halo, filters)]
    here = {kind + "0": parcel(kind, 0, acts[0]) for kind in ("kvc", "q")}
    sent = []
    for n, item in enumerate(order):
        if item == "acts":
            value, steps = acts[-1], 1
        else:
            kind, steps = item[:-1], int(item[-1])
            value = parcel(kind, steps, *acts[: int(n >= 2)])
        if n >= 2:
            value = after(value, sent[n - 2])
        sent.append(shift_z(value, steps, zs))
        if item == "acts":
            acts.append(sent[-1])
        else:
            here[item] = sent[-1]
    late = ["kc2", "v2"]
    there = {item: swap_core(here[item], zs) for item in here if item not in late}

    pace = [[], ["kvc1"], ["kvc3"], []]
    swapped = [[], ["kvc0", "q0"], ["q1", "q3"], ["kvc1"]]
    gain4 = gain.reshape(4, 1, width)
    half = rows // 2
    normed, diag0, diag1 = None, None, None
    every, early, last = tuple(range(zs)), (0, 1, 3), zs - 1

    def sides(*items):
        return [[side[item] for item in items] for side in (here, there)]

    def project_early(slabs, into=()):
        groups = [sides("q0", "q1", "q3"), sides("kvc0", "kvc1", "kvc3")]
        parts = ((0, 0), (1, 0), (1, depth))
        return project(place, normed, groups, parts, early, slabs, False, (), into)

    def project_last(item, sums, *others, apart=False):
        normed_then = after(normed, *others) if others else normed
        return project(place, normed_then, [sides(item)], ((0, 0),), (2,), every, True, (sums,), apart=apart)

    for j, own in enumerate(acts):
        own = after(own, *([diag0, diag1] if j else [here["q1"], here["q3"]]))
        from_x, from_y = swap_chan(own, 1), swap_chan(own, 2)
        if j:
            sums = project_early(every[:last]) if j == last else []
            normed = after(normed, *sums) if j == last else normed
            settled = [normed] + [there[item] for item in swapped[j]] + [here[item] for item in pace[j]]
            from_x, from_y = after(from_x, *settled), after(from_y, *settled)
        diag0 = swap_chan(from_x[:half], 2)
        diag1 = swap_chan(from_y[half:], 1)
        normed = norm(place, j, zs, own, from_x, from_y, diag0, diag1, gain4, normed)

    there["kc2"] = swap_core(after(here["kc2"], there["q2"], diag0, diag1), zs)
    q_sum, k_sum, v_sum = project_early(every[last:], sums)
    (q,) = project_last("q2", q_sum)
    kept = sum(sides("kvc0", "kvc1", "kc2", "kvc3"), [])
    ck, cv = pack(kept, [depth if i % zs == 2 else 2 * depth for i in range(2 * zs)], crow)
    k = project_last("kc2", k_sum, q, ck, apart=True)
    weights = weigh(place, q, k, [swap_core(slab, zs) for slab in k], ck)
    there["v2"] = swap_core(after(here["v2"], weights[2]), zs)
    (v,) = project_last("v2", v_sum)
    v_sib = swap_core(v, zs)
    pieces, out = {}, None
    for shifts, wait in (((2,), ()), ((1, 3), ()), ((0,), (2,))):
        ready = v if out is None else after(v, out[0], *[pieces[r] for r in wait])
        out = mix(shifts, place, *weights, ready, v_sib, cv)
        for r, piece in zip(shifts, out):
            pieces[r] = shift_z(piece, r, zs) if r else piece
    return join(place, [pieces[r] for r in range(zs)])


def shifted(value, axis, steps):
    count = lax.axis_size(axis)
    leading, last = (max(0, -steps), min(count, count - steps))
    return lax.ppermute(value, axis, [(source, source + steps) for source in range(leading, last)])


def body(hyena_in, prior_kv, filters, gain, w_qkv, cache_k, cache_v):
    rows_dev = hyena_in.shape[0]
    width = hyena_in.shape[2]
    history = prior_kv.shape[0]
    tap_count = filters.shape[1]
    head_size = D // HEADS
    heads_dev = width // head_size
    cache_rows = cache_k.shape[0]
    stride = cache_rows + rows_dev
    my_index = lax.axis_index("seq")
    stream_q = hyena_in[:, 0].astype(jnp.float32)
    kv_prod = (hyena_in[:, 1].astype(jnp.float32) * hyena_in[:, 2].astype(jnp.float32)).astype(
        jnp.bfloat16
    )
    before = shifted(kv_prod[rows_dev - history :], "seq", 1)
    before = jnp.where(my_index == 0, prior_kv, before)
    extended = jnp.concatenate([before, kv_prod], axis=0).astype(jnp.float32)
    tap_table = jnp.repeat(filters, width // filters.shape[0], axis=0).T

    def add_tap(tap_index, total):
        offset = (tap_count - 1 - tap_index).astype(jnp.int32)
        window = lax.dynamic_slice_in_dim(extended, offset, rows_dev, 0)
        coeff = lax.dynamic_index_in_dim(tap_table, tap_index.astype(jnp.int32), 0, keepdims=True)
        return total + coeff * window

    conv = lax.fori_loop(0, tap_count, add_tap, jnp.zeros((rows_dev, width), jnp.float32))
    hyena_out = (stream_q * conv).astype(jnp.bfloat16)
    whole = lax.all_gather(hyena_out, "chan", axis=1, tiled=True)
    as_float = whole.astype(jnp.float32)
    mean_sq = jnp.mean(as_float * as_float, axis=-1, keepdims=True)
    normed = (as_float * lax.rsqrt(mean_sq + 1e-06) * gain[None, :]).astype(jnp.bfloat16)
    piece = lax.all_gather(w_qkv, "seq", axis=0, tiled=True)
    flat_piece = piece.reshape(piece.shape[0], 3 * width)
    projected = jnp.dot(normed, flat_piece, preferred_element_type=jnp.float32)
    qkv = projected.astype(jnp.bfloat16).reshape(rows_dev, 3, width)
    scale = 1.0 / head_size**0.5
    keys_local = jnp.concatenate([cache_k, qkv[:, 1]], axis=0)
    vals_local = jnp.concatenate([cache_v, qkv[:, 2]], axis=0)
    head_q = qkv[:, 0].reshape(rows_dev, heads_dev, head_size)
    query_pos = my_index * rows_dev + jnp.arange(rows_dev, dtype=jnp.int32)
    run_max = jnp.full((heads_dev, rows_dev), -1e30, jnp.float32)
    key_piece = lax.all_gather(keys_local, "seq", axis=0, tiled=True)
    val_piece = lax.all_gather(vals_local, "seq", axis=0, tiled=True)
    count = key_piece.shape[0]
    row_ids = jnp.arange(count, dtype=jnp.int32)
    source = row_ids // stride
    within = row_ids % stride
    key_pos = jnp.where(within < cache_rows, -1, source * rows_dev + within - cache_rows)
    visible = (key_pos[None, :] <= query_pos[:, None])[None]
    scores = (
        jnp.einsum(
            "qhd,khd->hqk",
            head_q,
            key_piece.reshape(count, heads_dev, head_size),
            preferred_element_type=jnp.float32,
        )
        * scale
    )
    scores = jnp.where(visible, scores, jnp.float32(-1e30))
    new_max = jnp.maximum(run_max, jnp.max(scores, axis=-1))
    weights = jnp.where(visible, jnp.exp(scores - new_max[..., None]), jnp.float32(0.0))
    new_sum = jnp.sum(weights, axis=-1)
    probs = weights.astype(jnp.bfloat16)
    added = jnp.einsum(
        "hqk,khd->hqd",
        probs,
        val_piece.reshape(count, heads_dev, head_size),
        preferred_element_type=jnp.float32,
    )
    result = jnp.transpose(added / new_sum[..., None], (1, 0, 2))
    return result.reshape(rows_dev, width).astype(jnp.bfloat16)


def solution(mesh):
    sizes = mesh.shape
    paired = sizes["chan"] == 4 and HEADS // sizes["chan"] == sizes["seq"]
    return jax.shard_map(
        fast_body if paired else body,
        mesh=mesh,
        in_specs=(
            P("seq", None, "chan"),
            P(None, "chan"),
            P("chan", None),
            P(),
            P("seq", None, "chan"),
            P("seq", "chan"),
            P("seq", "chan"),
        ),
        out_specs=P("seq", "chan"),
        check_vma=False,
    )
```

```python
import functools

import jax
import jax.numpy as jnp
from jax import lax
from jax.experimental import pallas as pl
from jax.experimental.pallas import tpu as pltpu
from jax.sharding import PartitionSpec as P

D = 4096
HEADS = 32
HEAD = D // HEADS
LANES = 128
PAD = 8
BF16 = jnp.bfloat16
F32 = jnp.float32
MIB = 1024 * 1024


BRIEF = pl.CostEstimate(flops=1, transcendentals=0, bytes_accessed=1)


VMEM = pl.BlockSpec(memory_space=pltpu.VMEM)
SMEM = pl.BlockSpec(memory_space=pltpu.SMEM)


def whole(shape):
    return pl.BlockSpec(shape, lambda *_: (0,) * len(shape))


def conv_kernel(group, hin_ref, halo_ref, taps_ref, out_ref):
    taps = taps_ref[...]
    count = taps.shape[0]
    width = taps.shape[1]
    kv = (hin_ref[1].astype(F32) * hin_ref[2].astype(F32)).astype(BF16)
    ext = jnp.concatenate([halo_ref[...], kv], axis=0)
    rows = kv.shape[0]
    blocks = rows // width
    windows = jnp.concatenate(
        [ext[b * width : (b + 2) * width] for b in range(blocks)], axis=1
    )
    high = taps.astype(BF16)
    low = (taps - high.astype(F32)).astype(BF16)
    source = lax.broadcasted_iota(jnp.int32, (width, 2 * width), 0)
    column = lax.broadcasted_iota(jnp.int32, (width, 2 * width), 1)
    flip = jnp.where(source + column == width, 1.0, 0.0).astype(BF16)
    total = None
    for part in (high, low):
        first = jnp.dot(part, flip, preferred_element_type=F32)
        toeplitz = jnp.concatenate(
            [
                pltpu.roll(
                    jnp.broadcast_to(first[g : g + 1], (width, 2 * width)),
                    0,
                    1,
                    stride=1,
                    stride_axis=0,
                ).astype(BF16)
                for g in range(count)
            ],
            axis=0,
        )
        product = jnp.dot(toeplitz, windows, preferred_element_type=F32)
        total = product if total is None else total + product
    owner = lax.broadcasted_iota(jnp.int32, (width, blocks * LANES), 1) % LANES // group
    conv = total[:width]
    for g in range(1, count):
        conv = jnp.where(owner == g, total[g * width : (g + 1) * width], conv)
    query = hin_ref[0].astype(F32)
    for b in range(blocks):
        piece = query[b * width : (b + 1) * width] * conv[:, b * LANES : (b + 1) * LANES]
        out_ref[b * width : (b + 1) * width, :] = piece.astype(BF16)


def hyena(hin, halo, filters):
    _, rows, width = hin.shape
    taps = filters.shape[1]
    group = width // filters.shape[0]
    per_tile = LANES // group
    return pl.pallas_call(
        functools.partial(conv_kernel, group),
        grid=(width // LANES,),
        in_specs=[
            pl.BlockSpec((3, rows, LANES), lambda i: (0, 0, i)),
            pl.BlockSpec((taps, LANES), lambda i: (0, i)),
            pl.BlockSpec((per_tile, taps), lambda i: (i, 0)),
        ],
        out_specs=pl.BlockSpec((rows, LANES), lambda i: (0, i)),
        out_shape=jax.ShapeDtypeStruct((rows, width), BF16),
        compiler_params=pltpu.CompilerParams(vmem_limit_bytes=8 * MIB),
        cost_estimate=BRIEF,
        name="hyena_filters",
    )(hin, halo, filters)


def norm_kernel(j, place_ref, own_ref, x_ref, y_ref, d0_ref, d1_ref, gain_ref, *rest):
    out_ref = rest[-1]
    chan = place_ref[0]
    half = d0_ref.shape[0]
    step = 16

    def band(i, diag_ref, start):
        at = pl.ds(pl.multiple_of(start + i * step, step), step)
        refs = (own_ref.at[at], x_ref.at[at], y_ref.at[at], diag_ref.at[pl.ds(pl.multiple_of(i * step, step), step)])
        parts = [r[...].astype(F32) for r in refs]
        total = sum(jnp.sum(p * p, axis=-1, keepdims=True) for p in parts)
        factor = lax.rsqrt(total / D + 1e-6)
        for m, p in enumerate(parts):
            where = chan ^ m
            out_ref[j, where, at, :] = (p * factor * gain_ref[where]).astype(BF16)

    for diag_ref, start in ((d0_ref, 0), (d1_ref, half)):
        pl.loop(0, half // step, unroll=2)(functools.partial(band, diag_ref=diag_ref, start=start))


def norm(place, j, zs, own, from_x, from_y, diag0, diag1, gain, buffer):
    rows, width = own.shape
    args = [place, own, from_x, from_y, diag0, diag1, gain] + ([] if buffer is None else [buffer])
    return pl.pallas_call(
        functools.partial(norm_kernel, j),
        in_specs=[SMEM] + [VMEM] * (len(args) - 1),
        out_specs=VMEM,
        out_shape=jax.ShapeDtypeStruct((zs, 4, rows, width), BF16),
        input_output_aliases={} if buffer is None else {7: 0},
        compiler_params=pltpu.CompilerParams(vmem_limit_bytes=4 * MIB),
        cost_estimate=BRIEF,
        name="norm",
    )(*args)


def project_kernel(shifts, slabs, parts, zs, extra, apart, place_ref, normed_ref, *refs):
    groups = 1 + max(group for group, _ in parts)
    n = len(shifts)
    weights, rest = refs[: 2 * n * groups], refs[2 * n * groups :]
    before, outs = rest[:extra], rest[-len(parts) * (zs if apart else 1) :]
    z, core = place_ref[1], place_ref[2]
    depth = normed_ref.shape[3] // 2
    for part, (group, row) in enumerate(parts):
        for j in slabs:
            total = before[part][j] if before else None
            for i, shift in enumerate(shifts):
                block = lax.rem(z + zs - shift, zs)
                for k in range(2):
                    at = pl.multiple_of((core ^ k) * depth, depth)
                    left = normed_ref[j, block, :, pl.ds(at, depth)]
                    right = weights[(2 * group + k) * n + i][row : row + depth, :]
                    term = jnp.dot(left, right, preferred_element_type=F32)
                    total = term if total is None else total + term
            if apart:
                outs[part * zs + j][...] = total.astype(outs[0].dtype)
            else:
                outs[part][j] = total.astype(outs[0].dtype)


def project(place, normed, groups, parts, shifts, slabs, rounded, before=(), into=(), apart=False):
    zs, _, rows, _ = normed.shape
    weights = [w for own, sib in groups for w in (*own, *sib)]
    args = [place, normed, *weights, *before, *into]
    shape = (rows, weights[0].shape[1]) if apart else (zs, rows, weights[0].shape[1])
    out = [jax.ShapeDtypeStruct(shape, BF16 if rounded else F32)] * (len(parts) * (zs if apart else 1))
    return pl.pallas_call(
        functools.partial(project_kernel, shifts, slabs, parts, zs, len(before), apart),
        in_specs=[SMEM] + [VMEM] * (len(args) - 1),
        out_specs=[VMEM] * len(out),
        out_shape=out,
        input_output_aliases={len(args) - len(into) + i: i for i in range(len(into))},
        compiler_params=pltpu.CompilerParams(vmem_limit_bytes=8 * MIB),
        cost_estimate=BRIEF,
        name="project",
    )(*args)


NT = (((1,), (1,)), ((), ()))


def lanes(op, s):
    full = s.shape[1] - s.shape[1] % LANES
    rest = s[:, full:] if full < s.shape[1] else None
    return functools.reduce(op, [s[:, i : i + LANES] for i in range(0, full, LANES)]), rest


def weigh_kernel(place_ref, q_ref, ck_ref, *refs):
    z, core = place_ref[1], place_ref[2]
    zs, rows, cols = q_ref.shape
    k_refs, ks_refs, (old_ref, new_ref, sum_ref, k_ref, ks_ref, scratch) = refs[:zs], refs[zs : 2 * zs], refs[2 * zs :]
    for j in range(zs):
        k_ref[j], ks_ref[j] = k_refs[j][...], ks_refs[j][...]
    crow = ck_ref.shape[0]
    factor = 1.4426950408889634 / HEAD**0.5
    row = lax.broadcasted_iota(jnp.int32, (rows, rows), 0)
    col = lax.broadcasted_iota(jnp.int32, (rows, rows), 1)
    causal = col <= row
    slab = [lax.rem(z + zs - b, zs) for b in range(zs)]

    for block in range(zs):
        for h in range(cols // HEAD):
            hcol = slice(h * HEAD, (h + 1) * HEAD)
            query = q_ref[slab[block], :, hcol]

            def score(key):
                return lax.dot_general(query, key, NT, preferred_element_type=F32)

            s = score(ck_ref[:, hcol])
            scratch[h, :, :crow] = s
            top, end = lanes(jnp.maximum, s)
            for b in range(block + 1):
                s, t = score(k_ref[slab[b], :, hcol]), score(ks_ref[slab[b], :, hcol])
                if b == block:
                    s, t = jnp.where(causal, s, -1e30), jnp.where(core == 1, t, -1e30)
                at = crow + 2 * rows * b
                scratch[h, :, at : at + rows] = s
                scratch[h, :, at + rows : at + 2 * rows] = t
                top = jnp.maximum(top, jnp.maximum(lanes(jnp.maximum, s)[0], lanes(jnp.maximum, t)[0]))
            top = jnp.max(top, axis=-1, keepdims=True)
            if end is not None:
                top = jnp.maximum(top, jnp.max(end, axis=-1, keepdims=True))
            top = top * factor

            weights = jnp.exp2(scratch[h, :, :crow] * factor - top)
            old_ref[block, h] = weights.astype(BF16)
            total, end = lanes(jnp.add, weights)
            for b in range(block + 1):
                at = crow + 2 * rows * b
                weights = jnp.exp2(scratch[h, :, at : at + 2 * rows] * factor - top)
                new_ref[block, h, b] = weights.astype(BF16)
                total = total + lanes(jnp.add, weights)[0]
            total = jnp.sum(total, axis=-1, keepdims=True)
            if end is not None:
                total = total + jnp.sum(end, axis=-1, keepdims=True)
            sum_ref[block, h] = jnp.broadcast_to(total, (rows, HEAD))


def weigh(place, q, k, k_sib, ck):
    zs, rows, cols = q.shape
    heads, crow = cols // HEAD, ck.shape[0]
    return pl.pallas_call(
        weigh_kernel,
        in_specs=[SMEM] + [VMEM] * (2 + 2 * zs),
        out_specs=[VMEM] * 3,
        out_shape=[
            jax.ShapeDtypeStruct((zs, heads, rows, crow), BF16),
            jax.ShapeDtypeStruct((zs, heads, zs, rows, 2 * rows), BF16),
            jax.ShapeDtypeStruct((zs, heads, rows, HEAD), F32),
        ],
        scratch_shapes=[pltpu.VMEM((zs, rows, cols), BF16)] * 2
        + [pltpu.VMEM((heads, rows, -(-(crow + 2 * rows * zs) // LANES) * LANES), F32)],
        compiler_params=pltpu.CompilerParams(vmem_limit_bytes=14 * MIB),
        cost_estimate=BRIEF,
        name="weigh",
    )(place, q, ck, *k, *k_sib)


def mix_kernel(shifts, place_ref, old_ref, new_ref, sum_ref, v_ref, vs_ref, cv_ref, *outs):
    z = place_ref[1]
    zs, rows, cols = v_ref.shape
    heads = range(cols // HEAD)
    hcols = [slice(h * HEAD, (h + 1) * HEAD) for h in heads]
    for shift, out_ref in zip(shifts, outs):
        block = lax.rem(z + shift, zs)

        def add(b, state):
            at = lax.rem(z + zs - b, zs)
            result = []
            for h, summed in zip(heads, state):
                probs = new_ref[block, h, b]
                value = jnp.concatenate([v_ref[at, :, hcols[h]], vs_ref[at, :, hcols[h]]], axis=0)
                result.append(summed + jnp.dot(probs, value, preferred_element_type=F32))
            return tuple(result)

        state = tuple(
            jnp.dot(old_ref[block, h], cv_ref[:, hcols[h]], preferred_element_type=F32) for h in heads
        )
        state = lax.fori_loop(0, block + 1, add, state)
        for h, summed in zip(heads, state):
            out_ref[:, hcols[h]] = (summed / sum_ref[block, h]).astype(BF16)


def mix(shifts, place, old, new, sums, v, v_sib, cv):
    _, rows, cols = v.shape
    return pl.pallas_call(
        functools.partial(mix_kernel, shifts),
        in_specs=[SMEM] + [VMEM] * 6,
        out_specs=[VMEM] * len(shifts),
        out_shape=[jax.ShapeDtypeStruct((rows, cols), BF16)] * len(shifts),
        compiler_params=pltpu.CompilerParams(vmem_limit_bytes=8 * MIB),
        cost_estimate=BRIEF,
        name="mix",
    )(place, old, new, sums, v, v_sib, cv)


def pack_kernel(places, crow, *refs):
    parcels, outs, scratch = refs[: len(places)], refs[len(places) : -1], refs[-1]
    for n, out_ref in enumerate(outs):
        for i, (piece, at) in enumerate(zip(parcels, places)):
            at += n * (crow + PAD)
            scratch[i * crow : (i + 1) * crow, :] = piece[at : at + crow + PAD].astype(F32)[:crow]
        out_ref[...] = scratch[...].astype(BF16)


def pack(parcels, places, crow):
    out = (len(parcels) * crow, parcels[0].shape[1])
    return pl.pallas_call(
        functools.partial(pack_kernel, places, crow),
        in_specs=[VMEM] * len(parcels),
        out_specs=[VMEM] * 2,
        out_shape=[jax.ShapeDtypeStruct(out, BF16)] * 2,
        scratch_shapes=[pltpu.VMEM(out, F32)],
        compiler_params=pltpu.CompilerParams(vmem_limit_bytes=8 * MIB),
        cost_estimate=BRIEF,
        name="pack",
    )(*parcels)


def join_kernel(place_ref, *refs):
    pieces, out_ref = refs[:-1], refs[-1]
    zs = len(pieces)
    cols = pieces[0].shape[1]
    for r, piece in enumerate(pieces):
        at = lax.rem(place_ref[1] + zs - r, zs) * cols
        out_ref[:, pl.ds(pl.multiple_of(at, cols), cols)] = piece[...]


def join(place, pieces):
    rows, cols = pieces[0].shape
    out = (rows, cols * len(pieces))
    return pl.pallas_call(
        join_kernel,
        in_specs=[SMEM] + [VMEM] * len(pieces),
        out_specs=whole(out),
        out_shape=jax.ShapeDtypeStruct(out, BF16),
        name="join",
    )(place, *pieces)


def shift_z(value, steps, zs):
    pairs = [(2 * a + k, 2 * ((a + steps) % zs) + k) for a in range(zs) for k in range(2)]
    return lax.ppermute(value, "seq", pairs)


def swap_core(value, zs):
    return lax.ppermute(value, "seq", [(2 * a + k, 2 * a + 1 - k) for a in range(zs) for k in range(2)])


def swap_chan(value, bit):
    return lax.ppermute(value, "chan", [(c, c ^ bit) for c in range(4)])


def after(value, *others):
    return lax.optimization_barrier((value, *others))[0]


def fast_body(hyena_in, prior_kv, filters, gain, w_qkv, cache_k, cache_v):
    rows, _, width = hyena_in.shape
    seqs = lax.axis_size("seq")
    zs = seqs // 2
    taps = filters.shape[1]
    depth, crow = w_qkv.shape[0], cache_k.shape[0]
    cols = width // zs
    my_seq = lax.axis_index("seq")
    z, core = my_seq // 2, my_seq % 2
    chan = lax.axis_index("chan")
    place = jnp.stack([chan, z, core]).astype(jnp.int32)

    w_t = jnp.transpose(w_qkv, (1, 0, 2))
    caches = [jnp.pad(c, ((0, PAD), (0, 0))) for c in (cache_k, cache_v)]

    def parcel(kind, r, *others):
        at = (z + r) % zs * cols
        source = after(w_t, *others) if others else w_t
        parts = [
            lax.dynamic_slice(source, ("qkv".index(p), 0, at), (1, depth, cols))[0]
            for p in kind
            if p != "c"
        ]
        if "c" in kind:
            parts += [lax.dynamic_slice_in_dim(c, at, cols, 1) for c in caches]
        return jnp.concatenate(parts, axis=0)

    hin = jnp.transpose(hyena_in, (1, 0, 2))
    tail = (hin[1, rows - taps :].astype(F32) * hin[2, rows - taps :].astype(F32)).astype(BF16)
    halo = lax.ppermute(tail, "seq", [(s, s + 1) for s in range(seqs - 1)])
    halo = jnp.where(my_seq == 0, jnp.pad(prior_kv, ((taps - prior_kv.shape[0], 0), (0, 0))), halo)

    order = ["q1", "q3", "acts", "acts", "acts", "kvc1", "kvc3", "q2", "kc2", "v2"]
    acts = [hyena(hin, halo, filters)]
    here = {kind + "0": parcel(kind, 0, acts[0]) for kind in ("kvc", "q")}
    sent = []
    for n, item in enumerate(order):
        if item == "acts":
            value, steps = acts[-1], 1
        else:
            kind, steps = item[:-1], int(item[-1])
            value = parcel(kind, steps, *acts[: int(n >= 2)])
        if n >= 2:
            value = after(value, sent[n - 1] if item in ("kvc1", "kvc3") else sent[n - 2])
        sent.append(shift_z(value, steps, zs))
        if item == "acts":
            acts.append(sent[-1])
        else:
            here[item] = sent[-1]
    late = ["kc2", "v2"]
    there = {item: swap_core(here[item], zs) for item in here if item not in late}

    ahead = [[here["q1"], here["q3"]], [acts[2]], [acts[3]], [here["kvc3"]]]
    pace = [[], [], ["kvc1"], []]
    swapped = [[], ["kvc0", "q0"], ["q1", "q3"], ["kvc1"]]
    gain4 = gain.reshape(4, 1, width)
    half = rows // 2
    normed, diag0, diag1 = None, None, None
    every, early, last = tuple(range(zs)), (0, 1, 3), zs - 1

    def sides(*items):
        return [[side[item] for item in items] for side in (here, there)]

    def project_early(slabs, into=()):
        groups = [sides("q0", "q1", "q3"), sides("kvc0", "kvc1", "kvc3")]
        parts = ((0, 0), (1, 0), (1, depth))
        return project(place, normed, groups, parts, early, slabs, False, (), into)

    def project_last(item, sums, *others, apart=False):
        normed_then = after(normed, *others) if others else normed
        return project(place, normed_then, [sides(item)], ((0, 0),), (2,), every, True, (sums,), apart=apart)

    for j, own in enumerate(acts):
        own = after(own, *ahead[j], *([diag0, diag1] if j else []))
        from_x, from_y = swap_chan(own, 1), swap_chan(own, 2)
        if j:
            sums = project_early(every[:last]) if j == last else []
            normed = after(normed, *sums) if j == last else normed
            settled = [normed] + [there[item] for item in swapped[j]] + [here[item] for item in pace[j]]
            from_x, from_y = after(from_x, *settled), after(from_y, *settled)
        diag0 = swap_chan(from_x[:half], 2)
        diag1 = swap_chan(from_y[half:], 1)
        normed = norm(place, j, zs, own, from_x, from_y, diag0, diag1, gain4, normed)

    there["kc2"] = swap_core(after(here["kc2"], there["q2"], diag0, diag1), zs)
    q_sum, k_sum, v_sum = project_early(every[last:], sums)
    (q,) = project_last("q2", q_sum)
    kept = sum(sides("kvc0", "kvc1", "kc2", "kvc3"), [])
    ck, cv = pack(kept, [depth if i % zs == 2 else 2 * depth for i in range(2 * zs)], crow)
    k = project_last("kc2", k_sum, q, ck, apart=True)
    weights = weigh(place, q, k, [swap_core(slab, zs) for slab in k], ck)
    there["v2"] = swap_core(after(here["v2"], weights[2]), zs)
    (v,) = project_last("v2", v_sum)
    v_sib = swap_core(v, zs)
    pieces, out = {}, None
    for shifts, wait in (((2,), ()), ((1, 3), ()), ((0,), (2,))):
        ready = v if out is None else after(v, out[0], *[pieces[r] for r in wait])
        out = mix(shifts, place, *weights, ready, v_sib, cv)
        for r, piece in zip(shifts, out):
            pieces[r] = shift_z(piece, r, zs) if r else piece
    return join(place, [pieces[r] for r in range(zs)])


def shifted(value, axis, steps):
    count = lax.axis_size(axis)
    leading, last = (max(0, -steps), min(count, count - steps))
    return lax.ppermute(value, axis, [(source, source + steps) for source in range(leading, last)])


def body(hyena_in, prior_kv, filters, gain, w_qkv, cache_k, cache_v):
    rows_dev = hyena_in.shape[0]
    width = hyena_in.shape[2]
    history = prior_kv.shape[0]
    tap_count = filters.shape[1]
    head_size = D // HEADS
    heads_dev = width // head_size
    cache_rows = cache_k.shape[0]
    stride = cache_rows + rows_dev
    my_index = lax.axis_index("seq")
    stream_q = hyena_in[:, 0].astype(jnp.float32)
    kv_prod = (hyena_in[:, 1].astype(jnp.float32) * hyena_in[:, 2].astype(jnp.float32)).astype(
        jnp.bfloat16
    )
    before = shifted(kv_prod[rows_dev - history :], "seq", 1)
    before = jnp.where(my_index == 0, prior_kv, before)
    extended = jnp.concatenate([before, kv_prod], axis=0).astype(jnp.float32)
    tap_table = jnp.repeat(filters, width // filters.shape[0], axis=0).T

    def add_tap(tap_index, total):
        offset = (tap_count - 1 - tap_index).astype(jnp.int32)
        window = lax.dynamic_slice_in_dim(extended, offset, rows_dev, 0)
        coeff = lax.dynamic_index_in_dim(tap_table, tap_index.astype(jnp.int32), 0, keepdims=True)
        return total + coeff * window

    conv = lax.fori_loop(0, tap_count, add_tap, jnp.zeros((rows_dev, width), jnp.float32))
    hyena_out = (stream_q * conv).astype(jnp.bfloat16)
    whole = lax.all_gather(hyena_out, "chan", axis=1, tiled=True)
    as_float = whole.astype(jnp.float32)
    mean_sq = jnp.mean(as_float * as_float, axis=-1, keepdims=True)
    normed = (as_float * lax.rsqrt(mean_sq + 1e-06) * gain[None, :]).astype(jnp.bfloat16)
    piece = lax.all_gather(w_qkv, "seq", axis=0, tiled=True)
    flat_piece = piece.reshape(piece.shape[0], 3 * width)
    projected = jnp.dot(normed, flat_piece, preferred_element_type=jnp.float32)
    qkv = projected.astype(jnp.bfloat16).reshape(rows_dev, 3, width)
    scale = 1.0 / head_size**0.5
    keys_local = jnp.concatenate([cache_k, qkv[:, 1]], axis=0)
    vals_local = jnp.concatenate([cache_v, qkv[:, 2]], axis=0)
    head_q = qkv[:, 0].reshape(rows_dev, heads_dev, head_size)
    query_pos = my_index * rows_dev + jnp.arange(rows_dev, dtype=jnp.int32)
    run_max = jnp.full((heads_dev, rows_dev), -1e30, jnp.float32)
    key_piece = lax.all_gather(keys_local, "seq", axis=0, tiled=True)
    val_piece = lax.all_gather(vals_local, "seq", axis=0, tiled=True)
    count = key_piece.shape[0]
    row_ids = jnp.arange(count, dtype=jnp.int32)
    source = row_ids // stride
    within = row_ids % stride
    key_pos = jnp.where(within < cache_rows, -1, source * rows_dev + within - cache_rows)
    visible = (key_pos[None, :] <= query_pos[:, None])[None]
    scores = (
        jnp.einsum(
            "qhd,khd->hqk",
            head_q,
            key_piece.reshape(count, heads_dev, head_size),
            preferred_element_type=jnp.float32,
        )
        * scale
    )
    scores = jnp.where(visible, scores, jnp.float32(-1e30))
    new_max = jnp.maximum(run_max, jnp.max(scores, axis=-1))
    weights = jnp.where(visible, jnp.exp(scores - new_max[..., None]), jnp.float32(0.0))
    new_sum = jnp.sum(weights, axis=-1)
    probs = weights.astype(jnp.bfloat16)
    added = jnp.einsum(
        "hqk,khd->hqd",
        probs,
        val_piece.reshape(count, heads_dev, head_size),
        preferred_element_type=jnp.float32,
    )
    result = jnp.transpose(added / new_sum[..., None], (1, 0, 2))
    return result.reshape(rows_dev, width).astype(jnp.bfloat16)


def solution(mesh):
    sizes = mesh.shape
    paired = sizes["chan"] == 4 and HEADS // sizes["chan"] == sizes["seq"]
    return jax.shard_map(
        fast_body if paired else body,
        mesh=mesh,
        in_specs=(
            P("seq", None, "chan"),
            P(None, "chan"),
            P("chan", None),
            P(),
            P("seq", None, "chan"),
            P("seq", "chan"),
            P("seq", "chan"),
        ),
        out_specs=P("seq", "chan"),
        check_vma=False,
    )
```

```python
import functools

import jax
import jax.numpy as jnp
from jax import lax
from jax.experimental import pallas as pl
from jax.experimental.pallas import tpu as pltpu
from jax.sharding import PartitionSpec as P

D = 4096
HEADS = 32
HEAD = D // HEADS
LANES = 128
PAD = 8
BF16 = jnp.bfloat16
F32 = jnp.float32
MIB = 1024 * 1024


BRIEF = pl.CostEstimate(flops=1, transcendentals=0, bytes_accessed=1)


VMEM = pl.BlockSpec(memory_space=pltpu.VMEM)
SMEM = pl.BlockSpec(memory_space=pltpu.SMEM)


def whole(shape):
    return pl.BlockSpec(shape, lambda *_: (0,) * len(shape))


def conv_kernel(group, hin_ref, halo_ref, taps_ref, out_ref):
    taps = taps_ref[...]
    count = taps.shape[0]
    width = taps.shape[1]
    kv = (hin_ref[1].astype(F32) * hin_ref[2].astype(F32)).astype(BF16)
    ext = jnp.concatenate([halo_ref[...], kv], axis=0)
    rows = kv.shape[0]
    blocks = rows // width
    windows = jnp.concatenate(
        [ext[b * width : (b + 2) * width] for b in range(blocks)], axis=1
    )
    high = taps.astype(BF16)
    low = (taps - high.astype(F32)).astype(BF16)
    source = lax.broadcasted_iota(jnp.int32, (width, 2 * width), 0)
    column = lax.broadcasted_iota(jnp.int32, (width, 2 * width), 1)
    flip = jnp.where(source + column == width, 1.0, 0.0).astype(BF16)
    total = None
    for part in (high, low):
        first = jnp.dot(part, flip, preferred_element_type=F32)
        toeplitz = jnp.concatenate(
            [
                pltpu.roll(
                    jnp.broadcast_to(first[g : g + 1], (width, 2 * width)),
                    0,
                    1,
                    stride=1,
                    stride_axis=0,
                ).astype(BF16)
                for g in range(count)
            ],
            axis=0,
        )
        product = jnp.dot(toeplitz, windows, preferred_element_type=F32)
        total = product if total is None else total + product
    owner = lax.broadcasted_iota(jnp.int32, (width, blocks * LANES), 1) % LANES // group
    conv = total[:width]
    for g in range(1, count):
        conv = jnp.where(owner == g, total[g * width : (g + 1) * width], conv)
    query = hin_ref[0].astype(F32)
    for b in range(blocks):
        piece = query[b * width : (b + 1) * width] * conv[:, b * LANES : (b + 1) * LANES]
        out_ref[b * width : (b + 1) * width, :] = piece.astype(BF16)


def hyena(hin, halo, filters):
    _, rows, width = hin.shape
    taps = filters.shape[1]
    group = width // filters.shape[0]
    per_tile = LANES // group
    return pl.pallas_call(
        functools.partial(conv_kernel, group),
        grid=(width // LANES,),
        in_specs=[
            pl.BlockSpec((3, rows, LANES), lambda i: (0, 0, i)),
            pl.BlockSpec((taps, LANES), lambda i: (0, i)),
            pl.BlockSpec((per_tile, taps), lambda i: (i, 0)),
        ],
        out_specs=pl.BlockSpec((rows, LANES), lambda i: (0, i)),
        out_shape=jax.ShapeDtypeStruct((rows, width), BF16),
        compiler_params=pltpu.CompilerParams(vmem_limit_bytes=8 * MIB),
        cost_estimate=BRIEF,
        name="hyena_filters",
    )(hin, halo, filters)


def norm_kernel(j, place_ref, own_ref, x_ref, y_ref, d0_ref, d1_ref, gain_ref, *rest):
    out_ref = rest[-1]
    chan = place_ref[0]
    half = d0_ref.shape[0]
    step = 16

    def band(i, diag_ref, start):
        at = pl.ds(pl.multiple_of(start + i * step, step), step)
        refs = (own_ref.at[at], x_ref.at[at], y_ref.at[at], diag_ref.at[pl.ds(pl.multiple_of(i * step, step), step)])
        parts = [r[...].astype(F32) for r in refs]
        total = sum(jnp.sum(p * p, axis=-1, keepdims=True) for p in parts)
        factor = lax.rsqrt(total / D + 1e-6)
        for m, p in enumerate(parts):
            where = chan ^ m
            out_ref[j, where, at, :] = (p * factor * gain_ref[where]).astype(BF16)

    for diag_ref, start in ((d0_ref, 0), (d1_ref, half)):
        pl.loop(0, half // step, unroll=2)(functools.partial(band, diag_ref=diag_ref, start=start))


def norm(place, j, zs, own, from_x, from_y, diag0, diag1, gain, buffer):
    rows, width = own.shape
    args = [place, own, from_x, from_y, diag0, diag1, gain] + ([] if buffer is None else [buffer])
    return pl.pallas_call(
        functools.partial(norm_kernel, j),
        in_specs=[SMEM] + [VMEM] * (len(args) - 1),
        out_specs=VMEM,
        out_shape=jax.ShapeDtypeStruct((zs, 4, rows, width), BF16),
        input_output_aliases={} if buffer is None else {7: 0},
        compiler_params=pltpu.CompilerParams(vmem_limit_bytes=4 * MIB),
        cost_estimate=BRIEF,
        name="norm",
    )(*args)


def project_kernel(shifts, slabs, parts, zs, extra, apart, place_ref, normed_ref, *refs):
    groups = 1 + max(group for group, _ in parts)
    n = len(shifts)
    weights, rest = refs[: 2 * n * groups], refs[2 * n * groups :]
    before, outs = rest[:extra], rest[-len(parts) * (zs if apart else 1) :]
    z, core = place_ref[1], place_ref[2]
    depth = normed_ref.shape[3] // 2
    for part, (group, row_of) in enumerate(parts):
        for j in slabs:
            total = before[part][j] if before else None
            for i, shift in enumerate(shifts):
                block = lax.rem(z + zs - shift, zs)
                for k in range(2):
                    at = pl.multiple_of((core ^ k) * depth, depth)
                    left = normed_ref[j, block, :, pl.ds(at, depth)]
                    right = weights[(2 * group + k) * n + i][row_of[i] : row_of[i] + depth, :]
                    term = jnp.dot(left, right, preferred_element_type=F32)
                    total = term if total is None else total + term
            if apart:
                outs[part * zs + j][...] = total.astype(outs[0].dtype)
            else:
                outs[part][j] = total.astype(outs[0].dtype)


def project(place, normed, groups, parts, shifts, slabs, rounded, before=(), into=(), apart=False):
    zs, _, rows, _ = normed.shape
    weights = [w for own, sib in groups for w in (*own, *sib)]
    args = [place, normed, *weights, *before, *into]
    shape = (rows, weights[0].shape[1]) if apart else (zs, rows, weights[0].shape[1])
    out = [jax.ShapeDtypeStruct(shape, BF16 if rounded else F32)] * (len(parts) * (zs if apart else 1))
    return pl.pallas_call(
        functools.partial(project_kernel, shifts, slabs, parts, zs, len(before), apart),
        in_specs=[SMEM] + [VMEM] * (len(args) - 1),
        out_specs=[VMEM] * len(out),
        out_shape=out,
        input_output_aliases={len(args) - len(into) + i: i for i in range(len(into))},
        compiler_params=pltpu.CompilerParams(vmem_limit_bytes=8 * MIB),
        cost_estimate=BRIEF,
        name="project",
    )(*args)


NT = (((1,), (1,)), ((), ()))


def lanes(op, s):
    full = s.shape[1] - s.shape[1] % LANES
    rest = s[:, full:] if full < s.shape[1] else None
    return functools.reduce(op, [s[:, i : i + LANES] for i in range(0, full, LANES)]), rest


def weigh_kernel(place_ref, q_ref, ck_ref, *refs):
    core = place_ref[2]
    zs, rows, cols = q_ref.shape
    k_refs, ks_refs, (old_ref, new_ref, sum_ref, k_ref, ks_ref, scratch) = refs[:zs], refs[zs : 2 * zs], refs[2 * zs :]
    for j in range(zs):
        k_ref[j], ks_ref[j] = k_refs[j][...], ks_refs[j][...]
    crow = ck_ref.shape[0]
    factor = 1.4426950408889634 / HEAD**0.5
    row = lax.broadcasted_iota(jnp.int32, (rows, rows), 0)
    col = lax.broadcasted_iota(jnp.int32, (rows, rows), 1)
    causal = col <= row
    slab = [place_ref[3 + b] for b in range(zs)]

    for block in range(zs):
        for h in range(cols // HEAD):
            hcol = slice(h * HEAD, (h + 1) * HEAD)
            query = q_ref[slab[block], :, hcol]

            def score(key):
                return lax.dot_general(query, key, NT, preferred_element_type=F32)

            s = score(ck_ref[:, hcol])
            scratch[h, :, :crow] = s
            top, end = lanes(jnp.maximum, s)
            for b in range(block + 1):
                s, t = score(k_ref[slab[b], :, hcol]), score(ks_ref[slab[b], :, hcol])
                if b == block:
                    s, t = jnp.where(causal, s, -1e30), jnp.where(core == 1, t, -1e30)
                at = crow + 2 * rows * b
                scratch[h, :, at : at + rows] = s
                scratch[h, :, at + rows : at + 2 * rows] = t
                top = jnp.maximum(top, jnp.maximum(lanes(jnp.maximum, s)[0], lanes(jnp.maximum, t)[0]))
            top = jnp.max(top, axis=-1, keepdims=True)
            if end is not None:
                top = jnp.maximum(top, jnp.max(end, axis=-1, keepdims=True))
            top = top * factor

            weights = jnp.exp2(scratch[h, :, :crow] * factor - top)
            old_ref[block, h] = weights.astype(BF16)
            total, end = lanes(jnp.add, weights)
            for b in range(block + 1):
                at = crow + 2 * rows * b
                weights = jnp.exp2(scratch[h, :, at : at + 2 * rows] * factor - top)
                new_ref[block, h, b] = weights.astype(BF16)
                total = total + lanes(jnp.add, weights)[0]
            total = jnp.sum(total, axis=-1, keepdims=True)
            if end is not None:
                total = total + jnp.sum(end, axis=-1, keepdims=True)
            sum_ref[block, h] = jnp.broadcast_to(total, (rows, HEAD))


def weigh(place, q, k, k_sib, ck):
    zs, rows, cols = q.shape
    heads, crow = cols // HEAD, ck.shape[0]
    return pl.pallas_call(
        weigh_kernel,
        in_specs=[SMEM] + [VMEM] * (2 + 2 * zs),
        out_specs=[VMEM] * 3,
        out_shape=[
            jax.ShapeDtypeStruct((zs, heads, rows, crow), BF16),
            jax.ShapeDtypeStruct((zs, heads, zs, rows, 2 * rows), BF16),
            jax.ShapeDtypeStruct((zs, heads, rows, HEAD), F32),
        ],
        scratch_shapes=[pltpu.VMEM((zs, rows, cols), BF16)] * 2
        + [pltpu.VMEM((heads, rows, -(-(crow + 2 * rows * zs) // LANES) * LANES), F32)],
        compiler_params=pltpu.CompilerParams(vmem_limit_bytes=14 * MIB),
        cost_estimate=BRIEF,
        name="weigh",
    )(place, q, ck, *k, *k_sib)


def mix_kernel(shifts, place_ref, old_ref, new_ref, sum_ref, v_ref, vs_ref, cv_ref, *outs):
    z = place_ref[1]
    zs, rows, cols = v_ref.shape
    heads = range(cols // HEAD)
    hcols = [slice(h * HEAD, (h + 1) * HEAD) for h in heads]
    for shift, out_ref in zip(shifts, outs):
        block = lax.rem(z + shift, zs)

        def add(b, state):
            at = place_ref[3 + b]
            result = []
            for h, summed in zip(heads, state):
                probs = new_ref[block, h, b]
                value = jnp.concatenate([v_ref[at, :, hcols[h]], vs_ref[at, :, hcols[h]]], axis=0)
                result.append(summed + jnp.dot(probs, value, preferred_element_type=F32))
            return tuple(result)

        state = tuple(
            jnp.dot(old_ref[block, h], cv_ref[:, hcols[h]], preferred_element_type=F32) for h in heads
        )
        state = lax.fori_loop(0, block + 1, add, state)
        for h, summed in zip(heads, state):
            out_ref[:, hcols[h]] = (summed / sum_ref[block, h]).astype(BF16)


def mix(shifts, place, old, new, sums, v, v_sib, cv):
    _, rows, cols = v.shape
    return pl.pallas_call(
        functools.partial(mix_kernel, shifts),
        in_specs=[SMEM] + [VMEM] * 6,
        out_specs=[VMEM] * len(shifts),
        out_shape=[jax.ShapeDtypeStruct((rows, cols), BF16)] * len(shifts),
        compiler_params=pltpu.CompilerParams(vmem_limit_bytes=8 * MIB),
        cost_estimate=BRIEF,
        name="mix",
    )(place, old, new, sums, v, v_sib, cv)


def pack_kernel(places, crow, *refs):
    parcels, outs, scratch = refs[: len(places)], refs[len(places) : -1], refs[-1]
    for n, out_ref in enumerate(outs):
        for i, (piece, at) in enumerate(zip(parcels, places)):
            at += n * (crow + PAD)
            scratch[i * crow : (i + 1) * crow, :] = piece[at : at + crow + PAD].astype(F32)[:crow]
        out_ref[...] = scratch[...].astype(BF16)


def pack(parcels, places, crow):
    out = (len(parcels) * crow, parcels[0].shape[1])
    return pl.pallas_call(
        functools.partial(pack_kernel, places, crow),
        in_specs=[VMEM] * len(parcels),
        out_specs=[VMEM] * 2,
        out_shape=[jax.ShapeDtypeStruct(out, BF16)] * 2,
        scratch_shapes=[pltpu.VMEM(out, F32)],
        compiler_params=pltpu.CompilerParams(vmem_limit_bytes=8 * MIB),
        cost_estimate=BRIEF,
        name="pack",
    )(*parcels)


def join_kernel(place_ref, *refs):
    pieces, out_ref = refs[:-1], refs[-1]
    zs = len(pieces)
    cols = pieces[0].shape[1]
    for r, piece in enumerate(pieces):
        at = lax.rem(place_ref[1] + zs - r, zs) * cols
        out_ref[:, pl.ds(pl.multiple_of(at, cols), cols)] = piece[...]


def join(place, pieces):
    rows, cols = pieces[0].shape
    out = (rows, cols * len(pieces))
    return pl.pallas_call(
        join_kernel,
        in_specs=[SMEM] + [VMEM] * len(pieces),
        out_specs=whole(out),
        out_shape=jax.ShapeDtypeStruct(out, BF16),
        name="join",
    )(place, *pieces)


def shift_z(value, steps, zs):
    pairs = [(2 * a + k, 2 * ((a + steps) % zs) + k) for a in range(zs) for k in range(2)]
    return lax.ppermute(value, "seq", pairs)


def step_z(value, steps, sources):
    return lax.ppermute(value, "seq", [(2 * a + k, 2 * (a + steps) + k) for a in sources for k in range(2)])


def swap_core(value, zs):
    return lax.ppermute(value, "seq", [(2 * a + k, 2 * a + 1 - k) for a in range(zs) for k in range(2)])


def swap_chan(value, bit):
    return lax.ppermute(value, "chan", [(c, c ^ bit) for c in range(4)])


def after(value, *others):
    return lax.optimization_barrier((value, *others))[0]


def fast_body(hyena_in, prior_kv, filters, gain, w_qkv, cache_k, cache_v):
    rows, _, width = hyena_in.shape
    seqs = lax.axis_size("seq")
    zs = seqs // 2
    taps = filters.shape[1]
    depth, crow = w_qkv.shape[0], cache_k.shape[0]
    cols = width // zs
    my_seq = lax.axis_index("seq")
    z, core = my_seq // 2, my_seq % 2
    chan = lax.axis_index("chan")
    slabs = jnp.array([[0, 1, 2, 3], [3, 0, 1, 2], [2, 1, 0, 3], [3, 2, 1, 0]], jnp.int32)
    place = jnp.concatenate([jnp.stack([chan, z, core]).astype(jnp.int32), slabs[z]])

    w_t = jnp.transpose(w_qkv, (1, 0, 2))
    caches = [jnp.pad(c, ((0, PAD), (0, 0))) for c in (cache_k, cache_v)]

    def parcel(kind, r, *others):
        at = (z + r) % zs * cols
        source = after(w_t, *others) if others else w_t
        parts = [
            lax.dynamic_slice(source, ("qkv".index(p), 0, at), (1, depth, cols))[0]
            for p in kind
            if p != "c"
        ]
        if "c" in kind:
            parts += [lax.dynamic_slice_in_dim(c, at, cols, 1) for c in caches]
        return jnp.concatenate(parts, axis=0)

    hin = jnp.transpose(hyena_in, (1, 0, 2))
    tail = (hin[1, rows - taps :].astype(F32) * hin[2, rows - taps :].astype(F32)).astype(BF16)
    halo = lax.ppermute(tail, "seq", [(s, s + 1) for s in range(seqs - 1)])
    halo = jnp.where(my_seq == 0, jnp.pad(prior_kv, ((taps - prior_kv.shape[0], 0), (0, 0))), halo)

    here, there = {}, {}
    every, early, last = tuple(range(zs)), (0, 1, 3), zs - 1

    def send(item, *others):
        kind, shift = item[:-1], int(item[-1])
        value = parcel(kind, shift, *others)
        here[item] = shift_z(after(value, *others) if others else value, shift, zs) if shift else value

    def swap(item, *others):
        there[item] = swap_core(after(here[item], *others) if others else here[item], zs)

    def near(slab, *others):
        slab = after(slab, *others) if others else slab
        return slab, swap_chan(slab, 1), swap_chan(slab, 2)

    def far(slab, from_x, from_y, *others):
        from_x, from_y = after(from_x, *others), after(from_y, *others)
        return slab, from_x, from_y, swap_chan(from_x[:half], 2), swap_chan(from_y[half:], 1)

    def sides(*items):
        return [[side[item] for item in items] for side in (here, there)]

    def project_early(slabs, into=()):
        groups = [sides("qkvc0", "q1", "q3"), sides("qkvc0", "kvc1", "kvc3")]
        parts = ((0, (0, 0, 0)), (1, (depth, 0, 0)), (1, (2 * depth, depth, depth)))
        return project(place, normed, groups, parts, early, slabs, False, (), into)

    def project_last(item, sums, *others, apart=False):
        normed_then = after(normed, *others) if others else normed
        return project(place, normed_then, [sides(item)], ((0, (0,)),), (2,), every, True, (sums,), apart=apart)

    send("q1")
    send("q3")
    own = after(hyena(hin, halo, filters), here["q1"], here["q3"])
    send("qkvc0", own)
    swap("qkvc0")
    gain4 = gain.reshape(4, 1, width)
    half = rows // 2

    slab0 = near(own)
    up, down = step_z(own, 1, (0, 1, 2)), step_z(own, -1, (1, 2, 3))
    send("kvc1", up, down)
    slab = jnp.where(z < 2, down, up)
    rest = jnp.where(z == 1, up, down)
    up, down = after(up, *slab0), after(down, *slab0)
    up, down = step_z(up, 1, (1, 2)), step_z(down, -1, (1, 2))
    send("kvc3", here["kvc1"])
    slab0 = far(*slab0, rest)
    slab1 = near(slab, *slab0[3:])
    normed = norm(place, 0, zs, *slab0, gain4, None)
    slab = jnp.where(z < 2, down, up)
    ends = [(2 * a + k, 2 * b + k) for a, b in ((1, 0), (2, 3)) for k in range(2)]
    end = lax.ppermute(after(slab, *slab1), "seq", ends)
    slab1 = far(*slab1, normed, here["kvc1"], there["qkvc0"])
    slab2 = near(slab, *slab1[3:])
    normed = norm(place, 1, zs, *slab1, gain4, normed)
    slab = jnp.where(z % 3 == 0, end, rest)
    send("q2", end)
    swap("q1")
    swap("q3")
    swap("kvc1")
    slab2 = far(*slab2, normed, here["kvc3"], there["q1"], there["q3"], there["kvc1"])
    slab3 = near(slab, *slab2[3:])
    normed = norm(place, 2, zs, *slab2, gain4, normed)
    send("kc2", here["kvc3"])
    send("v2", here["q2"])
    swap("kvc3")
    swap("q2")
    sums = project_early(every[:last])
    slab3 = far(*slab3, *sums)
    normed = norm(place, 3, zs, *slab3, gain4, after(normed, *sums))

    swap("kc2", there["q2"], *slab3[3:])
    q_sum, k_sum, v_sum = project_early(every[last:], sums)
    (q,) = project_last("q2", q_sum)
    kept = sum(sides("qkvc0", "kvc1", "kc2", "kvc3"), [])
    ck, cv = pack(kept, [3 * depth, 2 * depth, depth, 2 * depth] * 2, crow)
    k = project_last("kc2", k_sum, q, ck, apart=True)
    weights = weigh(place, q, k, [swap_core(slab, zs) for slab in k], ck)
    swap("v2", weights[2])
    (v,) = project_last("v2", v_sum)
    v_sib = swap_core(v, zs)
    pieces, out = {}, None
    for shifts, wait in (((2,), ()), ((1, 3), ()), ((0,), (2,))):
        ready = v if out is None else after(v, out[0], *[pieces[r] for r in wait])
        out = mix(shifts, place, *weights, ready, v_sib, cv)
        for r, piece in zip(shifts, out):
            pieces[r] = shift_z(piece, r, zs) if r else piece
    return join(place, [pieces[r] for r in range(zs)])


def shifted(value, axis, steps):
    count = lax.axis_size(axis)
    leading, last = (max(0, -steps), min(count, count - steps))
    return lax.ppermute(value, axis, [(source, source + steps) for source in range(leading, last)])


def body(hyena_in, prior_kv, filters, gain, w_qkv, cache_k, cache_v):
    rows_dev = hyena_in.shape[0]
    width = hyena_in.shape[2]
    history = prior_kv.shape[0]
    tap_count = filters.shape[1]
    head_size = D // HEADS
    heads_dev = width // head_size
    cache_rows = cache_k.shape[0]
    stride = cache_rows + rows_dev
    my_index = lax.axis_index("seq")
    stream_q = hyena_in[:, 0].astype(jnp.float32)
    kv_prod = (hyena_in[:, 1].astype(jnp.float32) * hyena_in[:, 2].astype(jnp.float32)).astype(
        jnp.bfloat16
    )
    before = shifted(kv_prod[rows_dev - history :], "seq", 1)
    before = jnp.where(my_index == 0, prior_kv, before)
    extended = jnp.concatenate([before, kv_prod], axis=0).astype(jnp.float32)
    tap_table = jnp.repeat(filters, width // filters.shape[0], axis=0).T

    def add_tap(tap_index, total):
        offset = (tap_count - 1 - tap_index).astype(jnp.int32)
        window = lax.dynamic_slice_in_dim(extended, offset, rows_dev, 0)
        coeff = lax.dynamic_index_in_dim(tap_table, tap_index.astype(jnp.int32), 0, keepdims=True)
        return total + coeff * window

    conv = lax.fori_loop(0, tap_count, add_tap, jnp.zeros((rows_dev, width), jnp.float32))
    hyena_out = (stream_q * conv).astype(jnp.bfloat16)
    whole = lax.all_gather(hyena_out, "chan", axis=1, tiled=True)
    as_float = whole.astype(jnp.float32)
    mean_sq = jnp.mean(as_float * as_float, axis=-1, keepdims=True)
    normed = (as_float * lax.rsqrt(mean_sq + 1e-06) * gain[None, :]).astype(jnp.bfloat16)
    piece = lax.all_gather(w_qkv, "seq", axis=0, tiled=True)
    flat_piece = piece.reshape(piece.shape[0], 3 * width)
    projected = jnp.dot(normed, flat_piece, preferred_element_type=jnp.float32)
    qkv = projected.astype(jnp.bfloat16).reshape(rows_dev, 3, width)
    scale = 1.0 / head_size**0.5
    keys_local = jnp.concatenate([cache_k, qkv[:, 1]], axis=0)
    vals_local = jnp.concatenate([cache_v, qkv[:, 2]], axis=0)
    head_q = qkv[:, 0].reshape(rows_dev, heads_dev, head_size)
    query_pos = my_index * rows_dev + jnp.arange(rows_dev, dtype=jnp.int32)
    run_max = jnp.full((heads_dev, rows_dev), -1e30, jnp.float32)
    key_piece = lax.all_gather(keys_local, "seq", axis=0, tiled=True)
    val_piece = lax.all_gather(vals_local, "seq", axis=0, tiled=True)
    count = key_piece.shape[0]
    row_ids = jnp.arange(count, dtype=jnp.int32)
    source = row_ids // stride
    within = row_ids % stride
    key_pos = jnp.where(within < cache_rows, -1, source * rows_dev + within - cache_rows)
    visible = (key_pos[None, :] <= query_pos[:, None])[None]
    scores = (
        jnp.einsum(
            "qhd,khd->hqk",
            head_q,
            key_piece.reshape(count, heads_dev, head_size),
            preferred_element_type=jnp.float32,
        )
        * scale
    )
    scores = jnp.where(visible, scores, jnp.float32(-1e30))
    new_max = jnp.maximum(run_max, jnp.max(scores, axis=-1))
    weights = jnp.where(visible, jnp.exp(scores - new_max[..., None]), jnp.float32(0.0))
    new_sum = jnp.sum(weights, axis=-1)
    probs = weights.astype(jnp.bfloat16)
    added = jnp.einsum(
        "hqk,khd->hqd",
        probs,
        val_piece.reshape(count, heads_dev, head_size),
        preferred_element_type=jnp.float32,
    )
    result = jnp.transpose(added / new_sum[..., None], (1, 0, 2))
    return result.reshape(rows_dev, width).astype(jnp.bfloat16)


def solution(mesh):
    sizes = mesh.shape
    paired = sizes["chan"] == 4 and sizes["seq"] == 8
    return jax.shard_map(
        fast_body if paired else body,
        mesh=mesh,
        in_specs=(
            P("seq", None, "chan"),
            P(None, "chan"),
            P("chan", None),
            P(),
            P("seq", None, "chan"),
            P("seq", "chan"),
            P("seq", "chan"),
        ),
        out_specs=P("seq", "chan"),
        check_vma=False,
    )
```

```python
import functools

import jax
import jax.numpy as jnp
from jax import lax
from jax.experimental import pallas as pl
from jax.experimental.pallas import tpu as pltpu
from jax.sharding import PartitionSpec as P

D = 4096
HEADS = 32
HEAD = D // HEADS
LANES = 128
PAD = 8
BF16 = jnp.bfloat16
F32 = jnp.float32
MIB = 1024 * 1024


BRIEF = pl.CostEstimate(flops=1, transcendentals=0, bytes_accessed=1)


VMEM = pl.BlockSpec(memory_space=pltpu.VMEM)
SMEM = pl.BlockSpec(memory_space=pltpu.SMEM)


def whole(shape):
    return pl.BlockSpec(shape, lambda *_: (0,) * len(shape))


def conv_kernel(group, hin_ref, halo_ref, taps_ref, out_ref):
    taps = taps_ref[...]
    count = taps.shape[0]
    width = taps.shape[1]
    kv = (hin_ref[1].astype(F32) * hin_ref[2].astype(F32)).astype(BF16)
    ext = jnp.concatenate([halo_ref[...], kv], axis=0)
    rows = kv.shape[0]
    blocks = rows // width
    windows = jnp.concatenate(
        [ext[b * width : (b + 2) * width] for b in range(blocks)], axis=1
    )
    high = taps.astype(BF16)
    low = (taps - high.astype(F32)).astype(BF16)
    source = lax.broadcasted_iota(jnp.int32, (width, 2 * width), 0)
    column = lax.broadcasted_iota(jnp.int32, (width, 2 * width), 1)
    flip = jnp.where(source + column == width, 1.0, 0.0).astype(BF16)
    total = None
    for part in (high, low):
        first = jnp.dot(part, flip, preferred_element_type=F32)
        toeplitz = jnp.concatenate(
            [
                pltpu.roll(
                    jnp.broadcast_to(first[g : g + 1], (width, 2 * width)),
                    0,
                    1,
                    stride=1,
                    stride_axis=0,
                ).astype(BF16)
                for g in range(count)
            ],
            axis=0,
        )
        product = jnp.dot(toeplitz, windows, preferred_element_type=F32)
        total = product if total is None else total + product
    owner = lax.broadcasted_iota(jnp.int32, (width, blocks * LANES), 1) % LANES // group
    conv = total[:width]
    for g in range(1, count):
        conv = jnp.where(owner == g, total[g * width : (g + 1) * width], conv)
    query = hin_ref[0].astype(F32)
    for b in range(blocks):
        piece = query[b * width : (b + 1) * width] * conv[:, b * LANES : (b + 1) * LANES]
        out_ref[b * width : (b + 1) * width, :] = piece.astype(BF16)


def hyena(hin, halo, filters):
    _, rows, width = hin.shape
    taps = filters.shape[1]
    group = width // filters.shape[0]
    per_tile = LANES // group
    return pl.pallas_call(
        functools.partial(conv_kernel, group),
        grid=(width // LANES,),
        in_specs=[
            pl.BlockSpec((3, rows, LANES), lambda i: (0, 0, i)),
            pl.BlockSpec((taps, LANES), lambda i: (0, i)),
            pl.BlockSpec((per_tile, taps), lambda i: (i, 0)),
        ],
        out_specs=pl.BlockSpec((rows, LANES), lambda i: (0, i)),
        out_shape=jax.ShapeDtypeStruct((rows, width), BF16),
        compiler_params=pltpu.CompilerParams(vmem_limit_bytes=8 * MIB),
        cost_estimate=BRIEF,
        name="hyena_filters",
    )(hin, halo, filters)


def norm_kernel(j, place_ref, own_ref, x_ref, y_ref, d0_ref, d1_ref, gain_ref, *rest):
    out_ref = rest[-1]
    chan = place_ref[0]
    half = d0_ref.shape[0]
    step = 16

    def band(i, diag_ref, start):
        at = pl.ds(pl.multiple_of(start + i * step, step), step)
        refs = (own_ref.at[at], x_ref.at[at], y_ref.at[at], diag_ref.at[pl.ds(pl.multiple_of(i * step, step), step)])
        parts = [r[...].astype(F32) for r in refs]
        total = sum(jnp.sum(p * p, axis=-1, keepdims=True) for p in parts)
        factor = lax.rsqrt(total / D + 1e-6)
        for m, p in enumerate(parts):
            where = chan ^ m
            out_ref[j, where, at, :] = (p * factor * gain_ref[where]).astype(BF16)

    for diag_ref, start in ((d0_ref, 0), (d1_ref, half)):
        pl.loop(0, half // step, unroll=2)(functools.partial(band, diag_ref=diag_ref, start=start))


def norm(place, j, zs, own, from_x, from_y, diag0, diag1, gain, buffer):
    rows, width = own.shape
    args = [place, own, from_x, from_y, diag0, diag1, gain] + ([] if buffer is None else [buffer])
    return pl.pallas_call(
        functools.partial(norm_kernel, j),
        in_specs=[SMEM] + [VMEM] * (len(args) - 1),
        out_specs=VMEM,
        out_shape=jax.ShapeDtypeStruct((zs, 4, rows, width), BF16),
        input_output_aliases={} if buffer is None else {7: 0},
        compiler_params=pltpu.CompilerParams(vmem_limit_bytes=4 * MIB),
        cost_estimate=BRIEF,
        name="norm",
    )(*args)


def project_kernel(shifts, slabs, parts, zs, extra, apart, place_ref, normed_ref, *refs):
    groups = 1 + max(group for group, _ in parts)
    n = len(shifts)
    weights, rest = refs[: 2 * n * groups], refs[2 * n * groups :]
    before, outs = rest[:extra], rest[-len(parts) * (zs if apart else 1) :]
    z, core = place_ref[1], place_ref[2]
    depth = normed_ref.shape[3] // 2
    for part, (group, row) in enumerate(parts):
        for j in slabs:
            total = before[part][j] if before else None
            for i, shift in enumerate(shifts):
                block = lax.rem(z + zs - shift, zs)
                for k in range(2):
                    at = pl.multiple_of((core ^ k) * depth, depth)
                    left = normed_ref[j, block, :, pl.ds(at, depth)]
                    right = weights[(2 * group + k) * n + i][row : row + depth, :]
                    term = jnp.dot(left, right, preferred_element_type=F32)
                    total = term if total is None else total + term
            if apart:
                outs[part * zs + j][...] = total.astype(outs[0].dtype)
            else:
                outs[part][j] = total.astype(outs[0].dtype)


def project(place, normed, groups, parts, shifts, slabs, rounded, before=(), into=(), apart=False):
    zs, _, rows, _ = normed.shape
    weights = [w for own, sib in groups for w in (*own, *sib)]
    args = [place, normed, *weights, *before, *into]
    shape = (rows, weights[0].shape[1]) if apart else (zs, rows, weights[0].shape[1])
    out = [jax.ShapeDtypeStruct(shape, BF16 if rounded else F32)] * (len(parts) * (zs if apart else 1))
    return pl.pallas_call(
        functools.partial(project_kernel, shifts, slabs, parts, zs, len(before), apart),
        in_specs=[SMEM] + [VMEM] * (len(args) - 1),
        out_specs=[VMEM] * len(out),
        out_shape=out,
        input_output_aliases={len(args) - len(into) + i: i for i in range(len(into))},
        compiler_params=pltpu.CompilerParams(vmem_limit_bytes=8 * MIB),
        cost_estimate=BRIEF,
        name="project",
    )(*args)


NT = (((1,), (1,)), ((), ()))


def lanes(op, s):
    full = s.shape[1] - s.shape[1] % LANES
    rest = s[:, full:] if full < s.shape[1] else None
    return functools.reduce(op, [s[:, i : i + LANES] for i in range(0, full, LANES)]), rest


def weigh_kernel(blocks, place_ref, q_ref, ck_ref, *refs):
    z, core = place_ref[1], place_ref[2]
    zs, rows, cols = q_ref.shape
    k_refs, ks_refs, (old_ref, new_ref, sum_ref, k_ref, ks_ref, scratch) = refs[:zs], refs[zs : 2 * zs], refs[-6:]
    for j in range(zs):
        k_ref[j], ks_ref[j] = k_refs[j][...], ks_refs[j][...]
    crow = ck_ref.shape[0]
    factor = 1.4426950408889634 / HEAD**0.5
    row = lax.broadcasted_iota(jnp.int32, (rows, rows), 0)
    col = lax.broadcasted_iota(jnp.int32, (rows, rows), 1)
    causal = col <= row
    slab = [lax.rem(z + zs - b, zs) for b in range(zs)]

    for block in blocks:
        for h in range(cols // HEAD):
            hcol = slice(h * HEAD, (h + 1) * HEAD)
            query = q_ref[slab[block], :, hcol]

            def score(key):
                return lax.dot_general(query, key, NT, preferred_element_type=F32)

            s = score(ck_ref[:, hcol])
            scratch[h, :, :crow] = s
            top, end = lanes(jnp.maximum, s)
            for b in range(block + 1):
                s, t = score(k_ref[slab[b], :, hcol]), score(ks_ref[slab[b], :, hcol])
                if b == block:
                    s, t = jnp.where(causal, s, -1e30), jnp.where(core == 1, t, -1e30)
                at = crow + 2 * rows * b
                scratch[h, :, at : at + rows] = s
                scratch[h, :, at + rows : at + 2 * rows] = t
                top = jnp.maximum(top, jnp.maximum(lanes(jnp.maximum, s)[0], lanes(jnp.maximum, t)[0]))
            top = jnp.max(top, axis=-1, keepdims=True)
            if end is not None:
                top = jnp.maximum(top, jnp.max(end, axis=-1, keepdims=True))
            top = top * factor

            weights = jnp.exp2(scratch[h, :, :crow] * factor - top)
            old_ref[block, h] = weights.astype(BF16)
            total, end = lanes(jnp.add, weights)
            for b in range(block + 1):
                at = crow + 2 * rows * b
                weights = jnp.exp2(scratch[h, :, at : at + 2 * rows] * factor - top)
                new_ref[block, h, b] = weights.astype(BF16)
                total = total + lanes(jnp.add, weights)[0]
            total = jnp.sum(total, axis=-1, keepdims=True)
            if end is not None:
                total = total + jnp.sum(end, axis=-1, keepdims=True)
            sum_ref[block, h] = jnp.broadcast_to(total, (rows, HEAD))


def weigh(blocks, place, q, k, k_sib, ck, into=()):
    zs, rows, cols = q.shape
    heads, crow = cols // HEAD, ck.shape[0]
    return pl.pallas_call(
        functools.partial(weigh_kernel, blocks),
        in_specs=[SMEM] + [VMEM] * (2 + 2 * zs + len(into)),
        input_output_aliases={3 + 2 * zs + i: i for i in range(len(into))},
        out_specs=[VMEM] * 3,
        out_shape=[
            jax.ShapeDtypeStruct((zs, heads, rows, crow), BF16),
            jax.ShapeDtypeStruct((zs, heads, zs, rows, 2 * rows), BF16),
            jax.ShapeDtypeStruct((zs, heads, rows, HEAD), F32),
        ],
        scratch_shapes=[pltpu.VMEM((zs, rows, cols), BF16)] * 2
        + [pltpu.VMEM((heads, rows, -(-(crow + 2 * rows * zs) // LANES) * LANES), F32)],
        compiler_params=pltpu.CompilerParams(vmem_limit_bytes=14 * MIB),
        cost_estimate=BRIEF,
        name="weigh",
    )(place, q, ck, *k, *k_sib, *into)


def mix_kernel(shifts, place_ref, old_ref, new_ref, sum_ref, v_ref, vs_ref, cv_ref, *outs):
    z = place_ref[1]
    zs, rows, cols = v_ref.shape
    heads = range(cols // HEAD)
    hcols = [slice(h * HEAD, (h + 1) * HEAD) for h in heads]
    for shift, out_ref in zip(shifts, outs):
        block = lax.rem(z + shift, zs)

        def add(b, state):
            at = lax.rem(z + zs - b, zs)
            result = []
            for h, summed in zip(heads, state):
                probs = new_ref[block, h, b]
                value = jnp.concatenate([v_ref[at, :, hcols[h]], vs_ref[at, :, hcols[h]]], axis=0)
                result.append(summed + jnp.dot(probs, value, preferred_element_type=F32))
            return tuple(result)

        state = tuple(
            jnp.dot(old_ref[block, h], cv_ref[:, hcols[h]], preferred_element_type=F32) for h in heads
        )
        state = lax.fori_loop(0, block + 1, add, state)
        for h, summed in zip(heads, state):
            out_ref[:, hcols[h]] = (summed / sum_ref[block, h]).astype(BF16)


def mix(shifts, place, old, new, sums, v, v_sib, cv):
    _, rows, cols = v.shape
    return pl.pallas_call(
        functools.partial(mix_kernel, shifts),
        in_specs=[SMEM] + [VMEM] * 6,
        out_specs=[VMEM] * len(shifts),
        out_shape=[jax.ShapeDtypeStruct((rows, cols), BF16)] * len(shifts),
        compiler_params=pltpu.CompilerParams(vmem_limit_bytes=8 * MIB),
        cost_estimate=BRIEF,
        name="mix",
    )(place, old, new, sums, v, v_sib, cv)


def pack_kernel(places, crow, *refs):
    parcels, outs, scratch = refs[: len(places)], refs[len(places) : -1], refs[-1]
    for n, out_ref in enumerate(outs):
        for i, (piece, at) in enumerate(zip(parcels, places)):
            at += n * (crow + PAD)
            scratch[i * crow : (i + 1) * crow, :] = piece[at : at + crow + PAD].astype(F32)[:crow]
        out_ref[...] = scratch[...].astype(BF16)


def pack(parcels, places, crow):
    out = (len(parcels) * crow, parcels[0].shape[1])
    return pl.pallas_call(
        functools.partial(pack_kernel, places, crow),
        in_specs=[VMEM] * len(parcels),
        out_specs=[VMEM] * 2,
        out_shape=[jax.ShapeDtypeStruct(out, BF16)] * 2,
        scratch_shapes=[pltpu.VMEM(out, F32)],
        compiler_params=pltpu.CompilerParams(vmem_limit_bytes=8 * MIB),
        cost_estimate=BRIEF,
        name="pack",
    )(*parcels)


def join_kernel(place_ref, *refs):
    pieces, (out_ref, sems) = refs[:-2], refs[-2:]
    zs = len(pieces)
    cols = pieces[0].shape[1]
    copies = []
    for r, piece in enumerate(pieces):
        at = pl.multiple_of(lax.rem(place_ref[1] + zs - r, zs) * cols, cols)
        copies.append(pltpu.make_async_copy(piece, out_ref.at[:, pl.ds(at, cols)], sems.at[r]))
    for copy in copies:
        copy.start()
    for copy in copies:
        copy.wait()


def join(place, pieces):
    rows, cols = pieces[0].shape
    out = (rows, cols * len(pieces))
    return pl.pallas_call(
        join_kernel,
        in_specs=[SMEM] + [VMEM] * len(pieces),
        out_specs=pl.BlockSpec(memory_space=pl.ANY),
        out_shape=jax.ShapeDtypeStruct(out, BF16),
        scratch_shapes=[pltpu.SemaphoreType.DMA((len(pieces),))],
        name="join",
    )(place, *pieces)


def shift_z(value, steps, zs):
    pairs = [(2 * a + k, 2 * ((a + steps) % zs) + k) for a in range(zs) for k in range(2)]
    return lax.ppermute(value, "seq", pairs)


def swap_core(value, zs):
    return lax.ppermute(value, "seq", [(2 * a + k, 2 * a + 1 - k) for a in range(zs) for k in range(2)])


def swap_chan(value, bit):
    return lax.ppermute(value, "chan", [(c, c ^ bit) for c in range(4)])


def after(value, *others):
    return lax.optimization_barrier((value, *others))[0]


def fast_body(hyena_in, prior_kv, filters, gain, w_qkv, cache_k, cache_v):
    rows, _, width = hyena_in.shape
    seqs = lax.axis_size("seq")
    zs = seqs // 2
    taps = filters.shape[1]
    depth, crow = w_qkv.shape[0], cache_k.shape[0]
    cols = width // zs
    my_seq = lax.axis_index("seq")
    z, core = my_seq // 2, my_seq % 2
    chan = lax.axis_index("chan")
    place = jnp.stack([chan, z, core]).astype(jnp.int32)

    w_t = jnp.transpose(w_qkv, (1, 0, 2))
    caches = [jnp.pad(c, ((0, PAD), (0, 0))) for c in (cache_k, cache_v)]

    def parcel(kind, r, *others):
        at = (z + r) % zs * cols
        source = after(w_t, *others) if others else w_t
        parts = [
            lax.dynamic_slice(source, ("qkv".index(p), 0, at), (1, depth, cols))[0]
            for p in kind
            if p != "c"
        ]
        if "c" in kind:
            parts += [lax.dynamic_slice_in_dim(c, at, cols, 1) for c in caches]
        return jnp.concatenate(parts, axis=0)

    hin = jnp.transpose(hyena_in, (1, 0, 2))
    tail = (hin[1, rows - taps :].astype(F32) * hin[2, rows - taps :].astype(F32)).astype(BF16)
    halo = lax.ppermute(tail, "seq", [(s, s + 1) for s in range(seqs - 1)])
    halo = jnp.where(my_seq == 0, jnp.pad(prior_kv, ((taps - prior_kv.shape[0], 0), (0, 0))), halo)

    order = ["q1", "q3", "acts", "kvc1", "acts", "kvc3", "acts", "q2", "kc2", "v2"]
    acts = [hyena(hin, halo, filters)]
    here = {kind + "0": parcel(kind, 0, acts[0]) for kind in ("kvc", "q")}
    sent = []
    for n, item in enumerate(order):
        if item == "acts":
            value, steps = acts[-1], 1
        else:
            kind, steps = item[:-1], int(item[-1])
            value = parcel(kind, steps, *acts[: int(n >= 2)])
        if n >= 2:
            value = after(value, sent[n - {"kvc3": 1, "kc2": 1}.get(item, 2)])
        sent.append(shift_z(value, steps, zs))
        if item == "acts":
            acts.append(sent[-1])
        else:
            here[item] = sent[-1]
    late = ["q2", "kc2", "v2"]
    there = {item: swap_core(here[item], zs) for item in here if item not in late}

    pace = [[], ["kvc1"], ["kvc3"], []]
    swapped = [[], ["kvc0", "q0"], ["q1", "q3"], ["kvc1"]]
    gain4 = gain.reshape(4, 1, width)
    half = rows // 2
    normed, diag0, diag1 = None, None, None
    every, early, last = tuple(range(zs)), (0, 1, 3), zs - 1

    def sides(*items):
        return [[side[item] for item in items] for side in (here, there)]

    def project_early(slabs, into=()):
        groups = [sides("q0", "q1", "q3"), sides("kvc0", "kvc1", "kvc3")]
        parts = ((0, 0), (1, 0), (1, depth))
        return project(place, normed, groups, parts, early, slabs, False, (), into)

    def project_last(item, sums, *others, apart=False):
        normed_then = after(normed, *others) if others else normed
        return project(place, normed_then, [sides(item)], ((0, 0),), (2,), every, True, (sums,), apart=apart)

    for j, own in enumerate(acts):
        own = after(own, *([diag0, diag1] if j else [here["q1"], here["q3"]]))
        from_x, from_y = swap_chan(own, 1), swap_chan(own, 2)
        if j:
            sums = project_early(every[:last]) if j == last else []
            normed = after(normed, *sums) if j == last else normed
            settled = [normed] + [there[item] for item in swapped[j]] + [here[item] for item in pace[j]]
            from_x, from_y = after(from_x, *settled), after(from_y, *settled)
        diag0 = swap_chan(from_x[:half], 2)
        diag1 = swap_chan(from_y[half:], 1)
        normed = norm(place, j, zs, own, from_x, from_y, diag0, diag1, gain4, normed)

    there["q2"] = swap_core(after(here["q2"], diag0, diag1), zs)
    there["kc2"] = swap_core(after(here["kc2"], diag0, diag1), zs)
    q_sum, k_sum, v_sum = project_early(every[last:], sums)
    (q,) = project_last("q2", q_sum)
    kept = sum(sides("kvc0", "kvc1", "kc2", "kvc3"), [])
    ck, cv = pack(kept, [depth if i % zs == 2 else 2 * depth for i in range(2 * zs)], crow)
    k = project_last("kc2", k_sum, q, ck, apart=True)
    k_sib = [swap_core(slab, zs) for slab in k]
    weights = weigh((3, 0), place, q, k, k_sib, ck)
    there["v2"] = swap_core(after(here["v2"], weights[2]), zs)
    weights = weigh((1,), place, q, k, k_sib, ck, weights)
    (v,) = project_last("v2", v_sum, weights[2])
    v_sib = swap_core(v, zs)
    weights = weigh((2,), place, q, k, k_sib, ck, weights)
    pieces, out = {}, None
    for shifts, wait in (((2,), ()), ((1, 3), ()), ((0,), (2,))):
        ready = v if out is None else after(v, out[0], *[pieces[r] for r in wait])
        out = mix(shifts, place, *weights, ready, v_sib, cv)
        for r, piece in zip(shifts, out):
            pieces[r] = shift_z(piece, r, zs) if r else piece
    return join(place, [pieces[r] for r in range(zs)])


def shifted(value, axis, steps):
    count = lax.axis_size(axis)
    leading, last = (max(0, -steps), min(count, count - steps))
    return lax.ppermute(value, axis, [(source, source + steps) for source in range(leading, last)])


def body(hyena_in, prior_kv, filters, gain, w_qkv, cache_k, cache_v):
    rows_dev = hyena_in.shape[0]
    width = hyena_in.shape[2]
    history = prior_kv.shape[0]
    tap_count = filters.shape[1]
    head_size = D // HEADS
    heads_dev = width // head_size
    cache_rows = cache_k.shape[0]
    stride = cache_rows + rows_dev
    my_index = lax.axis_index("seq")
    stream_q = hyena_in[:, 0].astype(jnp.float32)
    kv_prod = (hyena_in[:, 1].astype(jnp.float32) * hyena_in[:, 2].astype(jnp.float32)).astype(
        jnp.bfloat16
    )
    before = shifted(kv_prod[rows_dev - history :], "seq", 1)
    before = jnp.where(my_index == 0, prior_kv, before)
    extended = jnp.concatenate([before, kv_prod], axis=0).astype(jnp.float32)
    tap_table = jnp.repeat(filters, width // filters.shape[0], axis=0).T

    def add_tap(tap_index, total):
        offset = (tap_count - 1 - tap_index).astype(jnp.int32)
        window = lax.dynamic_slice_in_dim(extended, offset, rows_dev, 0)
        coeff = lax.dynamic_index_in_dim(tap_table, tap_index.astype(jnp.int32), 0, keepdims=True)
        return total + coeff * window

    conv = lax.fori_loop(0, tap_count, add_tap, jnp.zeros((rows_dev, width), jnp.float32))
    hyena_out = (stream_q * conv).astype(jnp.bfloat16)
    whole = lax.all_gather(hyena_out, "chan", axis=1, tiled=True)
    as_float = whole.astype(jnp.float32)
    mean_sq = jnp.mean(as_float * as_float, axis=-1, keepdims=True)
    normed = (as_float * lax.rsqrt(mean_sq + 1e-06) * gain[None, :]).astype(jnp.bfloat16)
    piece = lax.all_gather(w_qkv, "seq", axis=0, tiled=True)
    flat_piece = piece.reshape(piece.shape[0], 3 * width)
    projected = jnp.dot(normed, flat_piece, preferred_element_type=jnp.float32)
    qkv = projected.astype(jnp.bfloat16).reshape(rows_dev, 3, width)
    scale = 1.0 / head_size**0.5
    keys_local = jnp.concatenate([cache_k, qkv[:, 1]], axis=0)
    vals_local = jnp.concatenate([cache_v, qkv[:, 2]], axis=0)
    head_q = qkv[:, 0].reshape(rows_dev, heads_dev, head_size)
    query_pos = my_index * rows_dev + jnp.arange(rows_dev, dtype=jnp.int32)
    run_max = jnp.full((heads_dev, rows_dev), -1e30, jnp.float32)
    key_piece = lax.all_gather(keys_local, "seq", axis=0, tiled=True)
    val_piece = lax.all_gather(vals_local, "seq", axis=0, tiled=True)
    count = key_piece.shape[0]
    row_ids = jnp.arange(count, dtype=jnp.int32)
    source = row_ids // stride
    within = row_ids % stride
    key_pos = jnp.where(within < cache_rows, -1, source * rows_dev + within - cache_rows)
    visible = (key_pos[None, :] <= query_pos[:, None])[None]
    scores = (
        jnp.einsum(
            "qhd,khd->hqk",
            head_q,
            key_piece.reshape(count, heads_dev, head_size),
            preferred_element_type=jnp.float32,
        )
        * scale
    )
    scores = jnp.where(visible, scores, jnp.float32(-1e30))
    new_max = jnp.maximum(run_max, jnp.max(scores, axis=-1))
    weights = jnp.where(visible, jnp.exp(scores - new_max[..., None]), jnp.float32(0.0))
    new_sum = jnp.sum(weights, axis=-1)
    probs = weights.astype(jnp.bfloat16)
    added = jnp.einsum(
        "hqk,khd->hqd",
        probs,
        val_piece.reshape(count, heads_dev, head_size),
        preferred_element_type=jnp.float32,
    )
    result = jnp.transpose(added / new_sum[..., None], (1, 0, 2))
    return result.reshape(rows_dev, width).astype(jnp.bfloat16)


def solution(mesh):
    sizes = mesh.shape
    paired = sizes["chan"] == 4 and HEADS // sizes["chan"] == sizes["seq"]
    return jax.shard_map(
        fast_body if paired else body,
        mesh=mesh,
        in_specs=(
            P("seq", None, "chan"),
            P(None, "chan"),
            P("chan", None),
            P(),
            P("seq", None, "chan"),
            P("seq", "chan"),
            P("seq", "chan"),
        ),
        out_specs=P("seq", "chan"),
        check_vma=False,
    )
```

```python
import functools

import jax
import jax.numpy as jnp
from jax import lax
from jax.experimental import pallas as pl
from jax.experimental.pallas import tpu as pltpu
from jax.sharding import PartitionSpec as P

D = 4096
HEADS = 32
HEAD = D // HEADS
LANES = 128
PAD = 8
BF16 = jnp.bfloat16
F32 = jnp.float32
MIB = 1024 * 1024


BRIEF = pl.CostEstimate(flops=1, transcendentals=0, bytes_accessed=1)


VMEM = pl.BlockSpec(memory_space=pltpu.VMEM)
SMEM = pl.BlockSpec(memory_space=pltpu.SMEM)


def whole(shape):
    return pl.BlockSpec(shape, lambda *_: (0,) * len(shape))


def conv_kernel(group, hin_ref, halo_ref, taps_ref, out_ref):
    taps = taps_ref[...]
    count = taps.shape[0]
    width = taps.shape[1]
    kv = (hin_ref[1].astype(F32) * hin_ref[2].astype(F32)).astype(BF16)
    ext = jnp.concatenate([halo_ref[...], kv], axis=0)
    rows = kv.shape[0]
    blocks = rows // width
    windows = jnp.concatenate(
        [ext[b * width : (b + 2) * width] for b in range(blocks)], axis=1
    )
    high = taps.astype(BF16)
    low = (taps - high.astype(F32)).astype(BF16)
    source = lax.broadcasted_iota(jnp.int32, (width, 2 * width), 0)
    column = lax.broadcasted_iota(jnp.int32, (width, 2 * width), 1)
    flip = jnp.where(source + column == width, 1.0, 0.0).astype(BF16)
    total = None
    for part in (high, low):
        first = jnp.dot(part, flip, preferred_element_type=F32)
        toeplitz = jnp.concatenate(
            [
                pltpu.roll(
                    jnp.broadcast_to(first[g : g + 1], (width, 2 * width)),
                    0,
                    1,
                    stride=1,
                    stride_axis=0,
                ).astype(BF16)
                for g in range(count)
            ],
            axis=0,
        )
        product = jnp.dot(toeplitz, windows, preferred_element_type=F32)
        total = product if total is None else total + product
    owner = lax.broadcasted_iota(jnp.int32, (width, blocks * LANES), 1) % LANES // group
    conv = total[:width]
    for g in range(1, count):
        conv = jnp.where(owner == g, total[g * width : (g + 1) * width], conv)
    query = hin_ref[0].astype(F32)
    for b in range(blocks):
        piece = query[b * width : (b + 1) * width] * conv[:, b * LANES : (b + 1) * LANES]
        out_ref[b * width : (b + 1) * width, :] = piece.astype(BF16)


def hyena(hin, halo, filters):
    _, rows, width = hin.shape
    taps = filters.shape[1]
    group = width // filters.shape[0]
    per_tile = LANES // group
    return pl.pallas_call(
        functools.partial(conv_kernel, group),
        grid=(width // LANES,),
        in_specs=[
            pl.BlockSpec((3, rows, LANES), lambda i: (0, 0, i)),
            pl.BlockSpec((taps, LANES), lambda i: (0, i)),
            pl.BlockSpec((per_tile, taps), lambda i: (i, 0)),
        ],
        out_specs=pl.BlockSpec((rows, LANES), lambda i: (0, i)),
        out_shape=jax.ShapeDtypeStruct((rows, width), BF16),
        compiler_params=pltpu.CompilerParams(vmem_limit_bytes=12 * MIB),
        cost_estimate=BRIEF,
        name="hyena_filters",
    )(hin, halo, filters)


def norm_kernel(j, place_ref, own_ref, x_ref, y_ref, d0_ref, d1_ref, gain_ref, *rest):
    out_ref = rest[-1]
    chan = place_ref[0]
    half = d0_ref.shape[0]
    step = 16

    def band(i, diag_ref, start):
        at = pl.ds(pl.multiple_of(start + i * step, step), step)
        refs = (own_ref.at[at], x_ref.at[at], y_ref.at[at], diag_ref.at[pl.ds(pl.multiple_of(i * step, step), step)])
        parts = [r[...].astype(F32) for r in refs]
        total = sum(jnp.sum(p * p, axis=-1, keepdims=True) for p in parts)
        factor = lax.rsqrt(total / D + 1e-6)
        for m, p in enumerate(parts):
            where = chan ^ m
            out_ref[j, where, at, :] = (p * factor * gain_ref[where]).astype(BF16)

    for diag_ref, start in ((d0_ref, 0), (d1_ref, half)):
        pl.loop(0, half // step, unroll=2)(functools.partial(band, diag_ref=diag_ref, start=start))


def norm(place, j, zs, own, from_x, from_y, diag0, diag1, gain, buffer):
    rows, width = own.shape
    args = [place, own, from_x, from_y, diag0, diag1, gain] + ([] if buffer is None else [buffer])
    return pl.pallas_call(
        functools.partial(norm_kernel, j),
        in_specs=[SMEM] + [VMEM] * (len(args) - 1),
        out_specs=VMEM,
        out_shape=jax.ShapeDtypeStruct((zs, 4, rows, width), BF16),
        input_output_aliases={} if buffer is None else {7: 0},
        compiler_params=pltpu.CompilerParams(vmem_limit_bytes=16 * MIB),
        cost_estimate=BRIEF,
        name="norm",
    )(*args)


def project_kernel(shifts, zs, count, place_ref, normed_ref, *refs):
    n = len(shifts)
    own, sib, rest = refs[:n], refs[n : 2 * n], refs[2 * n :]
    before, outs = rest[:-count], rest[-count:]
    z, core = place_ref[1], place_ref[2]
    depth = normed_ref.shape[3] // 2
    for part, out_ref in enumerate(outs):
        for j in range(zs):
            total = before[part][j] if before else None
            for i, shift in enumerate(shifts):
                block = lax.rem(z + zs - shift, zs)
                for k, w_ref in enumerate((own[i], sib[i])):
                    at = pl.multiple_of((core ^ k) * depth, depth)
                    left = normed_ref[j, block, :, pl.ds(at, depth)]
                    right = w_ref[part * depth : (part + 1) * depth, :]
                    term = jnp.dot(left, right, preferred_element_type=F32)
                    total = term if total is None else total + term
            out_ref[j] = total.astype(out_ref.dtype)


def project(place, normed, own, sib, shifts, count, rounded, before=()):
    zs, _, rows, _ = normed.shape
    cols = own[0].shape[1]
    args = [place, normed, *own, *sib, *before]
    return pl.pallas_call(
        functools.partial(project_kernel, shifts, zs, count),
        in_specs=[SMEM] + [VMEM] * (len(args) - 1),
        out_specs=[VMEM] * count,
        out_shape=[jax.ShapeDtypeStruct((zs, rows, cols), BF16 if rounded else F32)] * count,
        compiler_params=pltpu.CompilerParams(vmem_limit_bytes=16 * MIB),
        cost_estimate=BRIEF,
        name="project",
    )(*args)


NT = (((1,), (1,)), ((), ()))


def lanes(op, s):
    full = s.shape[1] - s.shape[1] % LANES
    rest = s[:, full:] if full < s.shape[1] else None
    return functools.reduce(op, [s[:, i : i + LANES] for i in range(0, full, LANES)]), rest


def attend_kernel(shifts, place_ref, q_ref, k_ref, v_ref, ks_ref, vs_ref, ck_ref, cv_ref, *refs):
    outs, (old, new) = refs[: len(shifts)], refs[len(shifts) :]
    z, core = place_ref[1], place_ref[2]
    zs, rows, cols = k_ref.shape
    heads = range(cols // HEAD)
    factor = 1.4426950408889634 / HEAD**0.5
    low = -1e30
    hcols = [slice(h * HEAD, (h + 1) * HEAD) for h in heads]
    row = lax.broadcasted_iota(jnp.int32, (rows, rows), 0)
    col = lax.broadcasted_iota(jnp.int32, (rows, rows), 1)
    causal = col <= row

    for shift, out_ref in zip(shifts, outs):
        block = lax.rem(z + shift, zs)
        mine = lax.rem(zs - shift, zs)
        queries = [q_ref[mine, :, hcol] for hcol in hcols]

        def score(b, tops, diagonal):
            at = lax.rem(z + zs - b, zs)
            result = []
            for h, top in zip(heads, tops):
                s = lax.dot_general(queries[h], k_ref[at, :, hcols[h]], NT, preferred_element_type=F32)
                t = lax.dot_general(queries[h], ks_ref[at, :, hcols[h]], NT, preferred_element_type=F32)
                if diagonal:
                    s, t = jnp.where(causal, s, low), jnp.where(core == 1, t, low)
                new[h, b, :, :rows] = s
                new[h, b, :, rows:] = t
                folded = jnp.maximum(lanes(jnp.maximum, s)[0], lanes(jnp.maximum, t)[0])
                result.append(jnp.maximum(top, folded))
            return tuple(result)

        tops, ends = [], []
        for h in heads:
            s = lax.dot_general(queries[h], ck_ref[:, hcols[h]], NT, preferred_element_type=F32)
            old[h] = s
            folded, rest = lanes(jnp.maximum, s)
            tops.append(folded)
            ends.append(low if rest is None else jnp.max(rest, axis=-1, keepdims=True))
        tops = lax.fori_loop(0, block, functools.partial(score, diagonal=False), tuple(tops))
        tops = score(block, tops, True)
        tops = [
            jnp.maximum(jnp.max(top, axis=-1, keepdims=True), end) * factor
            for top, end in zip(tops, ends)
        ]

        def weigh(b, state):
            at = lax.rem(z + zs - b, zs)
            result = []
            for h, (total, summed) in zip(heads, state):
                weights = jnp.exp2(new[h, b] * factor - tops[h])
                probs = weights.astype(BF16)
                summed += jnp.dot(probs[:, :rows], v_ref[at, :, hcols[h]], preferred_element_type=F32)
                summed += jnp.dot(probs[:, rows:], vs_ref[at, :, hcols[h]], preferred_element_type=F32)
                result.append((total + lanes(jnp.add, weights)[0], summed))
            return tuple(result)

        state, ends = [], []
        for h in heads:
            weights = jnp.exp2(old[h] * factor - tops[h])
            folded, rest = lanes(jnp.add, weights)
            ends.append(0.0 if rest is None else jnp.sum(rest, axis=-1, keepdims=True))
            state.append(
                (folded, jnp.dot(weights.astype(BF16), cv_ref[:, hcols[h]], preferred_element_type=F32))
            )
        state = lax.fori_loop(0, block + 1, weigh, tuple(state))
        for h, (total, summed), end in zip(heads, state, ends):
            total = jnp.sum(total, axis=-1, keepdims=True) + end
            out_ref[:, hcols[h]] = (summed / total).astype(BF16)


def attend(shifts, place, q, k, v, k_sib, v_sib, ck, cv):
    zs, rows, cols = q.shape
    heads = cols // HEAD
    return pl.pallas_call(
        functools.partial(attend_kernel, shifts),
        in_specs=[SMEM] + [VMEM] * 7,
        out_specs=[VMEM] * len(shifts),
        out_shape=[jax.ShapeDtypeStruct((rows, cols), BF16)] * len(shifts),
        scratch_shapes=[
            pltpu.VMEM((heads, rows, ck.shape[0]), F32),
            pltpu.VMEM((heads, zs, rows, 2 * rows), F32),
        ],
        compiler_params=pltpu.CompilerParams(vmem_limit_bytes=20 * MIB),
        cost_estimate=BRIEF,
        name="attend",
    )(place, q, k, v, k_sib, v_sib, ck, cv)


def pack_kernel(places, crow, *refs):
    parcels, outs, scratch = refs[: len(places)], refs[len(places) : -1], refs[-1]
    for n, out_ref in enumerate(outs):
        for i, (piece, at) in enumerate(zip(parcels, places)):
            at += n * (crow + PAD)
            scratch[i * crow : (i + 1) * crow, :] = piece[at : at + crow + PAD].astype(F32)[:crow]
        out_ref[...] = scratch[...].astype(BF16)


def pack(parcels, places, crow):
    out = (len(parcels) * crow, parcels[0].shape[1])
    return pl.pallas_call(
        functools.partial(pack_kernel, places, crow),
        in_specs=[VMEM] * len(parcels),
        out_specs=[VMEM] * 2,
        out_shape=[jax.ShapeDtypeStruct(out, BF16)] * 2,
        scratch_shapes=[pltpu.VMEM(out, F32)],
        compiler_params=pltpu.CompilerParams(vmem_limit_bytes=12 * MIB),
        cost_estimate=BRIEF,
        name="pack",
    )(*parcels)


def join_kernel(place_ref, *refs):
    pieces, out_ref = refs[:-1], refs[-1]
    zs = len(pieces)
    cols = pieces[0].shape[1]
    for r, piece in enumerate(pieces):
        at = lax.rem(place_ref[1] + zs - r, zs) * cols
        out_ref[:, pl.ds(pl.multiple_of(at, cols), cols)] = piece[...]


def join(place, pieces):
    rows, cols = pieces[0].shape
    out = (rows, cols * len(pieces))
    return pl.pallas_call(
        join_kernel,
        in_specs=[SMEM] + [VMEM] * len(pieces),
        out_specs=whole(out),
        out_shape=jax.ShapeDtypeStruct(out, BF16),
        name="join",
    )(place, *pieces)


def shift_z(value, steps, zs):
    pairs = [(2 * a + k, 2 * ((a + steps) % zs) + k) for a in range(zs) for k in range(2)]
    return lax.ppermute(value, "seq", pairs)


def swap_core(value, zs):
    return lax.ppermute(value, "seq", [(2 * a + k, 2 * a + 1 - k) for a in range(zs) for k in range(2)])


def swap_chan(value, bit):
    return lax.ppermute(value, "chan", [(c, c ^ bit) for c in range(4)])


def after(value, *others):
    return lax.optimization_barrier((value, *others))[0]


def fast_body(hyena_in, prior_kv, filters, gain, w_qkv, cache_k, cache_v):
    rows, _, width = hyena_in.shape
    seqs = lax.axis_size("seq")
    zs = seqs // 2
    taps = filters.shape[1]
    depth, crow = w_qkv.shape[0], cache_k.shape[0]
    cols = width // zs
    my_seq = lax.axis_index("seq")
    z, core = my_seq // 2, my_seq % 2
    chan = lax.axis_index("chan")
    place = jnp.stack([chan, z, core]).astype(jnp.int32)

    w_t = jnp.transpose(w_qkv, (1, 0, 2))
    caches = [jnp.pad(c, ((0, PAD), (0, 0))) for c in (cache_k, cache_v)]

    def parcel(kind, r, *others):
        at = (z + r) % zs * cols
        source = after(w_t, *others) if others else w_t
        parts = [
            lax.dynamic_slice(source, ("qkv".index(p), 0, at), (1, depth, cols))[0]
            for p in kind
            if p != "c"
        ]
        if "c" in kind:
            parts += [lax.dynamic_slice_in_dim(c, at, cols, 1) for c in caches]
        return jnp.concatenate(parts, axis=0)

    hin = jnp.transpose(hyena_in, (1, 0, 2))
    tail = (hin[1, rows - taps :].astype(F32) * hin[2, rows - taps :].astype(F32)).astype(BF16)
    halo = lax.ppermute(tail, "seq", [(s, s + 1) for s in range(seqs - 1)])
    halo = jnp.where(my_seq == 0, jnp.pad(prior_kv, ((taps - prior_kv.shape[0], 0), (0, 0))), halo)

    order = ["q1", "q3", "acts", "kvc1", "acts", "kvc3", "acts", "q2", "kc2", "v2"]
    acts = [hyena(hin, halo, filters)]
    here = {kind + "0": parcel(kind, 0, acts[0]) for kind in ("kvc", "q")}
    sent = []
    for n, item in enumerate(order):
        if item == "acts":
            value, steps = acts[-1], 1
        else:
            kind, steps = item[:-1], int(item[-1])
            value = parcel(kind, steps, *acts[: int(n >= 2)])
        if n >= 2:
            value = after(value, sent[n - 2])
        sent.append(shift_z(value, steps, zs))
        if item == "acts":
            acts.append(sent[-1])
        else:
            here[item] = sent[-1]
    late = ["q2", "kc2", "v2"]
    there = {item: swap_core(here[item], zs) for item in here if item not in late}

    pace = [[], ["kvc1"], ["kvc3"], ["q2"]]
    swapped = [[], ["kvc0", "q0"], ["q1", "q3"], ["kvc1", "kvc3"]]
    gain4 = gain.reshape(4, 1, width)
    half = rows // 2
    normed, diag0, diag1 = None, None, None
    for j, own in enumerate(acts):
        own = after(own, *([diag0, diag1] if j else [here["q1"], here["q3"]]))
        from_x, from_y = swap_chan(own, 1), swap_chan(own, 2)
        if j:
            settled = [normed] + [there[item] for item in swapped[j]] + [here[item] for item in pace[j]]
            from_x, from_y = after(from_x, *settled), after(from_y, *settled)
        diag0 = swap_chan(from_x[:half], 2)
        diag1 = swap_chan(from_y[half:], 1)
        normed = norm(place, j, zs, own, from_x, from_y, diag0, diag1, gain4, normed)

    def sides(*items):
        return [[side[item] for item in items] for side in (here, there)]

    early = (0, 1, 3)
    there["q2"] = swap_core(after(here["q2"], diag0, diag1), zs)
    there["kc2"] = swap_core(after(here["kc2"], diag0, diag1), zs)
    (q,) = project(place, normed, *sides("q0", "q1", "q3", "q2"), early + (2,), 1, True)
    k_early, v_early = project(place, normed, *sides("kvc0", "kvc1", "kvc3"), early, 2, False)
    kept = sum(sides("kvc0", "kvc1", "kc2", "kvc3"), [])
    ck, cv = pack(kept, [depth if i % zs == 2 else 2 * depth for i in range(2 * zs)], crow)
    (k,) = project(place, after(normed, q, ck), *sides("kc2"), (2,), 1, True, (k_early,))
    k_sib = swap_core(k, zs)
    there["v2"] = swap_core(after(here["v2"], k), zs)
    (v,) = project(place, normed, *sides("v2"), (2,), 1, True, (v_early,))
    v_sib = swap_core(v, zs)
    pieces, out = {}, None
    for shifts, wait in (((2,), ()), ((1, 3), ()), ((0,), (2,))):
        ready = q if out is None else after(q, out[0], *[pieces[r] for r in wait])
        out = attend(shifts, place, ready, k, v, k_sib, v_sib, ck, cv)
        for r, piece in zip(shifts, out):
            pieces[r] = shift_z(piece, r, zs) if r else piece
    return join(place, [pieces[r] for r in range(zs)])


def shifted(value, axis, steps):
    count = lax.axis_size(axis)
    leading, last = (max(0, -steps), min(count, count - steps))
    return lax.ppermute(value, axis, [(source, source + steps) for source in range(leading, last)])


def body(hyena_in, prior_kv, filters, gain, w_qkv, cache_k, cache_v):
    rows_dev = hyena_in.shape[0]
    width = hyena_in.shape[2]
    history = prior_kv.shape[0]
    tap_count = filters.shape[1]
    head_size = D // HEADS
    heads_dev = width // head_size
    cache_rows = cache_k.shape[0]
    stride = cache_rows + rows_dev
    my_index = lax.axis_index("seq")
    stream_q = hyena_in[:, 0].astype(jnp.float32)
    kv_prod = (hyena_in[:, 1].astype(jnp.float32) * hyena_in[:, 2].astype(jnp.float32)).astype(
        jnp.bfloat16
    )
    before = shifted(kv_prod[rows_dev - history :], "seq", 1)
    before = jnp.where(my_index == 0, prior_kv, before)
    extended = jnp.concatenate([before, kv_prod], axis=0).astype(jnp.float32)
    tap_table = jnp.repeat(filters, width // filters.shape[0], axis=0).T

    def add_tap(tap_index, total):
        offset = (tap_count - 1 - tap_index).astype(jnp.int32)
        window = lax.dynamic_slice_in_dim(extended, offset, rows_dev, 0)
        coeff = lax.dynamic_index_in_dim(tap_table, tap_index.astype(jnp.int32), 0, keepdims=True)
        return total + coeff * window

    conv = lax.fori_loop(0, tap_count, add_tap, jnp.zeros((rows_dev, width), jnp.float32))
    hyena_out = (stream_q * conv).astype(jnp.bfloat16)
    whole = lax.all_gather(hyena_out, "chan", axis=1, tiled=True)
    as_float = whole.astype(jnp.float32)
    mean_sq = jnp.mean(as_float * as_float, axis=-1, keepdims=True)
    normed = (as_float * lax.rsqrt(mean_sq + 1e-06) * gain[None, :]).astype(jnp.bfloat16)
    piece = lax.all_gather(w_qkv, "seq", axis=0, tiled=True)
    flat_piece = piece.reshape(piece.shape[0], 3 * width)
    projected = jnp.dot(normed, flat_piece, preferred_element_type=jnp.float32)
    qkv = projected.astype(jnp.bfloat16).reshape(rows_dev, 3, width)
    scale = 1.0 / head_size**0.5
    keys_local = jnp.concatenate([cache_k, qkv[:, 1]], axis=0)
    vals_local = jnp.concatenate([cache_v, qkv[:, 2]], axis=0)
    head_q = qkv[:, 0].reshape(rows_dev, heads_dev, head_size)
    query_pos = my_index * rows_dev + jnp.arange(rows_dev, dtype=jnp.int32)
    run_max = jnp.full((heads_dev, rows_dev), -1e30, jnp.float32)
    key_piece = lax.all_gather(keys_local, "seq", axis=0, tiled=True)
    val_piece = lax.all_gather(vals_local, "seq", axis=0, tiled=True)
    count = key_piece.shape[0]
    row_ids = jnp.arange(count, dtype=jnp.int32)
    source = row_ids // stride
    within = row_ids % stride
    key_pos = jnp.where(within < cache_rows, -1, source * rows_dev + within - cache_rows)
    visible = (key_pos[None, :] <= query_pos[:, None])[None]
    scores = (
        jnp.einsum(
            "qhd,khd->hqk",
            head_q,
            key_piece.reshape(count, heads_dev, head_size),
            preferred_element_type=jnp.float32,
        )
        * scale
    )
    scores = jnp.where(visible, scores, jnp.float32(-1e30))
    new_max = jnp.maximum(run_max, jnp.max(scores, axis=-1))
    weights = jnp.where(visible, jnp.exp(scores - new_max[..., None]), jnp.float32(0.0))
    new_sum = jnp.sum(weights, axis=-1)
    probs = weights.astype(jnp.bfloat16)
    added = jnp.einsum(
        "hqk,khd->hqd",
        probs,
        val_piece.reshape(count, heads_dev, head_size),
        preferred_element_type=jnp.float32,
    )
    result = jnp.transpose(added / new_sum[..., None], (1, 0, 2))
    return result.reshape(rows_dev, width).astype(jnp.bfloat16)


def solution(mesh):
    sizes = mesh.shape
    paired = sizes["chan"] == 4 and HEADS // sizes["chan"] == sizes["seq"]
    return jax.shard_map(
        fast_body if paired else body,
        mesh=mesh,
        in_specs=(
            P("seq", None, "chan"),
            P(None, "chan"),
            P("chan", None),
            P(),
            P("seq", None, "chan"),
            P("seq", "chan"),
            P("seq", "chan"),
        ),
        out_specs=P("seq", "chan"),
        check_vma=False,
    )
```

```python
import functools

import jax
import jax.numpy as jnp
from jax import lax
from jax.experimental import pallas as pl
from jax.experimental.pallas import tpu as pltpu
from jax.sharding import PartitionSpec as P

D = 4096
HEADS = 32
HEAD = D // HEADS
LANES = 128
PAD = 8
BF16 = jnp.bfloat16
F32 = jnp.float32
MIB = 1024 * 1024


BRIEF = pl.CostEstimate(flops=1, transcendentals=0, bytes_accessed=1)


VMEM = pl.BlockSpec(memory_space=pltpu.VMEM)
SMEM = pl.BlockSpec(memory_space=pltpu.SMEM)


def whole(shape):
    return pl.BlockSpec(shape, lambda *_: (0,) * len(shape))


def conv_kernel(group, hin_ref, halo_ref, taps_ref, out_ref):
    taps = taps_ref[...]
    count = taps.shape[0]
    width = taps.shape[1]
    kv = (hin_ref[1].astype(F32) * hin_ref[2].astype(F32)).astype(BF16)
    ext = jnp.concatenate([halo_ref[...], kv], axis=0)
    rows = kv.shape[0]
    blocks = rows // width
    windows = jnp.concatenate(
        [ext[b * width : (b + 2) * width] for b in range(blocks)], axis=1
    )
    high = taps.astype(BF16)
    low = (taps - high.astype(F32)).astype(BF16)
    source = lax.broadcasted_iota(jnp.int32, (width, 2 * width), 0)
    column = lax.broadcasted_iota(jnp.int32, (width, 2 * width), 1)
    flip = jnp.where(source + column == width, 1.0, 0.0).astype(BF16)
    total = None
    for part in (high, low):
        first = jnp.dot(part, flip, preferred_element_type=F32)
        toeplitz = jnp.concatenate(
            [
                pltpu.roll(
                    jnp.broadcast_to(first[g : g + 1], (width, 2 * width)),
                    0,
                    1,
                    stride=1,
                    stride_axis=0,
                ).astype(BF16)
                for g in range(count)
            ],
            axis=0,
        )
        product = jnp.dot(toeplitz, windows, preferred_element_type=F32)
        total = product if total is None else total + product
    owner = lax.broadcasted_iota(jnp.int32, (width, blocks * LANES), 1) % LANES // group
    conv = total[:width]
    for g in range(1, count):
        conv = jnp.where(owner == g, total[g * width : (g + 1) * width], conv)
    query = hin_ref[0].astype(F32)
    for b in range(blocks):
        piece = query[b * width : (b + 1) * width] * conv[:, b * LANES : (b + 1) * LANES]
        out_ref[b * width : (b + 1) * width, :] = piece.astype(BF16)


def hyena(hin, halo, filters):
    _, rows, width = hin.shape
    taps = filters.shape[1]
    group = width // filters.shape[0]
    per_tile = LANES // group
    return pl.pallas_call(
        functools.partial(conv_kernel, group),
        grid=(width // LANES,),
        in_specs=[
            pl.BlockSpec((3, rows, LANES), lambda i: (0, 0, i)),
            pl.BlockSpec((taps, LANES), lambda i: (0, i)),
            pl.BlockSpec((per_tile, taps), lambda i: (i, 0)),
        ],
        out_specs=pl.BlockSpec((rows, LANES), lambda i: (0, i)),
        out_shape=jax.ShapeDtypeStruct((rows, width), BF16),
        compiler_params=pltpu.CompilerParams(vmem_limit_bytes=8 * MIB),
        cost_estimate=BRIEF,
        name="hyena_filters",
    )(hin, halo, filters)


def norm_kernel(j, place_ref, own_ref, x_ref, y_ref, d0_ref, d1_ref, gain_ref, *rest):
    out_ref = rest[-1]
    chan = place_ref[0]
    half = d0_ref.shape[0]
    step = 16

    def band(i, diag_ref, start):
        at = pl.ds(pl.multiple_of(start + i * step, step), step)
        refs = (own_ref.at[at], x_ref.at[at], y_ref.at[at], diag_ref.at[pl.ds(pl.multiple_of(i * step, step), step)])
        parts = [r[...].astype(F32) for r in refs]
        total = sum(jnp.sum(p * p, axis=-1, keepdims=True) for p in parts)
        factor = lax.rsqrt(total / D + 1e-6)
        for m, p in enumerate(parts):
            where = chan ^ m
            out_ref[j, where, at, :] = (p * factor * gain_ref[where]).astype(BF16)

    for diag_ref, start in ((d0_ref, 0), (d1_ref, half)):
        pl.loop(0, half // step, unroll=2)(functools.partial(band, diag_ref=diag_ref, start=start))


def norm(place, j, zs, own, from_x, from_y, diag0, diag1, gain, buffer):
    rows, width = own.shape
    args = [place, own, from_x, from_y, diag0, diag1, gain] + ([] if buffer is None else [buffer])
    return pl.pallas_call(
        functools.partial(norm_kernel, j),
        in_specs=[SMEM] + [VMEM] * (len(args) - 1),
        out_specs=VMEM,
        out_shape=jax.ShapeDtypeStruct((zs, 4, rows, width), BF16),
        input_output_aliases={} if buffer is None else {7: 0},
        compiler_params=pltpu.CompilerParams(vmem_limit_bytes=4 * MIB),
        cost_estimate=BRIEF,
        name="norm",
    )(*args)


def project_kernel(shifts, slabs, parts, zs, extra, apart, place_ref, normed_ref, *refs):
    groups = 1 + max(group for group, _ in parts)
    n = len(shifts)
    weights, rest = refs[: 2 * n * groups], refs[2 * n * groups :]
    before, outs = rest[:extra], rest[-len(parts) * (zs if apart else 1) :]
    z, core = place_ref[1], place_ref[2]
    depth = normed_ref.shape[3] // 2
    for part, (group, row) in enumerate(parts):
        for j in slabs:
            total = before[part][j] if before else None
            for i, shift in enumerate(shifts):
                block = lax.rem(z + zs - shift, zs)
                for k in range(2):
                    at = pl.multiple_of((core ^ k) * depth, depth)
                    left = normed_ref[j, block, :, pl.ds(at, depth)]
                    right = weights[(2 * group + k) * n + i][row : row + depth, :]
                    term = jnp.dot(left, right, preferred_element_type=F32)
                    total = term if total is None else total + term
            if apart:
                outs[part * zs + j][...] = total.astype(outs[0].dtype)
            else:
                outs[part][j] = total.astype(outs[0].dtype)


def project(place, normed, groups, parts, shifts, slabs, rounded, before=(), into=(), apart=False):
    zs, _, rows, _ = normed.shape
    weights = [w for own, sib in groups for w in (*own, *sib)]
    args = [place, normed, *weights, *before, *into]
    shape = (rows, weights[0].shape[1]) if apart else (zs, rows, weights[0].shape[1])
    out = [jax.ShapeDtypeStruct(shape, BF16 if rounded else F32)] * (len(parts) * (zs if apart else 1))
    return pl.pallas_call(
        functools.partial(project_kernel, shifts, slabs, parts, zs, len(before), apart),
        in_specs=[SMEM] + [VMEM] * (len(args) - 1),
        out_specs=[VMEM] * len(out),
        out_shape=out,
        input_output_aliases={len(args) - len(into) + i: i for i in range(len(into))},
        compiler_params=pltpu.CompilerParams(vmem_limit_bytes=8 * MIB),
        cost_estimate=BRIEF,
        name="project",
    )(*args)


NT = (((1,), (1,)), ((), ()))


def lanes(op, s):
    full = s.shape[1] - s.shape[1] % LANES
    rest = s[:, full:] if full < s.shape[1] else None
    return functools.reduce(op, [s[:, i : i + LANES] for i in range(0, full, LANES)]), rest


def weigh_kernel(blocks, place_ref, q_ref, ck_ref, *refs):
    z, core = place_ref[1], place_ref[2]
    zs, rows, cols = q_ref.shape
    k_refs, ks_refs, (old_ref, new_ref, sum_ref, k_ref, ks_ref, scratch) = refs[:zs], refs[zs : 2 * zs], refs[-6:]
    for j in range(zs):
        k_ref[j], ks_ref[j] = k_refs[j][...], ks_refs[j][...]
    crow = ck_ref.shape[0]
    factor = 1.4426950408889634 / HEAD**0.5
    row = lax.broadcasted_iota(jnp.int32, (rows, rows), 0)
    col = lax.broadcasted_iota(jnp.int32, (rows, rows), 1)
    causal = col <= row
    slab = [lax.rem(z + zs - b, zs) for b in range(zs)]

    for block in blocks:
        for h in range(cols // HEAD):
            hcol = slice(h * HEAD, (h + 1) * HEAD)
            query = q_ref[slab[block], :, hcol]

            def score(key):
                return lax.dot_general(query, key, NT, preferred_element_type=F32)

            s = score(ck_ref[:, hcol])
            scratch[h, :, :crow] = s
            top, end = lanes(jnp.maximum, s)
            for b in range(block + 1):
                s, t = score(k_ref[slab[b], :, hcol]), score(ks_ref[slab[b], :, hcol])
                if b == block:
                    s, t = jnp.where(causal, s, -1e30), jnp.where(core == 1, t, -1e30)
                at = crow + 2 * rows * b
                scratch[h, :, at : at + rows] = s
                scratch[h, :, at + rows : at + 2 * rows] = t
                top = jnp.maximum(top, jnp.maximum(lanes(jnp.maximum, s)[0], lanes(jnp.maximum, t)[0]))
            top = jnp.max(top, axis=-1, keepdims=True)
            if end is not None:
                top = jnp.maximum(top, jnp.max(end, axis=-1, keepdims=True))
            top = top * factor

            weights = jnp.exp2(scratch[h, :, :crow] * factor - top)
            old_ref[block, h] = weights.astype(BF16)
            total, end = lanes(jnp.add, weights)
            for b in range(block + 1):
                at = crow + 2 * rows * b
                weights = jnp.exp2(scratch[h, :, at : at + 2 * rows] * factor - top)
                new_ref[block, h, b] = weights.astype(BF16)
                total = total + lanes(jnp.add, weights)[0]
            total = jnp.sum(total, axis=-1, keepdims=True)
            if end is not None:
                total = total + jnp.sum(end, axis=-1, keepdims=True)
            sum_ref[block, h] = jnp.broadcast_to(total, (rows, HEAD))


def weigh(blocks, place, q, k, k_sib, ck, into=()):
    zs, rows, cols = q.shape
    heads, crow = cols // HEAD, ck.shape[0]
    return pl.pallas_call(
        functools.partial(weigh_kernel, blocks),
        in_specs=[SMEM] + [VMEM] * (2 + 2 * zs + len(into)),
        input_output_aliases={3 + 2 * zs + i: i for i in range(len(into))},
        out_specs=[VMEM] * 3,
        out_shape=[
            jax.ShapeDtypeStruct((zs, heads, rows, crow), BF16),
            jax.ShapeDtypeStruct((zs, heads, zs, rows, 2 * rows), BF16),
            jax.ShapeDtypeStruct((zs, heads, rows, HEAD), F32),
        ],
        scratch_shapes=[pltpu.VMEM((zs, rows, cols), BF16)] * 2
        + [pltpu.VMEM((heads, rows, -(-(crow + 2 * rows * zs) // LANES) * LANES), F32)],
        compiler_params=pltpu.CompilerParams(vmem_limit_bytes=14 * MIB),
        cost_estimate=BRIEF,
        name="weigh",
    )(place, q, ck, *k, *k_sib, *into)


def mix_kernel(shifts, place_ref, old_ref, new_ref, sum_ref, v_ref, vs_ref, cv_ref, *outs):
    z = place_ref[1]
    zs, rows, cols = v_ref.shape
    heads = range(cols // HEAD)
    hcols = [slice(h * HEAD, (h + 1) * HEAD) for h in heads]
    for shift, out_ref in zip(shifts, outs):
        block = lax.rem(z + shift, zs)

        def add(b, state):
            at = lax.rem(z + zs - b, zs)
            result = []
            for h, summed in zip(heads, state):
                probs = new_ref[block, h, b]
                value = jnp.concatenate([v_ref[at, :, hcols[h]], vs_ref[at, :, hcols[h]]], axis=0)
                result.append(summed + jnp.dot(probs, value, preferred_element_type=F32))
            return tuple(result)

        state = tuple(
            jnp.dot(old_ref[block, h], cv_ref[:, hcols[h]], preferred_element_type=F32) for h in heads
        )
        state = lax.fori_loop(0, block + 1, add, state)
        for h, summed in zip(heads, state):
            out_ref[:, hcols[h]] = (summed / sum_ref[block, h]).astype(BF16)


def mix(shifts, place, old, new, sums, v, v_sib, cv):
    _, rows, cols = v.shape
    return pl.pallas_call(
        functools.partial(mix_kernel, shifts),
        in_specs=[SMEM] + [VMEM] * 6,
        out_specs=[VMEM] * len(shifts),
        out_shape=[jax.ShapeDtypeStruct((rows, cols), BF16)] * len(shifts),
        compiler_params=pltpu.CompilerParams(vmem_limit_bytes=8 * MIB),
        cost_estimate=BRIEF,
        name="mix",
    )(place, old, new, sums, v, v_sib, cv)


def pack_kernel(places, crow, *refs):
    parcels, outs, scratch = refs[: len(places)], refs[len(places) : -1], refs[-1]
    for n, out_ref in enumerate(outs):
        for i, (piece, at) in enumerate(zip(parcels, places)):
            at += n * (crow + PAD)
            scratch[i * crow : (i + 1) * crow, :] = piece[at : at + crow + PAD].astype(F32)[:crow]
        out_ref[...] = scratch[...].astype(BF16)


def pack(parcels, places, crow):
    out = (len(parcels) * crow, parcels[0].shape[1])
    return pl.pallas_call(
        functools.partial(pack_kernel, places, crow),
        in_specs=[VMEM] * len(parcels),
        out_specs=[VMEM] * 2,
        out_shape=[jax.ShapeDtypeStruct(out, BF16)] * 2,
        scratch_shapes=[pltpu.VMEM(out, F32)],
        compiler_params=pltpu.CompilerParams(vmem_limit_bytes=8 * MIB),
        cost_estimate=BRIEF,
        name="pack",
    )(*parcels)


def join_kernel(place_ref, *refs):
    pieces, (out_ref, sems) = refs[:-2], refs[-2:]
    zs = len(pieces)
    cols = pieces[0].shape[1]
    copies = []
    for r, piece in enumerate(pieces):
        at = pl.multiple_of(lax.rem(place_ref[1] + zs - r, zs) * cols, cols)
        copies.append(pltpu.make_async_copy(piece, out_ref.at[:, pl.ds(at, cols)], sems.at[r]))
    for copy in copies:
        copy.start()
    for copy in copies:
        copy.wait()


def join(place, pieces):
    rows, cols = pieces[0].shape
    out = (rows, cols * len(pieces))
    return pl.pallas_call(
        join_kernel,
        in_specs=[SMEM] + [VMEM] * len(pieces),
        out_specs=pl.BlockSpec(memory_space=pl.ANY),
        out_shape=jax.ShapeDtypeStruct(out, BF16),
        scratch_shapes=[pltpu.SemaphoreType.DMA((len(pieces),))],
        name="join",
    )(place, *pieces)


def shift_z(value, steps, zs):
    pairs = [(2 * a + k, 2 * ((a + steps) % zs) + k) for a in range(zs) for k in range(2)]
    return lax.ppermute(value, "seq", pairs)


def swap_core(value, zs):
    return lax.ppermute(value, "seq", [(2 * a + k, 2 * a + 1 - k) for a in range(zs) for k in range(2)])


def swap_chan(value, bit):
    return lax.ppermute(value, "chan", [(c, c ^ bit) for c in range(4)])


def after(value, *others):
    return lax.optimization_barrier((value, *others))[0]


def fast_body(hyena_in, prior_kv, filters, gain, w_qkv, cache_k, cache_v):
    rows, _, width = hyena_in.shape
    seqs = lax.axis_size("seq")
    zs = seqs // 2
    taps = filters.shape[1]
    depth, crow = w_qkv.shape[0], cache_k.shape[0]
    cols = width // zs
    my_seq = lax.axis_index("seq")
    z, core = my_seq // 2, my_seq % 2
    chan = lax.axis_index("chan")
    place = jnp.stack([chan, z, core]).astype(jnp.int32)

    w_t = jnp.transpose(w_qkv, (1, 0, 2))
    caches = [jnp.pad(c, ((0, PAD), (0, 0))) for c in (cache_k, cache_v)]

    def parcel(kind, r, *others):
        at = (z + r) % zs * cols
        source = after(w_t, *others) if others else w_t
        parts = [
            lax.dynamic_slice(source, ("qkv".index(p), 0, at), (1, depth, cols))[0]
            for p in kind
            if p != "c"
        ]
        if "c" in kind:
            parts += [lax.dynamic_slice_in_dim(c, at, cols, 1) for c in caches]
        return jnp.concatenate(parts, axis=0)

    hin = jnp.transpose(hyena_in, (1, 0, 2))
    tail = (hin[1, rows - taps :].astype(F32) * hin[2, rows - taps :].astype(F32)).astype(BF16)
    halo = lax.ppermute(tail, "seq", [(s, s + 1) for s in range(seqs - 1)])
    halo = jnp.where(my_seq == 0, jnp.pad(prior_kv, ((taps - prior_kv.shape[0], 0), (0, 0))), halo)

    order = ["q1", "q3", "acts", "kvc1", "acts", "kvc3", "acts", "q2", "kc2", "v2"]
    acts = [hyena(hin, halo, filters)]
    here = {kind + "0": parcel(kind, 0, acts[0]) for kind in ("kvc", "q")}
    sent = []
    for n, item in enumerate(order):
        if item == "acts":
            value, steps = acts[-1], 1
        else:
            kind, steps = item[:-1], int(item[-1])
            value = parcel(kind, steps, *acts[: int(n >= 2)])
        if n >= 2:
            value = after(value, sent[n - 2])
        sent.append(shift_z(value, steps, zs))
        if item == "acts":
            acts.append(sent[-1])
        else:
            here[item] = sent[-1]
    late = ["q2", "kc2", "v2"]
    there = {item: swap_core(here[item], zs) for item in here if item not in late}

    pace = [[], ["kvc1"], ["kvc3"], []]
    swapped = [[], ["kvc0", "q0"], ["q1", "q3"], ["kvc1"]]
    gain4 = gain.reshape(4, 1, width)
    half = rows // 2
    normed, diag0, diag1 = None, None, None
    every, early, last = tuple(range(zs)), (0, 1, 3), zs - 1

    def sides(*items):
        return [[side[item] for item in items] for side in (here, there)]

    def project_early(slabs, into=()):
        groups = [sides("q0", "q1", "q3"), sides("kvc0", "kvc1", "kvc3")]
        parts = ((0, 0), (1, 0), (1, depth))
        return project(place, normed, groups, parts, early, slabs, False, (), into)

    def project_last(item, sums, *others, apart=False):
        normed_then = after(normed, *others) if others else normed
        return project(place, normed_then, [sides(item)], ((0, 0),), (2,), every, True, (sums,), apart=apart)

    for j, own in enumerate(acts):
        own = after(own, *([diag0, diag1] if j else [here["q1"], here["q3"]]))
        from_x, from_y = swap_chan(own, 1), swap_chan(own, 2)
        if j:
            sums = project_early(every[:last]) if j == last else []
            normed = after(normed, *sums) if j == last else normed
            settled = [normed] + [there[item] for item in swapped[j]] + [here[item] for item in pace[j]]
            from_x, from_y = after(from_x, *settled), after(from_y, *settled)
        diag0 = swap_chan(from_x[:half], 2)
        diag1 = swap_chan(from_y[half:], 1)
        normed = norm(place, j, zs, own, from_x, from_y, diag0, diag1, gain4, normed)

    there["kc2"] = swap_core(after(here["kc2"], diag0, diag1), zs)
    q_sum, k_sum, v_sum = project_early(every[last:], sums)
    kept = sum(sides("kvc0", "kvc1", "kc2", "kvc3"), [])
    ck, cv = pack(kept, [depth if i % zs == 2 else 2 * depth for i in range(2 * zs)], crow)
    k = project_last("kc2", k_sum, ck, apart=True)
    k_sib = [swap_core(slab, zs) for slab in k]
    there["q2"] = swap_core(after(here["q2"], k[0]), zs)
    (q,) = project_last("q2", q_sum)
    weights = weigh((3, 0), place, q, k, k_sib, ck)
    there["v2"] = swap_core(after(here["v2"], weights[2]), zs)
    weights = weigh((1,), place, q, k, k_sib, ck, weights)
    (v,) = project_last("v2", v_sum, weights[2])
    v_sib = swap_core(v, zs)
    weights = weigh((2,), place, q, k, k_sib, ck, weights)
    pieces, out = {}, None
    for shifts, wait in (((2,), ()), ((1, 3), ()), ((0,), (2,))):
        ready = v if out is None else after(v, out[0], *[pieces[r] for r in wait])
        out = mix(shifts, place, *weights, ready, v_sib, cv)
        for r, piece in zip(shifts, out):
            pieces[r] = shift_z(piece, r, zs) if r else piece
    return join(place, [pieces[r] for r in range(zs)])


def shifted(value, axis, steps):
    count = lax.axis_size(axis)
    leading, last = (max(0, -steps), min(count, count - steps))
    return lax.ppermute(value, axis, [(source, source + steps) for source in range(leading, last)])


def body(hyena_in, prior_kv, filters, gain, w_qkv, cache_k, cache_v):
    rows_dev = hyena_in.shape[0]
    width = hyena_in.shape[2]
    history = prior_kv.shape[0]
    tap_count = filters.shape[1]
    head_size = D // HEADS
    heads_dev = width // head_size
    cache_rows = cache_k.shape[0]
    stride = cache_rows + rows_dev
    my_index = lax.axis_index("seq")
    stream_q = hyena_in[:, 0].astype(jnp.float32)
    kv_prod = (hyena_in[:, 1].astype(jnp.float32) * hyena_in[:, 2].astype(jnp.float32)).astype(
        jnp.bfloat16
    )
    before = shifted(kv_prod[rows_dev - history :], "seq", 1)
    before = jnp.where(my_index == 0, prior_kv, before)
    extended = jnp.concatenate([before, kv_prod], axis=0).astype(jnp.float32)
    tap_table = jnp.repeat(filters, width // filters.shape[0], axis=0).T

    def add_tap(tap_index, total):
        offset = (tap_count - 1 - tap_index).astype(jnp.int32)
        window = lax.dynamic_slice_in_dim(extended, offset, rows_dev, 0)
        coeff = lax.dynamic_index_in_dim(tap_table, tap_index.astype(jnp.int32), 0, keepdims=True)
        return total + coeff * window

    conv = lax.fori_loop(0, tap_count, add_tap, jnp.zeros((rows_dev, width), jnp.float32))
    hyena_out = (stream_q * conv).astype(jnp.bfloat16)
    whole = lax.all_gather(hyena_out, "chan", axis=1, tiled=True)
    as_float = whole.astype(jnp.float32)
    mean_sq = jnp.mean(as_float * as_float, axis=-1, keepdims=True)
    normed = (as_float * lax.rsqrt(mean_sq + 1e-06) * gain[None, :]).astype(jnp.bfloat16)
    piece = lax.all_gather(w_qkv, "seq", axis=0, tiled=True)
    flat_piece = piece.reshape(piece.shape[0], 3 * width)
    projected = jnp.dot(normed, flat_piece, preferred_element_type=jnp.float32)
    qkv = projected.astype(jnp.bfloat16).reshape(rows_dev, 3, width)
    scale = 1.0 / head_size**0.5
    keys_local = jnp.concatenate([cache_k, qkv[:, 1]], axis=0)
    vals_local = jnp.concatenate([cache_v, qkv[:, 2]], axis=0)
    head_q = qkv[:, 0].reshape(rows_dev, heads_dev, head_size)
    query_pos = my_index * rows_dev + jnp.arange(rows_dev, dtype=jnp.int32)
    run_max = jnp.full((heads_dev, rows_dev), -1e30, jnp.float32)
    key_piece = lax.all_gather(keys_local, "seq", axis=0, tiled=True)
    val_piece = lax.all_gather(vals_local, "seq", axis=0, tiled=True)
    count = key_piece.shape[0]
    row_ids = jnp.arange(count, dtype=jnp.int32)
    source = row_ids // stride
    within = row_ids % stride
    key_pos = jnp.where(within < cache_rows, -1, source * rows_dev + within - cache_rows)
    visible = (key_pos[None, :] <= query_pos[:, None])[None]
    scores = (
        jnp.einsum(
            "qhd,khd->hqk",
            head_q,
            key_piece.reshape(count, heads_dev, head_size),
            preferred_element_type=jnp.float32,
        )
        * scale
    )
    scores = jnp.where(visible, scores, jnp.float32(-1e30))
    new_max = jnp.maximum(run_max, jnp.max(scores, axis=-1))
    weights = jnp.where(visible, jnp.exp(scores - new_max[..., None]), jnp.float32(0.0))
    new_sum = jnp.sum(weights, axis=-1)
    probs = weights.astype(jnp.bfloat16)
    added = jnp.einsum(
        "hqk,khd->hqd",
        probs,
        val_piece.reshape(count, heads_dev, head_size),
        preferred_element_type=jnp.float32,
    )
    result = jnp.transpose(added / new_sum[..., None], (1, 0, 2))
    return result.reshape(rows_dev, width).astype(jnp.bfloat16)


def solution(mesh):
    sizes = mesh.shape
    paired = sizes["chan"] == 4 and HEADS // sizes["chan"] == sizes["seq"]
    return jax.shard_map(
        fast_body if paired else body,
        mesh=mesh,
        in_specs=(
            P("seq", None, "chan"),
            P(None, "chan"),
            P("chan", None),
            P(),
            P("seq", None, "chan"),
            P("seq", "chan"),
            P("seq", "chan"),
        ),
        out_specs=P("seq", "chan"),
        check_vma=False,
    )
```

```python
import functools

import jax
import jax.numpy as jnp
from jax import lax
from jax.experimental import pallas as pl
from jax.experimental.pallas import tpu as pltpu
from jax.sharding import PartitionSpec as P

D = 4096
HEADS = 32
HEAD = D // HEADS
LANES = 128
PAD = 8
BF16 = jnp.bfloat16
F32 = jnp.float32
MIB = 1024 * 1024


BRIEF = pl.CostEstimate(flops=1, transcendentals=0, bytes_accessed=1)


VMEM = pl.BlockSpec(memory_space=pltpu.VMEM)
SMEM = pl.BlockSpec(memory_space=pltpu.SMEM)


def whole(shape):
    return pl.BlockSpec(shape, lambda *_: (0,) * len(shape))


def conv_kernel(group, hin_ref, halo_ref, taps_ref, out_ref):
    taps = taps_ref[...]
    count = taps.shape[0]
    width = taps.shape[1]
    kv = (hin_ref[1].astype(F32) * hin_ref[2].astype(F32)).astype(BF16)
    ext = jnp.concatenate([halo_ref[...], kv], axis=0)
    rows = kv.shape[0]
    blocks = rows // width
    windows = jnp.concatenate(
        [ext[b * width : (b + 2) * width] for b in range(blocks)], axis=1
    )
    high = taps.astype(BF16)
    low = (taps - high.astype(F32)).astype(BF16)
    source = lax.broadcasted_iota(jnp.int32, (width, 2 * width), 0)
    column = lax.broadcasted_iota(jnp.int32, (width, 2 * width), 1)
    flip = jnp.where(source + column == width, 1.0, 0.0).astype(BF16)
    total = None
    for part in (high, low):
        first = jnp.dot(part, flip, preferred_element_type=F32)
        toeplitz = jnp.concatenate(
            [
                pltpu.roll(
                    jnp.broadcast_to(first[g : g + 1], (width, 2 * width)),
                    0,
                    1,
                    stride=1,
                    stride_axis=0,
                ).astype(BF16)
                for g in range(count)
            ],
            axis=0,
        )
        product = jnp.dot(toeplitz, windows, preferred_element_type=F32)
        total = product if total is None else total + product
    owner = lax.broadcasted_iota(jnp.int32, (width, blocks * LANES), 1) % LANES // group
    conv = total[:width]
    for g in range(1, count):
        conv = jnp.where(owner == g, total[g * width : (g + 1) * width], conv)
    query = hin_ref[0].astype(F32)
    for b in range(blocks):
        piece = query[b * width : (b + 1) * width] * conv[:, b * LANES : (b + 1) * LANES]
        out_ref[b * width : (b + 1) * width, :] = piece.astype(BF16)


def hyena(hin, halo, filters):
    _, rows, width = hin.shape
    taps = filters.shape[1]
    group = width // filters.shape[0]
    per_tile = LANES // group
    return pl.pallas_call(
        functools.partial(conv_kernel, group),
        grid=(width // LANES,),
        in_specs=[
            pl.BlockSpec((3, rows, LANES), lambda i: (0, 0, i)),
            pl.BlockSpec((taps, LANES), lambda i: (0, i)),
            pl.BlockSpec((per_tile, taps), lambda i: (i, 0)),
        ],
        out_specs=pl.BlockSpec((rows, LANES), lambda i: (0, i)),
        out_shape=jax.ShapeDtypeStruct((rows, width), BF16),
        compiler_params=pltpu.CompilerParams(vmem_limit_bytes=8 * MIB),
        cost_estimate=BRIEF,
        name="hyena_filters",
    )(hin, halo, filters)


def norm_kernel(j, place_ref, own_ref, x_ref, y_ref, d0_ref, d1_ref, gain_ref, *rest):
    out_ref = rest[-1]
    chan = place_ref[0]
    half = d0_ref.shape[0]
    step = 16

    def band(i, diag_ref, start):
        at = pl.ds(pl.multiple_of(start + i * step, step), step)
        refs = (own_ref.at[at], x_ref.at[at], y_ref.at[at], diag_ref.at[pl.ds(pl.multiple_of(i * step, step), step)])
        parts = [r[...].astype(F32) for r in refs]
        total = sum(jnp.sum(p * p, axis=-1, keepdims=True) for p in parts)
        factor = lax.rsqrt(total / D + 1e-6)
        for m, p in enumerate(parts):
            where = chan ^ m
            out_ref[j, where, at, :] = (p * factor * gain_ref[where]).astype(BF16)

    for diag_ref, start in ((d0_ref, 0), (d1_ref, half)):
        pl.loop(0, half // step, unroll=2)(functools.partial(band, diag_ref=diag_ref, start=start))


def norm(place, j, zs, own, from_x, from_y, diag0, diag1, gain, buffer):
    rows, width = own.shape
    args = [place, own, from_x, from_y, diag0, diag1, gain] + ([] if buffer is None else [buffer])
    return pl.pallas_call(
        functools.partial(norm_kernel, j),
        in_specs=[SMEM] + [VMEM] * (len(args) - 1),
        out_specs=VMEM,
        out_shape=jax.ShapeDtypeStruct((zs, 4, rows, width), BF16),
        input_output_aliases={} if buffer is None else {7: 0},
        compiler_params=pltpu.CompilerParams(vmem_limit_bytes=4 * MIB),
        cost_estimate=BRIEF,
        name="norm",
    )(*args)


def project_kernel(shifts, slabs, parts, zs, extra, apart, place_ref, normed_ref, *refs):
    groups = 1 + max(group for group, _ in parts)
    n = len(shifts)
    weights, rest = refs[: 2 * n * groups], refs[2 * n * groups :]
    before, outs = rest[:extra], rest[-len(parts) * (zs if apart else 1) :]
    z, core = place_ref[1], place_ref[2]
    depth = normed_ref.shape[3] // 2
    for part, (group, row) in enumerate(parts):
        for j in slabs:
            total = before[part][j] if before else None
            for i, shift in enumerate(shifts):
                block = lax.rem(z + zs - shift, zs)
                for k in range(2):
                    at = pl.multiple_of((core ^ k) * depth, depth)
                    left = normed_ref[j, block, :, pl.ds(at, depth)]
                    right = weights[(2 * group + k) * n + i][row : row + depth, :]
                    term = jnp.dot(left, right, preferred_element_type=F32)
                    total = term if total is None else total + term
            if apart:
                outs[part * zs + j][...] = total.astype(outs[0].dtype)
            else:
                outs[part][j] = total.astype(outs[0].dtype)


def project(place, normed, groups, parts, shifts, slabs, rounded, before=(), into=(), apart=False):
    zs, _, rows, _ = normed.shape
    weights = [w for own, sib in groups for w in (*own, *sib)]
    args = [place, normed, *weights, *before, *into]
    shape = (rows, weights[0].shape[1]) if apart else (zs, rows, weights[0].shape[1])
    out = [jax.ShapeDtypeStruct(shape, BF16 if rounded else F32)] * (len(parts) * (zs if apart else 1))
    return pl.pallas_call(
        functools.partial(project_kernel, shifts, slabs, parts, zs, len(before), apart),
        in_specs=[SMEM] + [VMEM] * (len(args) - 1),
        out_specs=[VMEM] * len(out),
        out_shape=out,
        input_output_aliases={len(args) - len(into) + i: i for i in range(len(into))},
        compiler_params=pltpu.CompilerParams(vmem_limit_bytes=8 * MIB),
        cost_estimate=BRIEF,
        name="project",
    )(*args)


NT = (((1,), (1,)), ((), ()))


def lanes(op, s):
    full = s.shape[1] - s.shape[1] % LANES
    rest = s[:, full:] if full < s.shape[1] else None
    return functools.reduce(op, [s[:, i : i + LANES] for i in range(0, full, LANES)]), rest


def weigh_kernel(blocks, place_ref, q_ref, ck_ref, *refs):
    z, core = place_ref[1], place_ref[2]
    zs, rows, cols = q_ref.shape
    k_refs, ks_refs, (old_ref, new_ref, sum_ref, k_ref, ks_ref, scratch) = refs[:zs], refs[zs : 2 * zs], refs[-6:]
    for j in range(zs):
        k_ref[j], ks_ref[j] = k_refs[j][...], ks_refs[j][...]
    crow = ck_ref.shape[0]
    factor = 1.4426950408889634 / HEAD**0.5
    row = lax.broadcasted_iota(jnp.int32, (rows, rows), 0)
    col = lax.broadcasted_iota(jnp.int32, (rows, rows), 1)
    causal = col <= row
    slab = [lax.rem(z + zs - b, zs) for b in range(zs)]

    for block in blocks:
        for h in range(cols // HEAD):
            hcol = slice(h * HEAD, (h + 1) * HEAD)
            query = q_ref[slab[block], :, hcol]

            def score(key):
                return lax.dot_general(query, key, NT, preferred_element_type=F32)

            s = score(ck_ref[:, hcol])
            scratch[h, :, :crow] = s
            top, end = lanes(jnp.maximum, s)
            for b in range(block + 1):
                s, t = score(k_ref[slab[b], :, hcol]), score(ks_ref[slab[b], :, hcol])
                if b == block:
                    s, t = jnp.where(causal, s, -1e30), jnp.where(core == 1, t, -1e30)
                at = crow + 2 * rows * b
                scratch[h, :, at : at + rows] = s
                scratch[h, :, at + rows : at + 2 * rows] = t
                top = jnp.maximum(top, jnp.maximum(lanes(jnp.maximum, s)[0], lanes(jnp.maximum, t)[0]))
            top = jnp.max(top, axis=-1, keepdims=True)
            if end is not None:
                top = jnp.maximum(top, jnp.max(end, axis=-1, keepdims=True))
            top = top * factor

            weights = jnp.exp2(scratch[h, :, :crow] * factor - top)
            old_ref[block, h] = weights.astype(BF16)
            total, end = lanes(jnp.add, weights)
            for b in range(block + 1):
                at = crow + 2 * rows * b
                weights = jnp.exp2(scratch[h, :, at : at + 2 * rows] * factor - top)
                new_ref[block, h, b] = weights.astype(BF16)
                total = total + lanes(jnp.add, weights)[0]
            total = jnp.sum(total, axis=-1, keepdims=True)
            if end is not None:
                total = total + jnp.sum(end, axis=-1, keepdims=True)
            sum_ref[block, h] = jnp.broadcast_to(total, (rows, HEAD))


def weigh(blocks, place, q, k, k_sib, ck, into=()):
    zs, rows, cols = q.shape
    heads, crow = cols // HEAD, ck.shape[0]
    return pl.pallas_call(
        functools.partial(weigh_kernel, blocks),
        in_specs=[SMEM] + [VMEM] * (2 + 2 * zs + len(into)),
        input_output_aliases={3 + 2 * zs + i: i for i in range(len(into))},
        out_specs=[VMEM] * 3,
        out_shape=[
            jax.ShapeDtypeStruct((zs, heads, rows, crow), BF16),
            jax.ShapeDtypeStruct((zs, heads, zs, rows, 2 * rows), BF16),
            jax.ShapeDtypeStruct((zs, heads, rows, HEAD), F32),
        ],
        scratch_shapes=[pltpu.VMEM((zs, rows, cols), BF16)] * 2
        + [pltpu.VMEM((heads, rows, -(-(crow + 2 * rows * zs) // LANES) * LANES), F32)],
        compiler_params=pltpu.CompilerParams(vmem_limit_bytes=14 * MIB),
        cost_estimate=BRIEF,
        name="weigh",
    )(place, q, ck, *k, *k_sib, *into)


def mix_kernel(shifts, place_ref, old_ref, new_ref, sum_ref, v_ref, vs_ref, cv_ref, *outs):
    z = place_ref[1]
    zs, rows, cols = v_ref.shape
    heads = range(cols // HEAD)
    hcols = [slice(h * HEAD, (h + 1) * HEAD) for h in heads]
    for shift, out_ref in zip(shifts, outs):
        block = lax.rem(z + shift, zs)

        def add(b, state):
            at = lax.rem(z + zs - b, zs)
            result = []
            for h, summed in zip(heads, state):
                probs = new_ref[block, h, b]
                value = jnp.concatenate([v_ref[at, :, hcols[h]], vs_ref[at, :, hcols[h]]], axis=0)
                result.append(summed + jnp.dot(probs, value, preferred_element_type=F32))
            return tuple(result)

        state = tuple(
            jnp.dot(old_ref[block, h], cv_ref[:, hcols[h]], preferred_element_type=F32) for h in heads
        )
        state = lax.fori_loop(0, block + 1, add, state)
        for h, summed in zip(heads, state):
            out_ref[:, hcols[h]] = (summed / sum_ref[block, h]).astype(BF16)


def mix(shifts, place, old, new, sums, v, v_sib, cv):
    _, rows, cols = v.shape
    return pl.pallas_call(
        functools.partial(mix_kernel, shifts),
        in_specs=[SMEM] + [VMEM] * 6,
        out_specs=[VMEM] * len(shifts),
        out_shape=[jax.ShapeDtypeStruct((rows, cols), BF16)] * len(shifts),
        compiler_params=pltpu.CompilerParams(vmem_limit_bytes=8 * MIB),
        cost_estimate=BRIEF,
        name="mix",
    )(place, old, new, sums, v, v_sib, cv)


def pack_kernel(places, crow, *refs):
    parcels, outs, scratch = refs[: len(places)], refs[len(places) : -1], refs[-1]
    for n, out_ref in enumerate(outs):
        for i, (piece, at) in enumerate(zip(parcels, places)):
            at += n * (crow + PAD)
            scratch[i * crow : (i + 1) * crow, :] = piece[at : at + crow + PAD].astype(F32)[:crow]
        out_ref[...] = scratch[...].astype(BF16)


def pack(parcels, places, crow):
    out = (len(parcels) * crow, parcels[0].shape[1])
    return pl.pallas_call(
        functools.partial(pack_kernel, places, crow),
        in_specs=[VMEM] * len(parcels),
        out_specs=[VMEM] * 2,
        out_shape=[jax.ShapeDtypeStruct(out, BF16)] * 2,
        scratch_shapes=[pltpu.VMEM(out, F32)],
        compiler_params=pltpu.CompilerParams(vmem_limit_bytes=8 * MIB),
        cost_estimate=BRIEF,
        name="pack",
    )(*parcels)


def join_kernel(place_ref, *refs):
    pieces, (out_ref, sems) = refs[:-2], refs[-2:]
    zs = len(pieces)
    cols = pieces[0].shape[1]
    copies = []
    for r, piece in enumerate(pieces):
        at = pl.multiple_of(lax.rem(place_ref[1] + zs - r, zs) * cols, cols)
        copies.append(pltpu.make_async_copy(piece, out_ref.at[:, pl.ds(at, cols)], sems.at[r]))
    for copy in copies:
        copy.start()
    for copy in copies:
        copy.wait()


def join(place, pieces):
    rows, cols = pieces[0].shape
    out = (rows, cols * len(pieces))
    return pl.pallas_call(
        join_kernel,
        in_specs=[SMEM] + [VMEM] * len(pieces),
        out_specs=pl.BlockSpec(memory_space=pl.ANY),
        out_shape=jax.ShapeDtypeStruct(out, BF16),
        scratch_shapes=[pltpu.SemaphoreType.DMA((len(pieces),))],
        name="join",
    )(place, *pieces)


def shift_z(value, steps, zs):
    pairs = [(2 * a + k, 2 * ((a + steps) % zs) + k) for a in range(zs) for k in range(2)]
    return lax.ppermute(value, "seq", pairs)


def swap_core(value, zs):
    return lax.ppermute(value, "seq", [(2 * a + k, 2 * a + 1 - k) for a in range(zs) for k in range(2)])


def swap_chan(value, bit):
    return lax.ppermute(value, "chan", [(c, c ^ bit) for c in range(4)])


def after(value, *others):
    return lax.optimization_barrier((value, *others))[0]


def fast_body(hyena_in, prior_kv, filters, gain, w_qkv, cache_k, cache_v):
    rows, _, width = hyena_in.shape
    seqs = lax.axis_size("seq")
    zs = seqs // 2
    taps = filters.shape[1]
    depth, crow = w_qkv.shape[0], cache_k.shape[0]
    cols = width // zs
    my_seq = lax.axis_index("seq")
    z, core = my_seq // 2, my_seq % 2
    chan = lax.axis_index("chan")
    place = jnp.stack([chan, z, core]).astype(jnp.int32)

    w_t = jnp.transpose(w_qkv, (1, 0, 2))
    caches = [jnp.pad(c, ((0, PAD), (0, 0))) for c in (cache_k, cache_v)]

    def parcel(kind, r, *others):
        at = (z + r) % zs * cols
        source = after(w_t, *others) if others else w_t
        parts = [
            lax.dynamic_slice(source, ("qkv".index(p), 0, at), (1, depth, cols))[0]
            for p in kind
            if p != "c"
        ]
        if "c" in kind:
            parts += [lax.dynamic_slice_in_dim(c, at, cols, 1) for c in caches]
        return jnp.concatenate(parts, axis=0)

    hin = jnp.transpose(hyena_in, (1, 0, 2))
    tail = (hin[1, rows - taps :].astype(F32) * hin[2, rows - taps :].astype(F32)).astype(BF16)
    halo = lax.ppermute(tail, "seq", [(s, s + 1) for s in range(seqs - 1)])
    halo = jnp.where(my_seq == 0, jnp.pad(prior_kv, ((taps - prior_kv.shape[0], 0), (0, 0))), halo)

    order = ["q1", "q3", "acts", "kvc1", "acts", "kvc3", "acts", "q2", "kc2", "v2"]
    acts = [hyena(hin, halo, filters)]
    here = {kind + "0": parcel(kind, 0, acts[0]) for kind in ("kvc", "q")}
    sent = []
    for n, item in enumerate(order):
        if item == "acts":
            value, steps = acts[-1], 1
        else:
            kind, steps = item[:-1], int(item[-1])
            value = parcel(kind, steps, *acts[: int(n >= 2)])
        if n >= 2:
            value = after(value, sent[n - 2])
        sent.append(shift_z(value, steps, zs))
        if item == "acts":
            acts.append(sent[-1])
        else:
            here[item] = sent[-1]
    late = ["q2", "kc2", "v2"]
    there = {item: swap_core(here[item], zs) for item in here if item not in late}

    pace = [[], ["kvc1"], ["kvc3"], []]
    swapped = [[], ["q0"], ["kvc0", "q1", "q3"], ["kvc1"]]
    gain4 = gain.reshape(4, 1, width)
    half = rows // 2
    normed, diag0, diag1 = None, None, None
    every, early, last = tuple(range(zs)), (0, 1, 3), zs - 1

    def sides(*items):
        return [[side[item] for item in items] for side in (here, there)]

    def project_early(slabs, into=()):
        groups = [sides("q0", "q1", "q3"), sides("kvc0", "kvc1", "kvc3")]
        parts = ((0, 0), (1, 0), (1, depth))
        return project(place, normed, groups, parts, early, slabs, False, (), into)

    def project_last(item, sums, *others, apart=False):
        normed_then = after(normed, *others) if others else normed
        return project(place, normed_then, [sides(item)], ((0, 0),), (2,), every, True, (sums,), apart=apart)

    for j, own in enumerate(acts):
        own = after(own, *([diag0, diag1] if j else [here["q1"], here["q3"]]))
        from_x, from_y = swap_chan(own, 1), swap_chan(own, 2)
        if j:
            sums = project_early(every[:last]) if j == last else []
            normed = after(normed, *sums) if j == last else normed
            settled = [normed] + [there[item] for item in swapped[j]] + [here[item] for item in pace[j]]
            from_x, from_y = after(from_x, *settled), after(from_y, *settled)
        diag0 = swap_chan(from_x[:half], 2)
        diag1 = swap_chan(from_y[half:], 1)
        normed = norm(place, j, zs, own, from_x, from_y, diag0, diag1, gain4, normed)

    there["kc2"] = swap_core(after(here["kc2"], diag0, diag1), zs)
    q_sum, k_sum, v_sum = project_early(every[last:], sums)
    kept = sum(sides("kvc0", "kvc1", "kc2", "kvc3"), [])
    ck, cv = pack(kept, [depth if i % zs == 2 else 2 * depth for i in range(2 * zs)], crow)
    k = project_last("kc2", k_sum, ck, apart=True)
    k_sib = [swap_core(slab, zs) for slab in k]
    there["q2"] = swap_core(after(here["q2"], k[0]), zs)
    (q,) = project_last("q2", q_sum)
    weights = weigh((3, 0), place, q, k, k_sib, ck)
    there["v2"] = swap_core(after(here["v2"], weights[2]), zs)
    weights = weigh((1,), place, q, k, k_sib, ck, weights)
    (v,) = project_last("v2", v_sum, weights[2])
    v_sib = swap_core(v, zs)
    weights = weigh((2,), place, q, k, k_sib, ck, weights)
    pieces, out = {}, None
    for shifts, wait in (((2,), ()), ((1, 3), ()), ((0,), (2,))):
        ready = v if out is None else after(v, out[0], *[pieces[r] for r in wait])
        out = mix(shifts, place, *weights, ready, v_sib, cv)
        for r, piece in zip(shifts, out):
            pieces[r] = shift_z(piece, r, zs) if r else piece
    return join(place, [pieces[r] for r in range(zs)])


def shifted(value, axis, steps):
    count = lax.axis_size(axis)
    leading, last = (max(0, -steps), min(count, count - steps))
    return lax.ppermute(value, axis, [(source, source + steps) for source in range(leading, last)])


def body(hyena_in, prior_kv, filters, gain, w_qkv, cache_k, cache_v):
    rows_dev = hyena_in.shape[0]
    width = hyena_in.shape[2]
    history = prior_kv.shape[0]
    tap_count = filters.shape[1]
    head_size = D // HEADS
    heads_dev = width // head_size
    cache_rows = cache_k.shape[0]
    stride = cache_rows + rows_dev
    my_index = lax.axis_index("seq")
    stream_q = hyena_in[:, 0].astype(jnp.float32)
    kv_prod = (hyena_in[:, 1].astype(jnp.float32) * hyena_in[:, 2].astype(jnp.float32)).astype(
        jnp.bfloat16
    )
    before = shifted(kv_prod[rows_dev - history :], "seq", 1)
    before = jnp.where(my_index == 0, prior_kv, before)
    extended = jnp.concatenate([before, kv_prod], axis=0).astype(jnp.float32)
    tap_table = jnp.repeat(filters, width // filters.shape[0], axis=0).T

    def add_tap(tap_index, total):
        offset = (tap_count - 1 - tap_index).astype(jnp.int32)
        window = lax.dynamic_slice_in_dim(extended, offset, rows_dev, 0)
        coeff = lax.dynamic_index_in_dim(tap_table, tap_index.astype(jnp.int32), 0, keepdims=True)
        return total + coeff * window

    conv = lax.fori_loop(0, tap_count, add_tap, jnp.zeros((rows_dev, width), jnp.float32))
    hyena_out = (stream_q * conv).astype(jnp.bfloat16)
    whole = lax.all_gather(hyena_out, "chan", axis=1, tiled=True)
    as_float = whole.astype(jnp.float32)
    mean_sq = jnp.mean(as_float * as_float, axis=-1, keepdims=True)
    normed = (as_float * lax.rsqrt(mean_sq + 1e-06) * gain[None, :]).astype(jnp.bfloat16)
    piece = lax.all_gather(w_qkv, "seq", axis=0, tiled=True)
    flat_piece = piece.reshape(piece.shape[0], 3 * width)
    projected = jnp.dot(normed, flat_piece, preferred_element_type=jnp.float32)
    qkv = projected.astype(jnp.bfloat16).reshape(rows_dev, 3, width)
    scale = 1.0 / head_size**0.5
    keys_local = jnp.concatenate([cache_k, qkv[:, 1]], axis=0)
    vals_local = jnp.concatenate([cache_v, qkv[:, 2]], axis=0)
    head_q = qkv[:, 0].reshape(rows_dev, heads_dev, head_size)
    query_pos = my_index * rows_dev + jnp.arange(rows_dev, dtype=jnp.int32)
    run_max = jnp.full((heads_dev, rows_dev), -1e30, jnp.float32)
    key_piece = lax.all_gather(keys_local, "seq", axis=0, tiled=True)
    val_piece = lax.all_gather(vals_local, "seq", axis=0, tiled=True)
    count = key_piece.shape[0]
    row_ids = jnp.arange(count, dtype=jnp.int32)
    source = row_ids // stride
    within = row_ids % stride
    key_pos = jnp.where(within < cache_rows, -1, source * rows_dev + within - cache_rows)
    visible = (key_pos[None, :] <= query_pos[:, None])[None]
    scores = (
        jnp.einsum(
            "qhd,khd->hqk",
            head_q,
            key_piece.reshape(count, heads_dev, head_size),
            preferred_element_type=jnp.float32,
        )
        * scale
    )
    scores = jnp.where(visible, scores, jnp.float32(-1e30))
    new_max = jnp.maximum(run_max, jnp.max(scores, axis=-1))
    weights = jnp.where(visible, jnp.exp(scores - new_max[..., None]), jnp.float32(0.0))
    new_sum = jnp.sum(weights, axis=-1)
    probs = weights.astype(jnp.bfloat16)
    added = jnp.einsum(
        "hqk,khd->hqd",
        probs,
        val_piece.reshape(count, heads_dev, head_size),
        preferred_element_type=jnp.float32,
    )
    result = jnp.transpose(added / new_sum[..., None], (1, 0, 2))
    return result.reshape(rows_dev, width).astype(jnp.bfloat16)


def solution(mesh):
    sizes = mesh.shape
    paired = sizes["chan"] == 4 and HEADS // sizes["chan"] == sizes["seq"]
    return jax.shard_map(
        fast_body if paired else body,
        mesh=mesh,
        in_specs=(
            P("seq", None, "chan"),
            P(None, "chan"),
            P("chan", None),
            P(),
            P("seq", None, "chan"),
            P("seq", "chan"),
            P("seq", "chan"),
        ),
        out_specs=P("seq", "chan"),
        check_vma=False,
    )
```

```python
import functools

import jax
import jax.numpy as jnp
from jax import lax
from jax.experimental import pallas as pl
from jax.experimental.pallas import tpu as pltpu
from jax.sharding import PartitionSpec as P

D = 4096
HEADS = 32
HEAD = D // HEADS
LANES = 128
PAD = 8
BF16 = jnp.bfloat16
F32 = jnp.float32
MIB = 1024 * 1024


BRIEF = pl.CostEstimate(flops=1, transcendentals=0, bytes_accessed=1)


VMEM = pl.BlockSpec(memory_space=pltpu.VMEM)
SMEM = pl.BlockSpec(memory_space=pltpu.SMEM)


def whole(shape):
    return pl.BlockSpec(shape, lambda *_: (0,) * len(shape))


def conv_kernel(group, hin_ref, halo_ref, taps_ref, out_ref):
    taps = taps_ref[...]
    count = taps.shape[0]
    width = taps.shape[1]
    kv = (hin_ref[1].astype(F32) * hin_ref[2].astype(F32)).astype(BF16)
    ext = jnp.concatenate([halo_ref[...], kv], axis=0)
    rows = kv.shape[0]
    blocks = rows // width
    windows = jnp.concatenate(
        [ext[b * width : (b + 2) * width] for b in range(blocks)], axis=1
    )
    high = taps.astype(BF16)
    low = (taps - high.astype(F32)).astype(BF16)
    source = lax.broadcasted_iota(jnp.int32, (width, 2 * width), 0)
    column = lax.broadcasted_iota(jnp.int32, (width, 2 * width), 1)
    flip = jnp.where(source + column == width, 1.0, 0.0).astype(BF16)
    total = None
    for part in (high, low):
        first = jnp.dot(part, flip, preferred_element_type=F32)
        toeplitz = jnp.concatenate(
            [
                pltpu.roll(
                    jnp.broadcast_to(first[g : g + 1], (width, 2 * width)),
                    0,
                    1,
                    stride=1,
                    stride_axis=0,
                ).astype(BF16)
                for g in range(count)
            ],
            axis=0,
        )
        product = jnp.dot(toeplitz, windows, preferred_element_type=F32)
        total = product if total is None else total + product
    owner = lax.broadcasted_iota(jnp.int32, (width, blocks * LANES), 1) % LANES // group
    conv = total[:width]
    for g in range(1, count):
        conv = jnp.where(owner == g, total[g * width : (g + 1) * width], conv)
    query = hin_ref[0].astype(F32)
    for b in range(blocks):
        piece = query[b * width : (b + 1) * width] * conv[:, b * LANES : (b + 1) * LANES]
        out_ref[b * width : (b + 1) * width, :] = piece.astype(BF16)


def hyena(hin, halo, filters):
    _, rows, width = hin.shape
    taps = filters.shape[1]
    group = width // filters.shape[0]
    per_tile = LANES // group
    return pl.pallas_call(
        functools.partial(conv_kernel, group),
        grid=(width // LANES,),
        in_specs=[
            pl.BlockSpec((3, rows, LANES), lambda i: (0, 0, i)),
            pl.BlockSpec((taps, LANES), lambda i: (0, i)),
            pl.BlockSpec((per_tile, taps), lambda i: (i, 0)),
        ],
        out_specs=pl.BlockSpec((rows, LANES), lambda i: (0, i)),
        out_shape=jax.ShapeDtypeStruct((rows, width), BF16),
        compiler_params=pltpu.CompilerParams(vmem_limit_bytes=12 * MIB),
        cost_estimate=BRIEF,
        name="hyena_filters",
    )(hin, halo, filters)


def norm_kernel(j, place_ref, own_ref, x_ref, y_ref, d0_ref, d1_ref, gain_ref, *rest):
    out_ref = rest[-1]
    chan = place_ref[0]
    half = d0_ref.shape[0]
    step = 16

    def band(i, diag_ref, start):
        at = pl.ds(pl.multiple_of(start + i * step, step), step)
        refs = (own_ref.at[at], x_ref.at[at], y_ref.at[at], diag_ref.at[pl.ds(pl.multiple_of(i * step, step), step)])
        parts = [r[...].astype(F32) for r in refs]
        total = sum(jnp.sum(p * p, axis=-1, keepdims=True) for p in parts)
        factor = lax.rsqrt(total / D + 1e-6)
        for m, p in enumerate(parts):
            where = chan ^ m
            out_ref[j, where, at, :] = (p * factor * gain_ref[where]).astype(BF16)

    for diag_ref, start in ((d0_ref, 0), (d1_ref, half)):
        pl.loop(0, half // step, unroll=2)(functools.partial(band, diag_ref=diag_ref, start=start))


def norm(place, j, zs, own, from_x, from_y, diag0, diag1, gain, buffer):
    rows, width = own.shape
    args = [place, own, from_x, from_y, diag0, diag1, gain] + ([] if buffer is None else [buffer])
    return pl.pallas_call(
        functools.partial(norm_kernel, j),
        in_specs=[SMEM] + [VMEM] * (len(args) - 1),
        out_specs=VMEM,
        out_shape=jax.ShapeDtypeStruct((zs, 4, rows, width), BF16),
        input_output_aliases={} if buffer is None else {7: 0},
        compiler_params=pltpu.CompilerParams(vmem_limit_bytes=16 * MIB),
        cost_estimate=BRIEF,
        name="norm",
    )(*args)


def project_kernel(shifts, zs, count, place_ref, normed_ref, *refs):
    n = len(shifts)
    own, sib, rest = refs[:n], refs[n : 2 * n], refs[2 * n :]
    before, outs = rest[:-count], rest[-count:]
    z, core = place_ref[1], place_ref[2]
    depth = normed_ref.shape[3] // 2
    for part, out_ref in enumerate(outs):
        for j in range(zs):
            total = before[part][j] if before else None
            for i, shift in enumerate(shifts):
                block = lax.rem(z + zs - shift, zs)
                for k, w_ref in enumerate((own[i], sib[i])):
                    at = pl.multiple_of((core ^ k) * depth, depth)
                    left = normed_ref[j, block, :, pl.ds(at, depth)]
                    right = w_ref[part * depth : (part + 1) * depth, :]
                    term = jnp.dot(left, right, preferred_element_type=F32)
                    total = term if total is None else total + term
            out_ref[j] = total.astype(out_ref.dtype)


def project(place, normed, own, sib, shifts, count, rounded, before=()):
    zs, _, rows, _ = normed.shape
    cols = own[0].shape[1]
    args = [place, normed, *own, *sib, *before]
    return pl.pallas_call(
        functools.partial(project_kernel, shifts, zs, count),
        in_specs=[SMEM] + [VMEM] * (len(args) - 1),
        out_specs=[VMEM] * count,
        out_shape=[jax.ShapeDtypeStruct((zs, rows, cols), BF16 if rounded else F32)] * count,
        compiler_params=pltpu.CompilerParams(vmem_limit_bytes=16 * MIB),
        cost_estimate=BRIEF,
        name="project",
    )(*args)


NT = (((1,), (1,)), ((), ()))


def attend_kernel(shifts, place_ref, q_ref, k_ref, v_ref, ks_ref, vs_ref, ck_ref, cv_ref, *refs):
    outs, (old, new) = refs[: len(shifts)], refs[len(shifts) :]
    z, core = place_ref[1], place_ref[2]
    zs, rows, cols = k_ref.shape
    heads = range(cols // HEAD)
    factor = 1.4426950408889634 / HEAD**0.5
    low = -1e30
    hcols = [slice(h * HEAD, (h + 1) * HEAD) for h in heads]
    row = lax.broadcasted_iota(jnp.int32, (rows, rows), 0)
    col = lax.broadcasted_iota(jnp.int32, (rows, rows), 1)
    causal = row <= col

    def score(key, query):
        return lax.dot_general(key, query, NT, preferred_element_type=F32)

    def mix(value, probs):
        return lax.dot_general(value, probs, (((0,), (0,)), ((), ())), preferred_element_type=F32)

    def fold(op, s):
        return op(s.reshape(s.shape[0] // 8, 8, s.shape[1]), axis=0)

    for shift, out_ref in zip(shifts, outs):
        block = lax.rem(z + shift, zs)
        mine = lax.rem(zs - shift, zs)
        queries = [q_ref[mine, :, hcol] for hcol in hcols]

        def scores(b, tops, diagonal):
            at = lax.rem(z + zs - b, zs)
            result = []
            for h, top in zip(heads, tops):
                s, t = score(k_ref[at, :, hcols[h]], queries[h]), score(ks_ref[at, :, hcols[h]], queries[h])
                if diagonal:
                    s, t = jnp.where(causal, s, low), jnp.where(core == 1, t, low)
                new[h, b, :rows] = s
                new[h, b, rows:] = t
                result.append(jnp.maximum(top, jnp.maximum(fold(jnp.max, s), fold(jnp.max, t))))
            return tuple(result)

        tops = []
        for h in heads:
            s = score(ck_ref[:, hcols[h]], queries[h])
            old[h] = s
            tops.append(fold(jnp.max, s))
        tops = lax.fori_loop(0, block, functools.partial(scores, diagonal=False), tuple(tops))
        tops = scores(block, tops, True)
        tops = [jnp.max(top, axis=0, keepdims=True) * factor for top in tops]

        def weigh(b, state):
            at = lax.rem(z + zs - b, zs)
            result = []
            for h, (total, summed) in zip(heads, state):
                weights = jnp.exp2(new[h, b] * factor - tops[h])
                probs = weights.astype(BF16)
                summed += mix(v_ref[at, :, hcols[h]], probs[:rows]) + mix(vs_ref[at, :, hcols[h]], probs[rows:])
                result.append((total + fold(jnp.sum, weights), summed))
            return tuple(result)

        state = []
        for h in heads:
            weights = jnp.exp2(old[h] * factor - tops[h])
            state.append((fold(jnp.sum, weights), mix(cv_ref[:, hcols[h]], weights.astype(BF16))))
        state = lax.fori_loop(0, block + 1, weigh, tuple(state))
        for h, (total, summed) in zip(heads, state):
            result = summed / jnp.sum(total, axis=0, keepdims=True)
            out_ref[:, hcols[h]] = result.T.astype(BF16)


def attend(shifts, place, q, k, v, k_sib, v_sib, ck, cv):
    zs, rows, cols = q.shape
    heads = cols // HEAD
    return pl.pallas_call(
        functools.partial(attend_kernel, shifts),
        in_specs=[SMEM] + [VMEM] * 7,
        out_specs=[VMEM] * len(shifts),
        out_shape=[jax.ShapeDtypeStruct((rows, cols), BF16)] * len(shifts),
        scratch_shapes=[
            pltpu.VMEM((heads, ck.shape[0], rows), F32),
            pltpu.VMEM((heads, zs, 2 * rows, rows), F32),
        ],
        compiler_params=pltpu.CompilerParams(vmem_limit_bytes=20 * MIB),
        cost_estimate=BRIEF,
        name="attend",
    )(place, q, k, v, k_sib, v_sib, ck, cv)


def pack_kernel(places, crow, *refs):
    parcels, outs, scratch = refs[: len(places)], refs[len(places) : -1], refs[-1]
    for n, out_ref in enumerate(outs):
        for i, (piece, at) in enumerate(zip(parcels, places)):
            at += n * (crow + PAD)
            scratch[i * crow : (i + 1) * crow, :] = piece[at : at + crow + PAD].astype(F32)[:crow]
        out_ref[...] = scratch[...].astype(BF16)


def pack(parcels, places, crow):
    out = (len(parcels) * crow, parcels[0].shape[1])
    return pl.pallas_call(
        functools.partial(pack_kernel, places, crow),
        in_specs=[VMEM] * len(parcels),
        out_specs=[VMEM] * 2,
        out_shape=[jax.ShapeDtypeStruct(out, BF16)] * 2,
        scratch_shapes=[pltpu.VMEM(out, F32)],
        compiler_params=pltpu.CompilerParams(vmem_limit_bytes=12 * MIB),
        cost_estimate=BRIEF,
        name="pack",
    )(*parcels)


def join_kernel(place_ref, *refs):
    pieces, (out_ref, sems) = refs[:-2], refs[-2:]
    zs = len(pieces)
    cols = pieces[0].shape[1]
    copies = []
    for r, piece in enumerate(pieces):
        at = pl.multiple_of(lax.rem(place_ref[1] + zs - r, zs) * cols, cols)
        copies.append(pltpu.make_async_copy(piece, out_ref.at[:, pl.ds(at, cols)], sems.at[r]))
    for copy in copies:
        copy.start()
    for copy in copies:
        copy.wait()


def join(place, pieces):
    rows, cols = pieces[0].shape
    out = (rows, cols * len(pieces))
    return pl.pallas_call(
        join_kernel,
        in_specs=[SMEM] + [pl.BlockSpec(memory_space=pl.ANY)] * len(pieces),
        out_specs=pl.BlockSpec(memory_space=pl.ANY),
        out_shape=jax.ShapeDtypeStruct(out, BF16),
        scratch_shapes=[pltpu.SemaphoreType.DMA((len(pieces),))],
        name="join",
    )(place, *pieces)


def shift_z(value, steps, zs):
    pairs = [(2 * a + k, 2 * ((a + steps) % zs) + k) for a in range(zs) for k in range(2)]
    return lax.ppermute(value, "seq", pairs)


def swap_core(value, zs):
    return lax.ppermute(value, "seq", [(2 * a + k, 2 * a + 1 - k) for a in range(zs) for k in range(2)])


def swap_chan(value, bit):
    return lax.ppermute(value, "chan", [(c, c ^ bit) for c in range(4)])


def after(value, *others):
    return lax.optimization_barrier((value, *others))[0]


def fast_body(hyena_in, prior_kv, filters, gain, w_qkv, cache_k, cache_v):
    rows, _, width = hyena_in.shape
    seqs = lax.axis_size("seq")
    zs = seqs // 2
    taps = filters.shape[1]
    depth, crow = w_qkv.shape[0], cache_k.shape[0]
    cols = width // zs
    my_seq = lax.axis_index("seq")
    z, core = my_seq // 2, my_seq % 2
    chan = lax.axis_index("chan")
    place = jnp.stack([chan, z, core]).astype(jnp.int32)

    w_t = jnp.transpose(w_qkv, (1, 0, 2))
    caches = [jnp.pad(c, ((0, PAD), (0, 0))) for c in (cache_k, cache_v)]

    def parcel(kind, r, *others):
        at = (z + r) % zs * cols
        source = after(w_t, *others) if others else w_t
        parts = [
            lax.dynamic_slice(source, ("qkv".index(p), 0, at), (1, depth, cols))[0]
            for p in kind
            if p != "c"
        ]
        if "c" in kind:
            parts += [lax.dynamic_slice_in_dim(c, at, cols, 1) for c in caches]
        return jnp.concatenate(parts, axis=0)

    hin = jnp.transpose(hyena_in, (1, 0, 2))
    tail = (hin[1, rows - taps :].astype(F32) * hin[2, rows - taps :].astype(F32)).astype(BF16)
    halo = lax.ppermute(tail, "seq", [(s, s + 1) for s in range(seqs - 1)])
    halo = jnp.where(my_seq == 0, jnp.pad(prior_kv, ((taps - prior_kv.shape[0], 0), (0, 0))), halo)

    order = ["q1", "q3", "acts", "kvc1", "acts", "kvc3", "acts", "q2", "kc2", "v2"]
    acts = [hyena(hin, halo, filters)]
    here = {kind + "0": parcel(kind, 0, acts[0]) for kind in ("kvc", "q")}
    sent = []
    for n, item in enumerate(order):
        if item == "acts":
            value, steps = acts[-1], 1
        else:
            kind, steps = item[:-1], int(item[-1])
            value = parcel(kind, steps, *acts[: int(n >= 2)])
        if n >= 2:
            value = after(value, sent[n - 2])
        sent.append(shift_z(value, steps, zs))
        if item == "acts":
            acts.append(sent[-1])
        else:
            here[item] = sent[-1]
    late = ["q2", "kc2", "v2"]
    there = {item: swap_core(here[item], zs) for item in here if item not in late}

    pace = [[], ["kvc1"], ["kvc3"], ["q2"]]
    swapped = [[], ["kvc0", "q0"], ["q1", "q3"], ["kvc1"]]
    gain4 = gain.reshape(4, 1, width)
    half = rows // 2
    normed, diag0, diag1 = None, None, None
    for j, own in enumerate(acts):
        own = after(own, *([diag0, diag1] if j else [here["q1"], here["q3"]]))
        from_x, from_y = swap_chan(own, 1), swap_chan(own, 2)
        if j:
            settled = [normed] + [there[item] for item in swapped[j]] + [here[item] for item in pace[j]]
            from_x, from_y = after(from_x, *settled), after(from_y, *settled)
        diag0 = swap_chan(from_x[:half], 2)
        diag1 = swap_chan(from_y[half:], 1)
        normed = norm(place, j, zs, own, from_x, from_y, diag0, diag1, gain4, normed)

    def sides(*items):
        return [[side[item] for item in items] for side in (here, there)]

    early = (0, 1, 3)
    there["q2"] = swap_core(after(here["q2"], diag0, diag1), zs)
    there["kc2"] = swap_core(after(here["kc2"], diag0, diag1), zs)
    (q,) = project(place, normed, *sides("q0", "q1", "q3", "q2"), early + (2,), 1, True)
    k_early, v_early = project(place, normed, *sides("kvc0", "kvc1", "kvc3"), early, 2, False)
    kept = sum(sides("kvc0", "kvc1", "kc2", "kvc3"), [])
    ck, cv = pack(kept, [depth if i % zs == 2 else 2 * depth for i in range(2 * zs)], crow)
    (k,) = project(place, after(normed, q, ck), *sides("kc2"), (2,), 1, True, (k_early,))
    k_sib = swap_core(k, zs)
    there["v2"] = swap_core(after(here["v2"], k), zs)
    (v,) = project(place, normed, *sides("v2"), (2,), 1, True, (v_early,))
    v_sib = swap_core(v, zs)
    pieces, out = {}, None
    for shifts, wait in (((2,), ()), ((1, 3), ()), ((0,), (2,))):
        ready = q if out is None else after(q, out[0], *[pieces[r] for r in wait])
        out = attend(shifts, place, ready, k, v, k_sib, v_sib, ck, cv)
        for r, piece in zip(shifts, out):
            pieces[r] = shift_z(piece, r, zs) if r else piece
    return join(place, [pieces[r] for r in range(zs)])


def shifted(value, axis, steps):
    count = lax.axis_size(axis)
    leading, last = (max(0, -steps), min(count, count - steps))
    return lax.ppermute(value, axis, [(source, source + steps) for source in range(leading, last)])


def body(hyena_in, prior_kv, filters, gain, w_qkv, cache_k, cache_v):
    rows_dev = hyena_in.shape[0]
    width = hyena_in.shape[2]
    history = prior_kv.shape[0]
    tap_count = filters.shape[1]
    head_size = D // HEADS
    heads_dev = width // head_size
    cache_rows = cache_k.shape[0]
    stride = cache_rows + rows_dev
    my_index = lax.axis_index("seq")
    stream_q = hyena_in[:, 0].astype(jnp.float32)
    kv_prod = (hyena_in[:, 1].astype(jnp.float32) * hyena_in[:, 2].astype(jnp.float32)).astype(
        jnp.bfloat16
    )
    before = shifted(kv_prod[rows_dev - history :], "seq", 1)
    before = jnp.where(my_index == 0, prior_kv, before)
    extended = jnp.concatenate([before, kv_prod], axis=0).astype(jnp.float32)
    tap_table = jnp.repeat(filters, width // filters.shape[0], axis=0).T

    def add_tap(tap_index, total):
        offset = (tap_count - 1 - tap_index).astype(jnp.int32)
        window = lax.dynamic_slice_in_dim(extended, offset, rows_dev, 0)
        coeff = lax.dynamic_index_in_dim(tap_table, tap_index.astype(jnp.int32), 0, keepdims=True)
        return total + coeff * window

    conv = lax.fori_loop(0, tap_count, add_tap, jnp.zeros((rows_dev, width), jnp.float32))
    hyena_out = (stream_q * conv).astype(jnp.bfloat16)
    whole = lax.all_gather(hyena_out, "chan", axis=1, tiled=True)
    as_float = whole.astype(jnp.float32)
    mean_sq = jnp.mean(as_float * as_float, axis=-1, keepdims=True)
    normed = (as_float * lax.rsqrt(mean_sq + 1e-06) * gain[None, :]).astype(jnp.bfloat16)
    piece = lax.all_gather(w_qkv, "seq", axis=0, tiled=True)
    flat_piece = piece.reshape(piece.shape[0], 3 * width)
    projected = jnp.dot(normed, flat_piece, preferred_element_type=jnp.float32)
    qkv = projected.astype(jnp.bfloat16).reshape(rows_dev, 3, width)
    scale = 1.0 / head_size**0.5
    keys_local = jnp.concatenate([cache_k, qkv[:, 1]], axis=0)
    vals_local = jnp.concatenate([cache_v, qkv[:, 2]], axis=0)
    head_q = qkv[:, 0].reshape(rows_dev, heads_dev, head_size)
    query_pos = my_index * rows_dev + jnp.arange(rows_dev, dtype=jnp.int32)
    run_max = jnp.full((heads_dev, rows_dev), -1e30, jnp.float32)
    key_piece = lax.all_gather(keys_local, "seq", axis=0, tiled=True)
    val_piece = lax.all_gather(vals_local, "seq", axis=0, tiled=True)
    count = key_piece.shape[0]
    row_ids = jnp.arange(count, dtype=jnp.int32)
    source = row_ids // stride
    within = row_ids % stride
    key_pos = jnp.where(within < cache_rows, -1, source * rows_dev + within - cache_rows)
    visible = (key_pos[None, :] <= query_pos[:, None])[None]
    scores = (
        jnp.einsum(
            "qhd,khd->hqk",
            head_q,
            key_piece.reshape(count, heads_dev, head_size),
            preferred_element_type=jnp.float32,
        )
        * scale
    )
    scores = jnp.where(visible, scores, jnp.float32(-1e30))
    new_max = jnp.maximum(run_max, jnp.max(scores, axis=-1))
    weights = jnp.where(visible, jnp.exp(scores - new_max[..., None]), jnp.float32(0.0))
    new_sum = jnp.sum(weights, axis=-1)
    probs = weights.astype(jnp.bfloat16)
    added = jnp.einsum(
        "hqk,khd->hqd",
        probs,
        val_piece.reshape(count, heads_dev, head_size),
        preferred_element_type=jnp.float32,
    )
    result = jnp.transpose(added / new_sum[..., None], (1, 0, 2))
    return result.reshape(rows_dev, width).astype(jnp.bfloat16)


def solution(mesh):
    sizes = mesh.shape
    paired = sizes["chan"] == 4 and HEADS // sizes["chan"] == sizes["seq"]
    return jax.shard_map(
        fast_body if paired else body,
        mesh=mesh,
        in_specs=(
            P("seq", None, "chan"),
            P(None, "chan"),
            P("chan", None),
            P(),
            P("seq", None, "chan"),
            P("seq", "chan"),
            P("seq", "chan"),
        ),
        out_specs=P("seq", "chan"),
        check_vma=False,
    )
```

```python
import functools

import jax
import jax.numpy as jnp
from jax import lax
from jax.experimental import pallas as pl
from jax.experimental.pallas import tpu as pltpu
from jax.sharding import PartitionSpec as P

D = 4096
HEADS = 32
HEAD = D // HEADS
LANES = 128
PAD = 8
BF16 = jnp.bfloat16
F32 = jnp.float32
MIB = 1024 * 1024


BRIEF = pl.CostEstimate(flops=1, transcendentals=0, bytes_accessed=1)


VMEM = pl.BlockSpec(memory_space=pltpu.VMEM)
SMEM = pl.BlockSpec(memory_space=pltpu.SMEM)


def whole(shape):
    return pl.BlockSpec(shape, lambda *_: (0,) * len(shape))


def conv_kernel(group, hin_ref, halo_ref, taps_ref, out_ref):
    taps = taps_ref[...]
    count = taps.shape[0]
    width = taps.shape[1]
    kv = (hin_ref[1].astype(F32) * hin_ref[2].astype(F32)).astype(BF16)
    ext = jnp.concatenate([halo_ref[...], kv], axis=0)
    rows = kv.shape[0]
    blocks = rows // width
    windows = jnp.concatenate(
        [ext[b * width : (b + 2) * width] for b in range(blocks)], axis=1
    )
    high = taps.astype(BF16)
    low = (taps - high.astype(F32)).astype(BF16)
    source = lax.broadcasted_iota(jnp.int32, (width, 2 * width), 0)
    column = lax.broadcasted_iota(jnp.int32, (width, 2 * width), 1)
    flip = jnp.where(source + column == width, 1.0, 0.0).astype(BF16)
    total = None
    for part in (high, low):
        first = jnp.dot(part, flip, preferred_element_type=F32)
        toeplitz = jnp.concatenate(
            [
                pltpu.roll(
                    jnp.broadcast_to(first[g : g + 1], (width, 2 * width)),
                    0,
                    1,
                    stride=1,
                    stride_axis=0,
                ).astype(BF16)
                for g in range(count)
            ],
            axis=0,
        )
        product = jnp.dot(toeplitz, windows, preferred_element_type=F32)
        total = product if total is None else total + product
    owner = lax.broadcasted_iota(jnp.int32, (width, blocks * LANES), 1) % LANES // group
    conv = total[:width]
    for g in range(1, count):
        conv = jnp.where(owner == g, total[g * width : (g + 1) * width], conv)
    query = hin_ref[0].astype(F32)
    for b in range(blocks):
        piece = query[b * width : (b + 1) * width] * conv[:, b * LANES : (b + 1) * LANES]
        out_ref[b * width : (b + 1) * width, :] = piece.astype(BF16)


def hyena(hin, halo, filters):
    _, rows, width = hin.shape
    taps = filters.shape[1]
    group = width // filters.shape[0]
    per_tile = LANES // group
    return pl.pallas_call(
        functools.partial(conv_kernel, group),
        grid=(width // LANES,),
        in_specs=[
            pl.BlockSpec((3, rows, LANES), lambda i: (0, 0, i)),
            pl.BlockSpec((taps, LANES), lambda i: (0, i)),
            pl.BlockSpec((per_tile, taps), lambda i: (i, 0)),
        ],
        out_specs=pl.BlockSpec((rows, LANES), lambda i: (0, i)),
        out_shape=jax.ShapeDtypeStruct((rows, width), BF16),
        compiler_params=pltpu.CompilerParams(vmem_limit_bytes=12 * MIB),
        cost_estimate=BRIEF,
        name="hyena_filters",
    )(hin, halo, filters)


def norm_kernel(j, place_ref, own_ref, x_ref, y_ref, d0_ref, d1_ref, gain_ref, *rest):
    out_ref = rest[-1]
    chan = place_ref[0]
    half = d0_ref.shape[0]
    step = 16

    def band(i, diag_ref, start):
        at = pl.ds(pl.multiple_of(start + i * step, step), step)
        refs = (own_ref.at[at], x_ref.at[at], y_ref.at[at], diag_ref.at[pl.ds(pl.multiple_of(i * step, step), step)])
        parts = [r[...].astype(F32) for r in refs]
        total = sum(jnp.sum(p * p, axis=-1, keepdims=True) for p in parts)
        factor = lax.rsqrt(total / D + 1e-6)
        for m, p in enumerate(parts):
            where = chan ^ m
            out_ref[j, where, at, :] = (p * factor * gain_ref[where]).astype(BF16)

    for diag_ref, start in ((d0_ref, 0), (d1_ref, half)):
        pl.loop(0, half // step, unroll=2)(functools.partial(band, diag_ref=diag_ref, start=start))


def norm(place, j, zs, own, from_x, from_y, diag0, diag1, gain, buffer):
    rows, width = own.shape
    args = [place, own, from_x, from_y, diag0, diag1, gain] + ([] if buffer is None else [buffer])
    return pl.pallas_call(
        functools.partial(norm_kernel, j),
        in_specs=[SMEM] + [VMEM] * (len(args) - 1),
        out_specs=VMEM,
        out_shape=jax.ShapeDtypeStruct((zs, 4, rows, width), BF16),
        input_output_aliases={} if buffer is None else {7: 0},
        compiler_params=pltpu.CompilerParams(vmem_limit_bytes=16 * MIB),
        cost_estimate=BRIEF,
        name="norm",
    )(*args)


def project_kernel(shifts, zs, count, place_ref, normed_ref, *refs):
    n = len(shifts)
    own, sib, rest = refs[:n], refs[n : 2 * n], refs[2 * n :]
    before, outs = rest[:-count], rest[-count:]
    z, core = place_ref[1], place_ref[2]
    depth = normed_ref.shape[3] // 2
    for part, out_ref in enumerate(outs):
        for j in range(zs):
            total = before[part][j] if before else None
            for i, shift in enumerate(shifts):
                block = lax.rem(z + zs - shift, zs)
                for k, w_ref in enumerate((own[i], sib[i])):
                    at = pl.multiple_of((core ^ k) * depth, depth)
                    left = normed_ref[j, block, :, pl.ds(at, depth)]
                    right = w_ref[part * depth : (part + 1) * depth, :]
                    term = jnp.dot(left, right, preferred_element_type=F32)
                    total = term if total is None else total + term
            out_ref[j] = total.astype(out_ref.dtype)


def project(place, normed, own, sib, shifts, count, rounded, before=()):
    zs, _, rows, _ = normed.shape
    cols = own[0].shape[1]
    args = [place, normed, *own, *sib, *before]
    return pl.pallas_call(
        functools.partial(project_kernel, shifts, zs, count),
        in_specs=[SMEM] + [VMEM] * (len(args) - 1),
        out_specs=[VMEM] * count,
        out_shape=[jax.ShapeDtypeStruct((zs, rows, cols), BF16 if rounded else F32)] * count,
        compiler_params=pltpu.CompilerParams(vmem_limit_bytes=16 * MIB),
        cost_estimate=BRIEF,
        name="project",
    )(*args)


NT = (((1,), (1,)), ((), ()))


def lanes(op, s):
    full = s.shape[1] - s.shape[1] % LANES
    rest = s[:, full:] if full < s.shape[1] else None
    return functools.reduce(op, [s[:, i : i + LANES] for i in range(0, full, LANES)]), rest


def attend_kernel(shifts, place_ref, q_ref, k_ref, v_ref, ks_ref, vs_ref, ck_ref, cv_ref, *refs):
    outs, (old, new) = refs[: len(shifts)], refs[len(shifts) :]
    z, core = place_ref[1], place_ref[2]
    zs, rows, cols = k_ref.shape
    heads = range(cols // HEAD)
    factor = 1.4426950408889634 / HEAD**0.5
    low = -1e30
    hcols = [slice(h * HEAD, (h + 1) * HEAD) for h in heads]
    row = lax.broadcasted_iota(jnp.int32, (rows, rows), 0)
    col = lax.broadcasted_iota(jnp.int32, (rows, rows), 1)
    causal = col <= row

    for shift, out_ref in zip(shifts, outs):
        block = lax.rem(z + shift, zs)
        mine = lax.rem(zs - shift, zs)
        queries = [q_ref[mine, :, hcol] for hcol in hcols]

        def score(b, tops, diagonal):
            at = lax.rem(z + zs - b, zs)
            result = []
            for h, top in zip(heads, tops):
                s = lax.dot_general(queries[h], k_ref[at, :, hcols[h]], NT, preferred_element_type=F32)
                t = lax.dot_general(queries[h], ks_ref[at, :, hcols[h]], NT, preferred_element_type=F32)
                if diagonal:
                    s, t = jnp.where(causal, s, low), jnp.where(core == 1, t, low)
                new[h, b, :, :rows] = s
                new[h, b, :, rows:] = t
                folded = jnp.maximum(lanes(jnp.maximum, s)[0], lanes(jnp.maximum, t)[0])
                result.append(jnp.maximum(top, folded))
            return tuple(result)

        tops, ends = [], []
        for h in heads:
            s = lax.dot_general(queries[h], ck_ref[:, hcols[h]], NT, preferred_element_type=F32)
            old[h] = s
            folded, rest = lanes(jnp.maximum, s)
            tops.append(folded)
            ends.append(low if rest is None else jnp.max(rest, axis=-1, keepdims=True))
        tops = lax.fori_loop(0, block, functools.partial(score, diagonal=False), tuple(tops))
        tops = score(block, tops, True)
        tops = [
            jnp.maximum(jnp.max(top, axis=-1, keepdims=True), end) * factor
            for top, end in zip(tops, ends)
        ]

        def weigh(b, state):
            at = lax.rem(z + zs - b, zs)
            result = []
            for h, (total, summed) in zip(heads, state):
                weights = jnp.exp2(new[h, b] * factor - tops[h])
                probs = weights.astype(BF16)
                summed += jnp.dot(probs[:, :rows], v_ref[at, :, hcols[h]], preferred_element_type=F32)
                summed += jnp.dot(probs[:, rows:], vs_ref[at, :, hcols[h]], preferred_element_type=F32)
                result.append((total + lanes(jnp.add, weights)[0], summed))
            return tuple(result)

        state, ends = [], []
        for h in heads:
            weights = jnp.exp2(old[h] * factor - tops[h])
            folded, rest = lanes(jnp.add, weights)
            ends.append(0.0 if rest is None else jnp.sum(rest, axis=-1, keepdims=True))
            state.append(
                (folded, jnp.dot(weights.astype(BF16), cv_ref[:, hcols[h]], preferred_element_type=F32))
            )
        state = lax.fori_loop(0, block + 1, weigh, tuple(state))
        for h, (total, summed), end in zip(heads, state, ends):
            total = jnp.sum(total, axis=-1, keepdims=True) + end
            out_ref[:, hcols[h]] = (summed / total).astype(BF16)


def attend(shifts, place, q, k, v, k_sib, v_sib, ck, cv):
    zs, rows, cols = q.shape
    heads = cols // HEAD
    return pl.pallas_call(
        functools.partial(attend_kernel, shifts),
        in_specs=[SMEM] + [VMEM] * 7,
        out_specs=[VMEM] * len(shifts),
        out_shape=[jax.ShapeDtypeStruct((rows, cols), BF16)] * len(shifts),
        scratch_shapes=[
            pltpu.VMEM((heads, rows, ck.shape[0]), F32),
            pltpu.VMEM((heads, zs, rows, 2 * rows), F32),
        ],
        compiler_params=pltpu.CompilerParams(vmem_limit_bytes=20 * MIB),
        cost_estimate=BRIEF,
        name="attend",
    )(place, q, k, v, k_sib, v_sib, ck, cv)


def pack_kernel(places, crow, *refs):
    parcels, outs, scratch = refs[: len(places)], refs[len(places) : -1], refs[-1]
    for n, out_ref in enumerate(outs):
        for i, (piece, at) in enumerate(zip(parcels, places)):
            at += n * (crow + PAD)
            scratch[i * crow : (i + 1) * crow, :] = piece[at : at + crow + PAD].astype(F32)[:crow]
        out_ref[...] = scratch[...].astype(BF16)


def pack(parcels, places, crow):
    out = (len(parcels) * crow, parcels[0].shape[1])
    return pl.pallas_call(
        functools.partial(pack_kernel, places, crow),
        in_specs=[VMEM] * len(parcels),
        out_specs=[VMEM] * 2,
        out_shape=[jax.ShapeDtypeStruct(out, BF16)] * 2,
        scratch_shapes=[pltpu.VMEM(out, F32)],
        compiler_params=pltpu.CompilerParams(vmem_limit_bytes=12 * MIB),
        cost_estimate=BRIEF,
        name="pack",
    )(*parcels)


def join_kernel(place_ref, *refs):
    pieces, out_ref = refs[:-1], refs[-1]
    zs = len(pieces)
    cols = pieces[0].shape[1]
    for r, piece in enumerate(pieces):
        at = lax.rem(place_ref[1] + zs - r, zs) * cols
        out_ref[:, pl.ds(pl.multiple_of(at, cols), cols)] = piece[...]


def join(place, pieces):
    rows, cols = pieces[0].shape
    out = (rows, cols * len(pieces))
    return pl.pallas_call(
        join_kernel,
        in_specs=[SMEM] + [VMEM] * len(pieces),
        out_specs=whole(out),
        out_shape=jax.ShapeDtypeStruct(out, BF16),
        name="join",
    )(place, *pieces)


def shift_z(value, steps, zs):
    pairs = [(2 * a + k, 2 * ((a + steps) % zs) + k) for a in range(zs) for k in range(2)]
    return lax.ppermute(value, "seq", pairs)


def swap_core(value, zs):
    return lax.ppermute(value, "seq", [(2 * a + k, 2 * a + 1 - k) for a in range(zs) for k in range(2)])


def swap_chan(value, bit):
    return lax.ppermute(value, "chan", [(c, c ^ bit) for c in range(4)])


def after(value, *others):
    return lax.optimization_barrier((value, *others))[0]


def fast_body(hyena_in, prior_kv, filters, gain, w_qkv, cache_k, cache_v):
    rows, _, width = hyena_in.shape
    seqs = lax.axis_size("seq")
    zs = seqs // 2
    taps = filters.shape[1]
    depth, crow = w_qkv.shape[0], cache_k.shape[0]
    cols = width // zs
    my_seq = lax.axis_index("seq")
    z, core = my_seq // 2, my_seq % 2
    chan = lax.axis_index("chan")
    place = jnp.stack([chan, z, core]).astype(jnp.int32)

    w_t = jnp.transpose(w_qkv, (1, 0, 2))
    caches = [jnp.pad(c, ((0, PAD), (0, 0))) for c in (cache_k, cache_v)]

    def parcel(kind, r, *others):
        at = (z + r) % zs * cols
        source = after(w_t, *others) if others else w_t
        parts = [
            lax.dynamic_slice(source, ("qkv".index(p), 0, at), (1, depth, cols))[0]
            for p in kind
            if p != "c"
        ]
        if kind == "v":
            parts.append(jnp.zeros((16, cols), BF16))
        if "c" in kind:
            parts += [lax.dynamic_slice_in_dim(c, at, cols, 1) for c in caches]
        return jnp.concatenate(parts, axis=0)

    hin = jnp.transpose(hyena_in, (1, 0, 2))
    tail = (hin[1, rows - taps :].astype(F32) * hin[2, rows - taps :].astype(F32)).astype(BF16)
    halo = lax.ppermute(tail, "seq", [(s, s + 1) for s in range(seqs - 1)])
    halo = jnp.where(my_seq == 0, jnp.pad(prior_kv, ((taps - prior_kv.shape[0], 0), (0, 0))), halo)

    order = ["q1", "q3", "acts", "kvc1", "acts", "kvc3", "acts", "q2", "kc2", "v2"]
    acts = [hyena(hin, halo, filters)]
    here = {kind + "0": parcel(kind, 0, acts[0]) for kind in ("kvc", "q")}
    sent = []
    for n, item in enumerate(order):
        if item == "acts":
            value, steps = acts[-1], 1
        else:
            kind, steps = item[:-1], int(item[-1])
            value = parcel(kind, steps, *acts[: int(n >= 2)])
        if n >= 2:
            value = after(value, sent[n - 2])
        sent.append(shift_z(value, steps, zs))
        if item == "acts":
            acts.append(sent[-1])
        else:
            here[item] = sent[-1]
    late = ["q2", "kc2", "v2"]
    there = {item: swap_core(here[item], zs) for item in here if item not in late}

    pace = [[], ["kvc1"], ["kvc3"], ["q2"]]
    swapped = [[], ["kvc0", "q0"], ["q1", "q3"], ["kvc1"]]
    gain4 = gain.reshape(4, 1, width)
    half = rows // 2
    normed, diag0, diag1 = None, None, None
    for j, own in enumerate(acts):
        own = after(own, *([diag0, diag1] if j else [here["q1"], here["q3"]]))
        from_x, from_y = swap_chan(own, 1), swap_chan(own, 2)
        if j:
            settled = [normed] + [there[item] for item in swapped[j]] + [here[item] for item in pace[j]]
            from_x, from_y = after(from_x, *settled), after(from_y, *settled)
        diag0 = swap_chan(from_x[:half], 2)
        diag1 = swap_chan(from_y[half:], 1)
        normed = norm(place, j, zs, own, from_x, from_y, diag0, diag1, gain4, normed)

    def sides(*items):
        return [[side[item] for item in items] for side in (here, there)]

    early = (0, 1, 3)
    there["q2"] = swap_core(after(here["q2"], normed), zs)
    there["kc2"], far_cache = [
        swap_core(after(here["kc2"][a:b], normed), zs) for a, b in ((0, depth), (depth, None))
    ]
    (q,) = project(place, normed, *sides("q0", "q1", "q3", "q2"), early + (2,), 1, True)
    k_early, v_early = project(place, normed, *sides("kvc0", "kvc1", "kvc3"), early, 2, False)
    kept = sum(sides("kvc0", "kvc1", "kvc3"), []) + [here["kc2"], far_cache]
    ck, cv = pack(kept, [2 * depth] * (2 * zs - 2) + [depth, 0], crow)
    (k,) = project(place, after(normed, q, ck), *sides("kc2"), (2,), 1, True, (k_early,))
    k_sib = swap_core(k, zs)
    there["v2"] = swap_core(after(here["v2"], k), zs)
    (v,) = project(place, normed, *sides("v2"), (2,), 1, True, (v_early,))
    v_sib = swap_core(v, zs)
    pieces, out = {}, None
    for shifts, wait in (((2,), ()), ((1, 3), ()), ((0,), (2,))):
        ready = q if out is None else after(q, out[0], *[pieces[r] for r in wait])
        out = attend(shifts, place, ready, k, v, k_sib, v_sib, ck, cv)
        for r, piece in zip(shifts, out):
            pieces[r] = shift_z(piece, r, zs) if r else piece
    return join(place, [pieces[r] for r in range(zs)])


def shifted(value, axis, steps):
    count = lax.axis_size(axis)
    leading, last = (max(0, -steps), min(count, count - steps))
    return lax.ppermute(value, axis, [(source, source + steps) for source in range(leading, last)])


def body(hyena_in, prior_kv, filters, gain, w_qkv, cache_k, cache_v):
    rows_dev = hyena_in.shape[0]
    width = hyena_in.shape[2]
    history = prior_kv.shape[0]
    tap_count = filters.shape[1]
    head_size = D // HEADS
    heads_dev = width // head_size
    cache_rows = cache_k.shape[0]
    stride = cache_rows + rows_dev
    my_index = lax.axis_index("seq")
    stream_q = hyena_in[:, 0].astype(jnp.float32)
    kv_prod = (hyena_in[:, 1].astype(jnp.float32) * hyena_in[:, 2].astype(jnp.float32)).astype(
        jnp.bfloat16
    )
    before = shifted(kv_prod[rows_dev - history :], "seq", 1)
    before = jnp.where(my_index == 0, prior_kv, before)
    extended = jnp.concatenate([before, kv_prod], axis=0).astype(jnp.float32)
    tap_table = jnp.repeat(filters, width // filters.shape[0], axis=0).T

    def add_tap(tap_index, total):
        offset = (tap_count - 1 - tap_index).astype(jnp.int32)
        window = lax.dynamic_slice_in_dim(extended, offset, rows_dev, 0)
        coeff = lax.dynamic_index_in_dim(tap_table, tap_index.astype(jnp.int32), 0, keepdims=True)
        return total + coeff * window

    conv = lax.fori_loop(0, tap_count, add_tap, jnp.zeros((rows_dev, width), jnp.float32))
    hyena_out = (stream_q * conv).astype(jnp.bfloat16)
    whole = lax.all_gather(hyena_out, "chan", axis=1, tiled=True)
    as_float = whole.astype(jnp.float32)
    mean_sq = jnp.mean(as_float * as_float, axis=-1, keepdims=True)
    normed = (as_float * lax.rsqrt(mean_sq + 1e-06) * gain[None, :]).astype(jnp.bfloat16)
    piece = lax.all_gather(w_qkv, "seq", axis=0, tiled=True)
    flat_piece = piece.reshape(piece.shape[0], 3 * width)
    projected = jnp.dot(normed, flat_piece, preferred_element_type=jnp.float32)
    qkv = projected.astype(jnp.bfloat16).reshape(rows_dev, 3, width)
    scale = 1.0 / head_size**0.5
    keys_local = jnp.concatenate([cache_k, qkv[:, 1]], axis=0)
    vals_local = jnp.concatenate([cache_v, qkv[:, 2]], axis=0)
    head_q = qkv[:, 0].reshape(rows_dev, heads_dev, head_size)
    query_pos = my_index * rows_dev + jnp.arange(rows_dev, dtype=jnp.int32)
    run_max = jnp.full((heads_dev, rows_dev), -1e30, jnp.float32)
    key_piece = lax.all_gather(keys_local, "seq", axis=0, tiled=True)
    val_piece = lax.all_gather(vals_local, "seq", axis=0, tiled=True)
    count = key_piece.shape[0]
    row_ids = jnp.arange(count, dtype=jnp.int32)
    source = row_ids // stride
    within = row_ids % stride
    key_pos = jnp.where(within < cache_rows, -1, source * rows_dev + within - cache_rows)
    visible = (key_pos[None, :] <= query_pos[:, None])[None]
    scores = (
        jnp.einsum(
            "qhd,khd->hqk",
            head_q,
            key_piece.reshape(count, heads_dev, head_size),
            preferred_element_type=jnp.float32,
        )
        * scale
    )
    scores = jnp.where(visible, scores, jnp.float32(-1e30))
    new_max = jnp.maximum(run_max, jnp.max(scores, axis=-1))
    weights = jnp.where(visible, jnp.exp(scores - new_max[..., None]), jnp.float32(0.0))
    new_sum = jnp.sum(weights, axis=-1)
    probs = weights.astype(jnp.bfloat16)
    added = jnp.einsum(
        "hqk,khd->hqd",
        probs,
        val_piece.reshape(count, heads_dev, head_size),
        preferred_element_type=jnp.float32,
    )
    result = jnp.transpose(added / new_sum[..., None], (1, 0, 2))
    return result.reshape(rows_dev, width).astype(jnp.bfloat16)


def solution(mesh):
    sizes = mesh.shape
    paired = sizes["chan"] == 4 and HEADS // sizes["chan"] == sizes["seq"]
    return jax.shard_map(
        fast_body if paired else body,
        mesh=mesh,
        in_specs=(
            P("seq", None, "chan"),
            P(None, "chan"),
            P("chan", None),
            P(),
            P("seq", None, "chan"),
            P("seq", "chan"),
            P("seq", "chan"),
        ),
        out_specs=P("seq", "chan"),
        check_vma=False,
    )
```

```python
import functools

import jax
import jax.numpy as jnp
from jax import lax
from jax.experimental import pallas as pl
from jax.experimental.pallas import tpu as pltpu
from jax.sharding import PartitionSpec as P

D = 4096
HEADS = 32
HEAD = D // HEADS
LANES = 128
PAD = 8
BF16 = jnp.bfloat16
F32 = jnp.float32
MIB = 1024 * 1024


BRIEF = pl.CostEstimate(flops=1, transcendentals=0, bytes_accessed=1)


VMEM = pl.BlockSpec(memory_space=pltpu.VMEM)
SMEM = pl.BlockSpec(memory_space=pltpu.SMEM)


def whole(shape):
    return pl.BlockSpec(shape, lambda *_: (0,) * len(shape))


def conv_kernel(group, hin_ref, halo_ref, taps_ref, out_ref):
    taps = taps_ref[...]
    count = taps.shape[0]
    width = taps.shape[1]
    kv = (hin_ref[1].astype(F32) * hin_ref[2].astype(F32)).astype(BF16)
    ext = jnp.concatenate([halo_ref[...], kv], axis=0)
    rows = kv.shape[0]
    blocks = rows // width
    windows = jnp.concatenate(
        [ext[b * width : (b + 2) * width] for b in range(blocks)], axis=1
    )
    high = taps.astype(BF16)
    low = (taps - high.astype(F32)).astype(BF16)
    source = lax.broadcasted_iota(jnp.int32, (width, 2 * width), 0)
    column = lax.broadcasted_iota(jnp.int32, (width, 2 * width), 1)
    flip = jnp.where(source + column == width, 1.0, 0.0).astype(BF16)
    total = None
    for part in (high, low):
        first = jnp.dot(part, flip, preferred_element_type=F32)
        toeplitz = jnp.concatenate(
            [
                pltpu.roll(
                    jnp.broadcast_to(first[g : g + 1], (width, 2 * width)),
                    0,
                    1,
                    stride=1,
                    stride_axis=0,
                ).astype(BF16)
                for g in range(count)
            ],
            axis=0,
        )
        product = jnp.dot(toeplitz, windows, preferred_element_type=F32)
        total = product if total is None else total + product
    owner = lax.broadcasted_iota(jnp.int32, (width, blocks * LANES), 1) % LANES // group
    conv = total[:width]
    for g in range(1, count):
        conv = jnp.where(owner == g, total[g * width : (g + 1) * width], conv)
    query = hin_ref[0].astype(F32)
    for b in range(blocks):
        piece = query[b * width : (b + 1) * width] * conv[:, b * LANES : (b + 1) * LANES]
        out_ref[b * width : (b + 1) * width, :] = piece.astype(BF16)


def hyena(hin, halo, filters):
    _, rows, width = hin.shape
    taps = filters.shape[1]
    group = width // filters.shape[0]
    per_tile = LANES // group
    return pl.pallas_call(
        functools.partial(conv_kernel, group),
        grid=(width // LANES,),
        in_specs=[
            pl.BlockSpec((3, rows, LANES), lambda i: (0, 0, i)),
            pl.BlockSpec((taps, LANES), lambda i: (0, i)),
            pl.BlockSpec((per_tile, taps), lambda i: (i, 0)),
        ],
        out_specs=pl.BlockSpec((rows, LANES), lambda i: (0, i)),
        out_shape=jax.ShapeDtypeStruct((rows, width), BF16),
        compiler_params=pltpu.CompilerParams(vmem_limit_bytes=12 * MIB),
        cost_estimate=BRIEF,
        name="hyena_filters",
    )(hin, halo, filters)


def norm_kernel(j, place_ref, own_ref, x_ref, y_ref, d0_ref, d1_ref, gain_ref, *rest):
    out_ref = rest[-1]
    chan = place_ref[0]
    half = d0_ref.shape[0]
    step = 16

    def band(i, diag_ref, start):
        at = pl.ds(pl.multiple_of(start + i * step, step), step)
        refs = (own_ref.at[at], x_ref.at[at], y_ref.at[at], diag_ref.at[pl.ds(pl.multiple_of(i * step, step), step)])
        parts = [r[...].astype(F32) for r in refs]
        total = sum(jnp.sum(p * p, axis=-1, keepdims=True) for p in parts)
        factor = lax.rsqrt(total / D + 1e-6)
        for m, p in enumerate(parts):
            where = chan ^ m
            out_ref[j, where, at, :] = (p * factor * gain_ref[where]).astype(BF16)

    for diag_ref, start in ((d0_ref, 0), (d1_ref, half)):
        pl.loop(0, half // step, unroll=2)(functools.partial(band, diag_ref=diag_ref, start=start))


def norm(place, j, zs, own, from_x, from_y, diag0, diag1, gain, buffer):
    rows, width = own.shape
    args = [place, own, from_x, from_y, diag0, diag1, gain] + ([] if buffer is None else [buffer])
    return pl.pallas_call(
        functools.partial(norm_kernel, j),
        in_specs=[SMEM] + [VMEM] * (len(args) - 1),
        out_specs=VMEM,
        out_shape=jax.ShapeDtypeStruct((zs, 4, rows, width), BF16),
        input_output_aliases={} if buffer is None else {7: 0},
        compiler_params=pltpu.CompilerParams(vmem_limit_bytes=16 * MIB),
        cost_estimate=BRIEF,
        name="norm",
    )(*args)


def project_kernel(shifts, zs, count, place_ref, normed_ref, *refs):
    n = len(shifts)
    own, sib, rest = refs[:n], refs[n : 2 * n], refs[2 * n :]
    before, outs = rest[:-count], rest[-count:]
    z, core = place_ref[1], place_ref[2]
    depth = normed_ref.shape[3] // 2
    for part, out_ref in enumerate(outs):
        for j in range(zs):
            total = before[part][j] if before else None
            for i, shift in enumerate(shifts):
                block = lax.rem(z + zs - shift, zs)
                for k, w_ref in enumerate((own[i], sib[i])):
                    at = pl.multiple_of((core ^ k) * depth, depth)
                    left = normed_ref[j, block, :, pl.ds(at, depth)]
                    right = w_ref[part * depth : (part + 1) * depth, :]
                    term = jnp.dot(left, right, preferred_element_type=F32)
                    total = term if total is None else total + term
            out_ref[j] = total.astype(out_ref.dtype)


def project(place, normed, own, sib, shifts, count, rounded, before=()):
    zs, _, rows, _ = normed.shape
    cols = own[0].shape[1]
    args = [place, normed, *own, *sib, *before]
    return pl.pallas_call(
        functools.partial(project_kernel, shifts, zs, count),
        in_specs=[SMEM] + [VMEM] * (len(args) - 1),
        out_specs=[VMEM] * count,
        out_shape=[jax.ShapeDtypeStruct((zs, rows, cols), BF16 if rounded else F32)] * count,
        compiler_params=pltpu.CompilerParams(vmem_limit_bytes=16 * MIB),
        cost_estimate=BRIEF,
        name="project",
    )(*args)


NT = (((1,), (1,)), ((), ()))


def lanes(op, s):
    full = s.shape[1] - s.shape[1] % LANES
    rest = s[:, full:] if full < s.shape[1] else None
    return functools.reduce(op, [s[:, i : i + LANES] for i in range(0, full, LANES)]), rest


def attend_kernel(shifts, place_ref, q_ref, k_ref, v_ref, ks_ref, vs_ref, ck_ref, cv_ref, *refs):
    outs, (old, new) = refs[: len(shifts)], refs[len(shifts) :]
    z, core = place_ref[1], place_ref[2]
    zs, rows, cols = k_ref.shape
    heads = range(cols // HEAD)
    factor = 1.4426950408889634 / HEAD**0.5
    low = -1e30
    hcols = [slice(h * HEAD, (h + 1) * HEAD) for h in heads]
    row = lax.broadcasted_iota(jnp.int32, (rows, rows), 0)
    col = lax.broadcasted_iota(jnp.int32, (rows, rows), 1)
    causal = col <= row

    for shift, out_ref in zip(shifts, outs):
        block = lax.rem(z + shift, zs)
        mine = lax.rem(zs - shift, zs)
        queries = [q_ref[mine, :, hcol] for hcol in hcols]

        def score(b, tops, diagonal):
            at = lax.rem(z + zs - b, zs)
            result = []
            for h, top in zip(heads, tops):
                s = lax.dot_general(queries[h], k_ref[at, :, hcols[h]], NT, preferred_element_type=F32)
                t = lax.dot_general(queries[h], ks_ref[at, :, hcols[h]], NT, preferred_element_type=F32)
                if diagonal:
                    s, t = jnp.where(causal, s, low), jnp.where(core == 1, t, low)
                new[h, b, :, :rows] = s
                new[h, b, :, rows:] = t
                folded = jnp.maximum(lanes(jnp.maximum, s)[0], lanes(jnp.maximum, t)[0])
                result.append(jnp.maximum(top, folded))
            return tuple(result)

        tops, ends = [], []
        for h in heads:
            s = lax.dot_general(queries[h], ck_ref[:, hcols[h]], NT, preferred_element_type=F32)
            old[h] = s
            folded, rest = lanes(jnp.maximum, s)
            tops.append(folded)
            ends.append(low if rest is None else jnp.max(rest, axis=-1, keepdims=True))
        tops = lax.fori_loop(0, block, functools.partial(score, diagonal=False), tuple(tops))
        tops = score(block, tops, True)
        tops = [
            jnp.maximum(jnp.max(top, axis=-1, keepdims=True), end) * factor
            for top, end in zip(tops, ends)
        ]

        def weigh(b, state):
            at = lax.rem(z + zs - b, zs)
            result = []
            for h, (total, summed) in zip(heads, state):
                weights = jnp.exp2(new[h, b] * factor - tops[h])
                probs = weights.astype(BF16)
                summed += jnp.dot(probs[:, :rows], v_ref[at, :, hcols[h]], preferred_element_type=F32)
                summed += jnp.dot(probs[:, rows:], vs_ref[at, :, hcols[h]], preferred_element_type=F32)
                result.append((total + lanes(jnp.add, weights)[0], summed))
            return tuple(result)

        state, ends = [], []
        for h in heads:
            weights = jnp.exp2(old[h] * factor - tops[h])
            folded, rest = lanes(jnp.add, weights)
            ends.append(0.0 if rest is None else jnp.sum(rest, axis=-1, keepdims=True))
            state.append(
                (folded, jnp.dot(weights.astype(BF16), cv_ref[:, hcols[h]], preferred_element_type=F32))
            )
        state = lax.fori_loop(0, block + 1, weigh, tuple(state))
        for h, (total, summed), end in zip(heads, state, ends):
            total = jnp.sum(total, axis=-1, keepdims=True) + end
            out_ref[:, hcols[h]] = (summed / total).astype(BF16)


def attend(shifts, place, q, k, v, k_sib, v_sib, ck, cv):
    zs, rows, cols = q.shape
    heads = cols // HEAD
    return pl.pallas_call(
        functools.partial(attend_kernel, shifts),
        in_specs=[SMEM] + [VMEM] * 7,
        out_specs=[VMEM] * len(shifts),
        out_shape=[jax.ShapeDtypeStruct((rows, cols), BF16)] * len(shifts),
        scratch_shapes=[
            pltpu.VMEM((heads, rows, ck.shape[0]), F32),
            pltpu.VMEM((heads, zs, rows, 2 * rows), F32),
        ],
        compiler_params=pltpu.CompilerParams(vmem_limit_bytes=20 * MIB),
        cost_estimate=BRIEF,
        name="attend",
    )(place, q, k, v, k_sib, v_sib, ck, cv)


def pack_kernel(places, crow, *refs):
    parcels, outs, scratch = refs[: len(places)], refs[len(places) : -1], refs[-1]
    for n, out_ref in enumerate(outs):
        for i, (piece, at) in enumerate(zip(parcels, places)):
            at += n * (crow + PAD)
            scratch[i * crow : (i + 1) * crow, :] = piece[at : at + crow + PAD].astype(F32)[:crow]
        out_ref[...] = scratch[...].astype(BF16)


def pack(parcels, places, crow):
    out = (len(parcels) * crow, parcels[0].shape[1])
    return pl.pallas_call(
        functools.partial(pack_kernel, places, crow),
        in_specs=[VMEM] * len(parcels),
        out_specs=[VMEM] * 2,
        out_shape=[jax.ShapeDtypeStruct(out, BF16)] * 2,
        scratch_shapes=[pltpu.VMEM(out, F32)],
        compiler_params=pltpu.CompilerParams(vmem_limit_bytes=12 * MIB),
        cost_estimate=BRIEF,
        name="pack",
    )(*parcels)


def join_kernel(place_ref, *refs):
    pieces, out_ref = refs[:-1], refs[-1]
    zs = len(pieces)
    cols = pieces[0].shape[1]
    for r, piece in enumerate(pieces):
        at = lax.rem(place_ref[1] + zs - r, zs) * cols
        out_ref[:, pl.ds(pl.multiple_of(at, cols), cols)] = piece[...]


def join(place, pieces):
    rows, cols = pieces[0].shape
    out = (rows, cols * len(pieces))
    return pl.pallas_call(
        join_kernel,
        in_specs=[SMEM] + [VMEM] * len(pieces),
        out_specs=whole(out),
        out_shape=jax.ShapeDtypeStruct(out, BF16),
        name="join",
    )(place, *pieces)


def shift_z(value, steps, zs):
    pairs = [(2 * a + k, 2 * ((a + steps) % zs) + k) for a in range(zs) for k in range(2)]
    return lax.ppermute(value, "seq", pairs)


def swap_core(value, zs):
    return lax.ppermute(value, "seq", [(2 * a + k, 2 * a + 1 - k) for a in range(zs) for k in range(2)])


def swap_chan(value, bit):
    return lax.ppermute(value, "chan", [(c, c ^ bit) for c in range(4)])


def after(value, *others):
    return lax.optimization_barrier((value, *others))[0]


def fast_body(hyena_in, prior_kv, filters, gain, w_qkv, cache_k, cache_v):
    rows, _, width = hyena_in.shape
    seqs = lax.axis_size("seq")
    zs = seqs // 2
    taps = filters.shape[1]
    depth, crow = w_qkv.shape[0], cache_k.shape[0]
    cols = width // zs
    my_seq = lax.axis_index("seq")
    z, core = my_seq // 2, my_seq % 2
    chan = lax.axis_index("chan")
    place = jnp.stack([chan, z, core]).astype(jnp.int32)

    w_t = jnp.transpose(w_qkv, (1, 0, 2))
    caches = [jnp.pad(c, ((0, PAD), (0, 0))) for c in (cache_k, cache_v)]

    def parcel(kind, r, *others):
        at = (z + r) % zs * cols
        source = after(w_t, *others) if others else w_t
        parts = [
            lax.dynamic_slice(source, ("qkv".index(p), 0, at), (1, depth, cols))[0]
            for p in kind
            if p != "c"
        ]
        if kind == "v":
            parts.append(jnp.zeros((16, cols), BF16))
        if "c" in kind:
            parts += [lax.dynamic_slice_in_dim(c, at, cols, 1) for c in caches]
        return jnp.concatenate(parts, axis=0)

    hin = jnp.transpose(hyena_in, (1, 0, 2))
    tail = (hin[1, rows - taps :].astype(F32) * hin[2, rows - taps :].astype(F32)).astype(BF16)
    halo = lax.ppermute(tail, "seq", [(s, s + 1) for s in range(seqs - 1)])
    halo = jnp.where(my_seq == 0, jnp.pad(prior_kv, ((taps - prior_kv.shape[0], 0), (0, 0))), halo)

    order = ["q1", "q3", "acts", "kvc1", "acts", "kvc3", "acts", "q2", "kc2", "v2"]
    acts = [hyena(hin, halo, filters)]
    here = {kind + "0": parcel(kind, 0, acts[0]) for kind in ("kvc", "q")}
    sent = []
    for n, item in enumerate(order):
        if item == "acts":
            value, steps = acts[-1], 1
        else:
            kind, steps = item[:-1], int(item[-1])
            value = parcel(kind, steps, *acts[: int(n >= 2)])
        if n >= 2:
            value = after(value, sent[n - 2])
        sent.append(shift_z(value, steps, zs))
        if item == "acts":
            acts.append(sent[-1])
        else:
            here[item] = sent[-1]
    late = ["q2", "kc2", "v2"]
    there = {item: swap_core(here[item], zs) for item in here if item not in late}

    pace = [[], ["kvc1"], ["kvc3"], ["q2"]]
    swapped = [[], ["kvc0", "q0"], ["q1", "q3"], ["kvc1"]]
    gain4 = gain.reshape(4, 1, width)
    half = rows // 2
    normed, diag0, diag1 = None, None, None
    for j, own in enumerate(acts):
        own = after(own, *([diag0, diag1] if j else [here["q1"], here["q3"]]))
        from_x, from_y = swap_chan(own, 1), swap_chan(own, 2)
        if j:
            settled = [normed] + [there[item] for item in swapped[j]] + [here[item] for item in pace[j]]
            from_x, from_y = after(from_x, *settled), after(from_y, *settled)
        diag0 = swap_chan(from_x[:half], 2)
        diag1 = swap_chan(from_y[half:], 1)
        normed = norm(place, j, zs, own, from_x, from_y, diag0, diag1, gain4, normed)

    def sides(*items):
        return [[side[item] for item in items] for side in (here, there)]

    early = (0, 1, 3)
    there["q2"] = swap_core(after(here["q2"], normed), zs)
    (q,) = project(place, normed, *sides("q0", "q1", "q3", "q2"), early + (2,), 1, True)
    k_early, v_early = project(place, normed, *sides("kvc0", "kvc1", "kvc3"), early, 2, False)
    here["kc2"] = after(here["kc2"], k_early, v_early)
    there["kc2"], far_cache = swap_core(here["kc2"][:depth], zs), swap_core(here["kc2"][depth:], zs)
    kept = sum(sides("kvc0", "kvc1", "kvc3"), []) + [here["kc2"], far_cache]
    ck, cv = pack(kept, [2 * depth] * (2 * zs - 2) + [depth, 0], crow)
    (k,) = project(place, after(normed, q, ck), *sides("kc2"), (2,), 1, True, (k_early,))
    k_sib = swap_core(k, zs)
    there["v2"] = swap_core(after(here["v2"], k), zs)
    (v,) = project(place, normed, *sides("v2"), (2,), 1, True, (v_early,))
    v_sib = swap_core(v, zs)
    pieces, out = {}, None
    for shifts, wait in (((2,), ()), ((1, 3), ()), ((0,), (2,))):
        ready = q if out is None else after(q, out[0], *[pieces[r] for r in wait])
        out = attend(shifts, place, ready, k, v, k_sib, v_sib, ck, cv)
        for r, piece in zip(shifts, out):
            pieces[r] = shift_z(piece, r, zs) if r else piece
    return join(place, [pieces[r] for r in range(zs)])


def shifted(value, axis, steps):
    count = lax.axis_size(axis)
    leading, last = (max(0, -steps), min(count, count - steps))
    return lax.ppermute(value, axis, [(source, source + steps) for source in range(leading, last)])


def body(hyena_in, prior_kv, filters, gain, w_qkv, cache_k, cache_v):
    rows_dev = hyena_in.shape[0]
    width = hyena_in.shape[2]
    history = prior_kv.shape[0]
    tap_count = filters.shape[1]
    head_size = D // HEADS
    heads_dev = width // head_size
    cache_rows = cache_k.shape[0]
    stride = cache_rows + rows_dev
    my_index = lax.axis_index("seq")
    stream_q = hyena_in[:, 0].astype(jnp.float32)
    kv_prod = (hyena_in[:, 1].astype(jnp.float32) * hyena_in[:, 2].astype(jnp.float32)).astype(
        jnp.bfloat16
    )
    before = shifted(kv_prod[rows_dev - history :], "seq", 1)
    before = jnp.where(my_index == 0, prior_kv, before)
    extended = jnp.concatenate([before, kv_prod], axis=0).astype(jnp.float32)
    tap_table = jnp.repeat(filters, width // filters.shape[0], axis=0).T

    def add_tap(tap_index, total):
        offset = (tap_count - 1 - tap_index).astype(jnp.int32)
        window = lax.dynamic_slice_in_dim(extended, offset, rows_dev, 0)
        coeff = lax.dynamic_index_in_dim(tap_table, tap_index.astype(jnp.int32), 0, keepdims=True)
        return total + coeff * window

    conv = lax.fori_loop(0, tap_count, add_tap, jnp.zeros((rows_dev, width), jnp.float32))
    hyena_out = (stream_q * conv).astype(jnp.bfloat16)
    whole = lax.all_gather(hyena_out, "chan", axis=1, tiled=True)
    as_float = whole.astype(jnp.float32)
    mean_sq = jnp.mean(as_float * as_float, axis=-1, keepdims=True)
    normed = (as_float * lax.rsqrt(mean_sq + 1e-06) * gain[None, :]).astype(jnp.bfloat16)
    piece = lax.all_gather(w_qkv, "seq", axis=0, tiled=True)
    flat_piece = piece.reshape(piece.shape[0], 3 * width)
    projected = jnp.dot(normed, flat_piece, preferred_element_type=jnp.float32)
    qkv = projected.astype(jnp.bfloat16).reshape(rows_dev, 3, width)
    scale = 1.0 / head_size**0.5
    keys_local = jnp.concatenate([cache_k, qkv[:, 1]], axis=0)
    vals_local = jnp.concatenate([cache_v, qkv[:, 2]], axis=0)
    head_q = qkv[:, 0].reshape(rows_dev, heads_dev, head_size)
    query_pos = my_index * rows_dev + jnp.arange(rows_dev, dtype=jnp.int32)
    run_max = jnp.full((heads_dev, rows_dev), -1e30, jnp.float32)
    key_piece = lax.all_gather(keys_local, "seq", axis=0, tiled=True)
    val_piece = lax.all_gather(vals_local, "seq", axis=0, tiled=True)
    count = key_piece.shape[0]
    row_ids = jnp.arange(count, dtype=jnp.int32)
    source = row_ids // stride
    within = row_ids % stride
    key_pos = jnp.where(within < cache_rows, -1, source * rows_dev + within - cache_rows)
    visible = (key_pos[None, :] <= query_pos[:, None])[None]
    scores = (
        jnp.einsum(
            "qhd,khd->hqk",
            head_q,
            key_piece.reshape(count, heads_dev, head_size),
            preferred_element_type=jnp.float32,
        )
        * scale
    )
    scores = jnp.where(visible, scores, jnp.float32(-1e30))
    new_max = jnp.maximum(run_max, jnp.max(scores, axis=-1))
    weights = jnp.where(visible, jnp.exp(scores - new_max[..., None]), jnp.float32(0.0))
    new_sum = jnp.sum(weights, axis=-1)
    probs = weights.astype(jnp.bfloat16)
    added = jnp.einsum(
        "hqk,khd->hqd",
        probs,
        val_piece.reshape(count, heads_dev, head_size),
        preferred_element_type=jnp.float32,
    )
    result = jnp.transpose(added / new_sum[..., None], (1, 0, 2))
    return result.reshape(rows_dev, width).astype(jnp.bfloat16)


def solution(mesh):
    sizes = mesh.shape
    paired = sizes["chan"] == 4 and HEADS // sizes["chan"] == sizes["seq"]
    return jax.shard_map(
        fast_body if paired else body,
        mesh=mesh,
        in_specs=(
            P("seq", None, "chan"),
            P(None, "chan"),
            P("chan", None),
            P(),
            P("seq", None, "chan"),
            P("seq", "chan"),
            P("seq", "chan"),
        ),
        out_specs=P("seq", "chan"),
        check_vma=False,
    )
```

```python
import functools

import jax
import jax.numpy as jnp
from jax import lax
from jax.experimental import pallas as pl
from jax.experimental.pallas import tpu as pltpu
from jax.sharding import PartitionSpec as P

D = 4096
HEADS = 32
HEAD = D // HEADS
LANES = 128
PAD = 8
BF16 = jnp.bfloat16
F32 = jnp.float32
MIB = 1024 * 1024


BRIEF = pl.CostEstimate(flops=1, transcendentals=0, bytes_accessed=1)


VMEM = pl.BlockSpec(memory_space=pltpu.VMEM)
SMEM = pl.BlockSpec(memory_space=pltpu.SMEM)


def whole(shape):
    return pl.BlockSpec(shape, lambda *_: (0,) * len(shape))


def conv_kernel(group, hin_ref, halo_ref, taps_ref, out_ref):
    taps = taps_ref[...]
    count = taps.shape[0]
    width = taps.shape[1]
    kv = (hin_ref[1].astype(F32) * hin_ref[2].astype(F32)).astype(BF16)
    ext = jnp.concatenate([halo_ref[...], kv], axis=0)
    rows = kv.shape[0]
    blocks = rows // width
    windows = jnp.concatenate(
        [ext[b * width : (b + 2) * width] for b in range(blocks)], axis=1
    )
    high = taps.astype(BF16)
    low = (taps - high.astype(F32)).astype(BF16)
    source = lax.broadcasted_iota(jnp.int32, (width, 2 * width), 0)
    column = lax.broadcasted_iota(jnp.int32, (width, 2 * width), 1)
    flip = jnp.where(source + column == width, 1.0, 0.0).astype(BF16)
    total = None
    for part in (high, low):
        first = jnp.dot(part, flip, preferred_element_type=F32)
        toeplitz = jnp.concatenate(
            [
                pltpu.roll(
                    jnp.broadcast_to(first[g : g + 1], (width, 2 * width)),
                    0,
                    1,
                    stride=1,
                    stride_axis=0,
                ).astype(BF16)
                for g in range(count)
            ],
            axis=0,
        )
        product = jnp.dot(toeplitz, windows, preferred_element_type=F32)
        total = product if total is None else total + product
    owner = lax.broadcasted_iota(jnp.int32, (width, blocks * LANES), 1) % LANES // group
    conv = total[:width]
    for g in range(1, count):
        conv = jnp.where(owner == g, total[g * width : (g + 1) * width], conv)
    query = hin_ref[0].astype(F32)
    for b in range(blocks):
        piece = query[b * width : (b + 1) * width] * conv[:, b * LANES : (b + 1) * LANES]
        out_ref[b * width : (b + 1) * width, :] = piece.astype(BF16)


def hyena(hin, halo, filters):
    _, rows, width = hin.shape
    taps = filters.shape[1]
    group = width // filters.shape[0]
    per_tile = LANES // group
    return pl.pallas_call(
        functools.partial(conv_kernel, group),
        grid=(width // LANES,),
        in_specs=[
            pl.BlockSpec((3, rows, LANES), lambda i: (0, 0, i)),
            pl.BlockSpec((taps, LANES), lambda i: (0, i)),
            pl.BlockSpec((per_tile, taps), lambda i: (i, 0)),
        ],
        out_specs=pl.BlockSpec((rows, LANES), lambda i: (0, i)),
        out_shape=jax.ShapeDtypeStruct((rows, width), BF16),
        compiler_params=pltpu.CompilerParams(vmem_limit_bytes=12 * MIB),
        cost_estimate=BRIEF,
        name="hyena_filters",
    )(hin, halo, filters)


def norm_kernel(j, place_ref, own_ref, x_ref, y_ref, d0_ref, d1_ref, gain_ref, *rest):
    out_ref = rest[-1]
    chan = place_ref[0]
    half = d0_ref.shape[0]
    step = 16

    def band(i, diag_ref, start):
        at = pl.ds(pl.multiple_of(start + i * step, step), step)
        refs = (own_ref.at[at], x_ref.at[at], y_ref.at[at], diag_ref.at[pl.ds(pl.multiple_of(i * step, step), step)])
        parts = [r[...].astype(F32) for r in refs]
        total = sum(jnp.sum(p * p, axis=-1, keepdims=True) for p in parts)
        factor = lax.rsqrt(total / D + 1e-6)
        for m, p in enumerate(parts):
            where = chan ^ m
            out_ref[j, where, at, :] = (p * factor * gain_ref[where]).astype(BF16)

    for diag_ref, start in ((d0_ref, 0), (d1_ref, half)):
        pl.loop(0, half // step, unroll=2)(functools.partial(band, diag_ref=diag_ref, start=start))


def norm(place, j, zs, own, from_x, from_y, diag0, diag1, gain, buffer):
    rows, width = own.shape
    args = [place, own, from_x, from_y, diag0, diag1, gain] + ([] if buffer is None else [buffer])
    return pl.pallas_call(
        functools.partial(norm_kernel, j),
        in_specs=[SMEM] + [VMEM] * (len(args) - 1),
        out_specs=VMEM,
        out_shape=jax.ShapeDtypeStruct((zs, 4, rows, width), BF16),
        input_output_aliases={} if buffer is None else {7: 0},
        compiler_params=pltpu.CompilerParams(vmem_limit_bytes=16 * MIB),
        cost_estimate=BRIEF,
        name="norm",
    )(*args)


def project_kernel(shifts, zs, count, place_ref, normed_ref, *refs):
    n = len(shifts)
    own, sib, rest = refs[:n], refs[n : 2 * n], refs[2 * n :]
    before, outs = rest[:-count], rest[-count:]
    z, core = place_ref[1], place_ref[2]
    depth = normed_ref.shape[3] // 2
    for part, out_ref in enumerate(outs):
        for j in range(zs):
            total = before[part][j] if before else None
            for i, shift in enumerate(shifts):
                block = lax.rem(z + zs - shift, zs)
                for k, w_ref in enumerate((own[i], sib[i])):
                    at = pl.multiple_of((core ^ k) * depth, depth)
                    left = normed_ref[j, block, :, pl.ds(at, depth)]
                    right = w_ref[part * depth : (part + 1) * depth, :]
                    term = jnp.dot(left, right, preferred_element_type=F32)
                    total = term if total is None else total + term
            out_ref[j] = total.astype(out_ref.dtype)


def project(place, normed, own, sib, shifts, count, rounded, before=()):
    zs, _, rows, _ = normed.shape
    cols = own[0].shape[1]
    args = [place, normed, *own, *sib, *before]
    return pl.pallas_call(
        functools.partial(project_kernel, shifts, zs, count),
        in_specs=[SMEM] + [VMEM] * (len(args) - 1),
        out_specs=[VMEM] * count,
        out_shape=[jax.ShapeDtypeStruct((zs, rows, cols), BF16 if rounded else F32)] * count,
        compiler_params=pltpu.CompilerParams(vmem_limit_bytes=16 * MIB),
        cost_estimate=BRIEF,
        name="project",
    )(*args)


NT = (((1,), (1,)), ((), ()))


def attend_kernel(shifts, place_ref, q_ref, k_ref, v_ref, ks_ref, vs_ref, ck_ref, cv_ref, *refs):
    outs, (old, new) = refs[: len(shifts)], refs[len(shifts) :]
    z, core = place_ref[1], place_ref[2]
    zs, rows, cols = k_ref.shape
    heads = range(cols // HEAD)
    factor = 1.4426950408889634 / HEAD**0.5
    low = -1e30
    hcols = [slice(h * HEAD, (h + 1) * HEAD) for h in heads]
    row = lax.broadcasted_iota(jnp.int32, (rows, rows), 0)
    col = lax.broadcasted_iota(jnp.int32, (rows, rows), 1)
    causal = row <= col

    def score(key, query):
        return lax.dot_general(key, query, NT, preferred_element_type=F32)

    def mix(value, probs):
        return lax.dot_general(value, probs, (((0,), (0,)), ((), ())), preferred_element_type=F32)

    def fold(op, s):
        return op(s.reshape(s.shape[0] // 8, 8, s.shape[1]), axis=0)

    for shift, out_ref in zip(shifts, outs):
        block = lax.rem(z + shift, zs)
        mine = lax.rem(zs - shift, zs)
        queries = [q_ref[mine, :, hcol] for hcol in hcols]

        def scores(b, tops, diagonal):
            at = lax.rem(z + zs - b, zs)
            result = []
            for h, top in zip(heads, tops):
                s, t = score(k_ref[at, :, hcols[h]], queries[h]), score(ks_ref[at, :, hcols[h]], queries[h])
                if diagonal:
                    s, t = jnp.where(causal, s, low), jnp.where(core == 1, t, low)
                new[h, b, :rows] = s
                new[h, b, rows:] = t
                result.append(jnp.maximum(top, jnp.maximum(fold(jnp.max, s), fold(jnp.max, t))))
            return tuple(result)

        tops = []
        for h in heads:
            s = score(ck_ref[:, hcols[h]], queries[h])
            old[h] = s
            tops.append(fold(jnp.max, s))
        tops = lax.fori_loop(0, block, functools.partial(scores, diagonal=False), tuple(tops))
        tops = scores(block, tops, True)
        tops = [jnp.max(top, axis=0, keepdims=True) * factor for top in tops]

        def weigh(b, state):
            at = lax.rem(z + zs - b, zs)
            result = []
            for h, (total, summed) in zip(heads, state):
                weights = jnp.exp2(new[h, b] * factor - tops[h])
                probs = weights.astype(BF16)
                summed += mix(v_ref[at, :, hcols[h]], probs[:rows]) + mix(vs_ref[at, :, hcols[h]], probs[rows:])
                result.append((total + fold(jnp.sum, weights), summed))
            return tuple(result)

        state = []
        for h in heads:
            weights = jnp.exp2(old[h] * factor - tops[h])
            state.append((fold(jnp.sum, weights), mix(cv_ref[:, hcols[h]], weights.astype(BF16))))
        state = lax.fori_loop(0, block + 1, weigh, tuple(state))
        for h, (total, summed) in zip(heads, state):
            result = summed / jnp.sum(total, axis=0, keepdims=True)
            out_ref[:, hcols[h]] = result.T.astype(BF16)


def attend(shifts, place, q, k, v, k_sib, v_sib, ck, cv):
    zs, rows, cols = q.shape
    heads = cols // HEAD
    return pl.pallas_call(
        functools.partial(attend_kernel, shifts),
        in_specs=[SMEM] + [VMEM] * 7,
        out_specs=[VMEM] * len(shifts),
        out_shape=[jax.ShapeDtypeStruct((rows, cols), BF16)] * len(shifts),
        scratch_shapes=[
            pltpu.VMEM((heads, ck.shape[0], rows), F32),
            pltpu.VMEM((heads, zs, 2 * rows, rows), F32),
        ],
        compiler_params=pltpu.CompilerParams(vmem_limit_bytes=20 * MIB),
        cost_estimate=BRIEF,
        name="attend",
    )(place, q, k, v, k_sib, v_sib, ck, cv)


def pack_kernel(places, crow, *refs):
    parcels, outs, scratch = refs[: len(places)], refs[len(places) : -1], refs[-1]
    for n, out_ref in enumerate(outs):
        for i, (piece, at) in enumerate(zip(parcels, places)):
            at += n * (crow + PAD)
            scratch[i * crow : (i + 1) * crow, :] = piece[at : at + crow + PAD].astype(F32)[:crow]
        out_ref[...] = scratch[...].astype(BF16)


def pack(parcels, places, crow):
    out = (len(parcels) * crow, parcels[0].shape[1])
    return pl.pallas_call(
        functools.partial(pack_kernel, places, crow),
        in_specs=[VMEM] * len(parcels),
        out_specs=[VMEM] * 2,
        out_shape=[jax.ShapeDtypeStruct(out, BF16)] * 2,
        scratch_shapes=[pltpu.VMEM(out, F32)],
        compiler_params=pltpu.CompilerParams(vmem_limit_bytes=12 * MIB),
        cost_estimate=BRIEF,
        name="pack",
    )(*parcels)


def join_kernel(place_ref, *refs):
    pieces, out_ref = refs[:-1], refs[-1]
    zs = len(pieces)
    cols = pieces[0].shape[1]
    for r, piece in enumerate(pieces):
        at = lax.rem(place_ref[1] + zs - r, zs) * cols
        out_ref[:, pl.ds(pl.multiple_of(at, cols), cols)] = piece[...]


def join(place, pieces):
    rows, cols = pieces[0].shape
    out = (rows, cols * len(pieces))
    return pl.pallas_call(
        join_kernel,
        in_specs=[SMEM] + [VMEM] * len(pieces),
        out_specs=whole(out),
        out_shape=jax.ShapeDtypeStruct(out, BF16),
        name="join",
    )(place, *pieces)


def shift_z(value, steps, zs):
    pairs = [(2 * a + k, 2 * ((a + steps) % zs) + k) for a in range(zs) for k in range(2)]
    return lax.ppermute(value, "seq", pairs)


def swap_core(value, zs):
    return lax.ppermute(value, "seq", [(2 * a + k, 2 * a + 1 - k) for a in range(zs) for k in range(2)])


def swap_chan(value, bit):
    return lax.ppermute(value, "chan", [(c, c ^ bit) for c in range(4)])


def after(value, *others):
    return lax.optimization_barrier((value, *others))[0]


def fast_body(hyena_in, prior_kv, filters, gain, w_qkv, cache_k, cache_v):
    rows, _, width = hyena_in.shape
    seqs = lax.axis_size("seq")
    zs = seqs // 2
    taps = filters.shape[1]
    depth, crow = w_qkv.shape[0], cache_k.shape[0]
    cols = width // zs
    my_seq = lax.axis_index("seq")
    z, core = my_seq // 2, my_seq % 2
    chan = lax.axis_index("chan")
    place = jnp.stack([chan, z, core]).astype(jnp.int32)

    w_t = jnp.transpose(w_qkv, (1, 0, 2))
    caches = [jnp.pad(c, ((0, PAD), (0, 0))) for c in (cache_k, cache_v)]

    def parcel(kind, r, *others):
        at = (z + r) % zs * cols
        source = after(w_t, *others) if others else w_t
        parts = [
            lax.dynamic_slice(source, ("qkv".index(p), 0, at), (1, depth, cols))[0]
            for p in kind
            if p != "c"
        ]
        if kind == "v":
            parts.append(jnp.zeros((16, cols), BF16))
        if "c" in kind:
            parts += [lax.dynamic_slice_in_dim(c, at, cols, 1) for c in caches]
        return jnp.concatenate(parts, axis=0)

    hin = jnp.transpose(hyena_in, (1, 0, 2))
    tail = (hin[1, rows - taps :].astype(F32) * hin[2, rows - taps :].astype(F32)).astype(BF16)
    halo = lax.ppermute(tail, "seq", [(s, s + 1) for s in range(seqs - 1)])
    halo = jnp.where(my_seq == 0, jnp.pad(prior_kv, ((taps - prior_kv.shape[0], 0), (0, 0))), halo)

    order = ["q1", "q3", "acts", "kvc1", "acts", "kvc3", "acts", "q2", "kc2", "v2"]
    acts = [hyena(hin, halo, filters)]
    here = {kind + "0": parcel(kind, 0, acts[0]) for kind in ("kvc", "q")}
    sent = []
    for n, item in enumerate(order):
        if item == "acts":
            value, steps = acts[-1], 1
        else:
            kind, steps = item[:-1], int(item[-1])
            value = parcel(kind, steps, *acts[: int(n >= 2)])
        if n >= 2:
            value = after(value, sent[n - 2])
        sent.append(shift_z(value, steps, zs))
        if item == "acts":
            acts.append(sent[-1])
        else:
            here[item] = sent[-1]
    late = ["q2", "kc2", "v2"]
    there = {item: swap_core(here[item], zs) for item in here if item not in late}

    pace = [[], ["kvc1"], ["kvc3"], ["q2"]]
    swapped = [[], ["kvc0", "q0"], ["q1", "q3"], ["kvc1"]]
    gain4 = gain.reshape(4, 1, width)
    half = rows // 2
    normed, diag0, diag1 = None, None, None
    for j, own in enumerate(acts):
        own = after(own, *([diag0, diag1] if j else [here["q1"], here["q3"]]))
        from_x, from_y = swap_chan(own, 1), swap_chan(own, 2)
        if j:
            settled = [normed] + [there[item] for item in swapped[j]] + [here[item] for item in pace[j]]
            from_x, from_y = after(from_x, *settled), after(from_y, *settled)
        diag0 = swap_chan(from_x[:half], 2)
        diag1 = swap_chan(from_y[half:], 1)
        normed = norm(place, j, zs, own, from_x, from_y, diag0, diag1, gain4, normed)

    def sides(*items):
        return [[side[item] for item in items] for side in (here, there)]

    early = (0, 1, 3)
    there["q2"] = swap_core(after(here["q2"], normed), zs)
    (q,) = project(place, normed, *sides("q0", "q1", "q3", "q2"), early + (2,), 1, True)
    k_early, v_early = project(place, normed, *sides("kvc0", "kvc1", "kvc3"), early, 2, False)
    here["kc2"] = after(here["kc2"], k_early, v_early)
    there["kc2"], far_cache = swap_core(here["kc2"][:depth], zs), swap_core(here["kc2"][depth:], zs)
    kept = sum(sides("kvc0", "kvc1", "kvc3"), []) + [here["kc2"], far_cache]
    ck, cv = pack(kept, [2 * depth] * (2 * zs - 2) + [depth, 0], crow)
    (k,) = project(place, after(normed, q, ck), *sides("kc2"), (2,), 1, True, (k_early,))
    k_sib = swap_core(k, zs)
    there["v2"] = swap_core(after(here["v2"], k), zs)
    (v,) = project(place, normed, *sides("v2"), (2,), 1, True, (v_early,))
    v_sib = swap_core(v, zs)
    pieces, out = {}, None
    for shifts, wait in (((2,), ()), ((1, 3), ()), ((0,), (2,))):
        ready = q if out is None else after(q, out[0], *[pieces[r] for r in wait])
        out = attend(shifts, place, ready, k, v, k_sib, v_sib, ck, cv)
        for r, piece in zip(shifts, out):
            pieces[r] = shift_z(piece, r, zs) if r else piece
    return join(place, [pieces[r] for r in range(zs)])


def shifted(value, axis, steps):
    count = lax.axis_size(axis)
    leading, last = (max(0, -steps), min(count, count - steps))
    return lax.ppermute(value, axis, [(source, source + steps) for source in range(leading, last)])


def body(hyena_in, prior_kv, filters, gain, w_qkv, cache_k, cache_v):
    rows_dev = hyena_in.shape[0]
    width = hyena_in.shape[2]
    history = prior_kv.shape[0]
    tap_count = filters.shape[1]
    head_size = D // HEADS
    heads_dev = width // head_size
    cache_rows = cache_k.shape[0]
    stride = cache_rows + rows_dev
    my_index = lax.axis_index("seq")
    stream_q = hyena_in[:, 0].astype(jnp.float32)
    kv_prod = (hyena_in[:, 1].astype(jnp.float32) * hyena_in[:, 2].astype(jnp.float32)).astype(
        jnp.bfloat16
    )
    before = shifted(kv_prod[rows_dev - history :], "seq", 1)
    before = jnp.where(my_index == 0, prior_kv, before)
    extended = jnp.concatenate([before, kv_prod], axis=0).astype(jnp.float32)
    tap_table = jnp.repeat(filters, width // filters.shape[0], axis=0).T

    def add_tap(tap_index, total):
        offset = (tap_count - 1 - tap_index).astype(jnp.int32)
        window = lax.dynamic_slice_in_dim(extended, offset, rows_dev, 0)
        coeff = lax.dynamic_index_in_dim(tap_table, tap_index.astype(jnp.int32), 0, keepdims=True)
        return total + coeff * window

    conv = lax.fori_loop(0, tap_count, add_tap, jnp.zeros((rows_dev, width), jnp.float32))
    hyena_out = (stream_q * conv).astype(jnp.bfloat16)
    whole = lax.all_gather(hyena_out, "chan", axis=1, tiled=True)
    as_float = whole.astype(jnp.float32)
    mean_sq = jnp.mean(as_float * as_float, axis=-1, keepdims=True)
    normed = (as_float * lax.rsqrt(mean_sq + 1e-06) * gain[None, :]).astype(jnp.bfloat16)
    piece = lax.all_gather(w_qkv, "seq", axis=0, tiled=True)
    flat_piece = piece.reshape(piece.shape[0], 3 * width)
    projected = jnp.dot(normed, flat_piece, preferred_element_type=jnp.float32)
    qkv = projected.astype(jnp.bfloat16).reshape(rows_dev, 3, width)
    scale = 1.0 / head_size**0.5
    keys_local = jnp.concatenate([cache_k, qkv[:, 1]], axis=0)
    vals_local = jnp.concatenate([cache_v, qkv[:, 2]], axis=0)
    head_q = qkv[:, 0].reshape(rows_dev, heads_dev, head_size)
    query_pos = my_index * rows_dev + jnp.arange(rows_dev, dtype=jnp.int32)
    run_max = jnp.full((heads_dev, rows_dev), -1e30, jnp.float32)
    key_piece = lax.all_gather(keys_local, "seq", axis=0, tiled=True)
    val_piece = lax.all_gather(vals_local, "seq", axis=0, tiled=True)
    count = key_piece.shape[0]
    row_ids = jnp.arange(count, dtype=jnp.int32)
    source = row_ids // stride
    within = row_ids % stride
    key_pos = jnp.where(within < cache_rows, -1, source * rows_dev + within - cache_rows)
    visible = (key_pos[None, :] <= query_pos[:, None])[None]
    scores = (
        jnp.einsum(
            "qhd,khd->hqk",
            head_q,
            key_piece.reshape(count, heads_dev, head_size),
            preferred_element_type=jnp.float32,
        )
        * scale
    )
    scores = jnp.where(visible, scores, jnp.float32(-1e30))
    new_max = jnp.maximum(run_max, jnp.max(scores, axis=-1))
    weights = jnp.where(visible, jnp.exp(scores - new_max[..., None]), jnp.float32(0.0))
    new_sum = jnp.sum(weights, axis=-1)
    probs = weights.astype(jnp.bfloat16)
    added = jnp.einsum(
        "hqk,khd->hqd",
        probs,
        val_piece.reshape(count, heads_dev, head_size),
        preferred_element_type=jnp.float32,
    )
    result = jnp.transpose(added / new_sum[..., None], (1, 0, 2))
    return result.reshape(rows_dev, width).astype(jnp.bfloat16)


def solution(mesh):
    sizes = mesh.shape
    paired = sizes["chan"] == 4 and HEADS // sizes["chan"] == sizes["seq"]
    return jax.shard_map(
        fast_body if paired else body,
        mesh=mesh,
        in_specs=(
            P("seq", None, "chan"),
            P(None, "chan"),
            P("chan", None),
            P(),
            P("seq", None, "chan"),
            P("seq", "chan"),
            P("seq", "chan"),
        ),
        out_specs=P("seq", "chan"),
        check_vma=False,
    )
```
